32 devices in a mesh: dp: 8 (over y, x, core), seq: 4 (over z).
Axes of the slice: x: 2, y: 2, z: 4, core: 2. Of those that a mesh axis runs over, the one named last changes fastest.
Arguments:
- latents: bfloat16 [64, 256, 1152], P('dp', 'seq'), may hold values from -6 to 6
- condition: bfloat16 [64, 1152], P('dp'), may hold values from -6 to 6
- keep_order: int32 [64, 256], P('dp', 'seq'), may hold values from 0 to 63, as said below
- keep_count: int32 [64, 4], P('dp', 'seq'), may hold values from 16 to 48, as said below
- ada_weight: bfloat16 [1152, 6912], P('dp'), may hold values from -0.1875 to 0.1875
- ada_bias: bfloat16 [6912], replicated, may hold values from -3 to 3
- qkv_weight: bfloat16 [1152, 3456], P('dp'), may hold values from -0.1875 to 0.1875
- out_weight: bfloat16 [1152, 1152], P('dp'), may hold values from -0.75 to 0.75
- fc1_weight: bfloat16 [1152, 4608], P('dp'), may hold values from -0.1875 to 0.1875
- fc1_bias: bfloat16 [4608], replicated, may hold values from -3 to 3
- fc2_weight: bfloat16 [4608, 1152], P('dp'), may hold values from -0.09375 to 0.09375
- cotangent: bfloat16 [64, 256, 1152], P('dp', 'seq'), may hold values from -6 to 6
Outputs:
- block_out: bfloat16 [64, 256, 1152], P('dp', 'seq')
- latents_grad: float32 [64, 256, 1152], P('dp', 'seq')
- condition_grad: float32 [64, 1152], P('dp')
- ada_weight_grad: float32 [1152, 6912], P('dp', 'seq')
- ada_bias_grad: float32 [6912], replicated
- qkv_weight_grad: float32 [1152, 3456], P('dp', 'seq')
- out_weight_grad: float32 [1152, 1152], P('dp', 'seq')
- fc1_weight_grad: float32 [1152, 4608], P('dp', 'seq')
- fc1_bias_grad: float32 [4608], replicated
- fc2_weight_grad: float32 [4608, 1152], P('dp', 'seq')
- kept_total: int32 [1], replicated
The draws below stay inside these ranges and needn't reach their ends.
Inputs may be any that keep to these rules, and one draw needn't show every extreme that they name: `keep_order`: in each aligned block of 64 tokens of a latent, a permutation of 0 to 63. `keep_count`: every latent has one block with 48 kept tokens and another with 16.
All inputs are finite; a program needn't handle non-finite values.
Results may differ from the reference program's by a relative error of at most 0.014.
The reference program's roundings to bfloat16 on the way count: a program that leaves them out, or rounds other values in their place, can miss the bound.
Values may be sent and summed in bfloat16 or wider, within the bound.
No kernel may reach another device: no remote copies, remote signals or barrier semaphores. Data moves between devices by JAX's collectives and lax.ppermute only.
A program may use at most 256 MiB of HBM per device.

```python
import math
import jax
import jax.numpy as jnp
from jax import lax

D = 1152
HEADS = 16
HEAD = 72
FF = 4608
S = 256
L_DEV = 8
B = 64
BLOCKS = 4
ROWS = 64


def draw_keep_order(key, part):
    key = jax.random.fold_in(key, 11)
    row_keys = jax.random.split(key, B * BLOCKS)
    shuffled = jax.vmap(lambda one_key: jax.random.permutation(one_key, ROWS))(row_keys)
    return shuffled.reshape(B, S).astype(jnp.int32)


def draw_keep_count(key, part):
    key = jax.random.fold_in(key, 23)
    counts = jax.random.randint(key, (B, BLOCKS), ROWS // 4, 3 * ROWS // 4 + 1)
    latent_ids = lax.broadcasted_iota(jnp.int32, (B, BLOCKS), 0)
    block_ids = lax.broadcasted_iota(jnp.int32, (B, BLOCKS), 1)
    counts = jnp.where(block_ids == latent_ids % BLOCKS, 3 * ROWS // 4, counts)
    counts = jnp.where(block_ids == (latent_ids + 2) % BLOCKS, ROWS // 4, counts)
    return counts.astype(jnp.int32)


def level_of(stream_key, dims, cuts, low, largest):
    gain, own = 1.0, jax.random.fold_in(stream_key, 6)
    for axis_at, parts in cuts:
        heights = jnp.exp(jax.random.uniform(jax.random.fold_in(own, axis_at), (parts,), jnp.float32, low / len(cuts), largest / len(cuts)))
        gain = gain * jnp.repeat(heights, dims[axis_at] // parts).reshape([-1 if axis == axis_at else 1 for axis in range(len(dims))])
    return gain


def bell_draw(own_key, extent, width, limit, cuts=(), dtype=jnp.bfloat16):
    factor_of = level_of(own_key, extent, cuts, -0.22, 0.18) if cuts else 1.0
    values = jax.random.normal(own_key, extent, jnp.float32) * width * factor_of
    return jnp.minimum(jnp.maximum(values, -limit), limit).astype(dtype)


def setup_inputs(seed: int = 0) -> dict:
    key_of = jax.random.split(jax.random.key(seed), 13)
    return {
        "latents": bell_draw(key_of[0], (B, S, D), 1.0, 6.0, ((0, 8), (1, 4))),
        "condition": bell_draw(key_of[1], (B, D), 1.0, 6.0, ((0, 8),)),
        "keep_order": draw_keep_order(jax.random.fold_in(key_of[12], 71), 0),
        "keep_count": draw_keep_count(jax.random.fold_in(key_of[12], 71), 0),
        "ada_weight": bell_draw(key_of[4], (D, 6 * D), D ** -0.5, 0.1875, ((0, 8),)),
        "ada_bias": bell_draw(key_of[5], (6 * D,), 0.5, 3.0),
        "qkv_weight": bell_draw(key_of[6], (D, 3 * D), D ** -0.5, 0.1875, ((0, 8),)),
        "out_weight": bell_draw(key_of[7], (D, D), HEAD ** -0.5, 0.75, ((0, 8),)),
        "fc1_weight": bell_draw(key_of[8], (D, FF), D ** -0.5, 0.1875, ((0, 8),)),
        "fc1_bias": bell_draw(key_of[9], (FF,), 0.5, 3.0),
        "fc2_weight": bell_draw(key_of[10], (FF, D), FF ** -0.5, 0.09375, ((0, 8),)),
        "cotangent": bell_draw(key_of[11], (B, S, D), 1.0, 6.0, ((0, 8), (1, 4))),
    }


@jax.custom_vjp
def low(v):
    return lax.optimization_barrier(v.astype(jnp.bfloat16)).astype(jnp.float32)

@jax.custom_vjp
def low_back(v):
    return v

def low_keep(v):
    return (low(v), None)

def low_pass(kept, grad):
    return (grad,)

def back_keep(v):
    return (v, None)

def back_low(kept, grad):
    return (low(grad),)
low.defvjp(low_keep, low_pass)
low_back.defvjp(back_keep, back_low)
layer_eps = 1e-06
far_below = -1e+30
highest = lax.Precision.HIGHEST

def normalize(rows_in):
    center = rows_in - lax.optimization_barrier(jnp.mean(rows_in, axis=-1, keepdims=True))
    return center * lax.rsqrt(lax.optimization_barrier(jnp.mean(center * center, axis=-1, keepdims=True)) + layer_eps)

def kept_rows(order_rows, count_rows):
    live_slot = lax.broadcasted_iota(jnp.int32, order_rows.shape, order_rows.ndim - 1) < count_rows
    positions = lax.broadcasted_iota(jnp.int32, order_rows.shape + (order_rows.shape[-1],), order_rows.ndim)
    matched = (order_rows[..., None] == positions) & live_slot[..., None]
    return jnp.any(matched, axis=-2)

def block_forward(params, inputs, cond_rows, kept_mask):
    ada_w, ada_b, qkv_w, out_w, fc1_w, fc1_b, fc2_w = params
    group_size = inputs.shape[0]
    silu_cond = low(jax.nn.silu(cond_rows))
    modulation = low_back(jnp.dot(silu_cond, ada_w, precision=highest)) + ada_b
    shift_attn, scale_attn, gate_attn, shift_mlp, scale_mlp, gate_mlp = [part_rows[:, None, :] for part_rows in jnp.split(modulation, 6, axis=1)]
    normed_one = normalize(inputs)
    mixed_one = low(normed_one * (1.0 + scale_attn) + shift_attn)
    qkv_rows = low_back(low(jnp.einsum('gsd,df->gsf', mixed_one, qkv_w, precision=highest)))
    qkv_rows = qkv_rows.reshape(group_size, S, 3, HEADS, HEAD)
    queries = qkv_rows[:, :, 0]
    key_rows = qkv_rows[:, :, 1]
    values = qkv_rows[:, :, 2]
    logits = low_back(jnp.einsum('gqhe,gkhe->gqhk', queries, key_rows, precision=highest) * (1.0 / math.sqrt(HEAD)))
    logits = jnp.where(kept_mask[:, None, None, :], logits, far_below)
    peak = lax.optimization_barrier(jnp.max(logits, axis=-1, keepdims=True))
    raised = jnp.exp(logits - peak)
    probabilities = raised / lax.optimization_barrier(jnp.sum(raised, axis=-1, keepdims=True))
    attended = jnp.einsum('gqhk,gkhe->gqhe', probabilities, values, precision=highest)
    attended = low_back(low(attended.reshape(group_size, S, D)))
    projected = low_back(jnp.einsum('gsd,df->gsf', attended, out_w, precision=highest))
    hidden_res = inputs + gate_attn * projected
    normed_two = normalize(hidden_res)
    mixed_two = low(normed_two * (1.0 + scale_mlp) + shift_mlp)
    pre_act = low_back(jnp.einsum('gsd,df->gsf', mixed_two, fc1_w, precision=highest) + fc1_b)
    activated = low(jax.nn.gelu(pre_act, approximate=True))
    mlp_out = low_back(jnp.einsum('gsf,fd->gsd', activated, fc2_w, precision=highest))
    block_res = hidden_res + gate_mlp * mlp_out
    return jnp.where(kept_mask[..., None], block_res, inputs)

def reference(latents, condition, keep_order, keep_count, ada_weight, ada_bias, qkv_weight, out_weight, fc1_weight, fc1_bias, fc2_weight, cotangent):
    params = tuple((weight_in.astype(jnp.float32) for weight_in in (ada_weight, ada_bias, qkv_weight, out_weight, fc1_weight, fc1_bias, fc2_weight)))
    group_count = B // L_DEV
    kept_all = kept_rows(keep_order.reshape(B, BLOCKS, ROWS), keep_count[..., None]).reshape(group_count, L_DEV, S)
    input_groups = latents.astype(jnp.float32).reshape(group_count, L_DEV, S, D)
    cond_groups = condition.astype(jnp.float32).reshape(group_count, L_DEV, D)
    grad_groups = cotangent.astype(jnp.float32).reshape(group_count, L_DEV, S, D)

    def group_step(running, sample_group):
        inputs, cond_rows, kept_mask, grad_out = sample_group
        output_rows, pullback = jax.vjp(lambda weights_in, rows_in, conds_in: block_forward(weights_in, rows_in, conds_in, kept_mask), params, inputs, cond_rows)
        grad_params, grad_inputs, grad_cond = pullback(grad_out)
        running = jax.tree.map(lambda left_sum, right_sum: left_sum + right_sum, running, grad_params)
        return (running, (output_rows.astype(jnp.bfloat16), grad_inputs, grad_cond))
    empty_sums = jax.tree.map(jnp.zeros_like, params)
    totals, (outputs, grad_inputs, grad_conds) = lax.scan(group_step, empty_sums, (input_groups, cond_groups, kept_all, grad_groups))
    kept_total = jnp.sum(keep_count).reshape(1).astype(jnp.int32)
    return (outputs.reshape(B, S, D), grad_inputs.reshape(B, S, D), grad_conds.reshape(B, D), totals[0], totals[1], totals[2], totals[3], totals[4], totals[5], totals[6], kept_total)
```

```python
import functools
import math

import jax
import jax.numpy as jnp
from jax import lax
from jax.experimental import pallas as pl
from jax.experimental.pallas import tpu as pltpu
from jax.sharding import PartitionSpec as P

HEADS = 16
HEAD = 72
LANES = 128
BLOCKS = 8

layer_eps = 1e-06
far_below = -1e30
att_scale = 1.0 / math.sqrt(HEAD)
gelu_c = math.sqrt(2.0 / math.pi)
gelu_k = 0.044715

BF = jnp.bfloat16
F32 = jnp.float32
VMEM = pl.BlockSpec(memory_space=pltpu.VMEM)
SMEM = pl.BlockSpec(memory_space=pltpu.SMEM)
ANY = pl.BlockSpec(memory_space=pl.ANY)
NT = (((1,), (1,)), ((), ()))
TN = (((0,), (0,)), ((), ()))


def swap(value, axis, step):
    return lax.ppermute(value, axis, [(i, i ^ step) for i in range(lax.axis_size(axis))])


def steps_of(axis):
    count = lax.axis_size(axis)
    return [1 << i for i in range(count.bit_length() - 1)]


def bit_set(axis, step):
    return (lax.axis_index(axis) & step) != 0


def gather_all(value, axis):
    value = value[None]
    for step in steps_of(axis):
        other = swap(value, axis, step)
        high = bit_set(axis, step)
        value = jnp.concatenate(
            [jnp.where(high, other, value), jnp.where(high, value, other)], axis=0
        )
    return value


def sum_own(value, axis):
    for step in reversed(steps_of(axis)):
        high = bit_set(axis, step)
        low_half, high_half = value[:step], value[step:]
        kept = jnp.where(high, high_half, low_half)
        value = kept + swap(jnp.where(high, low_half, high_half), axis, step)
    return value[0]


def trade_all(value, axis):
    count = value.shape[0]
    rest = value.shape[1:]
    for step in steps_of(axis):
        high = bit_set(axis, step)
        split = value.reshape((count // (2 * step), 2, step) + rest)
        low_half, high_half = split[:, 0], split[:, 1]
        kept = jnp.where(high, high_half, low_half)
        other = swap(jnp.where(high, low_half, high_half), axis, step)
        value = jnp.stack(
            [jnp.where(high, other, kept), jnp.where(high, kept, other)], axis=1
        ).reshape((count,) + rest)
    return value


def sum_everywhere(value):
    for axis in ("dp", "seq"):
        for step in steps_of(axis):
            value = value + swap(value, axis, step)
    return value


def after(value, *earlier):
    return lax.optimization_barrier((value,) + earlier)[0]


def halves_of(rows):
    first = (rows // 2 + 15) // 16 * 16
    return first, rows - first


def gather_weight(shard, first_after=(), second_after=()):
    rows = shard.shape[0]
    part, _ = halves_of(rows)
    if first_after:
        shard = after(shard, *first_after)
    beside_x = swap(shard, "dp", 2)
    beside_y = swap(shard, "dp", 4)
    own_pair = swap(shard, "dp", 1)
    across_a = swap(beside_y[:part], "dp", 2)
    across_b = swap(beside_x[part:], "dp", 4)
    held = [
        (shard, 0, 0),
        (beside_x, 2, 0),
        (beside_y, 4, 0),
        (across_a, 6, 0),
        (across_b, 6, part),
    ]
    pairs = [
        (own_pair, 1, 0),
        (swap(beside_x, "dp", 1), 3, 0),
        (swap(beside_y, "dp", 1), 5, 0),
        (swap(across_a, "dp", 1), 7, 0),
        (swap(across_b, "dp", 1), 7, part),
    ]
    return held + pairs, (beside_x, beside_y), (across_a, across_b)


def whole_weight(shard):
    full = lax.all_gather(shard, "dp", axis=0, tiled=True)
    rows = full.shape[0] // BLOCKS
    return [(full[k * rows : (k + 1) * rows], k, 0) for k in range(BLOCKS)]


def offsets_of(pieces, position, rows):
    return jnp.stack([position(k) * rows + first for _, k, first in pieces]).astype(jnp.int32)


def call(kernel, outs, ins, specs, scratch, flops, name):
    moved = sum(v.size * v.dtype.itemsize for v in ins) + sum(
        v.size * v.dtype.itemsize for v in jax.tree.leaves(outs)
    )
    return pl.pallas_call(
        kernel,
        out_shape=outs,
        in_specs=specs,
        out_specs=jax.tree.map(lambda _: VMEM, outs),
        scratch_shapes=scratch,
        name=name,
        cost_estimate=pl.CostEstimate(
            flops=int(flops), bytes_accessed=int(moved), transcendentals=0
        ),
        compiler_params=pltpu.CompilerParams(vmem_limit_bytes=56 * 1024 * 1024),
    )(*ins)


def start_pieces(offsets, refs, target, sem, lo, hi):
    copies = []
    for k, ref in enumerate(refs):
        rows = ref.shape[0]
        copies.append(
            pltpu.make_async_copy(
                ref.at[:, pl.ds(lo, hi - lo)],
                target.at[pl.ds(pl.multiple_of(offsets[k], 16), rows), :],
                sem.at[k],
            )
        )
    for one in copies:
        one.start()
    return copies


def wait_all(copies):
    for one in copies:
        one.wait()


def normal(rows_in):
    center = rows_in - jnp.mean(rows_in, axis=-1, keepdims=True)
    inverse = lax.rsqrt(jnp.mean(center * center, axis=-1, keepdims=True) + layer_eps)
    return center * inverse, inverse


def normal_back(grad_rows, normed, inverse):
    mean_grad = jnp.mean(grad_rows, axis=-1, keepdims=True)
    mean_proj = jnp.mean(grad_rows * normed, axis=-1, keepdims=True)
    return inverse * (grad_rows - mean_grad - normed * mean_proj)


def dot(left, right, dims=None):
    if dims is None:
        return jnp.dot(left, right, preferred_element_type=F32)
    return lax.dot_general(left, right, dims, preferred_element_type=F32)


def spans(total, width):
    return [(lo, min(lo + width, total)) for lo in range(0, total, width)]


def pack_rows(place_ref, piece_refs, latent, rows_out):
    gathered = jnp.concatenate([ref[latent] for ref in piece_refs], axis=0)
    slots = lax.broadcasted_iota(jnp.int32, (rows_out, gathered.shape[0]), 0)
    chosen = jnp.where(place_ref[latent] == slots, 1.0, 0.0).astype(BF)
    return dot(chosen, gathered)


def unpack_rows(place_ref, piece_refs, latent, packed, out_refs):
    rows_out = packed.shape[0]
    place = place_ref[latent]
    slots = lax.broadcasted_iota(jnp.int32, (place.shape[0], rows_out), 1)
    chosen = jnp.where(place == slots, 1.0, 0.0).astype(BF)
    spread = dot(chosen, packed)
    block = piece_refs[0].shape[1]
    for k, (piece, out) in enumerate(zip(piece_refs, out_refs)):
        here = slice(k * block, (k + 1) * block)
        out[latent] = jnp.where(
            place[here] >= 0, spread[here], piece[latent].astype(F32)
        ).astype(BF)


def split_parity(rows_low, order_ref, own_ref, other_ref):
    moved = dot(rows_low, order_ref[...]).astype(BF)
    width = own_ref.shape[1]
    own_ref[...] = moved[:, :width]
    other_ref[...] = moved[:, width:]


def enter_kernel(pieces, blocks, cap, *refs):
    (offsets, place, mod, order), refs = refs[:4], refs[4:]
    latents, refs = refs[:blocks], refs[blocks:]
    weights, refs = refs[:pieces], refs[pieces:]
    packed_out, qkv_out, own_out, other_out, weight, mixed, sem = refs
    width = qkv_out.shape[1]
    copies = start_pieces(offsets, weights, weight, sem, 0, width)
    for latent in range(mod.shape[0]):
        here = pl.ds(latent * cap, cap)
        rows = pack_rows(place, latents, latent, cap)
        packed_out[here, :] = rows.astype(BF)
        normed, _ = normal(rows)
        mixed[here, :] = (normed * (1.0 + mod[latent, 1:2, :]) + mod[latent, 0:1, :]).astype(BF)
    split_parity(mixed[...], order, own_out, other_out)
    wait_all(copies)
    for lo, hi in spans(width, 768):
        qkv_out[:, lo:hi] = dot(mixed[...], weight[:, lo:hi]).astype(BF)


def cot_kernel(blocks, cap, *refs):
    place, mod = refs[:2]
    cots = refs[2 : 2 + blocks]
    packed_out, mlp_out = refs[2 + blocks :]
    for latent in range(mod.shape[0]):
        here = pl.ds(latent * cap, cap)
        rows = pack_rows(place, cots, latent, cap)
        packed_out[here, :] = rows.astype(BF)
        mlp_out[here, :] = (mod[latent, 5:6, :] * rows).astype(BF)


def windows():
    found = []
    for head in range(HEADS):
        first = head * HEAD
        base = first // LANES * LANES
        width = LANES if first + HEAD <= base + LANES else 2 * LANES
        found.append((base, width, first - base))
    return found


def head_mask(width, first, dtype):
    lane = lax.broadcasted_iota(jnp.int32, (1, width), 1)
    return jnp.where((lane >= first) & (lane < first + HEAD), 1.0, 0.0).astype(dtype)


def attend_kernel(pieces, cap, model, *refs):
    (offsets, live, qkv, packed, mod, order), refs = refs[:6], refs[6:]
    weights, refs = refs[:pieces], refs[pieces:]
    (own_att, other_att, proj_out, hidden_out, mixed_out, own_mix, other_mix), refs = (
        refs[:7],
        refs[7:],
    )
    weight, attended, sem = refs
    copies = start_pieces(offsets, weights, weight, sem, 3 * model, 4 * model)
    attended[...] = jnp.zeros_like(attended)

    def one_latent(latent, carry):
        here = pl.ds(pl.multiple_of(latent * cap, 16), cap)
        count = live[latent]
        seen = lax.broadcasted_iota(jnp.int32, (cap, cap), 1) < count
        for base, width, first in windows():
            low_mask = head_mask(width, first, BF)
            query = qkv[here, base : base + width] * low_mask
            key = qkv[here, model + base : model + base + width]
            value = qkv[here, 2 * model + base : 2 * model + base + width]
            scores = jnp.where(seen, dot(query, key, NT) * att_scale, far_below)
            raised = jnp.exp(scores - jnp.max(scores, axis=-1, keepdims=True))
            total = jnp.sum(raised, axis=-1, keepdims=True)
            mixed = dot(raised.astype(BF), value) / total
            attended[here, base : base + width] += mixed * head_mask(width, first, F32)
        return carry

    lax.fori_loop(0, mod.shape[0], one_latent, 0)
    att_low = attended[...].astype(BF)
    split_parity(att_low, order, own_att, other_att)
    wait_all(copies)
    projected = dot(att_low, weight[...])
    proj_out[...] = projected
    for latent in range(mod.shape[0]):
        rows = slice(latent * cap, (latent + 1) * cap)
        hidden = packed[rows, :].astype(F32) + mod[latent, 2:3, :] * projected[rows]
        hidden_out[rows, :] = hidden
        normed, _ = normal(hidden)
        mixed_out[rows, :] = (
            normed * (1.0 + mod[latent, 4:5, :]) + mod[latent, 3:4, :]
        ).astype(BF)
    split_parity(mixed_out[...], order, own_mix, other_mix)


def first_kernel(pieces, *refs):
    (offsets, parity, mixed, bias), refs = refs[:4], refs[4:]
    weights, refs = refs[:pieces], refs[pieces:]
    own_act, other_act, own_slope, other_slope, weight, sem = refs
    copies = start_pieces(offsets, weights, weight, sem, 0, weight.shape[1])
    half = own_act.shape[1]
    wait_all(copies)
    for side, (act_out, slope_out) in enumerate(
        ((own_act, own_slope), (other_act, other_slope))
    ):
        base = (parity[0] ^ side) * half
        for lo, hi in spans(half, 768):
            cols = pl.ds(pl.multiple_of(base + lo, LANES), hi - lo)
            pre = dot(mixed[...], weight[:, cols]) + bias[:, cols]
            square = pre * pre
            curve = jnp.tanh(gelu_c * pre * (1.0 + gelu_k * square))
            cdf = 0.5 * (1.0 + curve)
            act_out[:, lo:hi] = (pre * cdf).astype(BF)
            slope = cdf + pre * (0.5 * gelu_c) * (1.0 - curve * curve) * (
                1.0 + 3.0 * gelu_k * square
            )
            slope_out[:, lo:hi] = slope.astype(BF)


def second_kernel(pieces, blocks, cap, *refs):
    (
        offsets,
        own_act,
        other_act,
        own_slope,
        other_slope,
        grad_mlp,
        grad_out,
        hidden,
        mod,
        place,
    ), refs = refs[:10], refs[10:]
    latents, refs = refs[:blocks], refs[blocks:]
    weights, refs = refs[:pieces], refs[pieces:]
    outs, refs = refs[:blocks], refs[blocks:]
    own_pre, other_pre, own_bias, other_bias, gate_grad, weight, sem = refs
    copies = start_pieces(offsets, weights, weight, sem, 0, weight.shape[1])
    half = own_act.shape[1]
    wait_all(copies)
    for side, (slope, pre_out, bias_out) in enumerate(
        ((own_slope, own_pre, own_bias), (other_slope, other_pre, other_bias))
    ):
        for lo, hi in spans(half, 768):
            grad_act = dot(grad_mlp[...], weight[side * half + lo : side * half + hi, :], NT)
            grad_pre = (grad_act * slope[:, lo:hi].astype(F32)).astype(BF)
            pre_out[:, lo:hi] = grad_pre
            bias_out[:, lo:hi] = jnp.sum(grad_pre.astype(F32), axis=0, keepdims=True)
    mlp = dot(own_act[...], weight[:half, :]) + dot(other_act[...], weight[half:, :])
    for latent in range(mod.shape[0]):
        rows = slice(latent * cap, (latent + 1) * cap)
        gate_grad[latent, :, :] = jnp.sum(
            grad_out[rows, :].astype(F32) * mlp[rows], axis=0, keepdims=True
        )
        block = (hidden[rows, :] + mod[latent, 5:6, :] * mlp[rows]).astype(BF)
        unpack_rows(place, latents, latent, block, outs)


def hidden_kernel(pieces, first_pieces, cap, model, *refs):
    (
        first_offsets,
        offsets,
        parity,
        own_pre,
        other_pre,
        hidden_in,
        projected,
        grad_out,
        mod,
    ), refs = refs[:9], refs[9:]
    first_weights, refs = refs[:first_pieces], refs[first_pieces:]
    out_weights, refs = refs[:pieces], refs[pieces:]
    grad_hidden, grad_proj, grad_att, mod_grads, first, out_weight, first_sem, out_sem = refs
    copies = start_pieces(first_offsets, first_weights, first, first_sem, 0, first.shape[1])
    later = start_pieces(offsets, out_weights, out_weight, out_sem, 3 * model, 4 * model)
    half = own_pre.shape[1]
    wait_all(copies)
    total = None
    for side, pre in enumerate((own_pre, other_pre)):
        base = (parity[0] ^ side) * half
        for lo, hi in spans(half, 768):
            cols = pl.ds(pl.multiple_of(base + lo, LANES), hi - lo)
            part = dot(pre[:, lo:hi], first[:, cols], NT)
            total = part if total is None else total + part
    for latent in range(mod.shape[0]):
        rows = slice(latent * cap, (latent + 1) * cap)
        normed, inverse = normal(hidden_in[rows, :])
        grad_mixed = total[rows]
        mod_grads[latent, 0:1, :] = jnp.sum(grad_mixed, axis=0, keepdims=True)
        mod_grads[latent, 1:2, :] = jnp.sum(grad_mixed * normed, axis=0, keepdims=True)
        grad = grad_out[rows, :].astype(F32) + normal_back(
            grad_mixed * (1.0 + mod[latent, 4:5, :]), normed, inverse
        )
        grad_hidden[rows, :] = grad
        mod_grads[latent, 2:3, :] = jnp.sum(grad * projected[rows, :], axis=0, keepdims=True)
        grad_proj[rows, :] = (mod[latent, 2:3, :] * grad).astype(BF)
    wait_all(later)
    grad_att[...] = dot(grad_proj[...], out_weight[...], NT).astype(BF)


def attend_back_kernel(cap, model, *refs):
    live, qkv, grad_att, grad_qkv, sums = refs
    sums[...] = jnp.zeros_like(sums)

    def one_latent(latent, carry):
        here = pl.ds(pl.multiple_of(latent * cap, 16), cap)
        count = live[latent]
        seen = lax.broadcasted_iota(jnp.int32, (cap, cap), 0) < count
        for base, width, first in windows():
            low_mask = head_mask(width, first, BF)
            wide_mask = head_mask(width, first, F32)
            cols = slice(base, base + width)
            key_cols = slice(model + base, model + base + width)
            value_cols = slice(2 * model + base, 2 * model + base + width)
            query, key, value = qkv[here, cols], qkv[here, key_cols], qkv[here, value_cols]
            grad = grad_att[here, cols]
            scores = jnp.where(seen, dot(key * low_mask, query, NT) * att_scale, far_below)
            raised = jnp.exp(scores - jnp.max(scores, axis=0, keepdims=True))
            probs = raised / jnp.sum(raised, axis=0, keepdims=True)
            grad_probs = dot(value * low_mask, grad, NT)
            delta = jnp.sum(probs * grad_probs, axis=0, keepdims=True)
            grad_scores = (probs * (grad_probs - delta)).astype(BF)
            scaled = wide_mask * att_scale
            sums[here, cols] += dot(grad_scores, key, TN) * scaled
            sums[here, key_cols] += dot(grad_scores, query) * scaled
            sums[here, value_cols] += dot(probs.astype(BF), grad) * wide_mask
        return carry

    lax.fori_loop(0, live.shape[0], one_latent, 0)
    grad_qkv[...] = sums[...].astype(BF)


def leave_kernel(pieces, blocks, cap, *refs):
    (offsets, grad_qkv, packed, grad_hidden, mod, place), refs = refs[:6], refs[6:]
    cots, refs = refs[:blocks], refs[blocks:]
    weights, refs = refs[:pieces], refs[pieces:]
    outs, refs = refs[:blocks], refs[blocks:]
    mod_grads, weight, sem = refs
    copies = start_pieces(offsets, weights, weight, sem, 0, weight.shape[1])
    wait_all(copies)
    total = None
    for lo, hi in spans(weight.shape[1], 768):
        part = dot(grad_qkv[:, lo:hi], weight[:, lo:hi], NT)
        total = part if total is None else total + part
    for latent in range(mod.shape[0]):
        rows = slice(latent * cap, (latent + 1) * cap)
        normed, inverse = normal(packed[rows, :].astype(F32))
        grad_mixed = total[rows]
        mod_grads[latent, 0:1, :] = jnp.sum(grad_mixed, axis=0, keepdims=True)
        mod_grads[latent, 1:2, :] = jnp.sum(grad_mixed * normed, axis=0, keepdims=True)
        grad = grad_hidden[rows, :] + normal_back(
            grad_mixed * (1.0 + mod[latent, 1:2, :]), normed, inverse
        )
        unpack_rows(place, cots, latent, grad.astype(BF), outs)


def outer_kernel(rows, used, sides, *refs):
    (block_at, own_left, pair_left), refs = refs[:3], refs[3:]
    own_rights, refs = refs[:sides], refs[sides:]
    pair_rights, refs = refs[:sides], refs[sides:]
    (send_x, send_y, keep, keep_x, keep_y), refs = refs[:5], refs[5:]
    result, sem = refs
    part, rest = halves_of(rows)
    left = jnp.concatenate([own_left[:, :used], pair_left[:, :used]], axis=0)
    base = 0
    for own, pair in zip(own_rights, pair_rights):
        width = own.shape[1]
        for lo, hi in spans(width, 768):
            right = jnp.concatenate([own[:, lo:hi], pair[:, lo:hi]], axis=0)
            result[:, base + lo : base + hi] = dot(left, right, TN).astype(BF)
        base += width

    def rows_at(k, first, count):
        return result.at[pl.ds(pl.multiple_of(block_at[k] * rows + first, 16), count), :]

    moves = [
        (rows_at(1, 0, part), send_x.at[0]),
        (rows_at(3, 0, part), send_x.at[1]),
        (rows_at(2, part, rest), send_y.at[0]),
        (rows_at(3, part, rest), send_y.at[1]),
        (rows_at(0, 0, rows), keep),
        (rows_at(1, part, rest), keep_x),
        (rows_at(2, 0, part), keep_y),
    ]
    copies = [pltpu.make_async_copy(a, b, sem.at[i]) for i, (a, b) in enumerate(moves)]
    for one in copies:
        one.start()
    wait_all(copies)


def outer_pair(own_left, pair_left, own_rights, pair_rights, rows, name):
    used = 4 * rows
    part, rest = halves_of(rows)
    width = sum(v.shape[1] for v in own_rights)
    block_at = jnp.stack([(lax.axis_index("dp") ^ (2 * k)) // 2 for k in range(4)]).astype(jnp.int32)
    ins = [block_at, own_left, pair_left, *own_rights, *pair_rights]
    specs = [SMEM] + [VMEM] * (len(ins) - 1)
    outs = (
        jax.ShapeDtypeStruct((2, part, width), BF),
        jax.ShapeDtypeStruct((2, rest, width), BF),
        jax.ShapeDtypeStruct((rows, width), BF),
        jax.ShapeDtypeStruct((rest, width), BF),
        jax.ShapeDtypeStruct((part, width), BF),
    )
    return pl.pallas_call(
        functools.partial(outer_kernel, rows, used, len(own_rights)),
        out_shape=outs,
        in_specs=specs,
        out_specs=tuple(ANY for _ in outs),
        scratch_shapes=[pltpu.VMEM((used, width), BF), pltpu.SemaphoreType.DMA((7,))],
        name=name,
        cost_estimate=pl.CostEstimate(
            flops=2 * used * width * own_left.shape[0] * 2,
            bytes_accessed=2 * (2 * used * width),
            transcendentals=0,
        ),
        compiler_params=pltpu.CompilerParams(vmem_limit_bytes=56 * 1024 * 1024),
    )(*ins)


def spread_blocks(cut, rows):
    send_x, send_y, keep, keep_x, keep_y = cut
    part, _ = halves_of(rows)
    from_x = swap(send_x, "dp", 2)
    from_y = swap(send_y, "dp", 4)
    on_y = (keep_y.astype(F32) + from_x[1].astype(F32)).astype(BF)
    on_x = (keep_x.astype(F32) + from_y[1].astype(F32)).astype(BF)
    last_y = swap(on_y, "dp", 4)
    last_x = swap(on_x, "dp", 2)
    near = jnp.concatenate([from_x[0], from_y[0]], axis=0).astype(F32)
    far = jnp.concatenate([last_y, last_x], axis=0).astype(F32)
    return keep.astype(F32) + near + far


def spread_columns(block, cut_columns):
    count = lax.axis_size("seq")
    at = lax.axis_index("seq")
    parts = jnp.stack([cut_columns(block, j) for j in range(count)])
    low_parts = parts.astype(BF)
    total = lax.dynamic_index_in_dim(parts, at, 0, keepdims=False)
    for step in range(1, count):
        piece = lax.dynamic_index_in_dim(low_parts, at ^ step, 0, keepdims=False)
        total = total + swap(piece, "seq", step).astype(F32)
    return total


def plain_columns(block, j):
    width = block.shape[1] // lax.axis_size("seq")
    return block[:, j * width : (j + 1) * width]


def spread_plain(grad):
    grad = lax.psum_scatter(grad, "dp", scatter_dimension=0, tiled=True)
    return lax.psum_scatter(grad, "seq", scatter_dimension=1, tiled=True)


def body(
    latents,
    condition,
    keep_order,
    keep_count,
    ada_weight,
    ada_bias,
    qkv_weight,
    out_weight,
    fc1_weight,
    fc1_bias,
    fc2_weight,
    cotangent,
):
    latent_count, block_rows, model = latents.shape
    hidden_units = fc1_weight.shape[1]
    half_units = hidden_units // 2
    unit_rows = hidden_units // BLOCKS
    model_rows = model // BLOCKS
    dp_count, seq_count = lax.axis_size("dp"), lax.axis_size("seq")
    dp_at, seq_at = lax.axis_index("dp"), lax.axis_index("seq")
    group = latent_count // seq_count
    cap = (seq_count - 1) * (block_rows * 3 // 4) + block_rows // 4
    rows_all = group * cap
    paired = dp_count == BLOCKS
    parity = (dp_at & 1) if paired else jnp.zeros_like(dp_at)
    parity_in = parity.reshape(1).astype(jnp.int32)

    joint = jnp.concatenate([qkv_weight, out_weight], axis=1)
    unit_order = lambda v: jnp.swapaxes(
        v.reshape(v.shape[0], BLOCKS // 2, 2, unit_rows), 1, 2
    ).reshape(v.shape[0], hidden_units)
    first_shard = unit_order(fc1_weight)
    if paired:
        joint_pieces, mark_a, mark_b = gather_weight(joint)
        first_pieces, mark_c, mark_d = gather_weight(first_shard, mark_a)
        second_pieces, _, _ = gather_weight(fc2_weight, mark_c)
        whose = lambda k: dp_at ^ k
    else:
        joint_pieces = whole_weight(joint)
        first_pieces = whole_weight(first_shard)
        second_pieces = whole_weight(fc2_weight)
        whose = lambda k: jnp.int32(k)
    joint_at = offsets_of(joint_pieces, whose, model_rows)
    first_at = offsets_of(first_pieces, whose, model_rows)
    second_at = offsets_of(
        second_pieces,
        lambda k: ((whose(k) & 1) ^ parity) * (BLOCKS // 2) + whose(k) // 2,
        unit_rows,
    )
    joint_w = [v for v, _, _ in joint_pieces]
    first_w = [v for v, _, _ in first_pieces]
    second_w = [v for v, _, _ in second_pieces]
    n_joint, n_first, n_second = len(joint_w), len(first_w), len(second_w)

    slot = lax.broadcasted_iota(jnp.int32, (1, block_rows, 1), 1)
    token = lax.broadcasted_iota(jnp.int32, (1, 1, block_rows), 2)
    found = (keep_order[:, :, None] == token) & (slot < keep_count[:, :, None])
    rank = jnp.max(jnp.where(found, slot, -1), axis=1)
    ranks = gather_all(rank, "seq")
    ranks = lax.dynamic_slice_in_dim(ranks, seq_at * group, group, 1)
    ranks = jnp.stack(
        [lax.dynamic_index_in_dim(ranks, seq_at ^ k, 0, keepdims=False) for k in range(seq_count)],
        axis=1,
    )
    counts = jnp.sum((ranks >= 0).astype(jnp.int32), axis=2)
    starts = jnp.cumsum(counts, axis=1) - counts
    live = jnp.sum(counts, axis=1).astype(jnp.int32)
    place = jnp.where(ranks >= 0, ranks + starts[:, :, None], -1).reshape(
        group, seq_count * block_rows
    )
    place_row = place[:, None, :]
    place_col = place[:, :, None]

    def to_whole(blocks_in):
        pieces = []
        for k in range(seq_count):
            piece = lax.dynamic_slice_in_dim(blocks_in, (seq_at ^ k) * group, group, 0)
            pieces.append(swap(piece, "seq", k) if k else piece)
        return pieces

    def to_blocks(pieces, dtype):
        result = jnp.zeros((latent_count, block_rows, model), dtype)
        for k, piece in enumerate(pieces):
            piece = swap(piece, "seq", k) if k else piece
            result = lax.dynamic_update_slice_in_dim(
                result, piece.astype(dtype), (seq_at ^ k) * group, 0
            )
        return result

    latent_pieces = to_whole(latents)
    cot_pieces = to_whole(cotangent)

    cond_wide = condition.astype(F32)
    silu_cond = jax.nn.silu(cond_wide).astype(BF)
    silu_mine = lax.dynamic_slice_in_dim(silu_cond, seq_at * group, group, 0)
    share = model // dp_count
    silu_rows = trade_all(
        jnp.swapaxes(silu_mine.reshape(group, dp_count, share), 0, 1), "dp"
    )
    partial = jnp.dot(
        silu_rows.reshape(dp_count * group, share), ada_weight, preferred_element_type=F32
    ).reshape(dp_count, group, 6 * model)
    mod = sum_own(partial, "dp") + ada_bias.astype(F32)
    mod = mod.reshape(group, 6, model)
    silu_all = gather_all(silu_rows, "seq")

    pad = -(-(model // 2) // LANES) * LANES
    column = lax.broadcasted_iota(jnp.int32, (1, 2 * pad), 1)
    side, inner = column // pad, column % pad
    source = (2 * (inner // model_rows) + (parity ^ side)) * model_rows + inner % model_rows
    source = jnp.where(inner < model // 2, source, -1)
    order = (lax.broadcasted_iota(jnp.int32, (model, 1), 0) == source).astype(BF)

    sds = jax.ShapeDtypeStruct
    flops = 2 * rows_all * model
    dma = lambda n: pltpu.SemaphoreType.DMA((n,))
    half_width = pad
    packed, qkv, mixa_own, mixa_other = call(
        functools.partial(enter_kernel, n_joint, seq_count, cap),
        (
            sds((rows_all, model), BF),
            sds((rows_all, 3 * model), BF),
            sds((rows_all, half_width), BF),
            sds((rows_all, half_width), BF),
        ),
        [joint_at, place_row, mod, order, *latent_pieces, *joint_w],
        [SMEM, VMEM, VMEM, VMEM] + [VMEM] * seq_count + [ANY] * n_joint,
        [pltpu.VMEM((model, 3 * model), BF), pltpu.VMEM((rows_all, model), BF), dma(n_joint)],
        flops * 4 * model,
        "enter",
    )
    grad_out, grad_mlp = call(
        functools.partial(cot_kernel, seq_count, cap),
        (sds((rows_all, model), BF), sds((rows_all, model), BF)),
        [place_row, mod, *cot_pieces],
        [VMEM] * (2 + seq_count),
        [],
        flops * 256,
        "cotangent",
    )
    att_own, att_other, projected, hidden, mixed, mixm_own, mixm_other = call(
        functools.partial(attend_kernel, n_joint, cap, model),
        (
            sds((rows_all, half_width), BF),
            sds((rows_all, half_width), BF),
            sds((rows_all, model), F32),
            sds((rows_all, model), F32),
            sds((rows_all, model), BF),
            sds((rows_all, half_width), BF),
            sds((rows_all, half_width), BF),
        ),
        [joint_at, live, qkv, packed, mod, order, *joint_w],
        [SMEM, SMEM, VMEM, VMEM, VMEM, VMEM] + [ANY] * n_joint,
        [pltpu.VMEM((model, model), BF), pltpu.VMEM((rows_all, model), F32), dma(n_joint)],
        flops * 6 * model,
        "attend",
    )
    bias_row = unit_order(fc1_bias.astype(F32)[None])
    act_own, act_other, slope_own, slope_other = call(
        functools.partial(first_kernel, n_first),
        tuple(sds((rows_all, half_units), BF) for _ in range(4)),
        [first_at, parity_in, mixed, bias_row, *first_w],
        [SMEM, SMEM, VMEM, VMEM] + [ANY] * n_first,
        [pltpu.VMEM((model, hidden_units), BF), dma(n_first)],
        flops * hidden_units,
        "first",
    )

    def weight_grad(left_own, left_other, rights, rows, name):
        pair_left = swap(left_other, "dp", 1)
        pair_rights = [swap(v, "dp", 1) for v in rights]
        if len(rights) == 2:
            pair_rights = pair_rights[::-1]
        cut = outer_pair(left_own, pair_left, rights, pair_rights, rows, name)
        return spread_blocks(cut, rows)

    join_left = lambda a, b: jnp.stack(
        [a[:, : model // 2].reshape(rows_all, 4, model_rows), b[:, : model // 2].reshape(rows_all, 4, model_rows)],
        axis=2,
    ).reshape(rows_all, model)
    inner = lambda a, b: dot(a, b, TN)

    if paired:
        fc2_grad = weight_grad(act_own, act_other, [grad_mlp], unit_rows, "fc2_grad")
        fc2_grad = spread_columns(fc2_grad, plain_columns)
    else:
        act = jnp.concatenate([act_own, act_other], axis=1)
        act = jnp.swapaxes(act.reshape(rows_all, 2, 4, unit_rows), 1, 2).reshape(
            rows_all, hidden_units
        )
        fc2_grad = spread_plain(inner(act, grad_mlp))

    result = call(
        functools.partial(second_kernel, n_second, seq_count, cap),
        tuple(sds((group, block_rows, model), BF) for _ in range(seq_count))
        + (
            sds((rows_all, half_units), BF),
            sds((rows_all, half_units), BF),
            sds((1, half_units), F32),
            sds((1, half_units), F32),
            sds((group, 1, model), F32),
        ),
        [
            second_at,
            act_own,
            act_other,
            slope_own,
            slope_other,
            grad_mlp,
            grad_out,
            hidden,
            mod,
            place_col,
            *latent_pieces,
            *second_w,
        ],
        [SMEM] + [VMEM] * (9 + seq_count) + [ANY] * n_second,
        [pltpu.VMEM((hidden_units, model), BF), dma(n_second)],
        flops * 2 * hidden_units,
        "second",
    )
    block_pieces = result[:seq_count]
    pre_own, pre_other, bias_own, bias_other, gate_m_grad = result[seq_count:]
    block_out = to_blocks(block_pieces, BF)

    if paired:
        fc1_grad = weight_grad(mixm_own, mixm_other, [pre_own, pre_other], model_rows, "fc1_grad")

        def unit_columns(block, j):
            a = block[:, j * unit_rows : (j + 1) * unit_rows]
            b = block[:, half_units + j * unit_rows : half_units + (j + 1) * unit_rows]
            return jnp.concatenate([a, b], axis=1)

        fc1_grad = spread_columns(fc1_grad, unit_columns)
        fc1_grad = jnp.where(
            parity == 1,
            jnp.concatenate([fc1_grad[:, unit_rows:], fc1_grad[:, :unit_rows]], axis=1),
            fc1_grad,
        )
    else:
        pre = jnp.concatenate([pre_own, pre_other], axis=1)
        pre = jnp.swapaxes(pre.reshape(rows_all, 2, 4, unit_rows), 1, 2).reshape(
            rows_all, hidden_units
        )
        fc1_grad = spread_plain(inner(join_left(mixm_own, mixm_other), pre))

    grad_hidden, grad_proj, grad_att, mod_grads = call(
        functools.partial(hidden_kernel, n_joint, n_first, cap, model),
        (
            sds((rows_all, model), F32),
            sds((rows_all, model), BF),
            sds((rows_all, model), BF),
            sds((group, 3, model), F32),
        ),
        [
            first_at,
            joint_at,
            parity_in,
            pre_own,
            pre_other,
            hidden,
            projected,
            grad_out,
            mod,
            *first_w,
            *joint_w,
        ],
        [SMEM, SMEM, SMEM] + [VMEM] * 6 + [ANY] * (n_first + n_joint),
        [
            pltpu.VMEM((model, hidden_units), BF),
            pltpu.VMEM((model, model), BF),
            dma(n_first),
            dma(n_joint),
        ],
        flops * 5 * model,
        "hidden_back",
    )
    grad_qkv = call(
        functools.partial(attend_back_kernel, cap, model),
        sds((rows_all, 3 * model), BF),
        [live, qkv, grad_att],
        [SMEM, VMEM, VMEM],
        [pltpu.VMEM((rows_all, 3 * model), F32)],
        flops * 8 * model,
        "attend_back",
    )
    if paired:
        out_grad = weight_grad(att_own, att_other, [grad_proj], model_rows, "out_grad")
        out_grad = spread_columns(out_grad, plain_columns)
        qkv_grad = weight_grad(mixa_own, mixa_other, [grad_qkv], model_rows, "qkv_grad")
        qkv_grad = spread_columns(qkv_grad, plain_columns)
    else:
        out_grad = spread_plain(inner(join_left(att_own, att_other), grad_proj))
        qkv_grad = spread_plain(inner(join_left(mixa_own, mixa_other), grad_qkv))

    result = call(
        functools.partial(leave_kernel, n_joint, seq_count, cap),
        tuple(sds((group, block_rows, model), BF) for _ in range(seq_count))
        + (sds((group, 2, model), F32),),
        [joint_at, grad_qkv, packed, grad_hidden, mod, place_col, *cot_pieces, *joint_w],
        [SMEM] + [VMEM] * (5 + seq_count) + [ANY] * n_joint,
        [pltpu.VMEM((model, 3 * model), BF), dma(n_joint)],
        flops * 3 * model,
        "leave",
    )
    latents_grad = to_blocks(result[:seq_count], F32)
    mod_first = result[seq_count]

    grad_mod = jnp.concatenate(
        [mod_first, mod_grads[:, 2:3], mod_grads[:, :2], gate_m_grad], axis=1
    ).reshape(group, 6 * model)
    bias_pair = jnp.where(
        parity == 1,
        jnp.concatenate([bias_other, bias_own], axis=0),
        jnp.concatenate([bias_own, bias_other], axis=0),
    )
    bias_part = jnp.swapaxes(bias_pair.reshape(2, BLOCKS // 2, unit_rows), 0, 1).reshape(
        hidden_units
    )
    kept_part = jnp.sum(keep_count).astype(F32).reshape(1)
    sums = sum_everywhere(jnp.concatenate([jnp.sum(grad_mod, axis=0), bias_part, kept_part]))
    ada_bias_grad = sums[: 6 * model]
    fc1_bias_grad = sums[6 * model : 6 * model + hidden_units]
    kept_total = sums[6 * model + hidden_units :].astype(jnp.int32)

    grad_mod_all = gather_all(grad_mod.astype(BF), "dp")
    column_share = 6 * model // seq_count
    by_column = jnp.stack(
        [grad_mod_all[:, :, j * column_share : (j + 1) * column_share] for j in range(seq_count)]
    )
    by_column = trade_all(by_column, "seq")
    ada_grad = dot(
        silu_all.reshape(seq_count * dp_count * group, share),
        by_column.reshape(seq_count * dp_count * group, column_share),
        TN,
    )
    cond_part = dot(grad_mod_all.reshape(dp_count * group, 6 * model), ada_weight, NT)
    cond_cols = trade_all(cond_part.reshape(dp_count, group, share), "dp")
    cond_mine = jnp.swapaxes(cond_cols, 0, 1).reshape(group, model)
    cond_rows = gather_all(cond_mine, "seq").reshape(latent_count, model)
    _, silu_back = jax.vjp(jax.nn.silu, cond_wide)
    condition_grad = silu_back(cond_rows)[0]
    return (
        block_out,
        latents_grad,
        condition_grad,
        ada_grad,
        ada_bias_grad,
        qkv_grad,
        out_grad,
        fc1_grad,
        fc1_bias_grad,
        fc2_grad,
        kept_total,
    )


def solution(mesh):
    placed = (
        P("dp", "seq", None),
        P("dp", None),
        P("dp", "seq"),
        P("dp", "seq"),
        P("dp", None),
        P(),
        P("dp", None),
        P("dp", None),
        P("dp", None),
        P(),
        P("dp", None),
        P("dp", "seq", None),
    )
    return jax.shard_map(
        body,
        mesh=mesh,
        in_specs=placed,
        out_specs=(
            P("dp", "seq", None),
            P("dp", "seq", None),
            P("dp", None),
            P("dp", "seq"),
            P(),
            P("dp", "seq"),
            P("dp", "seq"),
            P("dp", "seq"),
            P(),
            P("dp", "seq"),
            P(),
        ),
        check_vma=False,
    )
```

```python
import functools
import math

import jax
import jax.numpy as jnp
from jax import lax
from jax.experimental import pallas as pl
from jax.experimental.pallas import tpu as pltpu
from jax.sharding import PartitionSpec as P

HEADS = 16
HEAD = 72
LANES = 128
BLOCKS = 8

layer_eps = 1e-06
far_below = -1e30
att_scale = 1.0 / math.sqrt(HEAD)
gelu_c = math.sqrt(2.0 / math.pi)
gelu_k = 0.044715

BF = jnp.bfloat16
F32 = jnp.float32
VMEM = pl.BlockSpec(memory_space=pltpu.VMEM)
SMEM = pl.BlockSpec(memory_space=pltpu.SMEM)
ANY = pl.BlockSpec(memory_space=pl.ANY)
NT = (((1,), (1,)), ((), ()))
TN = (((0,), (0,)), ((), ()))


def swap(value, axis, step):
    return lax.ppermute(value, axis, [(i, i ^ step) for i in range(lax.axis_size(axis))])


def steps_of(axis):
    count = lax.axis_size(axis)
    return [1 << i for i in range(count.bit_length() - 1)]


def bit_set(axis, step):
    return (lax.axis_index(axis) & step) != 0


def gather_all(value, axis):
    value = value[None]
    for step in steps_of(axis):
        value = jnp.concatenate([value, swap(value, axis, step)], axis=0)
    return value


def sum_own(value, axis):
    for step in reversed(steps_of(axis)):
        value = value[:step] + swap(value[step:], axis, step)
    return value[0]


def trade_all(value, axis):
    count = value.shape[0]
    rest = value.shape[1:]
    for step in steps_of(axis):
        split = value.reshape((count // (2 * step), 2, step) + rest)
        value = jnp.stack([split[:, 0], swap(split[:, 1], axis, step)], axis=1).reshape(
            (count,) + rest
        )
    return value


def in_order(value, axis):
    count = value.shape[0]
    rest = value.shape[1:]
    for step in steps_of(axis):
        split = value.reshape((count // (2 * step), 2, step) + rest)
        value = jnp.where(bit_set(axis, step), split[:, ::-1], split).reshape((count,) + rest)
    return value


def sum_everywhere(value):
    for axis in ("dp", "seq"):
        for step in steps_of(axis):
            value = value + swap(value, axis, step)
    return value


def after(value, *earlier):
    return lax.optimization_barrier((value,) + earlier)[0]


def halves_of(rows):
    first = (rows // 2 + 15) // 16 * 16
    return first, rows - first


def pieces_of(own, own_pair, beside, beside_pair, across, across_pair, part):
    return [
        (own, 0, 0),
        (own_pair, 1, 0),
        (beside[0], 2, 0),
        (beside_pair[0], 3, 0),
        (beside[1], 4, 0),
        (beside_pair[1], 5, 0),
        (across[0], 6, 0),
        (across[1], 6, part),
        (across_pair[0], 7, 0),
        (across_pair[1], 7, part),
    ]


def beside_of(shard):
    return swap(shard, "dp", 2), swap(shard, "dp", 4)


def across_of(beside, part):
    return swap(beside[1][:part], "dp", 2), swap(beside[0][part:], "dp", 4)


def pair_of(values):
    return tuple(swap(v, "dp", 1) for v in values)


def whole_weight(shard):
    full = lax.all_gather(shard, "dp", axis=0, tiled=True)
    rows = full.shape[0] // BLOCKS
    return [(full[k * rows : (k + 1) * rows], k, 0) for k in range(BLOCKS)]


def offsets_of(pieces, position, rows):
    return jnp.stack([position(k) * rows + first for _, k, first in pieces]).astype(jnp.int32)


def call(kernel, outs, ins, specs, scratch, name):
    return pl.pallas_call(
        kernel,
        out_shape=outs,
        in_specs=specs,
        out_specs=jax.tree.map(lambda _: VMEM, outs),
        scratch_shapes=scratch,
        name=name,
        compiler_params=pltpu.CompilerParams(vmem_limit_bytes=56 * 1024 * 1024),
    )(*ins)


def start_pieces(offsets, refs, target, sem, lo, hi):
    copies = []
    for k, ref in enumerate(refs):
        rows = ref.shape[0]
        copies.append(
            pltpu.make_async_copy(
                ref.at[:, pl.ds(lo, hi - lo)],
                target.at[pl.ds(pl.multiple_of(offsets[k], 16), rows), :],
                sem.at[k],
            )
        )
    for one in copies:
        one.start()
    return copies


def wait_all(copies):
    for one in copies:
        one.wait()


def normal(rows_in):
    center = rows_in - jnp.mean(rows_in, axis=-1, keepdims=True)
    inverse = lax.rsqrt(jnp.mean(center * center, axis=-1, keepdims=True) + layer_eps)
    return center * inverse, inverse


def normal_back(grad_rows, normed, inverse):
    mean_grad = jnp.mean(grad_rows, axis=-1, keepdims=True)
    mean_proj = jnp.mean(grad_rows * normed, axis=-1, keepdims=True)
    return inverse * (grad_rows - mean_grad - normed * mean_proj)


def dot(left, right, dims=None):
    if dims is None:
        return jnp.dot(left, right, preferred_element_type=F32)
    return lax.dot_general(left, right, dims, preferred_element_type=F32)


def spans(total, width):
    return [(lo, min(lo + width, total)) for lo in range(0, total, width)]


def pack_rows(place_ref, piece_refs, latent, rows_out):
    gathered = jnp.concatenate([ref[latent] for ref in piece_refs], axis=0)
    slots = lax.broadcasted_iota(jnp.int32, (rows_out, gathered.shape[0]), 0)
    chosen = jnp.where(place_ref[latent] == slots, 1.0, 0.0).astype(BF)
    return dot(chosen, gathered)


def unpack_rows(place_ref, piece_refs, latent, packed, out_refs):
    rows_out = packed.shape[0]
    place = place_ref[latent]
    slots = lax.broadcasted_iota(jnp.int32, (place.shape[0], rows_out), 1)
    chosen = jnp.where(place == slots, 1.0, 0.0).astype(BF)
    spread = dot(chosen, packed)
    block = piece_refs[0].shape[1]
    for k, (piece, out) in enumerate(zip(piece_refs, out_refs)):
        here = slice(k * block, (k + 1) * block)
        out[latent] = jnp.where(
            place[here] >= 0, spread[here], piece[latent].astype(F32)
        ).astype(BF)


def split_parity(rows_low, order_ref, own_ref, other_ref):
    moved = dot(rows_low, order_ref[...]).astype(BF)
    width = own_ref.shape[1]
    own_ref[...] = moved[:, :width]
    other_ref[...] = moved[:, width:]


def enter_kernel(pieces, blocks, cap, *refs):
    (offsets, place, mod, order), refs = refs[:4], refs[4:]
    latents, refs = refs[:blocks], refs[blocks:]
    weights, refs = refs[:pieces], refs[pieces:]
    packed_out, qkv_out, own_out, other_out, weight, mixed, sem = refs
    width = qkv_out.shape[1]
    copies = start_pieces(offsets, weights, weight, sem, 0, width)
    for latent in range(mod.shape[0]):
        here = pl.ds(latent * cap, cap)
        rows = pack_rows(place, latents, latent, cap)
        packed_out[here, :] = rows.astype(BF)
        normed, _ = normal(rows)
        mixed[here, :] = (normed * (1.0 + mod[latent, 1:2, :]) + mod[latent, 0:1, :]).astype(BF)
    split_parity(mixed[...], order, own_out, other_out)
    wait_all(copies)
    for lo, hi in spans(width, 768):
        qkv_out[:, lo:hi] = dot(mixed[...], weight[:, lo:hi]).astype(BF)


def cot_kernel(blocks, cap, *refs):
    place, mod = refs[:2]
    cots = refs[2 : 2 + blocks]
    packed_out, mlp_out = refs[2 + blocks :]
    for latent in range(mod.shape[0]):
        here = pl.ds(latent * cap, cap)
        rows = pack_rows(place, cots, latent, cap)
        packed_out[here, :] = rows.astype(BF)
        mlp_out[here, :] = (mod[latent, 5:6, :] * rows).astype(BF)


def windows():
    found = []
    for head in range(HEADS):
        first = head * HEAD
        base = first // LANES * LANES
        width = LANES if first + HEAD <= base + LANES else 2 * LANES
        found.append((base, width, first - base))
    return found


def head_mask(width, first, dtype):
    lane = lax.broadcasted_iota(jnp.int32, (1, width), 1)
    return jnp.where((lane >= first) & (lane < first + HEAD), 1.0, 0.0).astype(dtype)


def attend_kernel(pieces, cap, model, *refs):
    (offsets, live, qkv, packed, mod, order), refs = refs[:6], refs[6:]
    weights, refs = refs[:pieces], refs[pieces:]
    (own_att, other_att, proj_out, hidden_out, mixed_out, own_mix, other_mix), refs = (
        refs[:7],
        refs[7:],
    )
    weight, attended, sem = refs
    copies = start_pieces(offsets, weights, weight, sem, 3 * model, 4 * model)
    attended[...] = jnp.zeros_like(attended)

    def one_latent(latent, carry):
        here = pl.ds(pl.multiple_of(latent * cap, 16), cap)
        count = live[latent]
        seen = lax.broadcasted_iota(jnp.int32, (cap, cap), 1) < count
        for base, width, first in windows():
            low_mask = head_mask(width, first, BF)
            query = qkv[here, base : base + width] * low_mask
            key = qkv[here, model + base : model + base + width]
            value = qkv[here, 2 * model + base : 2 * model + base + width]
            scores = jnp.where(seen, dot(query, key, NT) * att_scale, far_below)
            raised = jnp.exp(scores - jnp.max(scores, axis=-1, keepdims=True))
            total = jnp.sum(raised, axis=-1, keepdims=True)
            mixed = dot(raised.astype(BF), value) / total
            attended[here, base : base + width] += mixed * head_mask(width, first, F32)
        return carry

    lax.fori_loop(0, mod.shape[0], one_latent, 0)
    att_low = attended[...].astype(BF)
    split_parity(att_low, order, own_att, other_att)
    wait_all(copies)
    projected = dot(att_low, weight[...])
    proj_out[...] = projected
    for latent in range(mod.shape[0]):
        rows = slice(latent * cap, (latent + 1) * cap)
        hidden = packed[rows, :].astype(F32) + mod[latent, 2:3, :] * projected[rows]
        hidden_out[rows, :] = hidden
        normed, _ = normal(hidden)
        mixed_out[rows, :] = (
            normed * (1.0 + mod[latent, 4:5, :]) + mod[latent, 3:4, :]
        ).astype(BF)
    split_parity(mixed_out[...], order, own_mix, other_mix)


def first_kernel(pieces, *refs):
    (offsets, parity, mixed, bias), refs = refs[:4], refs[4:]
    weights, refs = refs[:pieces], refs[pieces:]
    own_act, other_act, own_slope, other_slope, weight, sem = refs
    copies = start_pieces(offsets, weights, weight, sem, 0, weight.shape[1])
    half = own_act.shape[1]
    wait_all(copies)
    for side, (act_out, slope_out) in enumerate(
        ((own_act, own_slope), (other_act, other_slope))
    ):
        base = (parity[0] ^ side) * half
        for lo, hi in spans(half, 768):
            cols = pl.ds(pl.multiple_of(base + lo, LANES), hi - lo)
            pre = dot(mixed[...], weight[:, cols]) + bias[:, cols]
            square = pre * pre
            curve = jnp.tanh(gelu_c * pre * (1.0 + gelu_k * square))
            cdf = 0.5 * (1.0 + curve)
            act_out[:, lo:hi] = (pre * cdf).astype(BF)
            slope = cdf + pre * (0.5 * gelu_c) * (1.0 - curve * curve) * (
                1.0 + 3.0 * gelu_k * square
            )
            slope_out[:, lo:hi] = slope.astype(BF)


def second_kernel(pieces, blocks, cap, *refs):
    (
        offsets,
        own_act,
        other_act,
        own_slope,
        other_slope,
        grad_mlp,
        grad_out,
        hidden,
        mod,
        place,
    ), refs = refs[:10], refs[10:]
    latents, refs = refs[:blocks], refs[blocks:]
    weights, refs = refs[:pieces], refs[pieces:]
    outs, refs = refs[:blocks], refs[blocks:]
    own_pre, other_pre, own_bias, other_bias, gate_grad, weight, sem = refs
    copies = start_pieces(offsets, weights, weight, sem, 0, weight.shape[1])
    half = own_act.shape[1]
    wait_all(copies)
    for side, (slope, pre_out, bias_out) in enumerate(
        ((own_slope, own_pre, own_bias), (other_slope, other_pre, other_bias))
    ):
        for lo, hi in spans(half, 768):
            grad_act = dot(grad_mlp[...], weight[side * half + lo : side * half + hi, :], NT)
            grad_pre = (grad_act * slope[:, lo:hi].astype(F32)).astype(BF)
            pre_out[:, lo:hi] = grad_pre
            bias_out[:, lo:hi] = jnp.sum(grad_pre.astype(F32), axis=0, keepdims=True)
    mlp = dot(own_act[...], weight[:half, :]) + dot(other_act[...], weight[half:, :])
    for latent in range(mod.shape[0]):
        rows = slice(latent * cap, (latent + 1) * cap)
        gate_grad[latent, :, :] = jnp.sum(
            grad_out[rows, :].astype(F32) * mlp[rows], axis=0, keepdims=True
        )
        block = (hidden[rows, :] + mod[latent, 5:6, :] * mlp[rows]).astype(BF)
        unpack_rows(place, latents, latent, block, outs)


def hidden_kernel(pieces, first_pieces, cap, model, *refs):
    (
        first_offsets,
        offsets,
        parity,
        own_pre,
        other_pre,
        hidden_in,
        projected,
        grad_out,
        mod,
    ), refs = refs[:9], refs[9:]
    first_weights, refs = refs[:first_pieces], refs[first_pieces:]
    out_weights, refs = refs[:pieces], refs[pieces:]
    grad_hidden, grad_proj, grad_att, mod_grads, first, out_weight, first_sem, out_sem = refs
    copies = start_pieces(first_offsets, first_weights, first, first_sem, 0, first.shape[1])
    later = start_pieces(offsets, out_weights, out_weight, out_sem, 3 * model, 4 * model)
    half = own_pre.shape[1]
    wait_all(copies)
    total = None
    for side, pre in enumerate((own_pre, other_pre)):
        base = (parity[0] ^ side) * half
        for lo, hi in spans(half, 768):
            cols = pl.ds(pl.multiple_of(base + lo, LANES), hi - lo)
            part = dot(pre[:, lo:hi], first[:, cols], NT)
            total = part if total is None else total + part
    for latent in range(mod.shape[0]):
        rows = slice(latent * cap, (latent + 1) * cap)
        normed, inverse = normal(hidden_in[rows, :])
        grad_mixed = total[rows]
        mod_grads[latent, 0:1, :] = jnp.sum(grad_mixed, axis=0, keepdims=True)
        mod_grads[latent, 1:2, :] = jnp.sum(grad_mixed * normed, axis=0, keepdims=True)
        grad = grad_out[rows, :].astype(F32) + normal_back(
            grad_mixed * (1.0 + mod[latent, 4:5, :]), normed, inverse
        )
        grad_hidden[rows, :] = grad
        mod_grads[latent, 2:3, :] = jnp.sum(grad * projected[rows, :], axis=0, keepdims=True)
        grad_proj[rows, :] = (mod[latent, 2:3, :] * grad).astype(BF)
    wait_all(later)
    grad_att[...] = dot(grad_proj[...], out_weight[...], NT).astype(BF)


def attend_back_kernel(cap, model, *refs):
    live, qkv, grad_att, grad_qkv, sums = refs
    sums[...] = jnp.zeros_like(sums)

    def one_latent(latent, carry):
        here = pl.ds(pl.multiple_of(latent * cap, 16), cap)
        count = live[latent]
        seen = lax.broadcasted_iota(jnp.int32, (cap, cap), 0) < count
        for base, width, first in windows():
            low_mask = head_mask(width, first, BF)
            wide_mask = head_mask(width, first, F32)
            cols = slice(base, base + width)
            key_cols = slice(model + base, model + base + width)
            value_cols = slice(2 * model + base, 2 * model + base + width)
            query, key, value = qkv[here, cols], qkv[here, key_cols], qkv[here, value_cols]
            grad = grad_att[here, cols]
            scores = jnp.where(seen, dot(key * low_mask, query, NT) * att_scale, far_below)
            raised = jnp.exp(scores - jnp.max(scores, axis=0, keepdims=True))
            probs = raised / jnp.sum(raised, axis=0, keepdims=True)
            grad_probs = dot(value * low_mask, grad, NT)
            delta = jnp.sum(probs * grad_probs, axis=0, keepdims=True)
            grad_scores = (probs * (grad_probs - delta)).astype(BF)
            scaled = wide_mask * att_scale
            sums[here, cols] += dot(grad_scores, key, TN) * scaled
            sums[here, key_cols] += dot(grad_scores, query) * scaled
            sums[here, value_cols] += dot(probs.astype(BF), grad) * wide_mask
        return carry

    lax.fori_loop(0, live.shape[0], one_latent, 0)
    grad_qkv[...] = sums[...].astype(BF)


def leave_kernel(pieces, blocks, cap, *refs):
    (offsets, grad_qkv, packed, grad_hidden, mod, place), refs = refs[:6], refs[6:]
    cots, refs = refs[:blocks], refs[blocks:]
    weights, refs = refs[:pieces], refs[pieces:]
    outs, refs = refs[:blocks], refs[blocks:]
    mod_grads, weight, sem = refs
    copies = start_pieces(offsets, weights, weight, sem, 0, weight.shape[1])
    wait_all(copies)
    total = None
    for lo, hi in spans(weight.shape[1], 768):
        part = dot(grad_qkv[:, lo:hi], weight[:, lo:hi], NT)
        total = part if total is None else total + part
    for latent in range(mod.shape[0]):
        rows = slice(latent * cap, (latent + 1) * cap)
        normed, inverse = normal(packed[rows, :].astype(F32))
        grad_mixed = total[rows]
        mod_grads[latent, 0:1, :] = jnp.sum(grad_mixed, axis=0, keepdims=True)
        mod_grads[latent, 1:2, :] = jnp.sum(grad_mixed * normed, axis=0, keepdims=True)
        grad = grad_hidden[rows, :] + normal_back(
            grad_mixed * (1.0 + mod[latent, 1:2, :]), normed, inverse
        )
        unpack_rows(place, cots, latent, grad.astype(BF), outs)


def outer_kernel(rows, used, sides, *refs):
    block_at, refs = refs[0], refs[1:]
    total = sum(sides)
    lefts, refs = refs[: 2 * len(sides)], refs[2 * len(sides) :]
    rights, refs = refs[: 2 * total], refs[2 * total :]
    (send_x, send_y, keep, keep_x, keep_y), refs = refs[:5], refs[5:]
    result, sem = refs
    part, rest = halves_of(rows)
    base, at = 0, 0
    for group, count in enumerate(sides):
        own_left, pair_left = lefts[2 * group : 2 * group + 2]
        left = jnp.concatenate([own_left[:, :used], pair_left[:, :used]], axis=0)
        for own, pair in zip(rights[2 * at : 2 * (at + count) : 2], rights[2 * at + 1 : 2 * (at + count) : 2]):
            width = own.shape[1]
            for lo, hi in spans(width, 768):
                right = jnp.concatenate([own[:, lo:hi], pair[:, lo:hi]], axis=0)
                result[:, base + lo : base + hi] = dot(left, right, TN).astype(BF)
            base += width
        at += count

    def rows_at(k, first, count):
        return result.at[pl.ds(pl.multiple_of(block_at[k] * rows + first, 16), count), :]

    moves = [
        (rows_at(1, 0, part), send_x.at[0]),
        (rows_at(3, 0, part), send_x.at[1]),
        (rows_at(2, part, rest), send_y.at[0]),
        (rows_at(3, part, rest), send_y.at[1]),
        (rows_at(0, 0, rows), keep),
        (rows_at(1, part, rest), keep_x),
        (rows_at(2, 0, part), keep_y),
    ]
    copies = [pltpu.make_async_copy(a, b, sem.at[i]) for i, (a, b) in enumerate(moves)]
    for one in copies:
        one.start()
    wait_all(copies)


def reorder_kernel(unit, shard, whole):
    count = shard.shape[1] // unit
    for block in range(count):
        to = (block % 2) * (count // 2) + block // 2
        whole[:, to * unit : (to + 1) * unit] = shard[:, block * unit : (block + 1) * unit]


def fold_kernel(cuts, *refs):
    (at, keep, near_top, near_bottom, far_top, far_bottom), refs = refs[:6], refs[6:]
    count = len(cuts[0])
    outs, refs = refs[: count * len(cuts)], refs[count * len(cuts) :]
    scratch, sem = refs[:-1], refs[-1]
    part = far_top.shape[0]
    wide = lambda ref: ref[...].astype(F32)
    top = keep[:part, :].astype(F32) + wide(near_top) + wide(far_top)
    bottom = keep[part:, :].astype(F32) + wide(near_bottom) + wide(far_bottom)
    copies = []
    for group, parts in zip(cuts, scratch):
        for j, pieces in enumerate(group):
            first = 0
            for lo, hi in pieces:
                parts[j, :part, first : first + hi - lo] = top[:, lo:hi].astype(BF)
                parts[j, part:, first : first + hi - lo] = bottom[:, lo:hi].astype(BF)
                first += hi - lo
        for k in range(count):
            i = len(copies)
            copies.append(pltpu.make_async_copy(parts.at[at[0] ^ k], outs[i], sem.at[i]))
    for one in copies:
        one.start()
    wait_all(copies)


def outer_pair(groups, rows, name):
    used = 4 * rows
    part, rest = halves_of(rows)
    lefts = [v for left, _ in groups for v in left]
    rights = [v for _, pairs in groups for pair in pairs for v in pair]
    width = sum(v.shape[1] for v in rights) // 2
    sides = tuple(len(pairs) for _, pairs in groups)
    block_at = jnp.stack([(lax.axis_index("dp") ^ (2 * k)) // 2 for k in range(4)]).astype(jnp.int32)
    ins = [block_at, *lefts, *rights]
    outs = (
        jax.ShapeDtypeStruct((2, part, width), BF),
        jax.ShapeDtypeStruct((2, rest, width), BF),
        jax.ShapeDtypeStruct((rows, width), BF),
        jax.ShapeDtypeStruct((rest, width), BF),
        jax.ShapeDtypeStruct((part, width), BF),
    )
    return pl.pallas_call(
        functools.partial(outer_kernel, rows, used, sides),
        out_shape=outs,
        in_specs=[SMEM] + [VMEM] * (len(ins) - 1),
        out_specs=tuple(ANY for _ in outs),
        scratch_shapes=[pltpu.VMEM((used, width), BF), pltpu.SemaphoreType.DMA((7,))],
        name=name,
        compiler_params=pltpu.CompilerParams(vmem_limit_bytes=56 * 1024 * 1024),
    )(*ins)


def near_sums(cut, from_x, from_y):
    _, _, _, keep_x, keep_y = cut
    on_y = (keep_y.astype(F32) + from_x[1].astype(F32)).astype(BF)
    on_x = (keep_x.astype(F32) + from_y[1].astype(F32)).astype(BF)
    return on_x, on_y


def fold(keep, from_x, from_y, far_top, far_bottom, cuts, name):
    rows = keep.shape[0]
    count = lax.axis_size("seq")
    at = lax.axis_index("seq").reshape(1).astype(jnp.int32)
    widths = tuple(sum(hi - lo for lo, hi in group[0]) for group in cuts)
    outs = tuple(jax.ShapeDtypeStruct((rows, w), BF) for w in widths for _ in range(count))
    return pl.pallas_call(
        functools.partial(fold_kernel, cuts),
        out_shape=outs,
        in_specs=[SMEM] + [VMEM] * 5,
        out_specs=tuple(ANY for _ in outs),
        scratch_shapes=[pltpu.VMEM((count, rows, w), BF) for w in widths]
        + [pltpu.SemaphoreType.DMA((len(outs),))],
        name=name,
        compiler_params=pltpu.CompilerParams(vmem_limit_bytes=40 * 1024 * 1024),
    )(at, keep, from_x[0], from_y[0], far_top, far_bottom)


def plain_cuts(first, width, count):
    share = width // count
    return tuple(((first + j * share, first + (j + 1) * share),) for j in range(count))


def spread_plain(grad):
    grad = lax.psum_scatter(grad, "dp", scatter_dimension=0, tiled=True)
    return lax.psum_scatter(grad, "seq", scatter_dimension=1, tiled=True)


def body(
    latents,
    condition,
    keep_order,
    keep_count,
    ada_weight,
    ada_bias,
    qkv_weight,
    out_weight,
    fc1_weight,
    fc1_bias,
    fc2_weight,
    cotangent,
):
    latent_count, block_rows, model = latents.shape
    hidden_units = fc1_weight.shape[1]
    half_units = hidden_units // 2
    unit_rows = hidden_units // BLOCKS
    model_rows = model // BLOCKS
    dp_count, seq_count = lax.axis_size("dp"), lax.axis_size("seq")
    dp_at, seq_at = lax.axis_index("dp"), lax.axis_index("seq")
    group = latent_count // seq_count
    cap = (seq_count - 1) * (block_rows * 3 // 4) + block_rows // 4
    rows_all = group * cap
    share = model // dp_count
    column_share = 6 * model // seq_count
    paired = dp_count == BLOCKS and seq_count == 4
    parity = (dp_at & 1) if paired else jnp.zeros_like(dp_at)
    parity_in = parity.reshape(1).astype(jnp.int32)
    part, _ = halves_of(model_rows)
    unit_part, _ = halves_of(unit_rows)
    whose = (lambda k: dp_at ^ k) if paired else (lambda k: jnp.int32(k))
    sds = jax.ShapeDtypeStruct
    dma = lambda n: pltpu.SemaphoreType.DMA((n,))
    fence = lambda *values: lax.optimization_barrier(values)

    def rank_of():
        slot = lax.broadcasted_iota(jnp.int32, (1, block_rows, 1), 1)
        token = lax.broadcasted_iota(jnp.int32, (1, 1, block_rows), 2)
        found = (keep_order[:, :, None] == token) & (slot < keep_count[:, :, None])
        return jnp.max(jnp.where(found, slot, -1), axis=1)

    def places_of(ranks):
        ranks = lax.dynamic_slice_in_dim(ranks, seq_at * group, group, 1)
        ranks = jnp.swapaxes(ranks, 0, 1)
        counts = jnp.sum((ranks >= 0).astype(jnp.int32), axis=2)
        starts = jnp.cumsum(counts, axis=1) - counts
        live = jnp.sum(counts, axis=1).astype(jnp.int32)
        place = jnp.where(ranks >= 0, ranks + starts[:, :, None], -1).reshape(
            group, seq_count * block_rows
        )
        return live, place[:, None, :], place[:, :, None]

    def whole_slice(blocks_in, k):
        return lax.dynamic_slice_in_dim(blocks_in, (seq_at ^ k) * group, group, 0)

    def put_slices(pieces, dtype):
        result = jnp.zeros((latent_count, block_rows, model), dtype)
        for k, piece in enumerate(pieces):
            result = lax.dynamic_update_slice_in_dim(
                result, piece.astype(dtype), (seq_at ^ k) * group, 0
            )
        return result

    cond_wide = condition.astype(F32)
    silu_cond = jax.nn.silu(cond_wide).astype(BF)
    silu_mine = lax.dynamic_slice_in_dim(silu_cond, seq_at * group, group, 0)
    silu_mine = in_order(jnp.swapaxes(silu_mine.reshape(group, dp_count, share), 0, 1), "dp")

    def partial_mod(silu_rows):
        return jnp.dot(
            silu_rows.reshape(dp_count * group, share), ada_weight, preferred_element_type=F32
        ).reshape(dp_count, group, 6 * model)

    def whole_mod(total):
        return (total + ada_bias.astype(F32)).reshape(group, 6, model)

    unit_order = lambda v: jnp.swapaxes(
        v.reshape(v.shape[0], BLOCKS // 2, 2, unit_rows), 1, 2
    ).reshape(v.shape[0], hidden_units)
    bias_row = unit_order(fc1_bias.astype(F32)[None])

    pad = -(-(model // 2) // LANES) * LANES
    column = lax.broadcasted_iota(jnp.int32, (1, 2 * pad), 1)
    side, inner = column // pad, column % pad
    source = (2 * (inner // model_rows) + (parity ^ side)) * model_rows + inner % model_rows
    source = jnp.where(inner < model // 2, source, -1)
    order = (lax.broadcasted_iota(jnp.int32, (model, 1), 0) == source).astype(BF)

    model_position = lambda k: whose(k)
    unit_position = lambda k: ((whose(k) & 1) ^ parity) * (BLOCKS // 2) + whose(k) // 2

    def run_enter(joint, place_row, mod, latent_pieces):
        weights = [v for v, _, _ in joint]
        return call(
            functools.partial(enter_kernel, len(weights), seq_count, cap),
            (
                sds((rows_all, model), BF),
                sds((rows_all, 3 * model), BF),
                sds((rows_all, pad), BF),
                sds((rows_all, pad), BF),
            ),
            [
                offsets_of(joint, model_position, model_rows),
                place_row,
                mod,
                order,
                *latent_pieces,
                *weights,
            ],
            [SMEM, VMEM, VMEM, VMEM] + [VMEM] * seq_count + [ANY] * len(weights),
            [
                pltpu.VMEM((model, 3 * model), BF),
                pltpu.VMEM((rows_all, model), BF),
                dma(len(weights)),
            ],
            "enter",
        )

    def run_cot(place_row, mod, cot_pieces):
        return call(
            functools.partial(cot_kernel, seq_count, cap),
            (sds((rows_all, model), BF), sds((rows_all, model), BF)),
            [place_row, mod, *cot_pieces],
            [VMEM] * (2 + seq_count),
            [],
            "cotangent",
        )

    def run_attend(joint, live, qkv, packed, mod):
        weights = [v for v, _, _ in joint]
        return call(
            functools.partial(attend_kernel, len(weights), cap, model),
            (
                sds((rows_all, pad), BF),
                sds((rows_all, pad), BF),
                sds((rows_all, model), F32),
                sds((rows_all, model), F32),
                sds((rows_all, model), BF),
                sds((rows_all, pad), BF),
                sds((rows_all, pad), BF),
            ),
            [
                offsets_of(joint, model_position, model_rows),
                live,
                qkv,
                packed,
                mod,
                order,
                *weights,
            ],
            [SMEM, SMEM, VMEM, VMEM, VMEM, VMEM] + [ANY] * len(weights),
            [
                pltpu.VMEM((model, model), BF),
                pltpu.VMEM((rows_all, model), F32),
                dma(len(weights)),
            ],
            "attend",
        )

    def run_first(first, mixed):
        weights = [v for v, _, _ in first]
        return call(
            functools.partial(first_kernel, len(weights)),
            tuple(sds((rows_all, half_units), BF) for _ in range(4)),
            [
                offsets_of(first, model_position, model_rows),
                parity_in,
                mixed,
                bias_row,
                *weights,
            ],
            [SMEM, SMEM, VMEM, VMEM] + [ANY] * len(weights),
            [pltpu.VMEM((model, hidden_units), BF), dma(len(weights))],
            "first",
        )

    def run_second(second, acts, grad_mlp, grad_out, hidden, mod, place_col, latent_pieces):
        weights = [v for v, _, _ in second]
        result = call(
            functools.partial(second_kernel, len(weights), seq_count, cap),
            tuple(sds((group, block_rows, model), BF) for _ in range(seq_count))
            + (
                sds((rows_all, half_units), BF),
                sds((rows_all, half_units), BF),
                sds((1, half_units), F32),
                sds((1, half_units), F32),
                sds((group, 1, model), F32),
            ),
            [
                offsets_of(second, unit_position, unit_rows),
                *acts,
                grad_mlp,
                grad_out,
                hidden,
                mod,
                place_col,
                *latent_pieces,
                *weights,
            ],
            [SMEM] + [VMEM] * (9 + seq_count) + [ANY] * len(weights),
            [pltpu.VMEM((hidden_units, model), BF), dma(len(weights))],
            "second",
        )
        return result[:seq_count], result[seq_count:]

    def run_hidden(first, joint, pres, hidden, projected, grad_out, mod):
        first_w = [v for v, _, _ in first]
        joint_w = [v for v, _, _ in joint]
        return call(
            functools.partial(hidden_kernel, len(joint_w), len(first_w), cap, model),
            (
                sds((rows_all, model), F32),
                sds((rows_all, model), BF),
                sds((rows_all, model), BF),
                sds((group, 3, model), F32),
            ),
            [
                offsets_of(first, model_position, model_rows),
                offsets_of(joint, model_position, model_rows),
                parity_in,
                *pres,
                hidden,
                projected,
                grad_out,
                mod,
                *first_w,
                *joint_w,
            ],
            [SMEM, SMEM, SMEM] + [VMEM] * 6 + [ANY] * (len(first_w) + len(joint_w)),
            [
                pltpu.VMEM((model, hidden_units), BF),
                pltpu.VMEM((model, model), BF),
                dma(len(first_w)),
                dma(len(joint_w)),
            ],
            "hidden_back",
        )

    def run_attend_back(live, qkv, grad_att):
        return call(
            functools.partial(attend_back_kernel, cap, model),
            sds((rows_all, 3 * model), BF),
            [live, qkv, grad_att],
            [SMEM, VMEM, VMEM],
            [pltpu.VMEM((rows_all, 3 * model), F32)],
            "attend_back",
        )

    def run_leave(joint, grad_qkv, packed, grad_hidden, mod, place_col, cot_pieces):
        weights = [v for v, _, _ in joint]
        result = call(
            functools.partial(leave_kernel, len(weights), seq_count, cap),
            tuple(sds((group, block_rows, model), BF) for _ in range(seq_count))
            + (sds((group, 2, model), F32),),
            [
                offsets_of(joint, model_position, model_rows),
                grad_qkv,
                packed,
                grad_hidden,
                mod,
                place_col,
                *cot_pieces,
                *weights,
            ],
            [SMEM] + [VMEM] * (5 + seq_count) + [ANY] * len(weights),
            [pltpu.VMEM((model, 3 * model), BF), dma(len(weights))],
            "leave",
        )
        return result[:seq_count], result[seq_count]

    def join_mod(mod_first, mod_grads, gate_m_grad):
        return jnp.concatenate(
            [mod_first, mod_grads[:, 2:3], mod_grads[:, :2], gate_m_grad], axis=1
        ).reshape(group, 6 * model)

    def join_sums(grad_mod, bias_own, bias_other):
        bias_pair = jnp.where(
            parity == 1,
            jnp.concatenate([bias_other, bias_own], axis=0),
            jnp.concatenate([bias_own, bias_other], axis=0),
        )
        bias_part = jnp.swapaxes(bias_pair.reshape(2, BLOCKS // 2, unit_rows), 0, 1)
        kept_part = jnp.sum(keep_count).astype(F32).reshape(1)
        return jnp.concatenate(
            [jnp.sum(grad_mod, axis=0), bias_part.reshape(hidden_units), kept_part]
        )

    def by_columns(grad_mod_all):
        return in_order(
            jnp.stack(
                [
                    grad_mod_all[:, :, j * column_share : (j + 1) * column_share]
                    for j in range(seq_count)
                ]
            ),
            "seq",
        )

    def cond_product(grad_mod_all):
        return dot(grad_mod_all.reshape(dp_count * group, 6 * model), ada_weight, NT).reshape(
            dp_count, group, share
        )

    def ada_product(silu_all, columns):
        return dot(
            silu_all.reshape(seq_count * dp_count * group, share),
            columns.reshape(seq_count * dp_count * group, column_share),
            TN,
        )

    def cond_end(rows):
        rows = in_order(rows, "seq").reshape(latent_count, model)
        _, silu_back = jax.vjp(jax.nn.silu, cond_wide)
        return silu_back(rows)[0]

    def cond_mine_of(cols):
        return jnp.swapaxes(in_order(cols, "dp"), 0, 1).reshape(group, model)

    def split_sums(sums):
        return (
            sums[: 6 * model],
            sums[6 * model : 6 * model + hidden_units],
            sums[6 * model + hidden_units :].astype(jnp.int32),
        )

    if not paired:
        live, place_row, place_col = places_of(gather_all(rank_of(), "seq"))
        silu_rows = trade_all(silu_mine, "dp")
        mod = whole_mod(sum_own(partial_mod(silu_rows), "dp"))
        to_whole = lambda v: [
            swap(whole_slice(v, k), "seq", k) if k else whole_slice(v, k)
            for k in range(seq_count)
        ]
        latent_pieces, cot_pieces = to_whole(latents), to_whole(cotangent)
        joint = whole_weight(jnp.concatenate([qkv_weight, out_weight], axis=1))
        first = whole_weight(unit_order(fc1_weight))
        second = whole_weight(fc2_weight)
        packed, qkv, *mixa = run_enter(joint, place_row, mod, latent_pieces)
        grad_out, grad_mlp = run_cot(place_row, mod, cot_pieces)
        att_own, att_other, projected, hidden, mixed, *mixm = run_attend(
            joint, live, qkv, packed, mod
        )
        acts = run_first(first, mixed)
        block_pieces, (*pres, bias_own, bias_other, gate_m_grad) = run_second(
            second, acts, grad_mlp, grad_out, hidden, mod, place_col, latent_pieces
        )
        grad_hidden, grad_proj, grad_att, mod_grads = run_hidden(
            first, joint, pres, hidden, projected, grad_out, mod
        )
        grad_qkv = run_attend_back(live, qkv, grad_att)
        latent_grads, mod_first = run_leave(
            joint, grad_qkv, packed, grad_hidden, mod, place_col, cot_pieces
        )
        grad_mod = join_mod(mod_first, mod_grads, gate_m_grad)
        sums = sum_everywhere(join_sums(grad_mod, bias_own, bias_other))
        grad_mod_all = gather_all(grad_mod.astype(BF), "dp")
        ada_grad = ada_product(
            gather_all(silu_rows, "seq"), trade_all(by_columns(grad_mod_all), "seq")
        )
        cond_cols = trade_all(cond_product(grad_mod_all), "dp")
        condition_grad = cond_end(gather_all(cond_mine_of(cond_cols), "seq"))

        def mixed_sides(own, other, width):
            both = jnp.stack([own[:, : 4 * width], other[:, : 4 * width]], axis=1)
            return jnp.swapaxes(both.reshape(rows_all, 2, 4, width), 1, 2).reshape(
                rows_all, BLOCKS * width
            )

        product = lambda a, b: spread_plain(dot(a, b, TN))
        fc2_grad = product(mixed_sides(acts[0], acts[1], unit_rows), grad_mlp)
        fc1_grad = product(
            mixed_sides(*mixm, model_rows), mixed_sides(pres[0], pres[1], unit_rows)
        )
        out_grad = product(mixed_sides(att_own, att_other, model_rows), grad_proj)
        qkv_grad = product(mixed_sides(*mixa, model_rows), grad_qkv)
        home = lambda pieces: [swap(v, "seq", k) if k else v for k, v in enumerate(pieces)]
        block_out = put_slices(home(block_pieces), BF)
        latents_grad = put_slices(home(latent_grads), F32)
        return (
            block_out,
            latents_grad,
            condition_grad,
            ada_grad,
            *split_sums(sums)[:1],
            qkv_grad,
            out_grad,
            fc1_grad,
            split_sums(sums)[1],
            fc2_grad,
            split_sums(sums)[2],
        )

    trade = lambda value, axis, step: jnp.stack(
        [
            (lambda split: split[:, 0])(value.reshape((-1, 2, step) + value.shape[1:])),
            swap(value.reshape((-1, 2, step) + value.shape[1:])[:, 1], axis, step),
        ],
        axis=1,
    ).reshape(value.shape)
    grow = lambda value, axis, step: jnp.concatenate([value, swap(value, axis, step)], axis=0)

    joint_own = jnp.concatenate([qkv_weight, out_weight], axis=1)
    first_own = pl.pallas_call(
        functools.partial(reorder_kernel, unit_rows),
        out_shape=sds(fc1_weight.shape, BF),
        in_specs=[VMEM],
        out_specs=VMEM,
        name="reorder",
        compiler_params=pltpu.CompilerParams(vmem_limit_bytes=40 * 1024 * 1024),
    )(fc1_weight)

    ranks = rank_of()[None]
    ranks = grow(ranks, "seq", 1)
    silu_rows = trade(silu_mine, "dp", 2)
    (joint_pair,) = pair_of((joint_own,))
    ranks, silu_rows, joint_pair, joint_own = fence(ranks, silu_rows, joint_pair, joint_own)
    ranks = grow(ranks, "seq", 2)
    silu_rows = trade(silu_rows, "dp", 4)
    ranks, silu_rows, joint_own, latents_in = fence(ranks, silu_rows, joint_own, latents)

    live, place_row, place_col = places_of(ranks)
    latent_pieces = [whole_slice(latents_in, k) for k in range(seq_count)]
    joint_beside = beside_of(joint_own)
    latent_1 = swap(latent_pieces[1], "seq", 1)
    latent_2 = swap(latent_pieces[2], "seq", 2)
    silu_rows = trade(silu_rows, "dp", 1)
    partial = partial_mod(silu_rows)
    pairs = partial.reshape(4, 2, group, 6 * model)
    chip_sum = pairs[:, 0] + swap(pairs[:, 1], "dp", 1)
    latent_3 = latent_pieces[3]
    joint_beside, latent_1, latent_2, chip_sum, silu_rows, latent_3 = fence(
        joint_beside, latent_1, latent_2, chip_sum, silu_rows, latent_3
    )

    joint_beside_pair = pair_of(joint_beside)
    cut = 3 * model
    corners = chip_sum.reshape(2, 2, group, 6 * model)
    sum_a = corners[:, 0, :, :cut] + swap(corners[:, 1, :, :cut], "dp", 2)
    sum_b = corners[0, :, :, cut:] + swap(corners[1, :, :, cut:], "dp", 4)
    joint_tails = (joint_beside[1][:part], joint_beside[0][part:])
    joint_beside_pair, sum_a, sum_b, joint_tails, latent_3 = fence(
        joint_beside_pair, sum_a, sum_b, joint_tails, latent_3
    )
    sum_a = sum_a[0] + swap(sum_a[1], "dp", 4)
    sum_b = sum_b[0] + swap(sum_b[1], "dp", 2)
    mod = whole_mod(jnp.concatenate([sum_a, sum_b], axis=1))
    mod, joint_tails, latent_3 = fence(mod, joint_tails, latent_3)

    latent_3 = swap(latent_3, "seq", 3)
    joint_across = (swap(joint_tails[0], "dp", 2), swap(joint_tails[1], "dp", 4))
    joint_across, latent_3, first_own, cot_in = fence(
        joint_across, latent_3, first_own, cotangent
    )

    first_beside = beside_of(first_own)
    joint_across_pair = pair_of(joint_across)
    joint = pieces_of(
        joint_own, joint_pair, joint_beside, joint_beside_pair, joint_across, joint_across_pair, part
    )
    latent_pieces = [latent_pieces[0], latent_1, latent_2, latent_3]
    packed, qkv, mixa_own, mixa_other = run_enter(joint, place_row, mod, latent_pieces)
    cot_pieces = [whole_slice(cot_in, k) for k in range(seq_count)]
    cot_1 = swap(cot_pieces[1], "seq", 1)
    first_beside, packed, qkv, mixa_own, mixa_other, cot_1, cot_2, cot_3 = fence(
        first_beside, packed, qkv, mixa_own, mixa_other, cot_1, cot_pieces[2], cot_pieces[3]
    )

    first_across = across_of(first_beside, part)
    first_beside_pair = pair_of(first_beside)
    (first_pair,) = pair_of((first_own,))
    cot_2 = swap(cot_2, "seq", 2)
    att_own, att_other, projected, hidden, mixed, mixm_own, mixm_other = run_attend(
        joint, live, qkv, packed, mod
    )
    first_across, first_beside_pair, first_pair, cot_2, mixed, att_own, second_own, cot_3 = fence(
        first_across, first_beside_pair, first_pair, cot_2, mixed, att_own, fc2_weight, cot_3
    )

    second_beside = beside_of(second_own)
    first_across_pair = pair_of(first_across)
    cot_3 = swap(cot_3, "seq", 3)
    first = pieces_of(
        first_own, first_pair, first_beside, first_beside_pair, first_across, first_across_pair, part
    )
    acts = run_first(first, mixed)
    second_beside, acts, cot_3 = fence(second_beside, acts, cot_3)

    second_across = across_of(second_beside, unit_part)
    second_beside_pair = pair_of(second_beside)
    (second_pair,) = pair_of((second_own,))
    cot_pieces = [cot_pieces[0], cot_1, cot_2, cot_3]
    grad_out, grad_mlp = run_cot(place_row, mod, cot_pieces)
    act_pair, grad_mlp_pair = pair_of((acts[1], grad_mlp))
    fc2_cut = outer_pair(
        [((acts[0], act_pair), [(grad_mlp, grad_mlp_pair)])], unit_rows, "fc2_grad"
    )
    second_across, second_beside_pair, second_pair, fc2_cut, grad_out, grad_mlp = fence(
        second_across, second_beside_pair, second_pair, fc2_cut, grad_out, grad_mlp
    )

    fc2_x, fc2_y = swap(fc2_cut[0], "dp", 2), swap(fc2_cut[1], "dp", 4)
    second_across_pair = pair_of(second_across)
    second = pieces_of(
        second_own,
        second_pair,
        second_beside,
        second_beside_pair,
        second_across,
        second_across_pair,
        unit_part,
    )
    block_pieces, (pre_own, pre_other, bias_own, bias_other, gate_m_grad) = run_second(
        second, acts, grad_mlp, grad_out, hidden, mod, place_col, latent_pieces
    )
    fc2_x, fc2_y, block_pieces, pre_own, pre_other, mixm_other, att_other, mixa_other = fence(
        fc2_x, fc2_y, block_pieces, pre_own, pre_other, mixm_other, att_other, mixa_other
    )

    on_x, on_y = near_sums(fc2_cut, fc2_x, fc2_y)
    fc2_far = (swap(on_y, "dp", 4), swap(on_x, "dp", 2))
    pre_other_pair, pre_own_pair, mixm_pair = pair_of((pre_own, pre_other, mixm_other))
    grad_hidden, grad_proj, grad_att, mod_grads = run_hidden(
        first, joint, (pre_own, pre_other), hidden, projected, grad_out, mod
    )
    fc1_cut = outer_pair(
        [((mixm_own, mixm_pair), [(pre_own, pre_own_pair), (pre_other, pre_other_pair)])],
        model_rows,
        "fc1_grad",
    )
    block_1 = swap(block_pieces[1], "seq", 1)
    fc2_far, grad_att, grad_proj, fc1_cut, block_1, block_2, block_3 = fence(
        fc2_far, grad_att, grad_proj, fc1_cut, block_1, block_pieces[2], block_pieces[3]
    )

    fc1_x, fc1_y = swap(fc1_cut[0], "dp", 2), swap(fc1_cut[1], "dp", 4)
    fc2_parts = fold(
        fc2_cut[2],
        fc2_x,
        fc2_y,
        *fc2_far,
        (plain_cuts(0, model, seq_count),),
        "fc2_fold",
    )
    fc2_1 = swap(fc2_parts[1], "seq", 1)
    block_2 = swap(block_2, "seq", 2)
    grad_qkv = run_attend_back(live, qkv, grad_att)
    latent_grads, mod_first = run_leave(
        joint, grad_qkv, packed, grad_hidden, mod, place_col, cot_pieces
    )
    proj_pair, att_pair, mixa_pair, qkv_pair = pair_of((grad_proj, att_other, mixa_other, grad_qkv))
    grad_mod = join_mod(mod_first, mod_grads, gate_m_grad)
    sums = join_sums(grad_mod, bias_own, bias_other)
    grad_mod_all = grad_mod.astype(BF)[None]
    (
        fc1_x,
        fc1_y,
        fc2_1,
        fc2_2,
        fc2_3,
        block_2,
        block_3,
        latent_grads,
        grad_qkv,
        proj_pair,
        att_pair,
        mixa_pair,
        qkv_pair,
        sums,
        grad_mod_all,
    ) = fence(
        fc1_x,
        fc1_y,
        fc2_1,
        fc2_parts[2],
        fc2_parts[3],
        block_2,
        block_3,
        latent_grads,
        grad_qkv,
        proj_pair,
        att_pair,
        mixa_pair,
        qkv_pair,
        sums,
        grad_mod_all,
    )

    on_x, on_y = near_sums(fc1_cut, fc1_x, fc1_y)
    fc1_far = (swap(on_y, "dp", 4), swap(on_x, "dp", 2))
    block_3 = swap(block_3, "seq", 3)
    last_cut = outer_pair(
        [
            ((mixa_own, mixa_pair), [(grad_qkv, qkv_pair)]),
            ((att_own, att_pair), [(grad_proj, proj_pair)]),
        ],
        model_rows,
        "last_grad",
    )
    sums = sums + swap(sums, "dp", 1)
    grad_mod_all = grow(grad_mod_all, "dp", 1)
    fc1_far, block_3, last_cut, sums, grad_mod_all, fc2_2, fc2_3, latent_grads = fence(
        fc1_far, block_3, last_cut, sums, grad_mod_all, fc2_2, fc2_3, latent_grads
    )
    block_out = put_slices((block_pieces[0], block_1, block_2, block_3), BF)
    sums = sums + swap(sums, "dp", 4)
    grad_mod_all = grow(grad_mod_all, "dp", 2)
    sums, grad_mod_all, last_cut = fence(sums, grad_mod_all, last_cut)
    sums = sums + swap(sums, "dp", 2)
    grad_mod_all = grow(grad_mod_all, "dp", 4)
    sums, grad_mod_all, last_cut, fc2_2, fc2_3, latent_grads = fence(
        sums, grad_mod_all, last_cut, fc2_2, fc2_3, latent_grads
    )

    last_x, last_y = swap(last_cut[0], "dp", 2), swap(last_cut[1], "dp", 4)
    fc1_cuts = tuple(
        tuple((lo, lo + unit_rows) for lo in (j * unit_rows, half_units + j * unit_rows))
        for j in range(seq_count)
    )
    fc1_parts = fold(fc1_cut[2], fc1_x, fc1_y, *fc1_far, (fc1_cuts,), "fc1_fold")
    fc2_2 = swap(fc2_2, "seq", 2)
    fc2_3 = swap(fc2_3, "seq", 3)
    cond_cols = trade(cond_product(grad_mod_all), "dp", 1)
    columns = by_columns(grad_mod_all)
    latent_1 = swap(latent_grads[1], "seq", 1)
    sums = sums + swap(sums, "seq", 1)
    last_x, last_y, fc2_2, fc2_3, cond_cols, columns, latent_1, sums, fc1_parts = fence(
        last_x, last_y, fc2_2, fc2_3, cond_cols, columns, latent_1, sums, fc1_parts
    )
    cond_cols = trade(cond_cols, "dp", 2)
    columns = trade(columns, "seq", 1)
    cond_cols, columns, last_x, last_y = fence(cond_cols, columns, last_x, last_y)
    cond_cols = trade(cond_cols, "dp", 4)
    columns = trade(columns, "seq", 2)
    cond_cols, columns, last_x, last_y, latent_2, latent_3, fc1_parts = fence(
        cond_cols, columns, last_x, last_y, latent_grads[2], latent_grads[3], fc1_parts
    )

    on_x, on_y = near_sums(last_cut, last_x, last_y)
    last_far = (swap(on_y, "dp", 4), swap(on_x, "dp", 2))
    fc2_grad = (
        fc2_parts[0].astype(F32)
        + fc2_1.astype(F32)
        + fc2_2.astype(F32)
        + fc2_3.astype(F32)
    )
    cond_rows = grow(cond_mine_of(cond_cols)[None], "seq", 1)
    silu_all = gather_all(silu_rows, "seq")
    ada_grad = ada_product(silu_all, columns)
    latent_2 = swap(latent_2, "seq", 2)
    latent_3 = swap(latent_3, "seq", 3)
    last_far, cond_rows, fc1_parts, latent_2, latent_3, sums = fence(
        last_far, cond_rows, fc1_parts, latent_2, latent_3, sums
    )

    last_parts = fold(
        last_cut[2],
        last_x,
        last_y,
        *last_far,
        (plain_cuts(0, 3 * model, seq_count), plain_cuts(3 * model, model, seq_count)),
        "last_fold",
    )
    sums = sums + swap(sums, "seq", 2)
    condition_grad = cond_end(grow(cond_rows, "seq", 2))
    gather_parts = lambda parts: sum(
        (swap(parts[k], "seq", k) if k else parts[0]).astype(F32) for k in range(seq_count)
    )
    fc1_grad = gather_parts(fc1_parts)
    fc1_grad = jnp.where(
        parity == 1,
        jnp.concatenate([fc1_grad[:, unit_rows:], fc1_grad[:, :unit_rows]], axis=1),
        fc1_grad,
    )
    qkv_grad = gather_parts(last_parts[:seq_count])
    out_grad = gather_parts(last_parts[seq_count:])
    latents_grad = put_slices((latent_grads[0], latent_1, latent_2, latent_3), F32)
    ada_bias_grad, fc1_bias_grad, kept_total = split_sums(sums)
    return (
        block_out,
        latents_grad,
        condition_grad,
        ada_grad,
        ada_bias_grad,
        qkv_grad,
        out_grad,
        fc1_grad,
        fc1_bias_grad,
        fc2_grad,
        kept_total,
    )


def solution(mesh):
    placed = (
        P("dp", "seq", None),
        P("dp", None),
        P("dp", "seq"),
        P("dp", "seq"),
        P("dp", None),
        P(),
        P("dp", None),
        P("dp", None),
        P("dp", None),
        P(),
        P("dp", None),
        P("dp", "seq", None),
    )
    return jax.shard_map(
        body,
        mesh=mesh,
        in_specs=placed,
        out_specs=(
            P("dp", "seq", None),
            P("dp", "seq", None),
            P("dp", None),
            P("dp", "seq"),
            P(),
            P("dp", "seq"),
            P("dp", "seq"),
            P("dp", "seq"),
            P(),
            P("dp", "seq"),
            P(),
        ),
        check_vma=False,
    )
```

```python
import functools
import math

import jax
import jax.numpy as jnp
from jax import lax
from jax.experimental import pallas as pl
from jax.experimental.pallas import tpu as pltpu
from jax.sharding import PartitionSpec as P

HEADS = 16
HEAD = 72
LANES = 128
BLOCKS = 8

layer_eps = 1e-06
far_below = -1e30
att_scale = 1.0 / math.sqrt(HEAD)
gelu_c = math.sqrt(2.0 / math.pi)
gelu_k = 0.044715

BF = jnp.bfloat16
F32 = jnp.float32
VMEM = pl.BlockSpec(memory_space=pltpu.VMEM)
SMEM = pl.BlockSpec(memory_space=pltpu.SMEM)
ANY = pl.BlockSpec(memory_space=pl.ANY)
NT = (((1,), (1,)), ((), ()))
TN = (((0,), (0,)), ((), ()))


def swap(value, axis, step):
    return lax.ppermute(value, axis, [(i, i ^ step) for i in range(lax.axis_size(axis))])


def steps_of(axis):
    count = lax.axis_size(axis)
    return [1 << i for i in range(count.bit_length() - 1)]


def bit_set(axis, step):
    return (lax.axis_index(axis) & step) != 0


def gather_all(value, axis):
    value = value[None]
    for step in steps_of(axis):
        value = jnp.concatenate([value, swap(value, axis, step)], axis=0)
    return value


def sum_own(value, axis):
    for step in reversed(steps_of(axis)):
        value = value[:step] + swap(value[step:], axis, step)
    return value[0]


def trade_all(value, axis):
    count = value.shape[0]
    rest = value.shape[1:]
    for step in steps_of(axis):
        split = value.reshape((count // (2 * step), 2, step) + rest)
        value = jnp.stack([split[:, 0], swap(split[:, 1], axis, step)], axis=1).reshape(
            (count,) + rest
        )
    return value


def in_order(value, axis):
    count = value.shape[0]
    rest = value.shape[1:]
    for step in steps_of(axis):
        split = value.reshape((count // (2 * step), 2, step) + rest)
        value = jnp.where(bit_set(axis, step), split[:, ::-1], split).reshape((count,) + rest)
    return value


def sum_everywhere(value):
    for axis in ("dp", "seq"):
        for step in steps_of(axis):
            value = value + swap(value, axis, step)
    return value


def after(value, *earlier):
    return lax.optimization_barrier((value,) + earlier)[0]


def halves_of(rows):
    first = (rows // 2 + 15) // 16 * 16
    return first, rows - first


def pieces_of(own, own_pair, beside, beside_pair, across, across_pair, part):
    return [
        (own, 0, 0),
        (own_pair, 1, 0),
        (beside[0], 2, 0),
        (beside_pair[0], 3, 0),
        (beside[1], 4, 0),
        (beside_pair[1], 5, 0),
        (across[0], 6, 0),
        (across[1], 6, part),
        (across_pair[0], 7, 0),
        (across_pair[1], 7, part),
    ]


def beside_of(shard):
    return swap(shard, "dp", 2), swap(shard, "dp", 4)


def across_of(beside, part):
    return swap(beside[1][:part], "dp", 2), swap(beside[0][part:], "dp", 4)


def pair_of(values):
    return tuple(swap(v, "dp", 1) for v in values)


def placed(pieces, position, rows):
    starts = jnp.stack([position(k) * rows + first for _, k, first in pieces]).astype(jnp.int32)
    return [v for v, _, _ in pieces], starts


def whole_weight(shard):
    return [lax.all_gather(shard, "dp", axis=0, tiled=True)], jnp.zeros((1,), jnp.int32)


def call(kernel, outs, ins, specs, scratch, name):
    return pl.pallas_call(
        kernel,
        out_shape=outs,
        in_specs=specs,
        out_specs=jax.tree.map(lambda _: VMEM, outs),
        scratch_shapes=scratch,
        name=name,
        compiler_params=pltpu.CompilerParams(vmem_limit_bytes=60 * 1024 * 1024),
    )(*ins)


def start_pieces(offsets, refs, target, sem, lo, hi):
    copies = []
    for k, ref in enumerate(refs):
        rows = ref.shape[0]
        copies.append(
            pltpu.make_async_copy(
                ref.at[:, pl.ds(lo, hi - lo)],
                target.at[pl.ds(pl.multiple_of(offsets[k], 16), rows), :],
                sem.at[k],
            )
        )
    for one in copies:
        one.start()
    return copies


def wait_all(copies):
    for one in copies:
        one.wait()


def normal(rows_in):
    center = rows_in - jnp.mean(rows_in, axis=-1, keepdims=True)
    inverse = lax.rsqrt(jnp.mean(center * center, axis=-1, keepdims=True) + layer_eps)
    return center * inverse, inverse


def normal_back(grad_rows, normed, inverse):
    mean_grad = jnp.mean(grad_rows, axis=-1, keepdims=True)
    mean_proj = jnp.mean(grad_rows * normed, axis=-1, keepdims=True)
    return inverse * (grad_rows - mean_grad - normed * mean_proj)


def dot(left, right, dims=None):
    if dims is None:
        return jnp.dot(left, right, preferred_element_type=F32)
    return lax.dot_general(left, right, dims, preferred_element_type=F32)


def spans(total, width):
    return [(lo, min(lo + width, total)) for lo in range(0, total, width)]


def pack_rows(place_ref, piece_refs, latent, rows_out):
    gathered = jnp.concatenate([ref[latent] for ref in piece_refs], axis=0)
    slots = lax.broadcasted_iota(jnp.int32, (rows_out, gathered.shape[0]), 0)
    chosen = jnp.where(place_ref[latent] == slots, 1.0, 0.0).astype(BF)
    return dot(chosen, gathered)


def unpack_rows(slots_ref, latent, packed, out_refs):
    slots = slots_ref[latent]
    rows = lax.broadcasted_iota(jnp.int32, (slots.shape[0], packed.shape[0]), 1)
    spread = dot(jnp.where(slots == rows, 1.0, 0.0).astype(BF), packed).astype(BF)
    block = out_refs[0].shape[1]
    for k, out in enumerate(out_refs):
        out[latent] = spread[k * block : (k + 1) * block]


def home_kernel(at, rank, base, *refs):
    pieces, out = refs[:-1], refs[-1]
    group, slots, _ = pieces[0].shape
    for k, piece in enumerate(pieces):
        for j in range(group):
            latent = (at[0] ^ k) * group + j
            place = rank[latent]
            rows = lax.broadcasted_iota(jnp.int32, (place.shape[0], slots), 1)
            spread = dot(jnp.where(place == rows, 1.0, 0.0).astype(BF), piece[j])
            out[latent] = jnp.where(place >= 0, spread, base[latent].astype(F32)).astype(out.dtype)


def cut_kernel(first, top, bottom, top_out, bottom_out):
    top_out[...] = top[:first, :]
    bottom_out[...] = bottom[first:, :]


def split_parity(rows_low, order_ref, own_ref, other_ref):
    moved = dot(rows_low, order_ref[...]).astype(BF)
    width = own_ref.shape[1]
    own_ref[...] = moved[:, :width]
    other_ref[...] = moved[:, width:]


def enter_kernel(pieces, blocks, cap, *refs):
    (offsets, place, mod, order), refs = refs[:4], refs[4:]
    latents, refs = refs[:blocks], refs[blocks:]
    weights, refs = refs[:pieces], refs[pieces:]
    packed_out, qkv_out, own_out, other_out, weight, mixed, sem = refs
    width = qkv_out.shape[1]
    copies = start_pieces(offsets, weights, weight, sem, 0, width)
    for latent in range(mod.shape[0]):
        here = pl.ds(latent * cap, cap)
        rows = pack_rows(place, latents, latent, cap)
        packed_out[here, :] = rows.astype(BF)
        normed, _ = normal(rows)
        mixed[here, :] = (normed * (1.0 + mod[latent, 1:2, :]) + mod[latent, 0:1, :]).astype(BF)
    split_parity(mixed[...], order, own_out, other_out)
    wait_all(copies)
    for lo, hi in spans(width, 768):
        qkv_out[:, lo:hi] = dot(mixed[...], weight[:, lo:hi]).astype(BF)


def cot_kernel(blocks, cap, *refs):
    place, mod = refs[:2]
    cots = refs[2 : 2 + blocks]
    packed_out, mlp_out = refs[2 + blocks :]
    for latent in range(mod.shape[0]):
        here = pl.ds(latent * cap, cap)
        rows = pack_rows(place, cots, latent, cap)
        packed_out[here, :] = rows.astype(BF)
        mlp_out[here, :] = (mod[latent, 5:6, :] * rows).astype(BF)


def windows():
    found = []
    for head in range(HEADS):
        first = head * HEAD
        base = first // LANES * LANES
        width = LANES if first + HEAD <= base + LANES else 2 * LANES
        found.append((base, width, first - base))
    return found


def head_mask(width, first, dtype):
    lane = lax.broadcasted_iota(jnp.int32, (1, width), 1)
    return jnp.where((lane >= first) & (lane < first + HEAD), 1.0, 0.0).astype(dtype)


def attend_kernel(pieces, cap, model, *refs):
    (offsets, live, qkv, packed, mod, order), refs = refs[:6], refs[6:]
    weights, refs = refs[:pieces], refs[pieces:]
    (own_att, other_att, proj_out, hidden_out, mixed_out, own_mix, other_mix), refs = (
        refs[:7],
        refs[7:],
    )
    weight, attended, sem = refs
    copies = start_pieces(offsets, weights, weight, sem, 3 * model, 4 * model)
    attended[...] = jnp.zeros_like(attended)

    def one_latent(latent, carry):
        here = pl.ds(pl.multiple_of(latent * cap, 16), cap)
        count = live[latent]
        seen = lax.broadcasted_iota(jnp.int32, (cap, cap), 1) < count
        for base, width, first in windows():
            low_mask = head_mask(width, first, BF)
            query = qkv[here, base : base + width] * low_mask
            key = qkv[here, model + base : model + base + width]
            value = qkv[here, 2 * model + base : 2 * model + base + width]
            scores = jnp.where(seen, dot(query, key, NT) * att_scale, far_below)
            raised = jnp.exp(scores - jnp.max(scores, axis=-1, keepdims=True))
            total = jnp.sum(raised, axis=-1, keepdims=True)
            mixed = dot(raised.astype(BF), value) / total
            attended[here, base : base + width] += mixed * head_mask(width, first, F32)
        return carry

    lax.fori_loop(0, mod.shape[0], one_latent, 0)
    att_low = attended[...].astype(BF)
    split_parity(att_low, order, own_att, other_att)
    wait_all(copies)
    projected = dot(att_low, weight[...])
    proj_out[...] = projected
    for latent in range(mod.shape[0]):
        rows = slice(latent * cap, (latent + 1) * cap)
        hidden = packed[rows, :].astype(F32) + mod[latent, 2:3, :] * projected[rows]
        hidden_out[rows, :] = hidden
        normed, _ = normal(hidden)
        mixed_out[rows, :] = (
            normed * (1.0 + mod[latent, 4:5, :]) + mod[latent, 3:4, :]
        ).astype(BF)
    split_parity(mixed_out[...], order, own_mix, other_mix)


def first_kernel(pieces, *refs):
    (offsets, parity, mixed, bias), refs = refs[:4], refs[4:]
    weights, refs = refs[:pieces], refs[pieces:]
    own_act, other_act, own_slope, other_slope, weight, sem = refs
    copies = start_pieces(offsets, weights, weight, sem, 0, weight.shape[1])
    half = own_act.shape[1]
    wait_all(copies)
    for side, (act_out, slope_out) in enumerate(
        ((own_act, own_slope), (other_act, other_slope))
    ):
        base = (parity[0] ^ side) * half
        for lo, hi in spans(half, 768):
            cols = pl.ds(pl.multiple_of(base + lo, LANES), hi - lo)
            pre = dot(mixed[...], weight[:, cols]) + bias[:, cols]
            square = pre * pre
            curve = jnp.tanh(gelu_c * pre * (1.0 + gelu_k * square))
            cdf = 0.5 * (1.0 + curve)
            act_out[:, lo:hi] = (pre * cdf).astype(BF)
            slope = cdf + pre * (0.5 * gelu_c) * (1.0 - curve * curve) * (
                1.0 + 3.0 * gelu_k * square
            )
            slope_out[:, lo:hi] = slope.astype(BF)


def slope_kernel(pieces, *refs):
    (offsets, own_slope, other_slope, grad_mlp), refs = refs[:4], refs[4:]
    weights, refs = refs[:pieces], refs[pieces:]
    own_pre, other_pre, own_bias, other_bias, weight, sem = refs
    copies = start_pieces(offsets, weights, weight, sem, 0, weight.shape[1])
    half = own_pre.shape[1]
    wait_all(copies)
    for side, (slope, pre_out, bias_out) in enumerate(
        ((own_slope, own_pre, own_bias), (other_slope, other_pre, other_bias))
    ):
        for lo, hi in spans(half, 768):
            grad_act = dot(grad_mlp[...], weight[side * half + lo : side * half + hi, :], NT)
            grad_pre = (grad_act * slope[:, lo:hi].astype(F32)).astype(BF)
            pre_out[:, lo:hi] = grad_pre
            bias_out[:, lo:hi] = jnp.sum(grad_pre.astype(F32), axis=0, keepdims=True)


def second_kernel(pieces, blocks, cap, *refs):
    (offsets, own_act, other_act, grad_out, hidden, mod, slots), refs = refs[:7], refs[7:]
    weights, refs = refs[:pieces], refs[pieces:]
    outs, refs = refs[:blocks], refs[blocks:]
    gate_grad, weight, sem = refs
    copies = start_pieces(offsets, weights, weight, sem, 0, weight.shape[1])
    half = own_act.shape[1]
    wait_all(copies)
    mlp = dot(own_act[...], weight[:half, :]) + dot(other_act[...], weight[half:, :])
    for latent in range(mod.shape[0]):
        rows = slice(latent * cap, (latent + 1) * cap)
        gate_grad[latent, :, :] = jnp.sum(
            grad_out[rows, :].astype(F32) * mlp[rows], axis=0, keepdims=True
        )
        block = (hidden[rows, :] + mod[latent, 5:6, :] * mlp[rows]).astype(BF)
        unpack_rows(slots, latent, block, outs)


def hidden_kernel(pieces, first_pieces, cap, model, *refs):
    (
        first_offsets,
        offsets,
        parity,
        own_pre,
        other_pre,
        hidden_in,
        projected,
        grad_out,
        mod,
    ), refs = refs[:9], refs[9:]
    first_weights, refs = refs[:first_pieces], refs[first_pieces:]
    out_weights, refs = refs[:pieces], refs[pieces:]
    grad_hidden, grad_proj, grad_att, mod_grads, first, out_weight, first_sem, out_sem = refs
    copies = start_pieces(first_offsets, first_weights, first, first_sem, 0, first.shape[1])
    later = start_pieces(offsets, out_weights, out_weight, out_sem, 3 * model, 4 * model)
    half = own_pre.shape[1]
    wait_all(copies)
    total = None
    for side, pre in enumerate((own_pre, other_pre)):
        base = (parity[0] ^ side) * half
        for lo, hi in spans(half, 768):
            cols = pl.ds(pl.multiple_of(base + lo, LANES), hi - lo)
            part = dot(pre[:, lo:hi], first[:, cols], NT)
            total = part if total is None else total + part
    for latent in range(mod.shape[0]):
        rows = slice(latent * cap, (latent + 1) * cap)
        normed, inverse = normal(hidden_in[rows, :])
        grad_mixed = total[rows]
        mod_grads[latent, 0:1, :] = jnp.sum(grad_mixed, axis=0, keepdims=True)
        mod_grads[latent, 1:2, :] = jnp.sum(grad_mixed * normed, axis=0, keepdims=True)
        grad = grad_out[rows, :].astype(F32) + normal_back(
            grad_mixed * (1.0 + mod[latent, 4:5, :]), normed, inverse
        )
        grad_hidden[rows, :] = grad
        mod_grads[latent, 2:3, :] = jnp.sum(grad * projected[rows, :], axis=0, keepdims=True)
        grad_proj[rows, :] = (mod[latent, 2:3, :] * grad).astype(BF)
    wait_all(later)
    grad_att[...] = dot(grad_proj[...], out_weight[...], NT).astype(BF)


def attend_back_kernel(cap, model, *refs):
    live, qkv, grad_att, grad_qkv, sums = refs
    sums[...] = jnp.zeros_like(sums)

    def one_latent(latent, carry):
        here = pl.ds(pl.multiple_of(latent * cap, 16), cap)
        count = live[latent]
        seen = lax.broadcasted_iota(jnp.int32, (cap, cap), 0) < count
        for base, width, first in windows():
            low_mask = head_mask(width, first, BF)
            wide_mask = head_mask(width, first, F32)
            cols = slice(base, base + width)
            key_cols = slice(model + base, model + base + width)
            value_cols = slice(2 * model + base, 2 * model + base + width)
            query, key, value = qkv[here, cols], qkv[here, key_cols], qkv[here, value_cols]
            grad = grad_att[here, cols]
            scores = jnp.where(seen, dot(key * low_mask, query, NT) * att_scale, far_below)
            raised = jnp.exp(scores - jnp.max(scores, axis=0, keepdims=True))
            probs = raised / jnp.sum(raised, axis=0, keepdims=True)
            grad_probs = dot(value * low_mask, grad, NT)
            delta = jnp.sum(probs * grad_probs, axis=0, keepdims=True)
            grad_scores = (probs * (grad_probs - delta)).astype(BF)
            scaled = wide_mask * att_scale
            sums[here, cols] += dot(grad_scores, key, TN) * scaled
            sums[here, key_cols] += dot(grad_scores, query) * scaled
            sums[here, value_cols] += dot(probs.astype(BF), grad) * wide_mask
        return carry

    lax.fori_loop(0, live.shape[0], one_latent, 0)
    grad_qkv[...] = sums[...].astype(BF)


def leave_kernel(pieces, blocks, cap, *refs):
    (offsets, grad_qkv, packed, grad_hidden, mod, slots), refs = refs[:6], refs[6:]
    weights, refs = refs[:pieces], refs[pieces:]
    outs, refs = refs[:blocks], refs[blocks:]
    mod_grads, weight, sem = refs
    copies = start_pieces(offsets, weights, weight, sem, 0, weight.shape[1])
    wait_all(copies)
    total = None
    for lo, hi in spans(weight.shape[1], 768):
        part = dot(grad_qkv[:, lo:hi], weight[:, lo:hi], NT)
        total = part if total is None else total + part
    for latent in range(mod.shape[0]):
        rows = slice(latent * cap, (latent + 1) * cap)
        normed, inverse = normal(packed[rows, :].astype(F32))
        grad_mixed = total[rows]
        mod_grads[latent, 0:1, :] = jnp.sum(grad_mixed, axis=0, keepdims=True)
        mod_grads[latent, 1:2, :] = jnp.sum(grad_mixed * normed, axis=0, keepdims=True)
        grad = grad_hidden[rows, :] + normal_back(
            grad_mixed * (1.0 + mod[latent, 1:2, :]), normed, inverse
        )
        unpack_rows(slots, latent, grad.astype(BF), outs)


def outer_kernel(rows, used, sides, *refs):
    block_at, refs = refs[0], refs[1:]
    total = sum(sides)
    lefts, refs = refs[: 2 * len(sides)], refs[2 * len(sides) :]
    rights, refs = refs[: 2 * total], refs[2 * total :]
    (far_x, far_y, near_x, near_y, keep, keep_x, keep_y), refs = refs[:7], refs[7:]
    result, sem = refs
    part, rest = halves_of(rows)
    base, at = 0, 0
    for group, count in enumerate(sides):
        own_left, pair_left = lefts[2 * group : 2 * group + 2]
        left = jnp.concatenate([own_left[:, :used], pair_left[:, :used]], axis=0)
        for own, pair in zip(rights[2 * at : 2 * (at + count) : 2], rights[2 * at + 1 : 2 * (at + count) : 2]):
            width = own.shape[1]
            for lo, hi in spans(width, 768):
                right = jnp.concatenate([own[:, lo:hi], pair[:, lo:hi]], axis=0)
                result[:, base + lo : base + hi] = dot(left, right, TN).astype(BF)
            base += width
        at += count

    def rows_at(k, first, count):
        return result.at[pl.ds(pl.multiple_of(block_at[k] * rows + first, 16), count), :]

    moves = [
        (rows_at(3, 0, part), far_x),
        (rows_at(3, part, rest), far_y),
        (rows_at(1, 0, part), near_x),
        (rows_at(2, part, rest), near_y),
        (rows_at(0, 0, rows), keep),
        (rows_at(1, part, rest), keep_x),
        (rows_at(2, 0, part), keep_y),
    ]
    copies = [pltpu.make_async_copy(a, b, sem.at[i]) for i, (a, b) in enumerate(moves)]
    for one in copies:
        one.start()
    wait_all(copies)


def reorder_kernel(unit, shard, whole):
    count = shard.shape[1] // unit
    for block in range(count):
        to = (block % 2) * (count // 2) + block // 2
        whole[:, to * unit : (to + 1) * unit] = shard[:, block * unit : (block + 1) * unit]


def fold_kernel(cuts, turned, *refs):
    (at, keep, near_top, near_bottom, far_top, far_bottom), refs = refs[:6], refs[6:]
    count = len(cuts[0])
    outs, refs = refs[: 3 * len(cuts)], refs[3 * len(cuts) :]
    scratch, sem = refs[:-1], refs[-1]
    part = far_top.shape[0]
    wide = lambda ref: ref[...].astype(F32)
    top = keep[:part, :].astype(F32) + wide(near_top) + wide(far_top)
    bottom = keep[part:, :].astype(F32) + wide(near_bottom) + wide(far_bottom)
    copies = []
    if turned:
        top, bottom = top.T, bottom.T
    for i, (group, parts) in enumerate(zip(cuts, scratch)):
        for j, pieces in enumerate(group):
            first = 0
            for lo, hi in pieces:
                if turned:
                    parts[j, :, :part] = top[lo:hi, :].astype(BF)
                    parts[j, :, part:] = bottom[lo:hi, :].astype(BF)
                    continue
                parts[j, :part, first : first + hi - lo] = top[:, lo:hi].astype(BF)
                parts[j, part:, first : first + hi - lo] = bottom[:, lo:hi].astype(BF)
                first += hi - lo
        sent, own, across = outs[3 * i : 3 * i + 3]
        for k, out in ((1, sent.at[0]), (3, sent.at[1]), (0, own), (2, across)):
            copies.append(pltpu.make_async_copy(parts.at[at[0] ^ k], out, sem.at[len(copies)]))
    for one in copies:
        one.start()
    wait_all(copies)


def outer_pair(groups, rows, name):
    used = 4 * rows
    part, rest = halves_of(rows)
    lefts = [v for left, _ in groups for v in left]
    rights = [v for _, pairs in groups for pair in pairs for v in pair]
    width = sum(v.shape[1] for v in rights) // 2
    sides = tuple(len(pairs) for _, pairs in groups)
    block_at = jnp.stack([(lax.axis_index("dp") ^ (2 * k)) // 2 for k in range(4)]).astype(jnp.int32)
    ins = [block_at, *lefts, *rights]
    outs = (
        jax.ShapeDtypeStruct((part, width), BF),
        jax.ShapeDtypeStruct((rest, width), BF),
        jax.ShapeDtypeStruct((part, width), BF),
        jax.ShapeDtypeStruct((rest, width), BF),
        jax.ShapeDtypeStruct((rows, width), BF),
        jax.ShapeDtypeStruct((rest, width), BF),
        jax.ShapeDtypeStruct((part, width), BF),
    )
    return pl.pallas_call(
        functools.partial(outer_kernel, rows, used, sides),
        out_shape=outs,
        in_specs=[SMEM] + [VMEM] * (len(ins) - 1),
        out_specs=tuple(ANY for _ in outs),
        scratch_shapes=[pltpu.VMEM((used, width), BF), pltpu.SemaphoreType.DMA((7,))],
        name=name,
        compiler_params=pltpu.CompilerParams(vmem_limit_bytes=60 * 1024 * 1024),
    )(*ins)


def onward(cut, far):
    on_x = (cut[5].astype(F32) + far[1].astype(F32)).astype(BF)
    on_y = (cut[6].astype(F32) + far[0].astype(F32)).astype(BF)
    return on_x, on_y


def along_xy(pair):
    return swap(pair[0], "dp", 2), swap(pair[1], "dp", 4)


def fold(keep, near, last, cuts, name, turned=False):
    rows = keep.shape[0]
    count = lax.axis_size("seq")
    at = lax.axis_index("seq").reshape(1).astype(jnp.int32)
    widths = tuple(sum(hi - lo for lo, hi in group[0]) for group in cuts)
    blocks = [(w, rows) if turned else (rows, w) for w in widths]
    outs = tuple(
        jax.ShapeDtypeStruct(shape, BF) for block in blocks for shape in ((2,) + block, block, block)
    )
    return pl.pallas_call(
        functools.partial(fold_kernel, cuts, turned),
        out_shape=outs,
        in_specs=[SMEM] + [VMEM] * 5,
        out_specs=tuple(ANY for _ in outs),
        scratch_shapes=[pltpu.VMEM((count,) + block, BF) for block in blocks]
        + [pltpu.SemaphoreType.DMA((4 * len(cuts),))],
        name=name,
        compiler_params=pltpu.CompilerParams(vmem_limit_bytes=60 * 1024 * 1024),
    )(at, keep, near[0], near[1], last[1], last[0])


def plain_cuts(first, width, count):
    share = width // count
    return tuple(((first + j * share, first + (j + 1) * share),) for j in range(count))


def spread_plain(grad):
    grad = lax.psum_scatter(grad, "dp", scatter_dimension=0, tiled=True)
    return lax.psum_scatter(grad, "seq", scatter_dimension=1, tiled=True)


def body(
    latents,
    condition,
    keep_order,
    keep_count,
    ada_weight,
    ada_bias,
    qkv_weight,
    out_weight,
    fc1_weight,
    fc1_bias,
    fc2_weight,
    cotangent,
):
    latent_count, block_rows, model = latents.shape
    hidden_units = fc1_weight.shape[1]
    half_units = hidden_units // 2
    unit_rows = hidden_units // BLOCKS
    model_rows = model // BLOCKS
    dp_count, seq_count = lax.axis_size("dp"), lax.axis_size("seq")
    dp_at, seq_at = lax.axis_index("dp"), lax.axis_index("seq")
    group = latent_count // seq_count
    most = block_rows * 3 // 4
    cap = (seq_count - 1) * most + block_rows // 4
    rows_all = group * cap
    share = model // dp_count
    column_share = 6 * model // seq_count
    paired = dp_count == BLOCKS and seq_count == 4
    parity = (dp_at & 1) if paired else jnp.zeros_like(dp_at)
    parity_in = parity.reshape(1).astype(jnp.int32)
    part, _ = halves_of(model_rows)
    unit_part, _ = halves_of(unit_rows)
    whose = (lambda k: dp_at ^ k) if paired else (lambda k: jnp.int32(k))
    sds = jax.ShapeDtypeStruct
    dma = lambda n: pltpu.SemaphoreType.DMA((n,))
    fence = lambda *values: lax.optimization_barrier(values)

    def rank_of():
        slot = lax.broadcasted_iota(jnp.int32, (1, block_rows, 1), 1)
        token = lax.broadcasted_iota(jnp.int32, (1, 1, block_rows), 2)
        found = (keep_order[:, :, None] == token) & (slot < keep_count[:, :, None])
        return jnp.max(jnp.where(found, slot, -1), axis=1)

    def places_of(ranks):
        ranks = lax.dynamic_slice_in_dim(ranks, seq_at * group, group, 1)
        ranks = jnp.swapaxes(ranks, 0, 1)
        counts = jnp.sum((ranks >= 0).astype(jnp.int32), axis=2)
        starts = jnp.cumsum(counts, axis=1) - counts
        live = jnp.sum(counts, axis=1).astype(jnp.int32)
        place = jnp.where(ranks >= 0, ranks + starts[:, :, None], -1).reshape(
            group, seq_count * block_rows
        )
        slot = lax.broadcasted_iota(jnp.int32, (1, 1, most), 2)
        slots = jnp.where(slot < counts[:, :, None], starts[:, :, None] + slot, -1)
        return live, place[:, None, :], slots.reshape(group, seq_count * most, 1)

    def whole_slice(blocks_in, k):
        return lax.dynamic_slice_in_dim(blocks_in, (seq_at ^ k) * group, group, 0)

    rank = rank_of()

    def run_home(pieces, base, dtype, name):
        return call(
            home_kernel,
            sds((latent_count, block_rows, model), dtype),
            [seq_at.reshape(1).astype(jnp.int32), rank[:, :, None], base, *pieces],
            [SMEM] + [VMEM] * (2 + seq_count),
            [],
            name,
        )

    cond_wide = condition.astype(F32)
    silu_cond = jax.nn.silu(cond_wide).astype(BF)
    silu_mine = lax.dynamic_slice_in_dim(silu_cond, seq_at * group, group, 0)
    silu_mine = in_order(jnp.swapaxes(silu_mine.reshape(group, dp_count, share), 0, 1), "dp")

    def partial_mod(silu_rows):
        return jnp.dot(
            silu_rows.reshape(dp_count * group, share), ada_weight, preferred_element_type=F32
        ).reshape(dp_count, group, 6 * model)

    def whole_mod(total):
        return (total + ada_bias.astype(F32)).reshape(group, 6, model)

    unit_order = lambda v: jnp.swapaxes(
        v.reshape(v.shape[0], BLOCKS // 2, 2, unit_rows), 1, 2
    ).reshape(v.shape[0], hidden_units)
    bias_row = unit_order(fc1_bias.astype(F32)[None])

    pad = -(-(model // 2) // LANES) * LANES
    column = lax.broadcasted_iota(jnp.int32, (1, 2 * pad), 1)
    side, inner = column // pad, column % pad
    source = (2 * (inner // model_rows) + (parity ^ side)) * model_rows + inner % model_rows
    source = jnp.where(inner < model // 2, source, -1)
    order = (lax.broadcasted_iota(jnp.int32, (model, 1), 0) == source).astype(BF)

    model_position = lambda k: whose(k)
    unit_position = lambda k: ((whose(k) & 1) ^ parity) * (BLOCKS // 2) + whose(k) // 2

    def run_enter(joint, place_row, mod, latent_pieces):
        weights, offsets = joint
        return call(
            functools.partial(enter_kernel, len(weights), seq_count, cap),
            (
                sds((rows_all, model), BF),
                sds((rows_all, 3 * model), BF),
                sds((rows_all, pad), BF),
                sds((rows_all, pad), BF),
            ),
            [
                offsets,
                place_row,
                mod,
                order,
                *latent_pieces,
                *weights,
            ],
            [SMEM, VMEM, VMEM, VMEM] + [VMEM] * seq_count + [ANY] * len(weights),
            [
                pltpu.VMEM((model, 3 * model), BF),
                pltpu.VMEM((rows_all, model), BF),
                dma(len(weights)),
            ],
            "enter",
        )

    def run_cot(place_row, mod, cot_pieces):
        return call(
            functools.partial(cot_kernel, seq_count, cap),
            (sds((rows_all, model), BF), sds((rows_all, model), BF)),
            [place_row, mod, *cot_pieces],
            [VMEM] * (2 + seq_count),
            [],
            "cotangent",
        )

    def run_attend(joint, live, qkv, packed, mod):
        weights, offsets = joint
        return call(
            functools.partial(attend_kernel, len(weights), cap, model),
            (
                sds((rows_all, pad), BF),
                sds((rows_all, pad), BF),
                sds((rows_all, model), F32),
                sds((rows_all, model), F32),
                sds((rows_all, model), BF),
                sds((rows_all, pad), BF),
                sds((rows_all, pad), BF),
            ),
            [
                offsets,
                live,
                qkv,
                packed,
                mod,
                order,
                *weights,
            ],
            [SMEM, SMEM, VMEM, VMEM, VMEM, VMEM] + [ANY] * len(weights),
            [
                pltpu.VMEM((model, model), BF),
                pltpu.VMEM((rows_all, model), F32),
                dma(len(weights)),
            ],
            "attend",
        )

    def run_first(first, mixed):
        weights, offsets = first
        return call(
            functools.partial(first_kernel, len(weights)),
            tuple(sds((rows_all, half_units), BF) for _ in range(4)),
            [
                offsets,
                parity_in,
                mixed,
                bias_row,
                *weights,
            ],
            [SMEM, SMEM, VMEM, VMEM] + [ANY] * len(weights),
            [pltpu.VMEM((model, hidden_units), BF), dma(len(weights))],
            "first",
        )

    def run_slope(second, slopes, grad_mlp):
        weights, offsets = second
        return call(
            functools.partial(slope_kernel, len(weights)),
            (
                sds((rows_all, half_units), BF),
                sds((rows_all, half_units), BF),
                sds((1, half_units), F32),
                sds((1, half_units), F32),
            ),
            [offsets, *slopes, grad_mlp, *weights],
            [SMEM] + [VMEM] * 3 + [ANY] * len(weights),
            [pltpu.VMEM((hidden_units, model), BF), dma(len(weights))],
            "slope",
        )

    def run_second(second, acts, grad_out, hidden, mod, slots):
        weights, offsets = second
        result = call(
            functools.partial(second_kernel, len(weights), seq_count, cap),
            tuple(sds((group, most, model), BF) for _ in range(seq_count))
            + (sds((group, 1, model), F32),),
            [
                offsets,
                *acts,
                grad_out,
                hidden,
                mod,
                slots,
                *weights,
            ],
            [SMEM] + [VMEM] * 6 + [ANY] * len(weights),
            [pltpu.VMEM((hidden_units, model), BF), dma(len(weights))],
            "second",
        )
        return result[:seq_count], result[seq_count]

    def run_hidden(first, joint, pres, hidden, projected, grad_out, mod):
        (first_w, first_at), (joint_w, joint_at) = first, joint
        return call(
            functools.partial(hidden_kernel, len(joint_w), len(first_w), cap, model),
            (
                sds((rows_all, model), F32),
                sds((rows_all, model), BF),
                sds((rows_all, model), BF),
                sds((group, 3, model), F32),
            ),
            [
                first_at,
                joint_at,
                parity_in,
                *pres,
                hidden,
                projected,
                grad_out,
                mod,
                *first_w,
                *joint_w,
            ],
            [SMEM, SMEM, SMEM] + [VMEM] * 6 + [ANY] * (len(first_w) + len(joint_w)),
            [
                pltpu.VMEM((model, hidden_units), BF),
                pltpu.VMEM((model, model), BF),
                dma(len(first_w)),
                dma(len(joint_w)),
            ],
            "hidden_back",
        )

    def run_attend_back(live, qkv, grad_att):
        return call(
            functools.partial(attend_back_kernel, cap, model),
            sds((rows_all, 3 * model), BF),
            [live, qkv, grad_att],
            [SMEM, VMEM, VMEM],
            [pltpu.VMEM((rows_all, 3 * model), F32)],
            "attend_back",
        )

    def run_leave(joint, grad_qkv, packed, grad_hidden, mod, slots):
        weights, offsets = joint
        result = call(
            functools.partial(leave_kernel, len(weights), seq_count, cap),
            tuple(sds((group, most, model), BF) for _ in range(seq_count))
            + (sds((group, 2, model), F32),),
            [
                offsets,
                grad_qkv,
                packed,
                grad_hidden,
                mod,
                slots,
                *weights,
            ],
            [SMEM] + [VMEM] * 5 + [ANY] * len(weights),
            [pltpu.VMEM((model, 3 * model), BF), dma(len(weights))],
            "leave",
        )
        return result[:seq_count], result[seq_count]

    def join_mod(mod_first, mod_grads, gate_m_grad):
        return jnp.concatenate(
            [mod_first, mod_grads[:, 2:3], mod_grads[:, :2], gate_m_grad], axis=1
        ).reshape(group, 6 * model)

    def join_bias(bias_own, bias_other):
        bias_pair = jnp.where(
            parity == 1,
            jnp.concatenate([bias_other, bias_own], axis=0),
            jnp.concatenate([bias_own, bias_other], axis=0),
        )
        bias_part = jnp.swapaxes(bias_pair.reshape(2, BLOCKS // 2, unit_rows), 0, 1)
        kept_part = jnp.sum(keep_count).astype(F32).reshape(1)
        return jnp.concatenate([bias_part.reshape(hidden_units), kept_part])

    def latent_sum(grad_mod_all):
        total = jnp.sum(grad_mod_all.astype(F32), axis=1)
        while total.shape[0] > 1:
            total = total.reshape((total.shape[0] // 2, 2) + total.shape[1:])
            total = total[:, 0] + total[:, 1]
        return total[0]

    def by_columns(grad_mod_all):
        return in_order(
            jnp.stack(
                [
                    grad_mod_all[:, :, j * column_share : (j + 1) * column_share]
                    for j in range(seq_count)
                ]
            ),
            "seq",
        )

    def cond_product(grad_mod_all):
        return dot(grad_mod_all.reshape(dp_count * group, 6 * model), ada_weight, NT).reshape(
            dp_count, group, share
        )

    def ada_product(silu_all, columns):
        return dot(
            silu_all.reshape(seq_count * dp_count * group, share),
            columns.reshape(seq_count * dp_count * group, column_share),
            TN,
        )

    def cond_end(rows):
        rows = in_order(rows, "seq").reshape(latent_count, model)
        _, silu_back = jax.vjp(jax.nn.silu, cond_wide)
        return silu_back(rows)[0]

    def cond_mine_of(cols):
        return jnp.swapaxes(in_order(cols, "dp"), 0, 1).reshape(group, model)

    if not paired:
        live, place_row, slots = places_of(gather_all(rank, "seq"))
        silu_rows = trade_all(silu_mine, "dp")
        mod = whole_mod(sum_own(partial_mod(silu_rows), "dp"))
        to_whole = lambda v: [
            swap(whole_slice(v, k), "seq", k) if k else whole_slice(v, k)
            for k in range(seq_count)
        ]
        latent_pieces, cot_pieces = to_whole(latents), to_whole(cotangent)
        joint = whole_weight(jnp.concatenate([qkv_weight, out_weight], axis=1))
        first = whole_weight(unit_order(fc1_weight))
        full = whole_weight(fc2_weight)[0][0]
        second = placed(
            [(full[k * unit_rows : (k + 1) * unit_rows], k, 0) for k in range(BLOCKS)],
            unit_position,
            unit_rows,
        )
        packed, qkv, *mixa = run_enter(joint, place_row, mod, latent_pieces)
        grad_out, grad_mlp = run_cot(place_row, mod, cot_pieces)
        att_own, att_other, projected, hidden, mixed, *mixm = run_attend(
            joint, live, qkv, packed, mod
        )
        acts = run_first(first, mixed)
        *pres, bias_own, bias_other = run_slope(second, acts[2:], grad_mlp)
        block_pieces, gate_m_grad = run_second(
            second, acts[:2], grad_out, hidden, mod, slots
        )
        grad_hidden, grad_proj, grad_att, mod_grads = run_hidden(
            first, joint, pres, hidden, projected, grad_out, mod
        )
        grad_qkv = run_attend_back(live, qkv, grad_att)
        latent_grads, mod_first = run_leave(
            joint, grad_qkv, packed, grad_hidden, mod, slots
        )
        grad_mod = join_mod(mod_first, mod_grads, gate_m_grad)
        bias = sum_everywhere(join_bias(bias_own, bias_other))
        grad_mod_all = gather_all(grad_mod.astype(BF), "dp")
        ada_bias_grad = latent_sum(grad_mod_all)
        for step in steps_of("seq"):
            ada_bias_grad = ada_bias_grad + swap(ada_bias_grad, "seq", step)
        ada_grad = ada_product(
            gather_all(silu_rows, "seq"), trade_all(by_columns(grad_mod_all), "seq")
        )
        cond_cols = trade_all(cond_product(grad_mod_all), "dp")
        condition_grad = cond_end(gather_all(cond_mine_of(cond_cols), "seq"))

        def mixed_sides(own, other, width):
            both = jnp.stack([own[:, : 4 * width], other[:, : 4 * width]], axis=1)
            return jnp.swapaxes(both.reshape(rows_all, 2, 4, width), 1, 2).reshape(
                rows_all, BLOCKS * width
            )

        product = lambda a, b: spread_plain(dot(a, b, TN))
        fc2_grad = product(mixed_sides(acts[0], acts[1], unit_rows), grad_mlp)
        fc1_grad = product(
            mixed_sides(*mixm, model_rows), mixed_sides(pres[0], pres[1], unit_rows)
        )
        out_grad = product(mixed_sides(att_own, att_other, model_rows), grad_proj)
        qkv_grad = product(mixed_sides(*mixa, model_rows), grad_qkv)
        home = lambda pieces: [swap(v, "seq", k) if k else v for k, v in enumerate(pieces)]
        block_out = run_home(home(block_pieces), latents, BF, "home_out")
        latents_grad = run_home(home(latent_grads), cotangent, F32, "home_grad")
        return (
            block_out,
            latents_grad,
            condition_grad,
            ada_grad,
            ada_bias_grad,
            qkv_grad,
            out_grad,
            fc1_grad,
            bias[:hidden_units],
            fc2_grad,
            bias[hidden_units:].astype(jnp.int32),
        )

    def trade(value, axis, step):
        split = value.reshape((-1, 2, step) + value.shape[1:])
        return jnp.stack([split[:, 0], swap(split[:, 1], axis, step)], axis=1).reshape(value.shape)

    def grow(value, axis, step):
        return jnp.concatenate([value, swap(value, axis, step)], axis=0)

    def columns_first(parts):
        sent, own, across = parts
        return swap(sent, "seq", 1), own, across

    def columns_second(state):
        near, own, across = state
        on = (across.astype(F32) + near[1].astype(F32)).astype(BF)
        return swap(on, "seq", 2), own, near

    def columns_sum(state):
        far, own, near = state
        return own.astype(F32) + near[0].astype(F32) + far.astype(F32)

    joint_own = jnp.concatenate([qkv_weight, out_weight], axis=1)
    first_own = pl.pallas_call(
        functools.partial(reorder_kernel, unit_rows),
        out_shape=sds(fc1_weight.shape, BF),
        in_specs=[VMEM],
        out_specs=VMEM,
        name="reorder",
        compiler_params=pltpu.CompilerParams(vmem_limit_bytes=60 * 1024 * 1024),
    )(fc1_weight)

    def tails(beside, first):
        rows, width = beside[0].shape
        return call(
            functools.partial(cut_kernel, first),
            (sds((first, width), BF), sds((rows - first, width), BF)),
            [beside[1], beside[0]],
            [VMEM, VMEM],
            [],
            "cut",
        )

    corners_of = lambda value: [swap(value[q], "dp", 2 * q) for q in (1, 2, 3)]

    corners = silu_mine.reshape(4, 2, group, share)
    corners = jnp.stack([corners[0], *corners_of(corners)])
    corners, joint_own, first_own, latents_in, rank_in = fence(
        corners, joint_own, first_own, latents, rank
    )

    first = whole_weight(first_own)
    joint_beside = beside_of(joint_own)
    ranks = grow(grow(rank_in[None], "seq", 1), "seq", 2)
    silu_rows = trade(corners.reshape(8, group, share), "dp", 1)
    pairs = partial_mod(silu_rows).reshape(4, 2, group, 6 * model)
    corners = pairs[:, 0] + swap(pairs[:, 1], "dp", 1)
    latent_pieces = [whole_slice(latents_in, k) for k in range(seq_count)]
    latent_1 = swap(latent_pieces[1], "seq", 1)
    latent_2 = swap(latent_pieces[2], "seq", 2)
    (joint_pair,) = pair_of((joint_own,))
    joint_beside, latent_1, latent_2, latent_3, joint_pair, ranks, silu_rows, corners = fence(
        joint_beside,
        latent_1,
        latent_2,
        latent_pieces[3],
        joint_pair,
        ranks,
        silu_rows,
        corners,
    )

    sums = corners_of(corners)
    joint_tails = tails(joint_beside, part)
    sums, joint_tails, latent_3, joint_beside = fence(sums, joint_tails, latent_3, joint_beside)
    joint_across = (swap(joint_tails[0], "dp", 2), swap(joint_tails[1], "dp", 4))
    mod = whole_mod(sum(sums, corners[0]))
    latent_3 = swap(latent_3, "seq", 3)
    joint_x_pair, joint_y_pair = pair_of(joint_beside)
    live, place_row, slots = places_of(ranks)
    silu_all = gather_all(silu_rows, "seq")
    cot_pieces = [whole_slice(cotangent, k) for k in range(seq_count)]
    second_own = fc2_weight
    (
        joint_across,
        mod,
        latent_3,
        joint_x_pair,
        joint_y_pair,
        live,
        place_row,
        slots,
        cot_pieces,
        second_own,
        silu_all,
    ) = fence(
        joint_across,
        mod,
        latent_3,
        joint_x_pair,
        joint_y_pair,
        live,
        place_row,
        slots,
        cot_pieces,
        second_own,
        silu_all,
    )

    second_beside = beside_of(second_own)
    cot_1 = swap(cot_pieces[1], "seq", 1)
    cot_2 = swap(cot_pieces[2], "seq", 2)
    cot_3 = swap(cot_pieces[3], "seq", 3)
    joint = placed(
        pieces_of(
            joint_own,
            joint_pair,
            joint_beside,
            (joint_x_pair, joint_y_pair),
            joint_across,
            pair_of(joint_across),
            part,
        ),
        model_position,
        model_rows,
    )
    latent_pieces = [latent_pieces[0], latent_1, latent_2, latent_3]
    packed, qkv, mixa_own, mixa_other = run_enter(joint, place_row, mod, latent_pieces)
    att_own, att_other, projected, hidden, mixed, mixm_own, mixm_other = run_attend(
        joint, live, qkv, packed, mod
    )
    second_beside, cot_1, cot_2, cot_3, mixed, first = fence(
        second_beside, cot_1, cot_2, cot_3, mixed, first
    )

    second_tails = tails(second_beside, unit_part)
    second_across = (swap(second_tails[0], "dp", 2), swap(second_tails[1], "dp", 4))
    second_pair, second_x_pair, second_y_pair = pair_of((second_own, *second_beside))
    acts = run_first(first, mixed)
    cot_pieces = [cot_pieces[0], cot_1, cot_2, cot_3]
    grad_out, grad_mlp = run_cot(after(place_row, acts), mod, cot_pieces)
    second_across, second_pair, second_x_pair, second_y_pair, acts, grad_out, grad_mlp = fence(
        second_across, second_pair, second_x_pair, second_y_pair, acts, grad_out, grad_mlp
    )

    second_across_pair = pair_of(second_across)
    act_pair, grad_mlp_pair = pair_of((acts[1], grad_mlp))
    fc2_cut = outer_pair(
        [((acts[0], act_pair), [(grad_mlp, grad_mlp_pair)])], unit_rows, "fc2_grad"
    )
    second_across_pair, acts, grad_out, grad_mlp, fc2_cut, mixm_other, att_other, mixa_other = fence(
        second_across_pair, acts, grad_out, grad_mlp, fc2_cut, mixm_other, att_other, mixa_other
    )

    fc2_far = along_xy(fc2_cut[:2])
    mixm_pair, att_pair, mixa_pair = pair_of((mixm_other, att_other, mixa_other))
    second = placed(
        pieces_of(
            second_own,
            second_pair,
            second_beside,
            (second_x_pair, second_y_pair),
            second_across,
            second_across_pair,
            unit_part,
        ),
        unit_position,
        unit_rows,
    )
    pre_own, pre_other, bias_own, bias_other = run_slope(second, acts[2:], grad_mlp)
    bias = join_bias(bias_own, bias_other)
    fc2_far, fc2_cut, mixm_pair, att_pair, mixa_pair, pre_own, pre_other, bias, acts = fence(
        fc2_far, fc2_cut, mixm_pair, att_pair, mixa_pair, pre_own, pre_other, bias, acts
    )

    fc2_near = along_xy(fc2_cut[2:4])
    on = onward(fc2_cut, fc2_far)
    pre_other_pair, pre_own_pair = pair_of((pre_own, pre_other))
    bias = bias + swap(bias, "dp", 2)
    block_pieces, gate_m_grad = run_second(
        second, acts[:2], grad_out, hidden, mod, after(slots, on)
    )
    fc2_near, on, pre_other_pair, pre_own_pair, block_pieces, gate_m_grad, bias = fence(
        fc2_near, on, pre_other_pair, pre_own_pair, block_pieces, gate_m_grad, bias
    )

    fc2_last = along_xy(on)
    block_1 = swap(block_pieces[1], "seq", 1)
    block_2 = swap(block_pieces[2], "seq", 2)
    bias = bias + swap(bias, "dp", 4)
    fc1_cut = outer_pair(
        [((mixm_own, mixm_pair), [(pre_own, pre_own_pair), (pre_other, pre_other_pair)])],
        model_rows,
        "fc1_grad",
    )
    fc2_last, block_1, block_2, block_3, bias, fc1_cut, pre_own, pre_other, fc2_near = fence(
        fc2_last, block_1, block_2, block_pieces[3], bias, fc1_cut, pre_own, pre_other, fc2_near
    )

    fc1_far = along_xy(fc1_cut[:2])
    block_3 = swap(block_3, "seq", 3)
    bias = bias + swap(bias, "dp", 1)
    grad_hidden, grad_proj, grad_att, mod_grads = run_hidden(
        first, joint, (pre_own, pre_other), hidden, projected, grad_out, mod
    )
    fc2_parts = fold(
        after(fc2_cut[4], grad_att),
        fc2_near,
        fc2_last,
        (plain_cuts(0, model, seq_count),),
        "fc2_fold",
        True,
    )
    fc1_far, fc1_cut, block_3, bias, grad_proj, grad_att, fc2_parts = fence(
        fc1_far, fc1_cut, block_3, bias, grad_proj, grad_att, fc2_parts
    )

    fc1_near = along_xy(fc1_cut[2:4])
    on = onward(fc1_cut, fc1_far)
    fc2_state = columns_first(fc2_parts)
    (proj_pair,) = pair_of((grad_proj,))
    grad_qkv = run_attend_back(after(live, on), qkv, grad_att)
    fc1_near, on, fc2_state, proj_pair, grad_qkv = fence(
        fc1_near, on, fc2_state, proj_pair, grad_qkv
    )

    fc1_last = along_xy(on)
    fc2_state = columns_second(fc2_state)
    (qkv_pair,) = pair_of((grad_qkv,))
    last_cut = outer_pair(
        [
            ((mixa_own, mixa_pair), [(grad_qkv, qkv_pair)]),
            ((att_own, att_pair), [(grad_proj, proj_pair)]),
        ],
        model_rows,
        "last_grad",
    )
    fc1_last, last_cut, grad_qkv, fc1_near = fence(fc1_last, last_cut, grad_qkv, fc1_near)

    last_far = along_xy(last_cut[:2])
    fc1_cuts = tuple(
        tuple((lo, lo + unit_rows) for lo in (j * unit_rows, half_units + j * unit_rows))
        for j in range(seq_count)
    )
    fc1_parts = fold(fc1_cut[4], fc1_near, fc1_last, (fc1_cuts,), "fc1_fold")
    fc1_state = columns_first(fc1_parts)
    latent_grads, mod_first = run_leave(
        joint, after(grad_qkv, fc1_parts), packed, grad_hidden, mod, slots
    )
    grad_mod = join_mod(mod_first, mod_grads, gate_m_grad).astype(BF)
    last_far, last_cut, fc1_state, latent_grads, grad_mod, bias, fc2_state = fence(
        last_far, last_cut, fc1_state, latent_grads, grad_mod, bias, fc2_state
    )

    corners = jnp.stack([grad_mod] + [swap(grad_mod, "dp", 2 * q) for q in (1, 2, 3)])
    latent_1 = swap(latent_grads[1], "seq", 1)
    bias = bias + swap(bias, "seq", 1)
    corners, last_cut, last_far, latent_1, bias, fc1_state, fc2_state, block_pieces = fence(
        corners, last_cut, last_far, latent_1, bias, fc1_state, fc2_state, block_pieces
    )

    last_near = along_xy(last_cut[2:4])
    on = onward(last_cut, last_far)
    grad_mod_all = jnp.stack([corners, swap(corners, "dp", 1)], axis=1).reshape(
        8, group, 6 * model
    )
    cond_cols = trade(cond_product(grad_mod_all), "dp", 1).reshape(4, 2, group, share)
    columns = by_columns(grad_mod_all)
    ada_bias_grad = latent_sum(grad_mod_all)
    fc1_state = columns_second(fc1_state)
    bias = bias + swap(bias, "seq", 2)
    fc2_grad = columns_sum(fc2_state).T
    block_out = run_home(
        (block_pieces[0], block_1, block_2, block_3), latents, BF, "home_out"
    )
    last_near, on, cond_cols, columns, ada_bias_grad, fc1_state, bias, fc2_grad, block_out = fence(
        last_near, on, cond_cols, columns, ada_bias_grad, fc1_state, bias, fc2_grad, block_out
    )

    cond_cols = jnp.stack([cond_cols[0], *corners_of(cond_cols)])
    ada_bias_grad = ada_bias_grad + swap(ada_bias_grad, "seq", 1)
    columns = trade(columns, "seq", 1)
    cond_cols, on, last_near, ada_bias_grad, columns, latent_2 = fence(
        cond_cols, on, last_near, ada_bias_grad, columns, latent_grads[2]
    )

    last_last = along_xy(on)
    ada_bias_grad = ada_bias_grad + swap(ada_bias_grad, "seq", 2)
    columns = trade(columns, "seq", 2)
    cond_rows = grow(cond_mine_of(cond_cols.reshape(8, group, share))[None], "seq", 1)
    latent_2 = swap(latent_2, "seq", 2)
    fc1_grad = columns_sum(fc1_state)
    fc1_grad = jnp.where(
        parity == 1,
        jnp.concatenate([fc1_grad[:, unit_rows:], fc1_grad[:, :unit_rows]], axis=1),
        fc1_grad,
    )
    last_last, ada_bias_grad, columns, cond_rows, latent_2, latent_3, last_near, fc1_grad = fence(
        last_last,
        ada_bias_grad,
        columns,
        cond_rows,
        latent_2,
        latent_grads[3],
        last_near,
        fc1_grad,
    )

    qkv_share, out_share = 3 * model // seq_count, model // seq_count
    last_cuts = tuple(
        (
            (j * qkv_share, (j + 1) * qkv_share),
            (3 * model + j * out_share, 3 * model + (j + 1) * out_share),
        )
        for j in range(seq_count)
    )
    last_parts = fold(last_cut[4], last_near, last_last, (last_cuts,), "last_fold")
    last_state = columns_first(last_parts)
    latent_3 = swap(after(latent_3, last_parts), "seq", 3)
    condition_grad = cond_end(grow(after(cond_rows, last_parts), "seq", 2))
    ada_grad = ada_product(silu_all, after(columns, last_parts))
    last_state, latent_3, condition_grad, ada_grad = fence(
        last_state, latent_3, condition_grad, ada_grad
    )

    last_state = columns_second(last_state)
    latents_grad = run_home(
        (latent_grads[0], latent_1, latent_2, latent_3), cotangent, F32, "home_grad"
    )
    far, own, near = last_state
    qkv_grad = columns_sum((far[:, :qkv_share], own[:, :qkv_share], near[:, :, :qkv_share]))
    out_grad = columns_sum((far[:, qkv_share:], own[:, qkv_share:], near[:, :, qkv_share:]))
    return (
        block_out,
        latents_grad,
        condition_grad,
        ada_grad,
        ada_bias_grad,
        qkv_grad,
        out_grad,
        fc1_grad,
        bias[:hidden_units],
        fc2_grad,
        bias[hidden_units:].astype(jnp.int32),
    )


def solution(mesh):
    placed = (
        P("dp", "seq", None),
        P("dp", None),
        P("dp", "seq"),
        P("dp", "seq"),
        P("dp", None),
        P(),
        P("dp", None),
        P("dp", None),
        P("dp", None),
        P(),
        P("dp", None),
        P("dp", "seq", None),
    )
    return jax.shard_map(
        body,
        mesh=mesh,
        in_specs=placed,
        out_specs=(
            P("dp", "seq", None),
            P("dp", "seq", None),
            P("dp", None),
            P("dp", "seq"),
            P(),
            P("dp", "seq"),
            P("dp", "seq"),
            P("dp", "seq"),
            P(),
            P("dp", "seq"),
            P(),
        ),
        check_vma=False,
    )
```

```python
import functools
import math

import jax
import jax.numpy as jnp
from jax import lax
from jax.experimental import pallas as pl
from jax.experimental.pallas import tpu as pltpu
from jax.sharding import PartitionSpec as P

HEADS = 16
HEAD = 72
LANES = 128
BLOCKS = 8

layer_eps = 1e-06
far_below = -1e30
att_scale = 1.0 / math.sqrt(HEAD)
exp2_scale = att_scale / math.log(2.0)
gelu_c = math.sqrt(2.0 / math.pi)
gelu_k = 0.044715

BF = jnp.bfloat16
F32 = jnp.float32
VMEM = pl.BlockSpec(memory_space=pltpu.VMEM)
SMEM = pl.BlockSpec(memory_space=pltpu.SMEM)
ANY = pl.BlockSpec(memory_space=pl.ANY)
NT = (((1,), (1,)), ((), ()))
TN = (((0,), (0,)), ((), ()))


def swap(value, axis, step):
    return lax.ppermute(value, axis, [(i, i ^ step) for i in range(lax.axis_size(axis))])


def steps_of(axis):
    count = lax.axis_size(axis)
    return [1 << i for i in range(count.bit_length() - 1)]


def bit_set(axis, step):
    return (lax.axis_index(axis) & step) != 0


def gather_all(value, axis):
    value = value[None]
    for step in steps_of(axis):
        value = jnp.concatenate([value, swap(value, axis, step)], axis=0)
    return value


def sum_own(value, axis):
    for step in reversed(steps_of(axis)):
        value = value[:step] + swap(value[step:], axis, step)
    return value[0]


def trade_all(value, axis):
    count = value.shape[0]
    rest = value.shape[1:]
    for step in steps_of(axis):
        split = value.reshape((count // (2 * step), 2, step) + rest)
        value = jnp.stack([split[:, 0], swap(split[:, 1], axis, step)], axis=1).reshape(
            (count,) + rest
        )
    return value


def in_order(value, axis):
    count = value.shape[0]
    rest = value.shape[1:]
    for step in steps_of(axis):
        split = value.reshape((count // (2 * step), 2, step) + rest)
        value = jnp.where(bit_set(axis, step), split[:, ::-1], split).reshape((count,) + rest)
    return value


def sum_everywhere(value):
    for axis in ("dp", "seq"):
        for step in steps_of(axis):
            value = value + swap(value, axis, step)
    return value


def after(value, *earlier):
    return lax.optimization_barrier((value,) + earlier)[0]


def halves_of(rows):
    first = (rows // 2 + 15) // 16 * 16
    return first, rows - first


def pieces_of(own, own_pair, beside, beside_pair, across, across_pair, part):
    return [
        (own, 0, 0),
        (own_pair, 1, 0),
        (beside[0], 2, 0),
        (beside_pair[0], 3, 0),
        (beside[1], 4, 0),
        (beside_pair[1], 5, 0),
        (across[0], 6, 0),
        (across[1], 6, part),
        (across_pair[0], 7, 0),
        (across_pair[1], 7, part),
    ]


def beside_of(shard):
    return swap(shard, "dp", 2), swap(shard, "dp", 4)


def across_of(beside, part):
    return swap(beside[1][:part], "dp", 2), swap(beside[0][part:], "dp", 4)


def pair_of(values):
    return tuple(swap(v, "dp", 1) for v in values)


def placed(pieces, position, rows):
    starts = jnp.stack([position(k) * rows + first for _, k, first in pieces]).astype(jnp.int32)
    return [v for v, _, _ in pieces], starts


def whole_weight(shard):
    return lax.all_gather(shard, "dp", axis=0, tiled=True)


def call(kernel, outs, ins, specs, scratch, name, out_specs=None):
    return pl.pallas_call(
        kernel,
        out_shape=outs,
        in_specs=specs,
        out_specs=out_specs or jax.tree.map(lambda _: VMEM, outs),
        scratch_shapes=scratch,
        name=name,
        compiler_params=pltpu.CompilerParams(vmem_limit_bytes=60 * 1024 * 1024),
    )(*ins)


def start_pieces(offsets, refs, target, sem, lo, hi):
    copies = []
    shift = lo if target.shape[1] == hi - lo else 0
    for k, ref in enumerate(refs):
        rows = ref.shape[0]
        copies.append(
            pltpu.make_async_copy(
                ref.at[:, pl.ds(lo, hi - lo)],
                target.at[pl.ds(pl.multiple_of(offsets[k], 16), rows), pl.ds(lo - shift, hi - lo)],
                sem.at[k],
            )
        )
    for one in copies:
        one.start()
    return copies


def wait_all(copies):
    for one in copies:
        one.wait()


def normal(rows_in):
    center = rows_in - jnp.mean(rows_in, axis=-1, keepdims=True)
    inverse = lax.rsqrt(jnp.mean(center * center, axis=-1, keepdims=True) + layer_eps)
    return center * inverse, inverse


def normal_back(grad_rows, normed, inverse):
    mean_grad = jnp.mean(grad_rows, axis=-1, keepdims=True)
    mean_proj = jnp.mean(grad_rows * normed, axis=-1, keepdims=True)
    return inverse * (grad_rows - mean_grad - normed * mean_proj)


def dot(left, right, dims=None):
    if dims is None:
        return jnp.dot(left, right, preferred_element_type=F32)
    return lax.dot_general(left, right, dims, preferred_element_type=F32)


def spans(total, width):
    return [(lo, min(lo + width, total)) for lo in range(0, total, width)]


def pack_rows(place_ref, piece_refs, latent, rows_out):
    gathered = jnp.concatenate([ref[latent] for ref in piece_refs], axis=0)
    slots = lax.broadcasted_iota(jnp.int32, (rows_out, gathered.shape[0]), 0)
    chosen = jnp.where(place_ref[latent] == slots, 1.0, 0.0).astype(BF)
    return dot(chosen, gathered)


def unpack_rows(slots_ref, latent, packed, out_refs):
    slots = slots_ref[latent]
    rows = lax.broadcasted_iota(jnp.int32, (slots.shape[0], packed.shape[0]), 1)
    spread = dot(jnp.where(slots == rows, 1.0, 0.0).astype(BF), packed).astype(BF)
    block = out_refs[0].shape[1]
    for k, out in enumerate(out_refs):
        out[latent] = spread[k * block : (k + 1) * block]


def home_kernel(at, rank, base, *refs):
    pieces, out = refs[:-1], refs[-1]
    group, slots, _ = pieces[0].shape
    for k, piece in enumerate(pieces):
        for j in range(group):
            latent = (at[0] ^ k) * group + j
            place = rank[latent]
            rows = lax.broadcasted_iota(jnp.int32, (place.shape[0], slots), 1)
            spread = dot(jnp.where(place == rows, 1.0, 0.0).astype(BF), piece[j])
            out[latent] = jnp.where(place >= 0, spread, base[latent].astype(F32)).astype(out.dtype)


def cut_kernel(first, top, bottom, top_out, bottom_out, top_held, bottom_held, load_sem, store_sem):
    rows = bottom.shape[0]
    loads = [
        pltpu.make_async_copy(top.at[pl.ds(0, first), :], top_held, load_sem.at[0]),
        pltpu.make_async_copy(bottom.at[pl.ds(first, rows - first), :], bottom_held, load_sem.at[1]),
    ]
    stores = [
        pltpu.make_async_copy(top_held, top_out, store_sem.at[0]),
        pltpu.make_async_copy(bottom_held, bottom_out, store_sem.at[1]),
    ]
    for one in loads:
        one.start()
    for load, store in zip(loads, stores):
        load.wait()
        store.start()
    wait_all(stores)


def split_parity(rows_low, order_ref, own_ref, other_ref):
    moved = dot(rows_low, order_ref[...]).astype(BF)
    width = own_ref.shape[1]
    own_ref[...] = moved[:, :width]
    other_ref[...] = moved[:, width:]


def enter_kernel(pieces, blocks, cap, *refs):
    (offsets, place, mod, order), refs = refs[:4], refs[4:]
    latents, refs = refs[:blocks], refs[blocks:]
    weights, refs = refs[:pieces], refs[pieces:]
    packed_out, qkv_out, own_out, other_out, weight, mixed, sem = refs
    width = qkv_out.shape[1]
    chunks = spans(width, width // 3)
    loads = [
        start_pieces(offsets, weights, weight, sem.at[i], lo, hi) for i, (lo, hi) in enumerate(chunks)
    ]
    for latent in range(mod.shape[0]):
        here = pl.ds(latent * cap, cap)
        rows = pack_rows(place, latents, latent, cap)
        packed_out[here, :] = rows.astype(BF)
        normed, _ = normal(rows)
        mixed[here, :] = (normed * (1.0 + mod[latent, 1:2, :]) + mod[latent, 0:1, :]).astype(BF)
    split_parity(mixed[...], order, own_out, other_out)
    for i, (lo, hi) in enumerate(chunks):
        wait_all(loads[i])
        qkv_out[:, lo:hi] = dot(mixed[...], weight[:, lo:hi]).astype(BF)


def cot_kernel(cap, place, mod, *refs):
    cots, (packed_out, mlp_out) = refs[:-2], refs[-2:]
    for latent in range(mod.shape[0]):
        here = pl.ds(latent * cap, cap)
        rows = pack_rows(place, cots, latent, cap)
        packed_out[here, :] = rows.astype(BF)
        mlp_out[here, :] = (mod[latent, 5:6, :] * rows).astype(BF)


def windows():
    found = []
    for head in range(HEADS):
        first = head * HEAD
        base = first // LANES * LANES
        width = LANES if first + HEAD <= base + LANES else 2 * LANES
        found.append((base, width, first - base))
    return found[::2] + found[1::2]


def head_mask(width, first, dtype):
    lane = lax.broadcasted_iota(jnp.int32, (1, width), 1)
    return jnp.where((lane >= first) & (lane < first + HEAD), 1.0, 0.0).astype(dtype)


def attend_kernel(pieces, cap, model, *refs):
    (offsets, live, qkv, packed, mod, order), refs = refs[:6], refs[6:]
    weights, refs = refs[:pieces], refs[pieces:]
    (own_att, other_att, proj_out, hidden_out, mixed_out, own_mix, other_mix), refs = (
        refs[:7],
        refs[7:],
    )
    weight, attended, sem = refs
    copies = start_pieces(offsets, weights, weight, sem, 3 * model, 4 * model)
    attended[...] = jnp.zeros_like(attended)

    def one_latent(latent, carry):
        here = pl.ds(pl.multiple_of(latent * cap, 16), cap)
        count = live[latent]
        seen = lax.broadcasted_iota(jnp.int32, (cap, cap), 1) < count
        for base, width, first in windows():
            low_mask = head_mask(width, first, BF)
            query = qkv[here, base : base + width] * low_mask
            key = qkv[here, model + base : model + base + width]
            value = qkv[here, 2 * model + base : 2 * model + base + width] * low_mask
            scores = jnp.where(seen, dot(query, key, NT), far_below)
            raised = jnp.exp2((scores - jnp.max(scores, axis=-1, keepdims=True)) * exp2_scale)
            share = 1.0 / jnp.sum(raised, axis=-1, keepdims=True)
            attended[here, base : base + width] += dot(raised.astype(BF), value) * share
        return carry

    lax.fori_loop(0, mod.shape[0], one_latent, 0)
    att_low = attended[...].astype(BF)
    split_parity(att_low, order, own_att, other_att)
    wait_all(copies)
    projected = dot(att_low, weight[...])
    proj_out[...] = projected
    for latent in range(mod.shape[0]):
        rows = slice(latent * cap, (latent + 1) * cap)
        hidden = packed[rows, :].astype(F32) + mod[latent, 2:3, :] * projected[rows]
        hidden_out[rows, :] = hidden
        normed, _ = normal(hidden)
        mixed_out[rows, :] = (
            normed * (1.0 + mod[latent, 4:5, :]) + mod[latent, 3:4, :]
        ).astype(BF)
    split_parity(mixed_out[...], order, own_mix, other_mix)


def unit_chunks(parity, half):
    found = []
    for side in (0, 1):
        base = (parity[0] ^ side) * half
        for lo, hi in spans(half, 768):
            found.append((side, lo, hi, pl.ds(pl.multiple_of(base + lo, LANES), hi - lo)))
    return found


def start_chunks(offsets, refs, target, sem, chunks):
    found = []
    for i, (_, _, _, cols) in enumerate(chunks):
        found.append(
            [
                pltpu.make_async_copy(
                    ref.at[:, cols],
                    target.at[pl.ds(pl.multiple_of(offsets[k], 16), ref.shape[0]), cols],
                    sem.at[i, k],
                )
                for k, ref in enumerate(refs)
            ]
        )
        for one in found[-1]:
            one.start()
    return found


def first_kernel(pieces, offsets, parity, mixed, bias, *refs):
    weights, refs = refs[:pieces], refs[pieces:]
    acts, slopes = refs[0:2], refs[2:4]
    weight, act, slope, load_sem, act_sem, slope_sem = refs[4:]
    half = acts[0].shape[1]
    chunks = unit_chunks(parity, half)
    loads = start_chunks(offsets, weights, weight, load_sem, chunks)
    stores = []
    for i, (side, lo, hi, cols) in enumerate(chunks):
        wait_all(loads[i])
        pre = dot(mixed[...], weight[:, cols]) + bias[:, cols]
        square = pre * pre
        curve = jnp.tanh(pre * (gelu_c + (gelu_c * gelu_k) * square))
        cdf = 0.5 + 0.5 * curve
        act[side, :, lo:hi] = (pre * cdf).astype(BF)
        bend = (0.5 * gelu_c) + (1.5 * gelu_c * gelu_k) * square
        slope[side, :, lo:hi] = (cdf + pre * bend * (1.0 - curve * curve)).astype(BF)
        here = pl.ds(lo, hi - lo)
        for held, out, sem in ((act, acts, act_sem), (slope, slopes, slope_sem)):
            stores.append(
                pltpu.make_async_copy(held.at[side, :, here], out[side].at[:, here], sem.at[i])
            )
            stores[-1].start()
    wait_all(stores)


def start_halves(offsets, refs, sides, target, sem):
    found = ([], [])
    for side in (0, 1):
        for k, ref in enumerate(refs):
            if sides[k] != side:
                continue
            rows = ref.shape[0]
            found[side].append(
                pltpu.make_async_copy(
                    ref, target.at[pl.ds(pl.multiple_of(offsets[k], 16), rows), :], sem.at[k]
                )
            )
            found[side][-1].start()
    return found


def slope_kernel(sides, *refs):
    (offsets, own_slope, other_slope, grad_mlp), refs = refs[:4], refs[4:]
    weights, refs = refs[: len(sides)], refs[len(sides) :]
    own_pre, other_pre, own_bias, other_bias, weight, pre, sem, out_sem = refs
    halves = start_halves(offsets, weights, sides, weight, sem)
    half = own_pre.shape[1]
    stores = []
    for side, (slope, pre_out, bias_out) in enumerate(
        ((own_slope, own_pre, own_bias), (other_slope, other_pre, other_bias))
    ):
        wait_all(halves[side])
        for lo, hi in spans(half, 768):
            grad_act = dot(grad_mlp[...], weight[side * half + lo : side * half + hi, :], NT)
            grad_pre = (grad_act * slope[:, lo:hi].astype(F32)).astype(BF)
            pre[side, :, lo:hi] = grad_pre
            here = pl.ds(lo, hi - lo)
            stores.append(
                pltpu.make_async_copy(
                    pre.at[side, :, here], pre_out.at[:, here], out_sem.at[len(stores)]
                )
            )
            stores[-1].start()
            bias_out[:, lo:hi] = jnp.sum(grad_pre.astype(F32), axis=0, keepdims=True)
    wait_all(stores)


def second_kernel(sides, blocks, cap, *refs):
    (offsets, own_act, other_act, grad_out, hidden, mod, slots), refs = refs[:7], refs[7:]
    weights, refs = refs[: len(sides)], refs[len(sides) :]
    onward, refs = refs[:4], refs[4:]
    outs, refs = refs[:blocks], refs[blocks:]
    (gate_grad, *onward_outs), refs = refs[:3], refs[3:]
    weight, sem = refs[:2]
    held, onward_sem = refs[2:6], refs[6]
    halves = start_halves(offsets, weights, sides, weight, sem)
    loads = start_onward(onward, held, onward_sem)
    half = own_act.shape[1]
    wait_all(halves[0])
    mlp = dot(own_act[...], weight[:half, :])
    wait_all(halves[1])
    mlp = mlp + dot(other_act[...], weight[half:, :])
    for latent in range(mod.shape[0]):
        rows = slice(latent * cap, (latent + 1) * cap)
        gate_grad[latent, :, :] = jnp.sum(
            grad_out[rows, :].astype(F32) * mlp[rows], axis=0, keepdims=True
        )
        block = (hidden[rows, :] + mod[latent, 5:6, :] * mlp[rows]).astype(BF)
        unpack_rows(slots, latent, block, outs)
    wait_all(end_onward(loads, held, onward_outs, onward_sem))


def hidden_kernel(pieces, first_pieces, cap, model, *refs):
    (first_at, offsets, parity, own_pre, other_pre, hidden_in, projected_in, grad_in, mod), refs = (
        refs[:9],
        refs[9:],
    )
    first_weights, refs = refs[:first_pieces], refs[first_pieces:]
    out_weights, refs = refs[:pieces], refs[pieces:]
    (grad_hidden_out, grad_proj_out, grad_att, mod_grads), refs = refs[:4], refs[4:]
    first, out_weight, hidden, projected, grad_out, grad_hidden, grad_proj = refs[:7]
    first_sem, out_sem, in_sem, store_sem = refs[7:]
    half = own_pre.shape[1]
    chunks = unit_chunks(parity, half)
    loads = start_chunks(first_at, first_weights, first, first_sem, chunks)
    later = [
        pltpu.make_async_copy(there, here, in_sem.at[i])
        for i, (there, here) in enumerate(
            ((hidden_in, hidden), (projected_in, projected), (grad_in, grad_out))
        )
    ]
    for one in later:
        one.start()
    last = start_pieces(offsets, out_weights, out_weight, out_sem, 3 * model, 4 * model)
    total = None
    for i, (side, lo, hi, cols) in enumerate(chunks):
        wait_all(loads[i])
        part = dot((own_pre, other_pre)[side][:, lo:hi], first[:, cols], NT)
        total = part if total is None else total + part
    wait_all(later)
    stores = []
    for latent in range(mod.shape[0]):
        rows = slice(latent * cap, (latent + 1) * cap)
        normed, inverse = normal(hidden[rows, :])
        grad_mixed = total[rows]
        mod_grads[latent, 0:1, :] = jnp.sum(grad_mixed, axis=0, keepdims=True)
        mod_grads[latent, 1:2, :] = jnp.sum(grad_mixed * normed, axis=0, keepdims=True)
        grad = grad_out[rows, :].astype(F32) + normal_back(
            grad_mixed * (1.0 + mod[latent, 4:5, :]), normed, inverse
        )
        grad_hidden[rows, :] = grad
        mod_grads[latent, 2:3, :] = jnp.sum(grad * projected[rows, :], axis=0, keepdims=True)
        grad_proj[rows, :] = (mod[latent, 2:3, :] * grad).astype(BF)
        here = pl.ds(latent * cap, cap)
        for held, out in ((grad_hidden, grad_hidden_out), (grad_proj, grad_proj_out)):
            stores.append(
                pltpu.make_async_copy(
                    held.at[here, :], out.at[here, :], store_sem.at[len(stores)]
                )
            )
            stores[-1].start()
    wait_all(last)
    grad_att[...] = dot(grad_proj[...], out_weight[...], NT).astype(BF)
    wait_all(stores)


def start_onward(ins, held, sem):
    loads = [pltpu.make_async_copy(a, b, sem.at[i]) for i, (a, b) in enumerate(zip(ins, held))]
    for one in loads:
        one.start()
    return loads


def end_onward(loads, held, outs, sem):
    keep_x, keep_y, far_x, far_y = held
    wait_all(loads)
    keep_x[...] = (keep_x[...].astype(F32) + far_y[...].astype(F32)).astype(BF)
    keep_y[...] = (keep_y[...].astype(F32) + far_x[...].astype(F32)).astype(BF)
    stores = [
        pltpu.make_async_copy(a, b, sem.at[4 + i]) for i, (a, b) in enumerate(zip(held[:2], outs))
    ]
    for one in stores:
        one.start()
    return stores


def attend_back_kernel(cap, model, *refs):
    (live, qkv, grad_att), onward, (grad_qkv, *onward_outs) = refs[:3], refs[3:7], refs[7:10]
    sums, held, onward_sem = refs[10], refs[11:15], refs[15]
    loads = start_onward(onward, held, onward_sem)
    sums[...] = jnp.zeros_like(sums)

    def one_latent(latent, carry):
        here = pl.ds(pl.multiple_of(latent * cap, 16), cap)
        count = live[latent]
        seen = lax.broadcasted_iota(jnp.int32, (cap, cap), 0) < count
        for base, width, first in windows():
            mask = head_mask(width, first, BF)
            cols = slice(base, base + width)
            key_cols = slice(model + base, model + base + width)
            value_cols = slice(2 * model + base, 2 * model + base + width)
            query, key, value = qkv[here, cols] * mask, qkv[here, key_cols] * mask, qkv[here, value_cols]
            grad = grad_att[here, cols] * mask
            scores = jnp.where(seen, dot(key, query, NT), far_below)
            raised = jnp.exp2((scores - jnp.max(scores, axis=0, keepdims=True)) * exp2_scale)
            probs = raised * (1.0 / jnp.sum(raised, axis=0, keepdims=True))
            grad_probs = dot(value, grad, NT)
            delta = jnp.sum(probs * grad_probs, axis=0, keepdims=True)
            grad_scores = (probs * (grad_probs - delta)).astype(BF)
            sums[here, cols] += dot(grad_scores, key, TN)
            sums[here, key_cols] += dot(grad_scores, query)
            sums[here, value_cols] += dot(probs.astype(BF), grad)
        return carry

    lax.fori_loop(0, live.shape[0], one_latent, 0)
    stores = end_onward(loads, held, onward_outs, onward_sem)
    grad_qkv[:, : 2 * model] = (sums[:, : 2 * model] * att_scale).astype(BF)
    grad_qkv[:, 2 * model :] = sums[:, 2 * model :].astype(BF)
    wait_all(stores)


def leave_kernel(pieces, blocks, cap, *refs):
    (
        offsets,
        parity,
        live,
        grad_qkv,
        packed,
        grad_hidden,
        mod,
        slots,
        mod_grads,
        gate_m,
        own_bias,
        other_bias,
    ), refs = refs[:12], refs[12:]
    weights, refs = refs[:pieces], refs[pieces:]
    outs, refs = refs[:blocks], refs[blocks:]
    payload, weight, rows_wide, sem = refs
    model = packed.shape[1]
    group, half = mod.shape[0], own_bias.shape[1]
    rows_wide[...] = jnp.zeros_like(rows_wide)
    lane = lax.broadcasted_iota(jnp.int32, (1, LANES), 1)
    kept = jnp.zeros((1, LANES), F32)
    for latent in range(group):
        at = slice(latent, latent + 1)
        rows_wide[at, 2 * model : 3 * model] = mod_grads[latent, 2:3, :]
        rows_wide[at, 3 * model : 4 * model] = mod_grads[latent, 0:1, :]
        rows_wide[at, 4 * model : 5 * model] = mod_grads[latent, 1:2, :]
        rows_wide[at, 5 * model :] = gate_m[latent]
        kept = jnp.where(lane == latent, live[latent].astype(F32), kept)
    for side, bias in enumerate((own_bias, other_bias)):
        first = pl.multiple_of((parity[0] ^ side) * half, LANES)
        rows_wide[group : group + 1, pl.ds(first, half)] = bias[...]
    rows_wide[group : group + 1, 2 * half : 2 * half + LANES] = kept
    chunks = spans(weight.shape[1], model)
    loads = [
        start_pieces(offsets, weights, weight, sem.at[i], lo, hi) for i, (lo, hi) in enumerate(chunks)
    ]
    total = None
    for i, (lo, hi) in enumerate(chunks):
        wait_all(loads[i])
        part = dot(grad_qkv[:, lo:hi], weight[:, lo:hi], NT)
        total = part if total is None else total + part
    for latent in range(mod.shape[0]):
        rows = slice(latent * cap, (latent + 1) * cap)
        normed, inverse = normal(packed[rows, :].astype(F32))
        grad_mixed = total[rows]
        at = slice(latent, latent + 1)
        rows_wide[at, :model] = jnp.sum(grad_mixed, axis=0, keepdims=True)
        rows_wide[at, model : 2 * model] = jnp.sum(grad_mixed * normed, axis=0, keepdims=True)
        grad = grad_hidden[rows, :] + normal_back(
            grad_mixed * (1.0 + mod[latent, 1:2, :]), normed, inverse
        )
        unpack_rows(slots, latent, grad.astype(BF), outs)
    payload[...] = rows_wide[: group + 1, :].astype(BF)


def spread_kernel(corners, *refs):
    own, pair = refs[:corners], refs[corners : 2 * corners]
    (at, weight), refs = refs[2 * corners : 2 * corners + 2], refs[2 * corners + 2 :]
    cond_own, cond_pair, sent, kept, across, sums, rows, parts, sem = refs
    group = own[0].shape[0] - 1
    totals = []
    for q in range(corners):
        mine, theirs = own[q][...].astype(F32), pair[q][...].astype(F32)
        for side, wide in enumerate((mine, theirs)):
            first = (side * corners + q) * group
            rows[first : first + group, :] = wide[:group]
        totals.append(
            [
                sum(wide[latent : latent + 1] for latent in range(group))
                for wide in (mine, theirs)
            ]
            + [wide[group:] for wide in (mine, theirs)]
        )
    for i in range(2):
        by_corner = [one[2 * i] + one[2 * i + 1] for one in totals]
        while len(by_corner) > 1:
            by_corner = [a + b for a, b in zip(by_corner[::2], by_corner[1::2])]
        sums[i : i + 1, :] = by_corner[0]
    low = rows[...].astype(BF)
    cond = dot(low, weight[...], NT)
    half = corners * group
    cond_own[...] = cond[:half]
    cond_pair[...] = cond[half:]
    count, _, width = parts.shape
    for j in range(count):
        parts[j] = low[:, j * width : (j + 1) * width]
    copies = [
        pltpu.make_async_copy(parts.at[at[0] ^ k], out, sem.at[k])
        for k, out in ((1, sent.at[0]), (3, sent.at[1]), (0, kept), (2, across))
    ]
    for one in copies:
        one.start()
    wait_all(copies)


def outer_kernel(rows, used, sides, *refs):
    block_at, refs = refs[0], refs[1:]
    total = sum(sides)
    lefts, refs = refs[: 2 * len(sides)], refs[2 * len(sides) :]
    rights, refs = refs[: 2 * total], refs[2 * total :]
    (far_x, far_y, near_x, near_y, keep, keep_x, keep_y), refs = refs[:7], refs[7:]
    result, sem = refs
    part, rest = halves_of(rows)
    base, at = 0, 0
    for group, count in enumerate(sides):
        own_left, pair_left = lefts[2 * group : 2 * group + 2]
        left = jnp.concatenate([own_left[:, :used], pair_left[:, :used]], axis=0)
        for own, pair in zip(rights[2 * at : 2 * (at + count) : 2], rights[2 * at + 1 : 2 * (at + count) : 2]):
            width = own.shape[1]
            for lo, hi in spans(width, 768):
                right = jnp.concatenate([own[:, lo:hi], pair[:, lo:hi]], axis=0)
                result[:, base + lo : base + hi] = dot(left, right, TN).astype(BF)
            base += width
        at += count

    def rows_at(k, first, count):
        return result.at[pl.ds(pl.multiple_of(block_at[k] * rows + first, 16), count), :]

    moves = [
        (rows_at(3, 0, part), far_x),
        (rows_at(3, part, rest), far_y),
        (rows_at(1, 0, part), near_x),
        (rows_at(2, part, rest), near_y),
        (rows_at(0, 0, rows), keep),
        (rows_at(1, part, rest), keep_x),
        (rows_at(2, 0, part), keep_y),
    ]
    copies = [pltpu.make_async_copy(a, b, sem.at[i]) for i, (a, b) in enumerate(moves)]
    for one in copies:
        one.start()
    wait_all(copies)


def reorder_kernel(unit, shard, whole):
    count = shard.shape[1] // unit
    for block in range(count):
        to = (block % 2) * (count // 2) + block // 2
        whole[:, to * unit : (to + 1) * unit] = shard[:, block * unit : (block + 1) * unit]


def fold_kernel(cuts, turned, *refs):
    (at, keep, near_top, near_bottom, far_top, far_bottom), refs = refs[:6], refs[6:]
    count = len(cuts[0])
    outs, refs = refs[: 3 * len(cuts)], refs[3 * len(cuts) :]
    scratch, sem = refs[:-1], refs[-1]
    part = far_top.shape[0]
    wide = lambda ref: ref[...].astype(F32)
    top = keep[:part, :].astype(F32) + wide(near_top) + wide(far_top)
    bottom = keep[part:, :].astype(F32) + wide(near_bottom) + wide(far_bottom)
    copies = []
    top, bottom = top.astype(BF), bottom.astype(BF)
    if turned:
        top, bottom = top.T, bottom.T
    for i, (group, parts) in enumerate(zip(cuts, scratch)):
        for j, pieces in enumerate(group):
            first = 0
            for lo, hi in pieces:
                if turned:
                    parts[j, :, :part] = top[lo:hi, :]
                    parts[j, :, part:] = bottom[lo:hi, :]
                    continue
                parts[j, :part, first : first + hi - lo] = top[:, lo:hi]
                parts[j, part:, first : first + hi - lo] = bottom[:, lo:hi]
                first += hi - lo
        sent, own, across = outs[3 * i : 3 * i + 3]
        for k, out in ((1, sent.at[0]), (3, sent.at[1]), (0, own), (2, across)):
            copies.append(pltpu.make_async_copy(parts.at[at[0] ^ k], out, sem.at[len(copies)]))
    for one in copies:
        one.start()
    wait_all(copies)


def outer_pair(groups, rows, name):
    used = 4 * rows
    part, rest = halves_of(rows)
    lefts = [v for left, _ in groups for v in left]
    rights = [v for _, pairs in groups for pair in pairs for v in pair]
    width = sum(v.shape[1] for v in rights) // 2
    sides = tuple(len(pairs) for _, pairs in groups)
    block_at = jnp.stack([(lax.axis_index("dp") ^ (2 * k)) // 2 for k in range(4)]).astype(jnp.int32)
    ins = [block_at, *lefts, *rights]
    outs = (
        jax.ShapeDtypeStruct((part, width), BF),
        jax.ShapeDtypeStruct((rest, width), BF),
        jax.ShapeDtypeStruct((part, width), BF),
        jax.ShapeDtypeStruct((rest, width), BF),
        jax.ShapeDtypeStruct((rows, width), BF),
        jax.ShapeDtypeStruct((rest, width), BF),
        jax.ShapeDtypeStruct((part, width), BF),
    )
    return pl.pallas_call(
        functools.partial(outer_kernel, rows, used, sides),
        out_shape=outs,
        in_specs=[SMEM] + [VMEM] * (len(ins) - 1),
        out_specs=tuple(ANY for _ in outs),
        scratch_shapes=[pltpu.VMEM((used, width), BF), pltpu.SemaphoreType.DMA((7,))],
        name=name,
        compiler_params=pltpu.CompilerParams(vmem_limit_bytes=60 * 1024 * 1024),
    )(*ins)


def onward_kernel(keep_x, keep_y, far_x, far_y, on_x, on_y):
    on_x[...] = (keep_x[...].astype(F32) + far_y[...].astype(F32)).astype(BF)
    on_y[...] = (keep_y[...].astype(F32) + far_x[...].astype(F32)).astype(BF)


def onward(cut, far):
    keep_x, keep_y = cut[5:]
    outs = tuple(jax.ShapeDtypeStruct(v.shape, BF) for v in (keep_x, keep_y))
    ins = [keep_x, keep_y, *far]
    return call(onward_kernel, outs, ins, [VMEM] * 4, [], "onward")


def along_xy(pair):
    return swap(pair[0], "dp", 2), swap(pair[1], "dp", 4)


def fold(keep, near, last, cuts, name, turned=False):
    rows = keep.shape[0]
    count = lax.axis_size("seq")
    at = lax.axis_index("seq").reshape(1).astype(jnp.int32)
    widths = tuple(sum(hi - lo for lo, hi in group[0]) for group in cuts)
    blocks = [(w, rows) if turned else (rows, w) for w in widths]
    outs = tuple(
        jax.ShapeDtypeStruct(shape, BF) for block in blocks for shape in ((2,) + block, block, block)
    )
    return pl.pallas_call(
        functools.partial(fold_kernel, cuts, turned),
        out_shape=outs,
        in_specs=[SMEM] + [VMEM] * 5,
        out_specs=tuple(ANY for _ in outs),
        scratch_shapes=[pltpu.VMEM((count,) + block, BF) for block in blocks]
        + [pltpu.SemaphoreType.DMA((4 * len(cuts),))],
        name=name,
        compiler_params=pltpu.CompilerParams(vmem_limit_bytes=60 * 1024 * 1024),
    )(at, keep, near[0], near[1], last[1], last[0])


def plain_cuts(first, width, count):
    share = width // count
    return tuple(((first + j * share, first + (j + 1) * share),) for j in range(count))


def spread_plain(grad):
    grad = lax.psum_scatter(grad, "dp", scatter_dimension=0, tiled=True)
    return lax.psum_scatter(grad, "seq", scatter_dimension=1, tiled=True)


def body(
    latents,
    condition,
    keep_order,
    keep_count,
    ada_weight,
    ada_bias,
    qkv_weight,
    out_weight,
    fc1_weight,
    fc1_bias,
    fc2_weight,
    cotangent,
):
    latent_count, block_rows, model = latents.shape
    hidden_units = fc1_weight.shape[1]
    half_units = hidden_units // 2
    unit_rows = hidden_units // BLOCKS
    model_rows = model // BLOCKS
    dp_count, seq_count = lax.axis_size("dp"), lax.axis_size("seq")
    dp_at, seq_at = lax.axis_index("dp"), lax.axis_index("seq")
    group = latent_count // seq_count
    most = block_rows * 3 // 4
    cap = (seq_count - 1) * most + block_rows // 4
    rows_all = group * cap
    share = model // dp_count
    column_share = 6 * model // seq_count
    paired = dp_count == BLOCKS and seq_count == 4
    parity = (dp_at & 1) if paired else jnp.zeros_like(dp_at)
    parity_in = parity.reshape(1).astype(jnp.int32)
    part, _ = halves_of(model_rows)
    unit_part, _ = halves_of(unit_rows)
    whose = (lambda k: dp_at ^ k) if paired else (lambda k: jnp.int32(k))
    sds = jax.ShapeDtypeStruct
    dma = lambda n: pltpu.SemaphoreType.DMA((n,))
    fence = lambda *values: lax.optimization_barrier(values)

    def rank_of():
        slot = lax.broadcasted_iota(jnp.int32, (1, block_rows, 1), 1)
        token = lax.broadcasted_iota(jnp.int32, (1, 1, block_rows), 2)
        found = (keep_order[:, :, None] == token) & (slot < keep_count[:, :, None])
        return jnp.max(jnp.where(found, slot, -1), axis=1)

    def places_of(ranks):
        ranks = lax.dynamic_slice_in_dim(ranks, seq_at * group, group, 1)
        ranks = jnp.swapaxes(ranks, 0, 1)
        counts = jnp.sum((ranks >= 0).astype(jnp.int32), axis=2)
        starts = jnp.cumsum(counts, axis=1) - counts
        live = jnp.sum(counts, axis=1).astype(jnp.int32)
        place = jnp.where(ranks >= 0, ranks + starts[:, :, None], -1).reshape(
            group, seq_count * block_rows
        )
        slot = lax.broadcasted_iota(jnp.int32, (1, 1, most), 2)
        slots = jnp.where(slot < counts[:, :, None], starts[:, :, None] + slot, -1)
        return live, place[:, None, :], slots.reshape(group, seq_count * most, 1)

    def whole_slice(blocks_in, k):
        return lax.dynamic_slice_in_dim(blocks_in, (seq_at ^ k) * group, group, 0)

    rank = rank_of()

    def run_home(pieces, base, dtype, name):
        return call(
            home_kernel,
            sds((latent_count, block_rows, model), dtype),
            [seq_at.reshape(1).astype(jnp.int32), rank[:, :, None], base, *pieces],
            [SMEM] + [VMEM] * (2 + seq_count),
            [],
            name,
        )

    cond_wide = condition.astype(F32)
    silu_cond = jax.nn.silu(cond_wide).astype(BF)
    silu_parts = in_order(
        jnp.swapaxes(silu_cond.reshape(latent_count, dp_count, share), 0, 1), "dp"
    )

    def silu_of(rows):
        mine = lax.dynamic_slice_in_dim(rows, seq_at * group, group, 1)
        groups = rows.reshape(dp_count, seq_count, group, share)
        return mine, in_order(jnp.swapaxes(groups, 0, 1), "seq")


    def partial_mod(silu_rows):
        return jnp.dot(
            silu_rows.reshape(dp_count * group, share), ada_weight, preferred_element_type=F32
        ).reshape(dp_count, group, 6 * model)

    def whole_mod(total):
        return (total + ada_bias.astype(F32)).reshape(group, 6, model)

    unit_order = lambda v: jnp.swapaxes(
        v.reshape(v.shape[0], BLOCKS // 2, 2, unit_rows), 1, 2
    ).reshape(v.shape[0], hidden_units)
    bias_row = unit_order(fc1_bias.astype(F32)[None])

    pad = -(-(model // 2) // LANES) * LANES

    def order_of(parity):
        column = lax.broadcasted_iota(jnp.int32, (1, 2 * pad), 1)
        side, inner = column // pad, column % pad
        source = (2 * (inner // model_rows) + (parity ^ side)) * model_rows + inner % model_rows
        source = jnp.where(inner < model // 2, source, -1)
        return (lax.broadcasted_iota(jnp.int32, (model, 1), 0) == source).astype(BF)

    model_position = lambda k: whose(k)
    unit_position = lambda k: ((whose(k) & 1) ^ parity) * (BLOCKS // 2) + whose(k) // 2

    def run_enter(joint, place_row, mod, pieces, order):
        weights, offsets = joint
        return call(
            functools.partial(enter_kernel, len(weights), seq_count, cap),
            (
                sds((rows_all, model), BF),
                sds((rows_all, 3 * model), BF),
                sds((rows_all, pad), BF),
                sds((rows_all, pad), BF),
            ),
            [
                offsets,
                place_row,
                mod,
                order,
                *pieces,
                *weights,
            ],
            [SMEM, VMEM, VMEM, VMEM] + [VMEM] * seq_count + [ANY] * len(weights),
            [
                pltpu.VMEM((model, 3 * model), BF),
                pltpu.VMEM((rows_all, model), BF),
                pltpu.SemaphoreType.DMA((3, len(weights))),
            ],
            "enter",
        )

    def run_cot(place_row, mod, cot_pieces):
        low = sds((rows_all, model), BF)
        ins = [place_row, mod, *cot_pieces]
        return call(functools.partial(cot_kernel, cap), (low, low), ins, [VMEM] * len(ins), [], "cotangent")

    def run_attend(joint, live, qkv, packed, mod, order):
        weights, offsets = joint
        return call(
            functools.partial(attend_kernel, len(weights), cap, model),
            (
                sds((rows_all, pad), BF),
                sds((rows_all, pad), BF),
                sds((rows_all, model), F32),
                sds((rows_all, model), F32),
                sds((rows_all, model), BF),
                sds((rows_all, pad), BF),
                sds((rows_all, pad), BF),
            ),
            [
                offsets,
                live,
                qkv,
                packed,
                mod,
                order,
                *weights,
            ],
            [SMEM, SMEM, VMEM, VMEM, VMEM, VMEM] + [ANY] * len(weights),
            [
                pltpu.VMEM((model, model), BF),
                pltpu.VMEM((rows_all, model), F32),
                dma(len(weights)),
            ],
            "attend",
        )

    def run_first(first, mixed):
        weights, offsets = first
        half_rows = sds((rows_all, half_units), BF)
        chunks = 2 * len(spans(half_units, 768))
        return call(
            functools.partial(first_kernel, len(weights)),
            (half_rows,) * 4,
            [offsets, parity_in, mixed, bias_row, *weights],
            [SMEM, SMEM, VMEM, VMEM] + [ANY] * len(weights),
            [
                pltpu.VMEM((model, hidden_units), BF),
                pltpu.VMEM((2, rows_all, half_units), BF),
                pltpu.VMEM((2, rows_all, half_units), BF),
                pltpu.SemaphoreType.DMA((chunks, len(weights))),
                dma(chunks),
                dma(chunks),
            ],
            "first",
            (ANY,) * 4,
        )

    def run_slope(second, slopes, grad_mlp):
        weights, offsets, sides = second
        half_rows = sds((rows_all, half_units), BF)
        return call(
            functools.partial(slope_kernel, sides),
            (half_rows, half_rows, sds((1, half_units), F32), sds((1, half_units), F32)),
            [offsets, *slopes, grad_mlp, *weights],
            [SMEM] + [VMEM] * 3 + [ANY] * len(weights),
            [
                pltpu.VMEM((hidden_units, model), BF),
                pltpu.VMEM((2, rows_all, half_units), BF),
                dma(len(weights)),
                dma(2 * len(spans(half_units, 768))),
            ],
            "slope",
            (ANY, ANY, VMEM, VMEM),
        )

    def onward_parts(cut, far):
        ins = [cut[5], cut[6], *far]
        return (
            ins,
            tuple(sds(v.shape, BF) for v in ins[:2]),
            [pltpu.VMEM(v.shape, BF) for v in ins] + [dma(6)],
        )

    def run_second(second, acts, grad_out, hidden, mod, slots, cut, far):
        weights, offsets, sides = second
        ins, outs, scratch = onward_parts(cut, far)
        result = call(
            functools.partial(second_kernel, sides, seq_count, cap),
            tuple(sds((group, most, model), BF) for _ in range(seq_count))
            + (sds((group, 1, model), F32),)
            + outs,
            [offsets, *acts, grad_out, hidden, mod, slots, *weights, *ins],
            [SMEM] + [VMEM] * 6 + [ANY] * (len(weights) + 4),
            [pltpu.VMEM((hidden_units, model), BF), dma(len(weights))] + scratch,
            "second",
            (VMEM,) * (seq_count + 1) + (ANY, ANY),
        )
        return result[:seq_count], result[seq_count], result[seq_count + 1 :]

    def run_hidden(first, joint, pres, hidden, projected, grad_out, mod):
        (weights, offsets), (first_w, first_at) = joint, first
        wide, low = sds((rows_all, model), F32), sds((rows_all, model), BF)
        return call(
            functools.partial(hidden_kernel, len(weights), len(first_w), cap, model),
            (wide, low, low, sds((group, 3, model), F32)),
            [
                first_at,
                offsets,
                parity_in,
                *pres,
                hidden,
                projected,
                grad_out,
                mod,
                *first_w,
                *weights,
            ],
            [SMEM, SMEM, SMEM, VMEM, VMEM, ANY, ANY, ANY, VMEM]
            + [ANY] * (len(first_w) + len(weights)),
            [
                pltpu.VMEM((model, hidden_units), BF),
                pltpu.VMEM((model, model), BF),
                pltpu.VMEM((rows_all, model), F32),
                pltpu.VMEM((rows_all, model), F32),
                pltpu.VMEM((rows_all, model), BF),
                pltpu.VMEM((rows_all, model), F32),
                pltpu.VMEM((rows_all, model), BF),
                pltpu.SemaphoreType.DMA((2 * len(spans(half_units, 768)), len(first_w))),
                dma(len(weights)),
                dma(3),
                dma(2 * group),
            ],
            "hidden_back",
            (ANY, ANY, VMEM, VMEM),
        )

    def run_attend_back(live, qkv, grad_att, cut, far):
        ins, outs, scratch = onward_parts(cut, far)
        grad_qkv, *on = call(
            functools.partial(attend_back_kernel, cap, model),
            (sds((rows_all, 3 * model), BF),) + outs,
            [live, qkv, grad_att, *ins],
            [SMEM, VMEM, VMEM] + [ANY] * 4,
            [pltpu.VMEM((rows_all, 3 * model), F32)] + scratch,
            "attend_back",
            (VMEM, ANY, ANY),
        )
        return grad_qkv, on

    def run_leave(
        joint, grad_qkv, packed, grad_hidden, mod, slots, live, mod_grads, gate_m, biases
    ):
        weights, offsets = joint
        result = call(
            functools.partial(leave_kernel, len(weights), seq_count, cap),
            tuple(sds((group, most, model), BF) for _ in range(seq_count))
            + (sds((group + 1, 6 * model), BF),),
            [
                offsets,
                parity_in,
                live,
                grad_qkv,
                packed,
                grad_hidden,
                mod,
                slots,
                mod_grads,
                gate_m,
                *biases,
                *weights,
            ],
            [SMEM, SMEM, SMEM] + [VMEM] * 9 + [ANY] * len(weights),
            [
                pltpu.VMEM((model, 3 * model), BF),
                pltpu.VMEM((8, 6 * model), F32),
                pltpu.SemaphoreType.DMA((3, len(weights))),
            ],
            "leave",
        )
        return result[:seq_count], result[seq_count]

    def split_sums(sums):
        units = jnp.swapaxes(
            sums[1, :hidden_units].reshape(2, BLOCKS // 2, unit_rows), 0, 1
        ).reshape(hidden_units)
        kept = jnp.sum(sums[1, hidden_units : hidden_units + group])
        return sums[0], units, kept.reshape(1).astype(jnp.int32)

    def sums_of(gathered):
        wide = gathered.astype(F32)
        total = jnp.stack([jnp.sum(wide[:, :group], axis=1), wide[:, group]], axis=1)
        while total.shape[0] > 1:
            total = total.reshape((total.shape[0] // 2, 2) + total.shape[1:])
            total = total[:, 0] + total[:, 1]
        return total[0]

    def by_columns(grad_mod_all):
        return in_order(
            jnp.stack(
                [
                    grad_mod_all[:, :, j * column_share : (j + 1) * column_share]
                    for j in range(seq_count)
                ]
            ),
            "seq",
        )

    def cond_product(grad_mod_all):
        return dot(grad_mod_all.reshape(dp_count * group, 6 * model), ada_weight, NT).reshape(
            dp_count, group, share
        )

    def ada_product(silu_all, columns):
        return dot(
            silu_all.reshape(seq_count * dp_count * group, share),
            columns.reshape(seq_count * dp_count * group, column_share),
            TN,
        )

    def cond_end(rows):
        rows = in_order(rows, "seq").reshape(latent_count, model)
        _, silu_back = jax.vjp(jax.nn.silu, cond_wide)
        return silu_back(rows)[0]

    def cond_mine_of(cols):
        return jnp.swapaxes(in_order(cols, "dp"), 0, 1).reshape(group, model)

    if not paired:
        order = order_of(parity)
        live, place_row, slots = places_of(gather_all(rank, "seq"))
        silu_rows, silu_all = silu_of(trade_all(silu_parts, "dp"))
        mod = whole_mod(sum_own(partial_mod(silu_rows), "dp"))
        to_whole = lambda v: [
            swap(whole_slice(v, k), "seq", k) if k else whole_slice(v, k)
            for k in range(seq_count)
        ]
        latent_pieces, cot_pieces = to_whole(latents), to_whole(cotangent)
        joint = whole_weight(jnp.concatenate([qkv_weight, out_weight], axis=1))
        joint = [joint], jnp.zeros((1,), jnp.int32)
        first = [whole_weight(unit_order(fc1_weight))], jnp.zeros((1,), jnp.int32)
        full = whole_weight(fc2_weight)
        second = placed(
            [(full[k * unit_rows : (k + 1) * unit_rows], k, 0) for k in range(BLOCKS)],
            unit_position,
            unit_rows,
        ) + (tuple(k & 1 for k in range(BLOCKS)),)
        packed, qkv, *mixa = run_enter(joint, place_row, mod, latent_pieces, order)
        grad_out, grad_mlp = run_cot(place_row, mod, cot_pieces)
        att_own, att_other, projected, hidden, mixed, *mixm = run_attend(
            joint, live, qkv, packed, mod, order
        )
        acts = run_first(first, mixed)
        *pres, bias_own, bias_other = run_slope(second, acts[2:], grad_mlp)
        none = [jnp.zeros((16, LANES), BF)] * 7
        block_pieces, gate_m_grad, _ = run_second(
            second, acts[:2], grad_out, hidden, mod, slots, none, none[:2]
        )
        grad_hidden, grad_proj, grad_att, mod_grads = run_hidden(
            first, joint, pres, hidden, projected, grad_out, mod
        )
        grad_qkv, _ = run_attend_back(live, qkv, grad_att, none, none[:2])
        latent_grads, payload = run_leave(
            joint,
            grad_qkv,
            packed,
            grad_hidden,
            mod,
            slots,
            live,
            mod_grads,
            gate_m_grad,
            (bias_own, bias_other),
        )
        gathered = gather_all(payload, "dp")
        grad_mod_all = gathered[:, :group]
        sums = sums_of(gathered)
        for step in steps_of("seq"):
            sums = sums + swap(sums, "seq", step)
        ada_bias_grad, fc1_bias_grad, kept_total = split_sums(sums)
        ada_grad = ada_product(silu_all, trade_all(by_columns(grad_mod_all), "seq"))
        cond_cols = trade_all(cond_product(grad_mod_all), "dp")
        condition_grad = cond_end(gather_all(cond_mine_of(cond_cols), "seq"))

        def mixed_sides(own, other, width):
            both = jnp.stack([own[:, : 4 * width], other[:, : 4 * width]], axis=1)
            return jnp.swapaxes(both.reshape(rows_all, 2, 4, width), 1, 2).reshape(
                rows_all, BLOCKS * width
            )

        product = lambda a, b: spread_plain(dot(a, b, TN))
        fc2_grad = product(mixed_sides(acts[0], acts[1], unit_rows), grad_mlp)
        fc1_grad = product(
            mixed_sides(*mixm, model_rows), mixed_sides(pres[0], pres[1], unit_rows)
        )
        out_grad = product(mixed_sides(att_own, att_other, model_rows), grad_proj)
        qkv_grad = product(mixed_sides(*mixa, model_rows), grad_qkv)
        home = lambda pieces: [swap(v, "seq", k) if k else v for k, v in enumerate(pieces)]
        block_out = run_home(home(block_pieces), latents, BF, "home_out")
        latents_grad = run_home(home(latent_grads), cotangent, F32, "home_grad")
        return (
            block_out,
            latents_grad,
            condition_grad,
            ada_grad,
            ada_bias_grad,
            qkv_grad,
            out_grad,
            fc1_grad,
            fc1_bias_grad,
            fc2_grad,
            kept_total,
        )

    def trade(value, axis, step):
        split = value.reshape((-1, 2, step) + value.shape[1:])
        return jnp.stack([split[:, 0], swap(split[:, 1], axis, step)], axis=1).reshape(value.shape)

    def grow(value, axis, step):
        return jnp.concatenate([value, swap(value, axis, step)], axis=0)

    def columns_first(parts):
        sent, own, across = parts
        return swap(sent, "seq", 1), own, across

    def columns_second(state):
        near, own, across = state
        on = (across.astype(F32) + near[1].astype(F32)).astype(BF)
        return swap(on, "seq", 2), own, near

    def columns_sum(state):
        far, own, near = state
        return own.astype(F32) + near[0].astype(F32) + far.astype(F32)

    def tails(beside, first):
        rows, width = beside[0].shape
        return call(
            functools.partial(cut_kernel, first),
            (sds((first, width), BF), sds((rows - first, width), BF)),
            [beside[1], beside[0]],
            [ANY, ANY],
            [pltpu.VMEM((first, width), BF), pltpu.VMEM((rows - first, width), BF), dma(2), dma(2)],
            "cut",
            (ANY, ANY),
        )

    joint_own = jnp.concatenate([qkv_weight, out_weight], axis=1)

    corners_of = lambda value: [swap(value[q], "dp", 2 * q) for q in (1, 2, 3)]

    corners = silu_parts.reshape(4, 2, latent_count, share)
    corners = jnp.stack([corners[0], *corners_of(corners)])
    corners, joint_own, fc1_in, latents_in, cot_in, rank_in, parity_late = fence(
        corners, joint_own, fc1_weight, latents, cotangent, rank, parity
    )

    joint_beside = beside_of(joint_own)
    latent_pieces = [whole_slice(latents_in, k) for k in range(seq_count)]
    latent_1 = swap(latent_pieces[1], "seq", 1)
    latent_2 = swap(latent_pieces[2], "seq", 2)
    latent_3 = swap(latent_pieces[3], "seq", 3)
    silu_corners = trade(corners.reshape(8, latent_count, share), "dp", 1)
    silu_rows, silu_all = silu_of(silu_corners)
    silu_all = jnp.swapaxes(silu_all.reshape(seq_count, 4, 2, group, share), 1, 2)
    pairs = partial_mod(silu_rows).reshape(4, 2, group, 6 * model)
    corners = pairs[:, 0] + swap(pairs[:, 1], "dp", 1)
    parity_late, fc1_in, cot_in = after((parity_late, fc1_in, cot_in), corners)
    order = order_of(parity_late)
    first_own = call(
        functools.partial(reorder_kernel, unit_rows),
        sds(fc1_in.shape, BF),
        [fc1_in],
        [VMEM],
        [],
        "reorder",
    )
    cot_pieces = [whole_slice(cot_in, k) for k in range(seq_count)]
    ranks = grow(grow(after(rank_in, latent_1)[None], "seq", 1), "seq", 2)
    (
        joint_beside,
        latent_1,
        latent_2,
        latent_3,
        silu_all,
        corners,
        joint_own,
        order,
        first_own,
        cot_pieces,
        ranks,
    ) = fence(
        joint_beside,
        latent_1,
        latent_2,
        latent_3,
        silu_all,
        corners,
        joint_own,
        order,
        first_own,
        cot_pieces,
        ranks,
    )

    sums = corners_of(corners)
    joint_tails = tails(joint_beside, part)
    sums, joint_tails, joint_beside, joint_own, ranks = fence(
        sums, joint_tails, joint_beside, joint_own, ranks
    )
    joint_across = (swap(joint_tails[0], "dp", 2), swap(joint_tails[1], "dp", 4))
    mod = whole_mod(sum(sums, corners[0]))
    joint_pair, joint_x_pair, joint_y_pair = pair_of((joint_own, *joint_beside))
    live, place_row, slots = places_of(ranks)
    (
        joint_across,
        mod,
        joint_pair,
        joint_x_pair,
        joint_y_pair,
        live,
        place_row,
        slots,
        first_own,
        cot_pieces,
    ) = fence(
        joint_across,
        mod,
        joint_pair,
        joint_x_pair,
        joint_y_pair,
        live,
        place_row,
        slots,
        first_own,
        cot_pieces,
    )

    first_beside = beside_of(first_own)
    cot_1 = swap(cot_pieces[1], "seq", 1)
    cot_2 = swap(cot_pieces[2], "seq", 2)
    cot_3 = swap(cot_pieces[3], "seq", 3)
    joint = placed(
        pieces_of(
            joint_own,
            joint_pair,
            joint_beside,
            (joint_x_pair, joint_y_pair),
            joint_across,
            pair_of(joint_across),
            part,
        ),
        model_position,
        model_rows,
    )
    packed, qkv, mixa_own, mixa_other = run_enter(
        joint, place_row, mod, (latent_pieces[0], latent_1, latent_2, latent_3), order
    )
    att_own, att_other, projected, hidden, mixed, mixm_own, mixm_other = run_attend(
        joint, live, qkv, packed, mod, order
    )
    first_beside, cot_1, cot_2, cot_3, mixed, first_own = fence(
        first_beside, cot_1, cot_2, cot_3, mixed, first_own
    )

    first_tails = tails(first_beside, part)
    first_across = (swap(first_tails[0], "dp", 2), swap(first_tails[1], "dp", 4))
    first_pair, first_x_pair, first_y_pair = pair_of((first_own, *first_beside))
    grad_out, grad_mlp = run_cot(place_row, mod, (cot_pieces[0], cot_1, cot_2, cot_3))
    second_own = (fc2_weight[:unit_part], fc2_weight[unit_part:])
    (
        first_across,
        first_pair,
        first_x_pair,
        first_y_pair,
        grad_out,
        grad_mlp,
        second_own,
        second_in,
    ) = fence(
        first_across,
        first_pair,
        first_x_pair,
        first_y_pair,
        grad_out,
        grad_mlp,
        second_own,
        fc2_weight,
    )

    second_ahead = swap(second_own[1], "dp", 2), swap(second_own[0], "dp", 4)
    first = placed(
        pieces_of(
            first_own,
            first_pair,
            first_beside,
            (first_x_pair, first_y_pair),
            first_across,
            pair_of(first_across),
            part,
        ),
        model_position,
        model_rows,
    )
    (grad_mlp_pair,) = pair_of((grad_mlp,))
    acts = run_first(first, mixed)
    second_ahead, second_own, grad_mlp_pair, acts = fence(
        second_ahead, second_own, grad_mlp_pair, acts
    )

    second_behind = swap(second_own[0], "dp", 2), swap(second_own[1], "dp", 4)
    (second_pair,) = pair_of((second_in,))
    (act_pair,) = pair_of((acts[1],))
    fc2_cut = outer_pair(
        [((acts[0], act_pair), [(grad_mlp, grad_mlp_pair)])], unit_rows, "fc2_grad"
    )
    second_behind, second_pair, second_ahead, fc2_cut, mixm_other, att_other, mixa_other = fence(
        second_behind, second_pair, second_ahead, fc2_cut, mixm_other, att_other, mixa_other
    )

    second_across = swap(second_ahead[1], "dp", 2), swap(second_ahead[0], "dp", 4)
    second_ahead_pair, second_behind_pair = pair_of(second_ahead), pair_of(second_behind)
    mixm_pair, att_pair, mixa_pair = pair_of((mixm_other, att_other, mixa_other))
    (
        second_across,
        second_ahead_pair,
        second_behind_pair,
        mixm_pair,
        att_pair,
        mixa_pair,
        fc2_cut,
        acts,
    ) = fence(
        second_across,
        second_ahead_pair,
        second_behind_pair,
        mixm_pair,
        att_pair,
        mixa_pair,
        fc2_cut,
        acts,
    )

    fc2_far = along_xy(fc2_cut[:2])
    pieces = [(second_in, 0, 0), (second_pair, 1, 0)]
    for side, ahead, behind, beyond in (
        (0, second_ahead, second_behind, second_across),
        (1, second_ahead_pair, second_behind_pair, pair_of(second_across)),
    ):
        pieces += [
            (behind[0], 2 + side, 0),
            (ahead[0], 2 + side, unit_part),
            (ahead[1], 4 + side, 0),
            (behind[1], 4 + side, unit_part),
            (beyond[0], 6 + side, 0),
            (beyond[1], 6 + side, unit_part),
        ]
    second = placed(pieces, unit_position, unit_rows) + (tuple(k & 1 for _, k, _ in pieces),)
    pre_own, pre_other, bias_own, bias_other = run_slope(second, acts[2:], grad_mlp)
    fc2_far, fc2_cut, pre_own, pre_other, acts = fence(
        fc2_far, fc2_cut, pre_own, pre_other, acts
    )

    fc2_near = along_xy(fc2_cut[2:4])
    pre_other_pair, pre_own_pair = pair_of((pre_own, pre_other))
    block_pieces, gate_m_grad, on = run_second(
        second, acts[:2], grad_out, hidden, mod, slots, fc2_cut, fc2_far
    )
    fc2_near, on, pre_other_pair, pre_own_pair, block_pieces, gate_m_grad = fence(
        fc2_near, on, pre_other_pair, pre_own_pair, block_pieces, gate_m_grad
    )

    fc2_last = along_xy(on)
    block_1 = swap(block_pieces[1], "seq", 1)
    block_2 = swap(block_pieces[2], "seq", 2)
    fc1_cut = outer_pair(
        [((mixm_own, mixm_pair), [(pre_own, pre_own_pair), (pre_other, pre_other_pair)])],
        model_rows,
        "fc1_grad",
    )
    fc2_last, block_1, block_2, block_3, fc1_cut, pre_own, pre_other, fc2_near = fence(
        fc2_last, block_1, block_2, block_pieces[3], fc1_cut, pre_own, pre_other, fc2_near
    )

    fc1_far = along_xy(fc1_cut[:2])
    fc2_parts = fold(
        fc2_cut[4], fc2_near, fc2_last, (plain_cuts(0, model, seq_count),), "fc2_fold", True
    )
    fc2_state = columns_first(fc2_parts)
    grad_hidden, grad_proj, grad_att, mod_grads = run_hidden(
        first, joint, after((pre_own, pre_other), fc2_parts), hidden, projected, grad_out, mod
    )
    fc1_far, fc1_cut, grad_proj, grad_att, fc2_state = fence(
        fc1_far, fc1_cut, grad_proj, grad_att, fc2_state
    )

    fc1_near = along_xy(fc1_cut[2:4])
    fc2_state = columns_second(fc2_state)
    (proj_pair,) = pair_of((grad_proj,))
    grad_qkv, on = run_attend_back(live, qkv, grad_att, fc1_cut, fc1_far)
    fc1_near, on, fc2_state, proj_pair, grad_qkv, block_3 = fence(
        fc1_near, on, fc2_state, proj_pair, grad_qkv, block_3
    )

    fc1_last = along_xy(on)
    (qkv_pair,) = pair_of((grad_qkv,))
    block_3 = swap(block_3, "seq", 3)
    last_cut = outer_pair(
        [
            ((mixa_own, mixa_pair), [(grad_qkv, qkv_pair)]),
            ((att_own, att_pair), [(grad_proj, proj_pair)]),
        ],
        model_rows,
        "last_grad",
    )
    fc1_last, last_cut, grad_qkv, fc1_near, block_3 = fence(
        fc1_last, last_cut, grad_qkv, fc1_near, block_3
    )

    last_far = along_xy(last_cut[:2])
    fc1_cuts = tuple(
        tuple((lo, lo + unit_rows) for lo in (j * unit_rows, half_units + j * unit_rows))
        for j in range(seq_count)
    )
    fc1_parts = fold(fc1_cut[4], fc1_near, fc1_last, (fc1_cuts,), "fc1_fold")
    fc1_state = columns_first(fc1_parts)
    latent_grads, payload = run_leave(
        joint,
        after(grad_qkv, fc1_parts),
        packed,
        grad_hidden,
        mod,
        slots,
        live,
        mod_grads,
        gate_m_grad,
        (bias_own, bias_other),
    )
    last_far, last_cut, fc1_state, latent_grads, payload = fence(
        last_far, last_cut, fc1_state, latent_grads, payload
    )

    corners = [payload] + [swap(payload, "dp", 2 * q) for q in (1, 2, 3)]
    corners, last_cut, last_far, latent_1, fc1_state, block_pieces = fence(
        corners, last_cut, last_far, latent_grads[1], fc1_state, block_pieces
    )

    last_near = along_xy(last_cut[2:4])
    on = onward(last_cut, last_far)
    corner_pairs = pair_of(corners)
    latent_1 = after(latent_1, corner_pairs)
    rows_here = 8 * group
    cond_own, cond_pair, column_sent, column_own, column_across, sums = call(
        functools.partial(spread_kernel, 4),
        (
            sds((rows_here // 2, share), F32),
            sds((rows_here // 2, share), F32),
            sds((2, rows_here, column_share), BF),
            sds((rows_here, column_share), BF),
            sds((rows_here, column_share), BF),
            sds((2, 6 * model), F32),
        ),
        [*corners, *corner_pairs, seq_at.reshape(1).astype(jnp.int32), ada_weight],
        [VMEM] * 8 + [SMEM, VMEM],
        [
            pltpu.VMEM((rows_here, 6 * model), F32),
            pltpu.VMEM((seq_count, rows_here, column_share), BF),
            dma(seq_count),
        ],
        "spread",
        (VMEM, VMEM, ANY, ANY, ANY, VMEM),
    )
    fc1_state = columns_second(fc1_state)
    latent_1 = swap(latent_1, "seq", 1)
    block_out = run_home(
        after((block_pieces[0], block_1, block_2, block_3), on, sums), latents, BF, "home_out"
    )
    (
        last_near,
        on,
        cond_own,
        cond_pair,
        column_sent,
        sums,
        fc1_state,
        latent_1,
        latent_2,
        latent_3,
        block_out,
        fc2_state,
    ) = fence(
        last_near,
        on,
        cond_own,
        cond_pair,
        column_sent,
        sums,
        fc1_state,
        latent_1,
        latent_grads[2],
        latent_grads[3],
        block_out,
        fc2_state,
    )

    last_last = along_xy(on)
    sums = sums + swap(sums, "seq", 1)
    column_near = swap(column_sent, "seq", 1)
    (cond_pair,) = pair_of((cond_pair,))
    latent_2 = swap(latent_2, "seq", 2)
    latent_3 = swap(latent_3, "seq", 3)
    (
        last_last,
        sums,
        column_near,
        latent_2,
        latent_3,
        last_near,
        fc1_state,
        fc2_state,
        cond_own,
        cond_pair,
    ) = fence(
        last_last,
        sums,
        column_near,
        latent_2,
        latent_3,
        last_near,
        fc1_state,
        fc2_state,
        cond_own,
        cond_pair,
    )

    qkv_share, out_share = 3 * model // seq_count, model // seq_count
    last_cuts = tuple(
        (
            (j * qkv_share, (j + 1) * qkv_share),
            (3 * model + j * out_share, 3 * model + (j + 1) * out_share),
        )
        for j in range(seq_count)
    )
    last_parts = fold(last_cut[4], last_near, last_last, (last_cuts,), "last_fold")
    last_state = columns_first(last_parts)
    cond_cols = jnp.stack([cond_own, cond_pair], axis=1).reshape(4, group, 2, share)
    cond_cols = jnp.swapaxes(cond_cols, 1, 2)
    cond_cols = jnp.stack([cond_cols[0], *corners_of(cond_cols)])
    cond_mine = cond_mine_of(cond_cols.reshape(8, group, share))
    column_across, column_near, sums = after((column_across, column_near, sums), last_parts)
    column_far = swap(jnp.stack([column_across, column_near[1]]), "seq", 2)
    columns = jnp.stack([column_own, column_near[0], column_far[0], column_far[1]])
    ada_grad = ada_product(silu_all, columns)
    sums = sums + swap(sums, "seq", 2)
    fc2_grad = columns_sum(fc2_state).T
    fc1_grad = columns_sum(fc1_state)
    fc1_grad = jnp.where(
        parity == 1,
        jnp.concatenate([fc1_grad[:, unit_rows:], fc1_grad[:, :unit_rows]], axis=1),
        fc1_grad,
    )
    last_state, cond_mine, ada_grad, sums, fc1_grad, fc2_grad = fence(
        last_state, cond_mine, ada_grad, sums, fc1_grad, fc2_grad
    )

    latents_grad = run_home(
        after((latent_grads[0], latent_1, latent_2, latent_3), last_state),
        cotangent,
        F32,
        "home_grad",
    )
    cond_mine, latents_grad = after((cond_mine, latents_grad), latents_grad)
    cond_rows = [swap(cond_mine, "seq", k) if k else cond_mine for k in range(seq_count)]
    condition_grad = cond_end(jnp.stack(cond_rows))
    far, own, near = columns_second(last_state)
    qkv_grad = columns_sum((far[:, :qkv_share], own[:, :qkv_share], near[:, :, :qkv_share]))
    out_grad = columns_sum((far[:, qkv_share:], own[:, qkv_share:], near[:, :, qkv_share:]))
    ada_bias_grad, fc1_bias_grad, kept_total = split_sums(sums)
    return (
        block_out,
        latents_grad,
        condition_grad,
        ada_grad,
        ada_bias_grad,
        qkv_grad,
        out_grad,
        fc1_grad,
        fc1_bias_grad,
        fc2_grad,
        kept_total,
    )


def solution(mesh):
    placed = (
        P("dp", "seq", None),
        P("dp", None),
        P("dp", "seq"),
        P("dp", "seq"),
        P("dp", None),
        P(),
        P("dp", None),
        P("dp", None),
        P("dp", None),
        P(),
        P("dp", None),
        P("dp", "seq", None),
    )
    return jax.shard_map(
        body,
        mesh=mesh,
        in_specs=placed,
        out_specs=(
            P("dp", "seq", None),
            P("dp", "seq", None),
            P("dp", None),
            P("dp", "seq"),
            P(),
            P("dp", "seq"),
            P("dp", "seq"),
            P("dp", "seq"),
            P(),
            P("dp", "seq"),
            P(),
        ),
        check_vma=False,
    )
```

```python
import functools
import math

import jax
import jax.numpy as jnp
from jax import lax
from jax.experimental import pallas as pl
from jax.experimental.pallas import tpu as pltpu
from jax.sharding import PartitionSpec as P

HEADS = 16
HEAD = 72
LANES = 128
BLOCKS = 8

layer_eps = 1e-06
far_below = -1e30
att_scale = 1.0 / math.sqrt(HEAD)
exp2_scale = att_scale / math.log(2.0)
gelu_c = math.sqrt(2.0 / math.pi)
gelu_k = 0.044715

BF = jnp.bfloat16
F32 = jnp.float32
VMEM = pl.BlockSpec(memory_space=pltpu.VMEM)
SMEM = pl.BlockSpec(memory_space=pltpu.SMEM)
ANY = pl.BlockSpec(memory_space=pl.ANY)
NT = (((1,), (1,)), ((), ()))
TN = (((0,), (0,)), ((), ()))


def swap(value, axis, step):
    return lax.ppermute(value, axis, [(i, i ^ step) for i in range(lax.axis_size(axis))])


def steps_of(axis):
    count = lax.axis_size(axis)
    return [1 << i for i in range(count.bit_length() - 1)]


def bit_set(axis, step):
    return (lax.axis_index(axis) & step) != 0


def gather_all(value, axis):
    value = value[None]
    for step in steps_of(axis):
        value = jnp.concatenate([value, swap(value, axis, step)], axis=0)
    return value


def sum_own(value, axis):
    for step in reversed(steps_of(axis)):
        value = value[:step] + swap(value[step:], axis, step)
    return value[0]


def trade_all(value, axis):
    count = value.shape[0]
    rest = value.shape[1:]
    for step in steps_of(axis):
        split = value.reshape((count // (2 * step), 2, step) + rest)
        value = jnp.stack([split[:, 0], swap(split[:, 1], axis, step)], axis=1).reshape(
            (count,) + rest
        )
    return value


def in_order(value, axis):
    count = value.shape[0]
    rest = value.shape[1:]
    for step in steps_of(axis):
        split = value.reshape((count // (2 * step), 2, step) + rest)
        value = jnp.where(bit_set(axis, step), split[:, ::-1], split).reshape((count,) + rest)
    return value


def sum_everywhere(value):
    for axis in ("dp", "seq"):
        for step in steps_of(axis):
            value = value + swap(value, axis, step)
    return value


def after(value, *earlier):
    return lax.optimization_barrier((value,) + earlier)[0]


def halves_of(rows):
    first = (rows // 2 + 15) // 16 * 16
    return first, rows - first


def pieces_of(own, own_pair, beside, beside_pair, across, across_pair, part):
    return [
        (own, 0, 0),
        (own_pair, 1, 0),
        (beside[0], 2, 0),
        (beside_pair[0], 3, 0),
        (beside[1], 4, 0),
        (beside_pair[1], 5, 0),
        (across[0], 6, 0),
        (across[1], 6, part),
        (across_pair[0], 7, 0),
        (across_pair[1], 7, part),
    ]


def beside_of(shard):
    return swap(shard, "dp", 2), swap(shard, "dp", 4)


def across_of(beside, part):
    return swap(beside[1][:part], "dp", 2), swap(beside[0][part:], "dp", 4)


def pair_of(values):
    return tuple(swap(v, "dp", 1) for v in values)


def placed(pieces, position, rows):
    starts = jnp.stack([position(k) * rows + first for _, k, first in pieces]).astype(jnp.int32)
    return [v for v, _, _ in pieces], starts


def whole_weight(shard):
    return lax.all_gather(shard, "dp", axis=0, tiled=True)


def call(kernel, outs, ins, specs, scratch, name, out_specs=None):
    return pl.pallas_call(
        kernel,
        out_shape=outs,
        in_specs=specs,
        out_specs=out_specs or jax.tree.map(lambda _: VMEM, outs),
        scratch_shapes=scratch,
        name=name,
        compiler_params=pltpu.CompilerParams(vmem_limit_bytes=60 * 1024 * 1024),
    )(*ins)


def start_pieces(offsets, refs, target, sem, lo, hi):
    copies = []
    shift = lo if target.shape[1] == hi - lo else 0
    for k, ref in enumerate(refs):
        rows = ref.shape[0]
        copies.append(
            pltpu.make_async_copy(
                ref.at[:, pl.ds(lo, hi - lo)],
                target.at[pl.ds(pl.multiple_of(offsets[k], 16), rows), pl.ds(lo - shift, hi - lo)],
                sem.at[k],
            )
        )
    for one in copies:
        one.start()
    return copies


def wait_all(copies):
    for one in copies:
        one.wait()


def normal(rows_in):
    center = rows_in - jnp.mean(rows_in, axis=-1, keepdims=True)
    inverse = lax.rsqrt(jnp.mean(center * center, axis=-1, keepdims=True) + layer_eps)
    return center * inverse, inverse


def normal_back(grad_rows, normed, inverse):
    mean_grad = jnp.mean(grad_rows, axis=-1, keepdims=True)
    mean_proj = jnp.mean(grad_rows * normed, axis=-1, keepdims=True)
    return inverse * (grad_rows - mean_grad - normed * mean_proj)


def dot(left, right, dims=None):
    if dims is None:
        return jnp.dot(left, right, preferred_element_type=F32)
    return lax.dot_general(left, right, dims, preferred_element_type=F32)


def spans(total, width):
    return [(lo, min(lo + width, total)) for lo in range(0, total, width)]


def pack_rows(place_ref, piece_refs, latent, rows_out):
    gathered = jnp.concatenate([ref[latent] for ref in piece_refs], axis=0)
    slots = lax.broadcasted_iota(jnp.int32, (rows_out, gathered.shape[0]), 0)
    chosen = jnp.where(place_ref[latent] == slots, 1.0, 0.0).astype(BF)
    return dot(chosen, gathered)


def unpack_rows(slots_ref, latent, packed, out_refs):
    slots = slots_ref[latent]
    rows = lax.broadcasted_iota(jnp.int32, (slots.shape[0], packed.shape[0]), 1)
    spread = dot(jnp.where(slots == rows, 1.0, 0.0).astype(BF), packed).astype(BF)
    block = out_refs[0].shape[1]
    for k, out in enumerate(out_refs):
        out[latent] = spread[k * block : (k + 1) * block]


def home_kernel(at, rank, base, *refs):
    pieces, out = refs[:-1], refs[-1]
    group, slots, _ = pieces[0].shape
    for k, piece in enumerate(pieces):
        for j in range(group):
            latent = (at[0] ^ k) * group + j
            place = rank[latent]
            rows = lax.broadcasted_iota(jnp.int32, (place.shape[0], slots), 1)
            spread = dot(jnp.where(place == rows, 1.0, 0.0).astype(BF), piece[j])
            out[latent] = jnp.where(place >= 0, spread, base[latent].astype(F32)).astype(out.dtype)


def cut_kernel(first, top, bottom, top_out, bottom_out, top_held, bottom_held, load_sem, store_sem):
    rows = bottom.shape[0]
    loads = [
        pltpu.make_async_copy(top.at[pl.ds(0, first), :], top_held, load_sem.at[0]),
        pltpu.make_async_copy(bottom.at[pl.ds(first, rows - first), :], bottom_held, load_sem.at[1]),
    ]
    stores = [
        pltpu.make_async_copy(top_held, top_out, store_sem.at[0]),
        pltpu.make_async_copy(bottom_held, bottom_out, store_sem.at[1]),
    ]
    for one in loads:
        one.start()
    for load, store in zip(loads, stores):
        load.wait()
        store.start()
    wait_all(stores)


def split_parity(rows_low, order_ref, own_ref, other_ref):
    moved = dot(rows_low, order_ref[...]).astype(BF)
    width = own_ref.shape[1]
    own_ref[...] = moved[:, :width]
    other_ref[...] = moved[:, width:]


def enter_kernel(pieces, blocks, cap, *refs):
    (offsets, place, mod, order), refs = refs[:4], refs[4:]
    latents, refs = refs[:blocks], refs[blocks:]
    weights, refs = refs[:pieces], refs[pieces:]
    packed_out, qkv_out, own_out, other_out, weight, mixed, sem = refs
    width = qkv_out.shape[1]
    chunks = spans(width, width // 3)
    loads = [
        start_pieces(offsets, weights, weight, sem.at[i], lo, hi) for i, (lo, hi) in enumerate(chunks)
    ]
    for latent in range(mod.shape[0]):
        here = pl.ds(latent * cap, cap)
        rows = pack_rows(place, latents, latent, cap)
        packed_out[here, :] = rows.astype(BF)
        normed, _ = normal(rows)
        mixed[here, :] = (normed * (1.0 + mod[latent, 1:2, :]) + mod[latent, 0:1, :]).astype(BF)
    split_parity(mixed[...], order, own_out, other_out)
    for i, (lo, hi) in enumerate(chunks):
        wait_all(loads[i])
        qkv_out[:, lo:hi] = dot(mixed[...], weight[:, lo:hi]).astype(BF)


def cot_kernel(cap, place, mod, *refs):
    cots, (packed_out, mlp_out) = refs[:-2], refs[-2:]
    for latent in range(mod.shape[0]):
        here = pl.ds(latent * cap, cap)
        rows = pack_rows(place, cots, latent, cap)
        packed_out[here, :] = rows.astype(BF)
        mlp_out[here, :] = (mod[latent, 5:6, :] * rows).astype(BF)


def windows():
    found = []
    for head in range(HEADS):
        first = head * HEAD
        base = first // LANES * LANES
        width = LANES if first + HEAD <= base + LANES else 2 * LANES
        found.append((base, width, first - base))
    return found[::2] + found[1::2]


def head_mask(width, first, dtype):
    lane = lax.broadcasted_iota(jnp.int32, (1, width), 1)
    return jnp.where((lane >= first) & (lane < first + HEAD), 1.0, 0.0).astype(dtype)


def attend_kernel(pieces, cap, model, *refs):
    (offsets, live, qkv, packed, mod, order), refs = refs[:6], refs[6:]
    weights, refs = refs[:pieces], refs[pieces:]
    (own_att, other_att, proj_out, hidden_out, mixed_out, own_mix, other_mix), refs = (
        refs[:7],
        refs[7:],
    )
    weight, attended, sem = refs
    copies = start_pieces(offsets, weights, weight, sem, 3 * model, 4 * model)
    attended[...] = jnp.zeros_like(attended)

    def one_latent(latent, carry):
        here = pl.ds(pl.multiple_of(latent * cap, 16), cap)
        count = live[latent]
        seen = lax.broadcasted_iota(jnp.int32, (cap, cap), 1) < count
        for base, width, first in windows():
            low_mask = head_mask(width, first, BF)
            query = qkv[here, base : base + width] * low_mask
            key = qkv[here, model + base : model + base + width]
            value = qkv[here, 2 * model + base : 2 * model + base + width] * low_mask
            scores = jnp.where(seen, dot(query, key, NT), far_below)
            raised = jnp.exp2((scores - jnp.max(scores, axis=-1, keepdims=True)) * exp2_scale)
            share = 1.0 / jnp.sum(raised, axis=-1, keepdims=True)
            attended[here, base : base + width] += dot(raised.astype(BF), value) * share
        return carry

    lax.fori_loop(0, mod.shape[0], one_latent, 0)
    att_low = attended[...].astype(BF)
    split_parity(att_low, order, own_att, other_att)
    wait_all(copies)
    projected = dot(att_low, weight[...])
    proj_out[...] = projected
    for latent in range(mod.shape[0]):
        rows = slice(latent * cap, (latent + 1) * cap)
        hidden = packed[rows, :].astype(F32) + mod[latent, 2:3, :] * projected[rows]
        hidden_out[rows, :] = hidden
        normed, _ = normal(hidden)
        mixed_out[rows, :] = (
            normed * (1.0 + mod[latent, 4:5, :]) + mod[latent, 3:4, :]
        ).astype(BF)
    split_parity(mixed_out[...], order, own_mix, other_mix)


def unit_chunks(parity, half):
    found = []
    for side in (0, 1):
        base = (parity[0] ^ side) * half
        for lo, hi in spans(half, 768):
            found.append((side, lo, hi, pl.ds(pl.multiple_of(base + lo, LANES), hi - lo)))
    return found


def start_chunks(offsets, refs, target, sem, chunks):
    found = []
    for i, (_, _, _, cols) in enumerate(chunks):
        found.append(
            [
                pltpu.make_async_copy(
                    ref.at[:, cols],
                    target.at[pl.ds(pl.multiple_of(offsets[k], 16), ref.shape[0]), cols],
                    sem.at[i, k],
                )
                for k, ref in enumerate(refs)
            ]
        )
        for one in found[-1]:
            one.start()
    return found


def first_kernel(pieces, offsets, parity, mixed, bias, *refs):
    weights, refs = refs[:pieces], refs[pieces:]
    acts, slopes = refs[0:2], refs[2:4]
    weight, act, slope, load_sem, act_sem, slope_sem = refs[4:]
    half = acts[0].shape[1]
    chunks = unit_chunks(parity, half)
    loads = start_chunks(offsets, weights, weight, load_sem, chunks)
    stores = []
    for i, (side, lo, hi, cols) in enumerate(chunks):
        wait_all(loads[i])
        pre = dot(mixed[...], weight[:, cols]) + bias[:, cols]
        square = pre * pre
        curve = jnp.tanh(pre * (gelu_c + (gelu_c * gelu_k) * square))
        cdf = 0.5 + 0.5 * curve
        act[side, :, lo:hi] = (pre * cdf).astype(BF)
        bend = (0.5 * gelu_c) + (1.5 * gelu_c * gelu_k) * square
        slope[side, :, lo:hi] = (cdf + pre * bend * (1.0 - curve * curve)).astype(BF)
        here = pl.ds(lo, hi - lo)
        for held, out, sem in ((act, acts, act_sem), (slope, slopes, slope_sem)):
            stores.append(
                pltpu.make_async_copy(held.at[side, :, here], out[side].at[:, here], sem.at[i])
            )
            stores[-1].start()
    wait_all(stores)


def start_halves(offsets, refs, sides, target, sem):
    found = ([], [])
    for side in (0, 1):
        for k, ref in enumerate(refs):
            if sides[k] != side:
                continue
            rows = ref.shape[0]
            found[side].append(
                pltpu.make_async_copy(
                    ref, target.at[pl.ds(pl.multiple_of(offsets[k], 16), rows), :], sem.at[k]
                )
            )
            found[side][-1].start()
    return found


def slope_kernel(sides, *refs):
    (offsets, own_slope, other_slope, grad_mlp), refs = refs[:4], refs[4:]
    weights, refs = refs[: len(sides)], refs[len(sides) :]
    own_pre, other_pre, own_bias, other_bias, weight, pre, sem, out_sem = refs
    halves = start_halves(offsets, weights, sides, weight, sem)
    half = own_pre.shape[1]
    stores = []
    for side, (slope, pre_out, bias_out) in enumerate(
        ((own_slope, own_pre, own_bias), (other_slope, other_pre, other_bias))
    ):
        wait_all(halves[side])
        for lo, hi in spans(half, 768):
            grad_act = dot(grad_mlp[...], weight[side * half + lo : side * half + hi, :], NT)
            grad_pre = (grad_act * slope[:, lo:hi].astype(F32)).astype(BF)
            pre[side, :, lo:hi] = grad_pre
            here = pl.ds(lo, hi - lo)
            stores.append(
                pltpu.make_async_copy(
                    pre.at[side, :, here], pre_out.at[:, here], out_sem.at[len(stores)]
                )
            )
            stores[-1].start()
            bias_out[:, lo:hi] = jnp.sum(grad_pre.astype(F32), axis=0, keepdims=True)
    wait_all(stores)


def second_kernel(sides, blocks, cap, *refs):
    (offsets, own_act, other_act, grad_out, hidden, mod, slots), refs = refs[:7], refs[7:]
    weights, refs = refs[: len(sides)], refs[len(sides) :]
    onward, refs = refs[:4], refs[4:]
    outs, refs = refs[:blocks], refs[blocks:]
    (gate_grad, *onward_outs), refs = refs[:3], refs[3:]
    weight, sem = refs[:2]
    held, onward_sem = refs[2:6], refs[6]
    halves = start_halves(offsets, weights, sides, weight, sem)
    loads = start_onward(onward, held, onward_sem)
    half = own_act.shape[1]
    wait_all(halves[0])
    mlp = dot(own_act[...], weight[:half, :])
    wait_all(halves[1])
    mlp = mlp + dot(other_act[...], weight[half:, :])
    for latent in range(mod.shape[0]):
        rows = slice(latent * cap, (latent + 1) * cap)
        gate_grad[latent, :, :] = jnp.sum(
            grad_out[rows, :].astype(F32) * mlp[rows], axis=0, keepdims=True
        )
        block = (hidden[rows, :] + mod[latent, 5:6, :] * mlp[rows]).astype(BF)
        unpack_rows(slots, latent, block, outs)
    wait_all(end_onward(loads, held, onward_outs, onward_sem))


def hidden_kernel(pieces, first_pieces, cap, model, *refs):
    (first_at, offsets, parity, own_pre, other_pre, hidden_in, projected_in, grad_in, mod), refs = (
        refs[:9],
        refs[9:],
    )
    first_weights, refs = refs[:first_pieces], refs[first_pieces:]
    out_weights, refs = refs[:pieces], refs[pieces:]
    (grad_hidden_out, grad_proj_out, grad_att, mod_grads), refs = refs[:4], refs[4:]
    first, out_weight, hidden, projected, grad_out, grad_hidden, grad_proj = refs[:7]
    first_sem, out_sem, in_sem, store_sem = refs[7:]
    half = own_pre.shape[1]
    chunks = unit_chunks(parity, half)
    loads = start_chunks(first_at, first_weights, first, first_sem, chunks)
    later = [
        pltpu.make_async_copy(there, here, in_sem.at[i])
        for i, (there, here) in enumerate(
            ((hidden_in, hidden), (projected_in, projected), (grad_in, grad_out))
        )
    ]
    for one in later:
        one.start()
    last = start_pieces(offsets, out_weights, out_weight, out_sem, 3 * model, 4 * model)
    total = None
    for i, (side, lo, hi, cols) in enumerate(chunks):
        wait_all(loads[i])
        part = dot((own_pre, other_pre)[side][:, lo:hi], first[:, cols], NT)
        total = part if total is None else total + part
    wait_all(later)
    stores = []
    for latent in range(mod.shape[0]):
        rows = slice(latent * cap, (latent + 1) * cap)
        normed, inverse = normal(hidden[rows, :])
        grad_mixed = total[rows]
        mod_grads[latent, 0:1, :] = jnp.sum(grad_mixed, axis=0, keepdims=True)
        mod_grads[latent, 1:2, :] = jnp.sum(grad_mixed * normed, axis=0, keepdims=True)
        grad = grad_out[rows, :].astype(F32) + normal_back(
            grad_mixed * (1.0 + mod[latent, 4:5, :]), normed, inverse
        )
        grad_hidden[rows, :] = grad
        mod_grads[latent, 2:3, :] = jnp.sum(grad * projected[rows, :], axis=0, keepdims=True)
        grad_proj[rows, :] = (mod[latent, 2:3, :] * grad).astype(BF)
        here = pl.ds(latent * cap, cap)
        for held, out in ((grad_hidden, grad_hidden_out), (grad_proj, grad_proj_out)):
            stores.append(
                pltpu.make_async_copy(
                    held.at[here, :], out.at[here, :], store_sem.at[len(stores)]
                )
            )
            stores[-1].start()
    wait_all(last)
    grad_att[...] = dot(grad_proj[...], out_weight[...], NT).astype(BF)
    wait_all(stores)


def start_onward(ins, held, sem):
    loads = [pltpu.make_async_copy(a, b, sem.at[i]) for i, (a, b) in enumerate(zip(ins, held))]
    for one in loads:
        one.start()
    return loads


def end_onward(loads, held, outs, sem):
    keep_x, keep_y, far_x, far_y = held
    wait_all(loads)
    keep_x[...] = (keep_x[...].astype(F32) + far_y[...].astype(F32)).astype(BF)
    keep_y[...] = (keep_y[...].astype(F32) + far_x[...].astype(F32)).astype(BF)
    stores = [
        pltpu.make_async_copy(a, b, sem.at[4 + i]) for i, (a, b) in enumerate(zip(held[:2], outs))
    ]
    for one in stores:
        one.start()
    return stores


def attend_back_kernel(cap, model, *refs):
    (live, qkv, grad_att), onward, (grad_qkv, *onward_outs) = refs[:3], refs[3:7], refs[7:10]
    sums, held, onward_sem = refs[10], refs[11:15], refs[15]
    loads = start_onward(onward, held, onward_sem)
    sums[...] = jnp.zeros_like(sums)

    def one_latent(latent, carry):
        here = pl.ds(pl.multiple_of(latent * cap, 16), cap)
        count = live[latent]
        seen = lax.broadcasted_iota(jnp.int32, (cap, cap), 0) < count
        found = windows()
        for some in range(0, len(found), 4):
            heads = []
            for base, width, first in found[some : some + 4]:
                mask = head_mask(width, first, BF)
                cols = [slice(part + base, part + base + width) for part in (0, model, 2 * model)]
                query, key = qkv[here, cols[0]] * mask, qkv[here, cols[1]] * mask
                grad = grad_att[here, cols[0]] * mask
                heads.append(
                    (cols, query, key, grad, dot(key, query, NT), dot(qkv[here, cols[2]], grad, NT))
                )
            weights = []
            for _, _, _, _, scores, grad_probs in heads:
                scores = jnp.where(seen, scores, far_below)
                raised = jnp.exp2((scores - jnp.max(scores, axis=0, keepdims=True)) * exp2_scale)
                probs = raised * (1.0 / jnp.sum(raised, axis=0, keepdims=True))
                delta = jnp.sum(probs * grad_probs, axis=0, keepdims=True)
                weights.append(((probs * (grad_probs - delta)).astype(BF), probs.astype(BF)))
            for (cols, query, key, grad, _, _), (grad_scores, probs) in zip(heads, weights):
                sums[here, cols[0]] += dot(grad_scores, key, TN)
                sums[here, cols[1]] += dot(grad_scores, query)
                sums[here, cols[2]] += dot(probs, grad)
        return carry

    lax.fori_loop(0, live.shape[0], one_latent, 0)
    stores = end_onward(loads, held, onward_outs, onward_sem)
    grad_qkv[:, : 2 * model] = (sums[:, : 2 * model] * att_scale).astype(BF)
    grad_qkv[:, 2 * model :] = sums[:, 2 * model :].astype(BF)
    wait_all(stores)


def leave_kernel(pieces, blocks, cap, *refs):
    (
        offsets,
        parity,
        live,
        grad_qkv,
        packed,
        grad_hidden,
        mod,
        slots,
        mod_grads,
        gate_m,
        own_bias,
        other_bias,
    ), refs = refs[:12], refs[12:]
    weights, refs = refs[:pieces], refs[pieces:]
    outs, refs = refs[:blocks], refs[blocks:]
    payload, weight, rows_wide, sem = refs
    model = packed.shape[1]
    group, half = mod.shape[0], own_bias.shape[1]
    rows_wide[...] = jnp.zeros_like(rows_wide)
    lane = lax.broadcasted_iota(jnp.int32, (1, LANES), 1)
    kept = jnp.zeros((1, LANES), F32)
    for latent in range(group):
        at = slice(latent, latent + 1)
        rows_wide[at, 2 * model : 3 * model] = mod_grads[latent, 2:3, :]
        rows_wide[at, 3 * model : 4 * model] = mod_grads[latent, 0:1, :]
        rows_wide[at, 4 * model : 5 * model] = mod_grads[latent, 1:2, :]
        rows_wide[at, 5 * model :] = gate_m[latent]
        kept = jnp.where(lane == latent, live[latent].astype(F32), kept)
    for side, bias in enumerate((own_bias, other_bias)):
        first = pl.multiple_of((parity[0] ^ side) * half, LANES)
        rows_wide[group : group + 1, pl.ds(first, half)] = bias[...]
    rows_wide[group : group + 1, 2 * half : 2 * half + LANES] = kept
    chunks = spans(weight.shape[1], model)
    loads = [
        start_pieces(offsets, weights, weight, sem.at[i], lo, hi) for i, (lo, hi) in enumerate(chunks)
    ]
    total = None
    for i, (lo, hi) in enumerate(chunks):
        wait_all(loads[i])
        part = dot(grad_qkv[:, lo:hi], weight[:, lo:hi], NT)
        total = part if total is None else total + part
    for latent in range(mod.shape[0]):
        rows = slice(latent * cap, (latent + 1) * cap)
        normed, inverse = normal(packed[rows, :].astype(F32))
        grad_mixed = total[rows]
        at = slice(latent, latent + 1)
        rows_wide[at, :model] = jnp.sum(grad_mixed, axis=0, keepdims=True)
        rows_wide[at, model : 2 * model] = jnp.sum(grad_mixed * normed, axis=0, keepdims=True)
        grad = grad_hidden[rows, :] + normal_back(
            grad_mixed * (1.0 + mod[latent, 1:2, :]), normed, inverse
        )
        unpack_rows(slots, latent, grad.astype(BF), outs)
    payload[...] = rows_wide[: group + 1, :].astype(BF)


def spread_kernel(corners, *refs):
    own, pair = refs[:corners], refs[corners : 2 * corners]
    (at, weight), refs = refs[2 * corners : 2 * corners + 2], refs[2 * corners + 2 :]
    cond_own, cond_pair, sent, kept, across, sums, rows, parts, sem = refs
    group = own[0].shape[0] - 1
    totals = []
    for q in range(corners):
        mine, theirs = own[q][...].astype(F32), pair[q][...].astype(F32)
        for side, wide in enumerate((mine, theirs)):
            first = (side * corners + q) * group
            rows[first : first + group, :] = wide[:group]
        totals.append(
            [
                sum(wide[latent : latent + 1] for latent in range(group))
                for wide in (mine, theirs)
            ]
            + [wide[group:] for wide in (mine, theirs)]
        )
    for i in range(2):
        by_corner = [one[2 * i] + one[2 * i + 1] for one in totals]
        while len(by_corner) > 1:
            by_corner = [a + b for a, b in zip(by_corner[::2], by_corner[1::2])]
        sums[i : i + 1, :] = by_corner[0]
    low = rows[...].astype(BF)
    cond = dot(low, weight[...], NT)
    half = corners * group
    cond_own[...] = cond[:half]
    cond_pair[...] = cond[half:]
    count, _, width = parts.shape
    for j in range(count):
        parts[j] = low[:, j * width : (j + 1) * width]
    copies = [
        pltpu.make_async_copy(parts.at[at[0] ^ k], out, sem.at[k])
        for k, out in ((1, sent.at[0]), (3, sent.at[1]), (0, kept), (2, across))
    ]
    for one in copies:
        one.start()
    wait_all(copies)


def outer_kernel(rows, used, sides, *refs):
    block_at, refs = refs[0], refs[1:]
    total = sum(sides)
    lefts, refs = refs[: 2 * len(sides)], refs[2 * len(sides) :]
    rights, refs = refs[: 2 * total], refs[2 * total :]
    (far_x, far_y, near_x, near_y, keep, keep_x, keep_y), refs = refs[:7], refs[7:]
    result, sem = refs
    part, rest = halves_of(rows)
    base, at = 0, 0
    for group, count in enumerate(sides):
        own_left, pair_left = lefts[2 * group : 2 * group + 2]
        left = jnp.concatenate([own_left[:, :used], pair_left[:, :used]], axis=0)
        for own, pair in zip(rights[2 * at : 2 * (at + count) : 2], rights[2 * at + 1 : 2 * (at + count) : 2]):
            width = own.shape[1]
            for lo, hi in spans(width, 768):
                right = jnp.concatenate([own[:, lo:hi], pair[:, lo:hi]], axis=0)
                result[:, base + lo : base + hi] = dot(left, right, TN).astype(BF)
            base += width
        at += count

    def rows_at(k, first, count):
        return result.at[pl.ds(pl.multiple_of(block_at[k] * rows + first, 16), count), :]

    moves = [
        (rows_at(3, 0, part), far_x),
        (rows_at(3, part, rest), far_y),
        (rows_at(1, 0, part), near_x),
        (rows_at(2, part, rest), near_y),
        (rows_at(0, 0, rows), keep),
        (rows_at(1, part, rest), keep_x),
        (rows_at(2, 0, part), keep_y),
    ]
    copies = [pltpu.make_async_copy(a, b, sem.at[i]) for i, (a, b) in enumerate(moves)]
    for one in copies:
        one.start()
    wait_all(copies)


def reorder_kernel(unit, shard, whole):
    count = shard.shape[1] // unit
    for block in range(count):
        to = (block % 2) * (count // 2) + block // 2
        whole[:, to * unit : (to + 1) * unit] = shard[:, block * unit : (block + 1) * unit]


def fold_kernel(cuts, turned, *refs):
    (at, keep, near_top, near_bottom, far_top, far_bottom), refs = refs[:6], refs[6:]
    count = len(cuts[0])
    outs, refs = refs[: 3 * len(cuts)], refs[3 * len(cuts) :]
    scratch, sem = refs[:-1], refs[-1]
    part = far_top.shape[0]
    wide = lambda ref: ref[...].astype(F32)
    top = keep[:part, :].astype(F32) + wide(near_top) + wide(far_top)
    bottom = keep[part:, :].astype(F32) + wide(near_bottom) + wide(far_bottom)
    copies = []
    top, bottom = top.astype(BF), bottom.astype(BF)
    if turned:
        top, bottom = top.T, bottom.T
    for i, (group, parts) in enumerate(zip(cuts, scratch)):
        for j, pieces in enumerate(group):
            first = 0
            for lo, hi in pieces:
                if turned:
                    parts[j, :, :part] = top[lo:hi, :]
                    parts[j, :, part:] = bottom[lo:hi, :]
                    continue
                parts[j, :part, first : first + hi - lo] = top[:, lo:hi]
                parts[j, part:, first : first + hi - lo] = bottom[:, lo:hi]
                first += hi - lo
        sent, own, across = outs[3 * i : 3 * i + 3]
        for k, out in ((1, sent.at[0]), (3, sent.at[1]), (0, own), (2, across)):
            copies.append(pltpu.make_async_copy(parts.at[at[0] ^ k], out, sem.at[len(copies)]))
    for one in copies:
        one.start()
    wait_all(copies)


def outer_pair(groups, rows, name):
    used = 4 * rows
    part, rest = halves_of(rows)
    lefts = [v for left, _ in groups for v in left]
    rights = [v for _, pairs in groups for pair in pairs for v in pair]
    width = sum(v.shape[1] for v in rights) // 2
    sides = tuple(len(pairs) for _, pairs in groups)
    block_at = jnp.stack([(lax.axis_index("dp") ^ (2 * k)) // 2 for k in range(4)]).astype(jnp.int32)
    ins = [block_at, *lefts, *rights]
    outs = (
        jax.ShapeDtypeStruct((part, width), BF),
        jax.ShapeDtypeStruct((rest, width), BF),
        jax.ShapeDtypeStruct((part, width), BF),
        jax.ShapeDtypeStruct((rest, width), BF),
        jax.ShapeDtypeStruct((rows, width), BF),
        jax.ShapeDtypeStruct((rest, width), BF),
        jax.ShapeDtypeStruct((part, width), BF),
    )
    return pl.pallas_call(
        functools.partial(outer_kernel, rows, used, sides),
        out_shape=outs,
        in_specs=[SMEM] + [VMEM] * (len(ins) - 1),
        out_specs=tuple(ANY for _ in outs),
        scratch_shapes=[pltpu.VMEM((used, width), BF), pltpu.SemaphoreType.DMA((7,))],
        name=name,
        compiler_params=pltpu.CompilerParams(vmem_limit_bytes=60 * 1024 * 1024),
    )(*ins)


def onward_kernel(keep_x, keep_y, far_x, far_y, on_x, on_y):
    on_x[...] = (keep_x[...].astype(F32) + far_y[...].astype(F32)).astype(BF)
    on_y[...] = (keep_y[...].astype(F32) + far_x[...].astype(F32)).astype(BF)


def onward(cut, far):
    keep_x, keep_y = cut[5:]
    outs = tuple(jax.ShapeDtypeStruct(v.shape, BF) for v in (keep_x, keep_y))
    ins = [keep_x, keep_y, *far]
    return call(onward_kernel, outs, ins, [VMEM] * 4, [], "onward")


def along_xy(pair):
    return swap(pair[0], "dp", 2), swap(pair[1], "dp", 4)


def fold(keep, near, last, cuts, name, turned=False):
    rows = keep.shape[0]
    count = lax.axis_size("seq")
    at = lax.axis_index("seq").reshape(1).astype(jnp.int32)
    widths = tuple(sum(hi - lo for lo, hi in group[0]) for group in cuts)
    blocks = [(w, rows) if turned else (rows, w) for w in widths]
    outs = tuple(
        jax.ShapeDtypeStruct(shape, BF) for block in blocks for shape in ((2,) + block, block, block)
    )
    return pl.pallas_call(
        functools.partial(fold_kernel, cuts, turned),
        out_shape=outs,
        in_specs=[SMEM] + [VMEM] * 5,
        out_specs=tuple(ANY for _ in outs),
        scratch_shapes=[pltpu.VMEM((count,) + block, BF) for block in blocks]
        + [pltpu.SemaphoreType.DMA((4 * len(cuts),))],
        name=name,
        compiler_params=pltpu.CompilerParams(vmem_limit_bytes=60 * 1024 * 1024),
    )(at, keep, near[0], near[1], last[1], last[0])


def plain_cuts(first, width, count):
    share = width // count
    return tuple(((first + j * share, first + (j + 1) * share),) for j in range(count))


def spread_plain(grad):
    grad = lax.psum_scatter(grad, "dp", scatter_dimension=0, tiled=True)
    return lax.psum_scatter(grad, "seq", scatter_dimension=1, tiled=True)


def body(
    latents,
    condition,
    keep_order,
    keep_count,
    ada_weight,
    ada_bias,
    qkv_weight,
    out_weight,
    fc1_weight,
    fc1_bias,
    fc2_weight,
    cotangent,
):
    latent_count, block_rows, model = latents.shape
    hidden_units = fc1_weight.shape[1]
    half_units = hidden_units // 2
    unit_rows = hidden_units // BLOCKS
    model_rows = model // BLOCKS
    dp_count, seq_count = lax.axis_size("dp"), lax.axis_size("seq")
    dp_at, seq_at = lax.axis_index("dp"), lax.axis_index("seq")
    group = latent_count // seq_count
    most = block_rows * 3 // 4
    cap = (seq_count - 1) * most + block_rows // 4
    rows_all = group * cap
    share = model // dp_count
    column_share = 6 * model // seq_count
    paired = dp_count == BLOCKS and seq_count == 4
    parity = (dp_at & 1) if paired else jnp.zeros_like(dp_at)
    parity_in = parity.reshape(1).astype(jnp.int32)
    part, _ = halves_of(model_rows)
    unit_part, _ = halves_of(unit_rows)
    whose = (lambda k: dp_at ^ k) if paired else (lambda k: jnp.int32(k))
    sds = jax.ShapeDtypeStruct
    dma = lambda n: pltpu.SemaphoreType.DMA((n,))
    fence = lambda *values: lax.optimization_barrier(values)

    def rank_of():
        slot = lax.broadcasted_iota(jnp.int32, (1, block_rows, 1), 1)
        token = lax.broadcasted_iota(jnp.int32, (1, 1, block_rows), 2)
        found = (keep_order[:, :, None] == token) & (slot < keep_count[:, :, None])
        return jnp.max(jnp.where(found, slot, -1), axis=1)

    def places_of(ranks):
        ranks = lax.dynamic_slice_in_dim(ranks, seq_at * group, group, 1)
        ranks = jnp.swapaxes(ranks, 0, 1)
        counts = jnp.sum((ranks >= 0).astype(jnp.int32), axis=2)
        starts = jnp.cumsum(counts, axis=1) - counts
        live = jnp.sum(counts, axis=1).astype(jnp.int32)
        place = jnp.where(ranks >= 0, ranks + starts[:, :, None], -1).reshape(
            group, seq_count * block_rows
        )
        slot = lax.broadcasted_iota(jnp.int32, (1, 1, most), 2)
        slots = jnp.where(slot < counts[:, :, None], starts[:, :, None] + slot, -1)
        return live, place[:, None, :], slots.reshape(group, seq_count * most, 1)

    def whole_slice(blocks_in, k):
        return lax.dynamic_slice_in_dim(blocks_in, (seq_at ^ k) * group, group, 0)

    rank = rank_of()

    def run_home(pieces, base, dtype, name):
        return call(
            home_kernel,
            sds((latent_count, block_rows, model), dtype),
            [seq_at.reshape(1).astype(jnp.int32), rank[:, :, None], base, *pieces],
            [SMEM] + [VMEM] * (2 + seq_count),
            [],
            name,
        )

    cond_wide = condition.astype(F32)
    silu_cond = jax.nn.silu(cond_wide).astype(BF)
    silu_parts = in_order(
        jnp.swapaxes(silu_cond.reshape(latent_count, dp_count, share), 0, 1), "dp"
    )

    def silu_of(rows):
        mine = lax.dynamic_slice_in_dim(rows, seq_at * group, group, 1)
        groups = rows.reshape(dp_count, seq_count, group, share)
        return mine, in_order(jnp.swapaxes(groups, 0, 1), "seq")


    def partial_mod(silu_rows):
        return jnp.dot(
            silu_rows.reshape(dp_count * group, share), ada_weight, preferred_element_type=F32
        ).reshape(dp_count, group, 6 * model)

    def whole_mod(total):
        return (total + ada_bias.astype(F32)).reshape(group, 6, model)

    unit_order = lambda v: jnp.swapaxes(
        v.reshape(v.shape[0], BLOCKS // 2, 2, unit_rows), 1, 2
    ).reshape(v.shape[0], hidden_units)
    bias_row = unit_order(fc1_bias.astype(F32)[None])

    pad = -(-(model // 2) // LANES) * LANES

    def order_of(parity):
        column = lax.broadcasted_iota(jnp.int32, (1, 2 * pad), 1)
        side, inner = column // pad, column % pad
        source = (2 * (inner // model_rows) + (parity ^ side)) * model_rows + inner % model_rows
        source = jnp.where(inner < model // 2, source, -1)
        return (lax.broadcasted_iota(jnp.int32, (model, 1), 0) == source).astype(BF)

    model_position = lambda k: whose(k)
    unit_position = lambda k: ((whose(k) & 1) ^ parity) * (BLOCKS // 2) + whose(k) // 2

    def run_enter(joint, place_row, mod, pieces, order):
        weights, offsets = joint
        return call(
            functools.partial(enter_kernel, len(weights), seq_count, cap),
            (
                sds((rows_all, model), BF),
                sds((rows_all, 3 * model), BF),
                sds((rows_all, pad), BF),
                sds((rows_all, pad), BF),
            ),
            [
                offsets,
                place_row,
                mod,
                order,
                *pieces,
                *weights,
            ],
            [SMEM, VMEM, VMEM, VMEM] + [VMEM] * seq_count + [ANY] * len(weights),
            [
                pltpu.VMEM((model, 3 * model), BF),
                pltpu.VMEM((rows_all, model), BF),
                pltpu.SemaphoreType.DMA((3, len(weights))),
            ],
            "enter",
        )

    def run_cot(place_row, mod, cot_pieces):
        low = sds((rows_all, model), BF)
        ins = [place_row, mod, *cot_pieces]
        return call(functools.partial(cot_kernel, cap), (low, low), ins, [VMEM] * len(ins), [], "cotangent")

    def run_attend(joint, live, qkv, packed, mod, order):
        weights, offsets = joint
        return call(
            functools.partial(attend_kernel, len(weights), cap, model),
            (
                sds((rows_all, pad), BF),
                sds((rows_all, pad), BF),
                sds((rows_all, model), F32),
                sds((rows_all, model), F32),
                sds((rows_all, model), BF),
                sds((rows_all, pad), BF),
                sds((rows_all, pad), BF),
            ),
            [
                offsets,
                live,
                qkv,
                packed,
                mod,
                order,
                *weights,
            ],
            [SMEM, SMEM, VMEM, VMEM, VMEM, VMEM] + [ANY] * len(weights),
            [
                pltpu.VMEM((model, model), BF),
                pltpu.VMEM((rows_all, model), F32),
                dma(len(weights)),
            ],
            "attend",
        )

    def run_first(first, mixed):
        weights, offsets = first
        half_rows = sds((rows_all, half_units), BF)
        chunks = 2 * len(spans(half_units, 768))
        return call(
            functools.partial(first_kernel, len(weights)),
            (half_rows,) * 4,
            [offsets, parity_in, mixed, bias_row, *weights],
            [SMEM, SMEM, VMEM, VMEM] + [ANY] * len(weights),
            [
                pltpu.VMEM((model, hidden_units), BF),
                pltpu.VMEM((2, rows_all, half_units), BF),
                pltpu.VMEM((2, rows_all, half_units), BF),
                pltpu.SemaphoreType.DMA((chunks, len(weights))),
                dma(chunks),
                dma(chunks),
            ],
            "first",
            (ANY,) * 4,
        )

    def run_slope(second, slopes, grad_mlp):
        weights, offsets, sides = second
        half_rows = sds((rows_all, half_units), BF)
        return call(
            functools.partial(slope_kernel, sides),
            (half_rows, half_rows, sds((1, half_units), F32), sds((1, half_units), F32)),
            [offsets, *slopes, grad_mlp, *weights],
            [SMEM] + [VMEM] * 3 + [ANY] * len(weights),
            [
                pltpu.VMEM((hidden_units, model), BF),
                pltpu.VMEM((2, rows_all, half_units), BF),
                dma(len(weights)),
                dma(2 * len(spans(half_units, 768))),
            ],
            "slope",
            (ANY, ANY, VMEM, VMEM),
        )

    def onward_parts(cut, far):
        ins = [cut[5], cut[6], *far]
        return (
            ins,
            tuple(sds(v.shape, BF) for v in ins[:2]),
            [pltpu.VMEM(v.shape, BF) for v in ins] + [dma(6)],
        )

    def run_second(second, acts, grad_out, hidden, mod, slots, cut, far):
        weights, offsets, sides = second
        ins, outs, scratch = onward_parts(cut, far)
        result = call(
            functools.partial(second_kernel, sides, seq_count, cap),
            tuple(sds((group, most, model), BF) for _ in range(seq_count))
            + (sds((group, 1, model), F32),)
            + outs,
            [offsets, *acts, grad_out, hidden, mod, slots, *weights, *ins],
            [SMEM] + [VMEM] * 6 + [ANY] * (len(weights) + 4),
            [pltpu.VMEM((hidden_units, model), BF), dma(len(weights))] + scratch,
            "second",
            (VMEM,) * (seq_count + 1) + (ANY, ANY),
        )
        return result[:seq_count], result[seq_count], result[seq_count + 1 :]

    def run_hidden(first, joint, pres, hidden, projected, grad_out, mod):
        (weights, offsets), (first_w, first_at) = joint, first
        wide, low = sds((rows_all, model), F32), sds((rows_all, model), BF)
        return call(
            functools.partial(hidden_kernel, len(weights), len(first_w), cap, model),
            (wide, low, low, sds((group, 3, model), F32)),
            [
                first_at,
                offsets,
                parity_in,
                *pres,
                hidden,
                projected,
                grad_out,
                mod,
                *first_w,
                *weights,
            ],
            [SMEM, SMEM, SMEM, VMEM, VMEM, ANY, ANY, ANY, VMEM]
            + [ANY] * (len(first_w) + len(weights)),
            [
                pltpu.VMEM((model, hidden_units), BF),
                pltpu.VMEM((model, model), BF),
                pltpu.VMEM((rows_all, model), F32),
                pltpu.VMEM((rows_all, model), F32),
                pltpu.VMEM((rows_all, model), BF),
                pltpu.VMEM((rows_all, model), F32),
                pltpu.VMEM((rows_all, model), BF),
                pltpu.SemaphoreType.DMA((2 * len(spans(half_units, 768)), len(first_w))),
                dma(len(weights)),
                dma(3),
                dma(2 * group),
            ],
            "hidden_back",
            (ANY, ANY, VMEM, VMEM),
        )

    def run_attend_back(live, qkv, grad_att, cut, far):
        ins, outs, scratch = onward_parts(cut, far)
        grad_qkv, *on = call(
            functools.partial(attend_back_kernel, cap, model),
            (sds((rows_all, 3 * model), BF),) + outs,
            [live, qkv, grad_att, *ins],
            [SMEM, VMEM, VMEM] + [ANY] * 4,
            [pltpu.VMEM((rows_all, 3 * model), F32)] + scratch,
            "attend_back",
            (VMEM, ANY, ANY),
        )
        return grad_qkv, on

    def run_leave(
        joint, grad_qkv, packed, grad_hidden, mod, slots, live, mod_grads, gate_m, biases
    ):
        weights, offsets = joint
        result = call(
            functools.partial(leave_kernel, len(weights), seq_count, cap),
            tuple(sds((group, most, model), BF) for _ in range(seq_count))
            + (sds((group + 1, 6 * model), BF),),
            [
                offsets,
                parity_in,
                live,
                grad_qkv,
                packed,
                grad_hidden,
                mod,
                slots,
                mod_grads,
                gate_m,
                *biases,
                *weights,
            ],
            [SMEM, SMEM, SMEM] + [VMEM] * 9 + [ANY] * len(weights),
            [
                pltpu.VMEM((model, 3 * model), BF),
                pltpu.VMEM((8, 6 * model), F32),
                pltpu.SemaphoreType.DMA((3, len(weights))),
            ],
            "leave",
        )
        return result[:seq_count], result[seq_count]

    def split_sums(sums):
        units = jnp.swapaxes(
            sums[1, :hidden_units].reshape(2, BLOCKS // 2, unit_rows), 0, 1
        ).reshape(hidden_units)
        kept = jnp.sum(sums[1, hidden_units : hidden_units + group])
        return sums[0], units, kept.reshape(1).astype(jnp.int32)

    def sums_of(gathered):
        wide = gathered.astype(F32)
        total = jnp.stack([jnp.sum(wide[:, :group], axis=1), wide[:, group]], axis=1)
        while total.shape[0] > 1:
            total = total.reshape((total.shape[0] // 2, 2) + total.shape[1:])
            total = total[:, 0] + total[:, 1]
        return total[0]

    def by_columns(grad_mod_all):
        return in_order(
            jnp.stack(
                [
                    grad_mod_all[:, :, j * column_share : (j + 1) * column_share]
                    for j in range(seq_count)
                ]
            ),
            "seq",
        )

    def cond_product(grad_mod_all):
        return dot(grad_mod_all.reshape(dp_count * group, 6 * model), ada_weight, NT).reshape(
            dp_count, group, share
        )

    def ada_product(silu_all, columns):
        return dot(
            silu_all.reshape(seq_count * dp_count * group, share),
            columns.reshape(seq_count * dp_count * group, column_share),
            TN,
        )

    def cond_end(rows):
        rows = in_order(rows, "seq").reshape(latent_count, model)
        _, silu_back = jax.vjp(jax.nn.silu, cond_wide)
        return silu_back(rows)[0]

    def cond_mine_of(cols):
        return jnp.swapaxes(in_order(cols, "dp"), 0, 1).reshape(group, model)

    if not paired:
        order = order_of(parity)
        live, place_row, slots = places_of(gather_all(rank, "seq"))
        silu_rows, silu_all = silu_of(trade_all(silu_parts, "dp"))
        mod = whole_mod(sum_own(partial_mod(silu_rows), "dp"))
        to_whole = lambda v: [
            swap(whole_slice(v, k), "seq", k) if k else whole_slice(v, k)
            for k in range(seq_count)
        ]
        latent_pieces, cot_pieces = to_whole(latents), to_whole(cotangent)
        joint = whole_weight(jnp.concatenate([qkv_weight, out_weight], axis=1))
        joint = [joint], jnp.zeros((1,), jnp.int32)
        first = [whole_weight(unit_order(fc1_weight))], jnp.zeros((1,), jnp.int32)
        full = whole_weight(fc2_weight)
        second = placed(
            [(full[k * unit_rows : (k + 1) * unit_rows], k, 0) for k in range(BLOCKS)],
            unit_position,
            unit_rows,
        ) + (tuple(k & 1 for k in range(BLOCKS)),)
        packed, qkv, *mixa = run_enter(joint, place_row, mod, latent_pieces, order)
        grad_out, grad_mlp = run_cot(place_row, mod, cot_pieces)
        att_own, att_other, projected, hidden, mixed, *mixm = run_attend(
            joint, live, qkv, packed, mod, order
        )
        acts = run_first(first, mixed)
        *pres, bias_own, bias_other = run_slope(second, acts[2:], grad_mlp)
        none = [jnp.zeros((16, LANES), BF)] * 7
        block_pieces, gate_m_grad, _ = run_second(
            second, acts[:2], grad_out, hidden, mod, slots, none, none[:2]
        )
        grad_hidden, grad_proj, grad_att, mod_grads = run_hidden(
            first, joint, pres, hidden, projected, grad_out, mod
        )
        grad_qkv, _ = run_attend_back(live, qkv, grad_att, none, none[:2])
        latent_grads, payload = run_leave(
            joint,
            grad_qkv,
            packed,
            grad_hidden,
            mod,
            slots,
            live,
            mod_grads,
            gate_m_grad,
            (bias_own, bias_other),
        )
        gathered = gather_all(payload, "dp")
        grad_mod_all = gathered[:, :group]
        sums = sums_of(gathered)
        for step in steps_of("seq"):
            sums = sums + swap(sums, "seq", step)
        ada_bias_grad, fc1_bias_grad, kept_total = split_sums(sums)
        ada_grad = ada_product(silu_all, trade_all(by_columns(grad_mod_all), "seq"))
        cond_cols = trade_all(cond_product(grad_mod_all), "dp")
        condition_grad = cond_end(gather_all(cond_mine_of(cond_cols), "seq"))

        def mixed_sides(own, other, width):
            both = jnp.stack([own[:, : 4 * width], other[:, : 4 * width]], axis=1)
            return jnp.swapaxes(both.reshape(rows_all, 2, 4, width), 1, 2).reshape(
                rows_all, BLOCKS * width
            )

        product = lambda a, b: spread_plain(dot(a, b, TN))
        fc2_grad = product(mixed_sides(acts[0], acts[1], unit_rows), grad_mlp)
        fc1_grad = product(
            mixed_sides(*mixm, model_rows), mixed_sides(pres[0], pres[1], unit_rows)
        )
        out_grad = product(mixed_sides(att_own, att_other, model_rows), grad_proj)
        qkv_grad = product(mixed_sides(*mixa, model_rows), grad_qkv)
        home = lambda pieces: [swap(v, "seq", k) if k else v for k, v in enumerate(pieces)]
        block_out = run_home(home(block_pieces), latents, BF, "home_out")
        latents_grad = run_home(home(latent_grads), cotangent, F32, "home_grad")
        return (
            block_out,
            latents_grad,
            condition_grad,
            ada_grad,
            ada_bias_grad,
            qkv_grad,
            out_grad,
            fc1_grad,
            fc1_bias_grad,
            fc2_grad,
            kept_total,
        )

    def trade(value, axis, step):
        split = value.reshape((-1, 2, step) + value.shape[1:])
        return jnp.stack([split[:, 0], swap(split[:, 1], axis, step)], axis=1).reshape(value.shape)

    def grow(value, axis, step):
        return jnp.concatenate([value, swap(value, axis, step)], axis=0)

    def columns_first(parts):
        sent, own, across = parts
        return swap(sent, "seq", 1), own, across

    def columns_second(state):
        near, own, across = state
        on = (across.astype(F32) + near[1].astype(F32)).astype(BF)
        return swap(on, "seq", 2), own, near

    def columns_sum(state):
        far, own, near = state
        return own.astype(F32) + near[0].astype(F32) + far.astype(F32)

    def tails(beside, first):
        rows, width = beside[0].shape
        return call(
            functools.partial(cut_kernel, first),
            (sds((first, width), BF), sds((rows - first, width), BF)),
            [beside[1], beside[0]],
            [ANY, ANY],
            [pltpu.VMEM((first, width), BF), pltpu.VMEM((rows - first, width), BF), dma(2), dma(2)],
            "cut",
            (ANY, ANY),
        )

    joint_own = jnp.concatenate([qkv_weight, out_weight], axis=1)

    corners_of = lambda value: [swap(value[q], "dp", 2 * q) for q in (1, 2, 3)]

    corners = silu_parts.reshape(4, 2, latent_count, share)
    corners = jnp.stack([corners[0], *corners_of(corners)])
    ranks = grow(rank[None], "seq", 1)
    corners, joint_own, fc1_in, latents_in, cot_in, ranks, parity_late = fence(
        corners, joint_own, fc1_weight, latents, cotangent, ranks, parity
    )

    joint_beside = beside_of(joint_own)
    ranks = grow(ranks, "seq", 2)
    latent_pieces = [whole_slice(latents_in, k) for k in range(seq_count)]
    latent_1 = swap(latent_pieces[1], "seq", 1)
    latent_2 = swap(latent_pieces[2], "seq", 2)
    latent_3 = swap(latent_pieces[3], "seq", 3)
    silu_corners = trade(corners.reshape(8, latent_count, share), "dp", 1)
    silu_rows, silu_all = silu_of(silu_corners)
    silu_all = jnp.swapaxes(silu_all.reshape(seq_count, 4, 2, group, share), 1, 2)
    pairs = partial_mod(silu_rows).reshape(4, 2, group, 6 * model)
    corners = pairs[:, 0] + swap(pairs[:, 1], "dp", 1)
    parity_late, fc1_in, cot_in = after((parity_late, fc1_in, cot_in), corners)
    order = order_of(parity_late)
    first_own = call(
        functools.partial(reorder_kernel, unit_rows),
        sds(fc1_in.shape, BF),
        [fc1_in],
        [VMEM],
        [],
        "reorder",
    )
    cot_pieces = [whole_slice(cot_in, k) for k in range(seq_count)]
    (
        joint_beside,
        latent_1,
        latent_2,
        latent_3,
        silu_all,
        corners,
        joint_own,
        order,
        first_own,
        cot_pieces,
        ranks,
    ) = fence(
        joint_beside,
        latent_1,
        latent_2,
        latent_3,
        silu_all,
        corners,
        joint_own,
        order,
        first_own,
        cot_pieces,
        ranks,
    )

    sums = corners_of(corners)
    joint_tails = tails(joint_beside, part)
    sums, joint_tails, joint_beside, joint_own, ranks = fence(
        sums, joint_tails, joint_beside, joint_own, ranks
    )
    joint_across = (swap(joint_tails[0], "dp", 2), swap(joint_tails[1], "dp", 4))
    mod = whole_mod(sum(sums, corners[0]))
    joint_pair, joint_x_pair, joint_y_pair = pair_of((joint_own, *joint_beside))
    live, place_row, slots = places_of(ranks)
    (
        joint_across,
        mod,
        joint_pair,
        joint_x_pair,
        joint_y_pair,
        live,
        place_row,
        slots,
        first_own,
        cot_pieces,
    ) = fence(
        joint_across,
        mod,
        joint_pair,
        joint_x_pair,
        joint_y_pair,
        live,
        place_row,
        slots,
        first_own,
        cot_pieces,
    )

    first_beside = beside_of(first_own)
    cot_1 = swap(cot_pieces[1], "seq", 1)
    cot_2 = swap(cot_pieces[2], "seq", 2)
    cot_3 = swap(cot_pieces[3], "seq", 3)
    joint = placed(
        pieces_of(
            joint_own,
            joint_pair,
            joint_beside,
            (joint_x_pair, joint_y_pair),
            joint_across,
            pair_of(joint_across),
            part,
        ),
        model_position,
        model_rows,
    )
    packed, qkv, mixa_own, mixa_other = run_enter(
        joint, place_row, mod, (latent_pieces[0], latent_1, latent_2, latent_3), order
    )
    att_own, att_other, projected, hidden, mixed, mixm_own, mixm_other = run_attend(
        joint, live, qkv, packed, mod, order
    )
    first_beside, cot_1, cot_2, cot_3, mixed, first_own = fence(
        first_beside, cot_1, cot_2, cot_3, mixed, first_own
    )

    first_tails = tails(first_beside, part)
    first_across = (swap(first_tails[0], "dp", 2), swap(first_tails[1], "dp", 4))
    first_pair, first_x_pair, first_y_pair = pair_of((first_own, *first_beside))
    grad_out, grad_mlp = run_cot(place_row, mod, (cot_pieces[0], cot_1, cot_2, cot_3))
    second_own = (fc2_weight[:unit_part], fc2_weight[unit_part:])
    (
        first_across,
        first_pair,
        first_x_pair,
        first_y_pair,
        grad_out,
        grad_mlp,
        second_own,
        second_in,
    ) = fence(
        first_across,
        first_pair,
        first_x_pair,
        first_y_pair,
        grad_out,
        grad_mlp,
        second_own,
        fc2_weight,
    )

    second_ahead = swap(second_own[1], "dp", 2), swap(second_own[0], "dp", 4)
    first = placed(
        pieces_of(
            first_own,
            first_pair,
            first_beside,
            (first_x_pair, first_y_pair),
            first_across,
            pair_of(first_across),
            part,
        ),
        model_position,
        model_rows,
    )
    (grad_mlp_pair,) = pair_of((grad_mlp,))
    acts = run_first(first, mixed)
    second_ahead, second_own, grad_mlp_pair, acts = fence(
        second_ahead, second_own, grad_mlp_pair, acts
    )

    second_behind = swap(second_own[0], "dp", 2), swap(second_own[1], "dp", 4)
    (second_pair,) = pair_of((second_in,))
    (act_pair,) = pair_of((acts[1],))
    fc2_cut = outer_pair(
        [((acts[0], act_pair), [(grad_mlp, grad_mlp_pair)])], unit_rows, "fc2_grad"
    )
    second_behind, second_pair, second_ahead, fc2_cut, mixm_other, att_other, mixa_other = fence(
        second_behind, second_pair, second_ahead, fc2_cut, mixm_other, att_other, mixa_other
    )

    second_across = swap(second_ahead[1], "dp", 2), swap(second_ahead[0], "dp", 4)
    second_ahead_pair, second_behind_pair = pair_of(second_ahead), pair_of(second_behind)
    mixm_pair, att_pair, mixa_pair = pair_of((mixm_other, att_other, mixa_other))
    (
        second_across,
        second_ahead_pair,
        second_behind_pair,
        mixm_pair,
        att_pair,
        mixa_pair,
        fc2_cut,
        acts,
    ) = fence(
        second_across,
        second_ahead_pair,
        second_behind_pair,
        mixm_pair,
        att_pair,
        mixa_pair,
        fc2_cut,
        acts,
    )

    fc2_far = along_xy(fc2_cut[:2])
    pieces = [(second_in, 0, 0), (second_pair, 1, 0)]
    for side, ahead, behind, beyond in (
        (0, second_ahead, second_behind, second_across),
        (1, second_ahead_pair, second_behind_pair, pair_of(second_across)),
    ):
        pieces += [
            (behind[0], 2 + side, 0),
            (ahead[0], 2 + side, unit_part),
            (ahead[1], 4 + side, 0),
            (behind[1], 4 + side, unit_part),
            (beyond[0], 6 + side, 0),
            (beyond[1], 6 + side, unit_part),
        ]
    second = placed(pieces, unit_position, unit_rows) + (tuple(k & 1 for _, k, _ in pieces),)
    pre_own, pre_other, bias_own, bias_other = run_slope(second, acts[2:], grad_mlp)
    fc2_far, fc2_cut, pre_own, pre_other, acts = fence(
        fc2_far, fc2_cut, pre_own, pre_other, acts
    )

    fc2_near = along_xy(fc2_cut[2:4])
    pre_other_pair, pre_own_pair = pair_of((pre_own, pre_other))
    block_pieces, gate_m_grad, on = run_second(
        second, acts[:2], grad_out, hidden, mod, slots, fc2_cut, fc2_far
    )
    fc2_near, on, pre_other_pair, pre_own_pair, block_pieces, gate_m_grad = fence(
        fc2_near, on, pre_other_pair, pre_own_pair, block_pieces, gate_m_grad
    )

    fc2_last = along_xy(on)
    block_1 = swap(block_pieces[1], "seq", 1)
    block_2 = swap(block_pieces[2], "seq", 2)
    fc1_cut = outer_pair(
        [((mixm_own, mixm_pair), [(pre_own, pre_own_pair), (pre_other, pre_other_pair)])],
        model_rows,
        "fc1_grad",
    )
    fc2_last, block_1, block_2, block_3, fc1_cut, pre_own, pre_other, fc2_near = fence(
        fc2_last, block_1, block_2, block_pieces[3], fc1_cut, pre_own, pre_other, fc2_near
    )

    fc1_far = along_xy(fc1_cut[:2])
    block_3 = swap(block_3, "seq", 3)
    grad_hidden, grad_proj, grad_att, mod_grads = run_hidden(
        first, joint, (pre_own, pre_other), hidden, projected, grad_out, mod
    )
    fc1_far, fc1_cut, grad_proj, grad_att, block_3, fc2_near, fc2_last = fence(
        fc1_far, fc1_cut, grad_proj, grad_att, block_3, fc2_near, fc2_last
    )

    fc1_near = along_xy(fc1_cut[2:4])
    (proj_pair,) = pair_of((grad_proj,))
    fc2_parts = fold(
        fc2_cut[4],
        fc2_near,
        fc2_last,
        (plain_cuts(0, model, seq_count),),
        "fc2_fold",
        True,
    )
    grad_qkv, on = run_attend_back(after(live, fc2_parts), qkv, grad_att, fc1_cut, fc1_far)
    fc1_near, on, fc2_parts, proj_pair, grad_qkv = fence(
        fc1_near, on, fc2_parts, proj_pair, grad_qkv
    )

    fc1_last = along_xy(on)
    (qkv_pair,) = pair_of((grad_qkv,))
    fc2_state = columns_first(fc2_parts)
    latent_grads, payload = run_leave(
        joint,
        grad_qkv,
        packed,
        grad_hidden,
        mod,
        slots,
        live,
        mod_grads,
        gate_m_grad,
        (bias_own, bias_other),
    )
    fc1_last, qkv_pair, latent_grads, payload, fc1_near, grad_qkv, fc2_state = fence(
        fc1_last, qkv_pair, latent_grads, payload, fc1_near, grad_qkv, fc2_state
    )

    corners = [payload] + [swap(payload, "dp", 2 * q) for q in (1, 2, 3)]
    latent_1 = swap(latent_grads[1], "seq", 1)
    latent_2 = swap(latent_grads[2], "seq", 2)
    last_cut = outer_pair(
        [
            ((mixa_own, mixa_pair), [(grad_qkv, qkv_pair)]),
            ((att_own, att_pair), [(grad_proj, proj_pair)]),
        ],
        model_rows,
        "last_grad",
    )
    corners, latent_1, latent_2, last_cut, fc1_last, block_pieces, fc2_state = fence(
        corners, latent_1, latent_2, last_cut, fc1_last, block_pieces, fc2_state
    )

    last_far = along_xy(last_cut[:2])
    corner_pairs = pair_of(corners)
    fc1_cuts = tuple(
        tuple((lo, lo + unit_rows) for lo in (j * unit_rows, half_units + j * unit_rows))
        for j in range(seq_count)
    )
    fc1_parts = fold(fc1_cut[4], fc1_near, fc1_last, (fc1_cuts,), "fc1_fold")
    fc2_state = columns_second(fc2_state)
    rows_here = 8 * group
    cond_own, cond_pair, column_sent, column_own, column_across, sums = call(
        functools.partial(spread_kernel, 4),
        (
            sds((rows_here // 2, share), F32),
            sds((rows_here // 2, share), F32),
            sds((2, rows_here, column_share), BF),
            sds((rows_here, column_share), BF),
            sds((rows_here, column_share), BF),
            sds((2, 6 * model), F32),
        ),
        [*corners, *corner_pairs, seq_at.reshape(1).astype(jnp.int32), ada_weight],
        [VMEM] * 8 + [SMEM, VMEM],
        [
            pltpu.VMEM((rows_here, 6 * model), F32),
            pltpu.VMEM((seq_count, rows_here, column_share), BF),
            dma(seq_count),
        ],
        "spread",
        (VMEM, VMEM, ANY, ANY, ANY, VMEM),
    )
    (
        last_far,
        last_cut,
        cond_own,
        cond_pair,
        column_sent,
        sums,
        fc1_parts,
        block_pieces,
        latent_3,
        fc2_state,
    ) = fence(
        last_far,
        last_cut,
        cond_own,
        cond_pair,
        column_sent,
        sums,
        fc1_parts,
        block_pieces,
        latent_grads[3],
        fc2_state,
    )

    last_near = along_xy(last_cut[2:4])
    on = onward(last_cut, last_far)
    (cond_pair,) = pair_of((cond_pair,))
    fc1_state = columns_first(fc1_parts)
    latent_3 = swap(latent_3, "seq", 3)
    block_out = run_home(
        after((block_pieces[0], block_1, block_2, block_3), on), latents, BF, "home_out"
    )
    last_near, on, sums, column_sent, cond_pair, fc1_state, latent_3, block_out = fence(
        last_near, on, sums, column_sent, cond_pair, fc1_state, latent_3, block_out
    )

    last_last = along_xy(on)
    fc1_state = columns_second(fc1_state)
    sums = sums + swap(sums, "seq", 1)
    column_near = swap(column_sent, "seq", 1)
    (
        last_last,
        sums,
        column_near,
        fc1_state,
        fc2_state,
        last_near,
        cond_own,
        cond_pair,
        latent_3,
    ) = fence(
        last_last,
        sums,
        column_near,
        fc1_state,
        fc2_state,
        last_near,
        cond_own,
        cond_pair,
        latent_3,
    )

    qkv_share, out_share = 3 * model // seq_count, model // seq_count
    last_cuts = tuple(
        (
            (j * qkv_share, (j + 1) * qkv_share),
            (3 * model + j * out_share, 3 * model + (j + 1) * out_share),
        )
        for j in range(seq_count)
    )
    last_parts = fold(last_cut[4], last_near, last_last, (last_cuts,), "last_fold")
    last_state = columns_first(last_parts)
    cond_own, cond_pair = after((cond_own, cond_pair), last_parts)
    cond_cols = jnp.stack([cond_own, cond_pair], axis=1).reshape(4, group, 2, share)
    cond_cols = jnp.swapaxes(cond_cols, 1, 2)
    cond_cols = jnp.stack([cond_cols[0], *corners_of(cond_cols)])
    cond_mine = cond_mine_of(cond_cols.reshape(8, group, share))
    sums, column_near, column_across = after((sums, column_near, column_across), last_parts)
    sums = sums + swap(sums, "seq", 2)
    column_far = swap(jnp.stack([column_across, column_near[1]]), "seq", 2)
    columns = jnp.stack([column_own, column_near[0], column_far[0], column_far[1]])
    ada_grad = ada_product(silu_all, columns)
    cond_rows = [swap(cond_mine, "seq", k) if k else cond_mine for k in range(seq_count)]
    condition_grad = cond_end(jnp.stack(cond_rows))
    fc1_state, fc2_state = after((fc1_state, fc2_state), last_parts)
    fc2_grad = columns_sum(fc2_state).T
    fc1_grad = columns_sum(fc1_state)
    fc1_grad = jnp.where(
        parity == 1,
        jnp.concatenate([fc1_grad[:, unit_rows:], fc1_grad[:, :unit_rows]], axis=1),
        fc1_grad,
    )
    last_state, condition_grad, sums, ada_grad, fc1_grad, fc2_grad, latent_3 = fence(
        last_state, condition_grad, sums, ada_grad, fc1_grad, fc2_grad, latent_3
    )

    latents_grad = run_home(
        (latent_grads[0], latent_1, latent_2, latent_3), cotangent, F32, "home_grad"
    )
    far, own, near = columns_second(last_state)
    qkv_grad = columns_sum((far[:, :qkv_share], own[:, :qkv_share], near[:, :, :qkv_share]))
    out_grad = columns_sum((far[:, qkv_share:], own[:, qkv_share:], near[:, :, qkv_share:]))
    ada_bias_grad, fc1_bias_grad, kept_total = split_sums(sums)
    return (
        block_out,
        latents_grad,
        condition_grad,
        ada_grad,
        ada_bias_grad,
        qkv_grad,
        out_grad,
        fc1_grad,
        fc1_bias_grad,
        fc2_grad,
        kept_total,
    )


def solution(mesh):
    placed = (
        P("dp", "seq", None),
        P("dp", None),
        P("dp", "seq"),
        P("dp", "seq"),
        P("dp", None),
        P(),
        P("dp", None),
        P("dp", None),
        P("dp", None),
        P(),
        P("dp", None),
        P("dp", "seq", None),
    )
    return jax.shard_map(
        body,
        mesh=mesh,
        in_specs=placed,
        out_specs=(
            P("dp", "seq", None),
            P("dp", "seq", None),
            P("dp", None),
            P("dp", "seq"),
            P(),
            P("dp", "seq"),
            P("dp", "seq"),
            P("dp", "seq"),
            P(),
            P("dp", "seq"),
            P(),
        ),
        check_vma=False,
    )
```

```python
import functools
import math

import jax
import jax.numpy as jnp
from jax import lax
from jax.experimental import pallas as pl
from jax.experimental.pallas import tpu as pltpu
from jax.sharding import PartitionSpec as P

HEADS = 16
HEAD = 72
LANES = 128
BLOCKS = 8

layer_eps = 1e-06
far_below = -1e30
att_scale = 1.0 / math.sqrt(HEAD)
exp2_scale = att_scale / math.log(2.0)
gelu_c = math.sqrt(2.0 / math.pi)
gelu_k = 0.044715

BF = jnp.bfloat16
F32 = jnp.float32
VMEM = pl.BlockSpec(memory_space=pltpu.VMEM)
SMEM = pl.BlockSpec(memory_space=pltpu.SMEM)
ANY = pl.BlockSpec(memory_space=pl.ANY)
NT = (((1,), (1,)), ((), ()))
TN = (((0,), (0,)), ((), ()))


def swap(value, axis, step):
    return lax.ppermute(value, axis, [(i, i ^ step) for i in range(lax.axis_size(axis))])


def steps_of(axis):
    count = lax.axis_size(axis)
    return [1 << i for i in range(count.bit_length() - 1)]


def bit_set(axis, step):
    return (lax.axis_index(axis) & step) != 0


def gather_all(value, axis):
    value = value[None]
    for step in steps_of(axis):
        value = jnp.concatenate([value, swap(value, axis, step)], axis=0)
    return value


def sum_own(value, axis):
    for step in reversed(steps_of(axis)):
        value = value[:step] + swap(value[step:], axis, step)
    return value[0]


def trade_all(value, axis):
    count = value.shape[0]
    rest = value.shape[1:]
    for step in steps_of(axis):
        split = value.reshape((count // (2 * step), 2, step) + rest)
        value = jnp.stack([split[:, 0], swap(split[:, 1], axis, step)], axis=1).reshape(
            (count,) + rest
        )
    return value


def in_order(value, axis):
    count = value.shape[0]
    rest = value.shape[1:]
    for step in steps_of(axis):
        split = value.reshape((count // (2 * step), 2, step) + rest)
        value = jnp.where(bit_set(axis, step), split[:, ::-1], split).reshape((count,) + rest)
    return value


def sum_everywhere(value):
    for axis in ("dp", "seq"):
        for step in steps_of(axis):
            value = value + swap(value, axis, step)
    return value


def after(value, *earlier):
    return lax.optimization_barrier((value,) + earlier)[0]


def halves_of(rows):
    first = (rows // 2 + 15) // 16 * 16
    return first, rows - first


def pieces_of(own, own_pair, beside, beside_pair, across, across_pair, part):
    return [
        (own, 0, 0),
        (own_pair, 1, 0),
        (beside[0], 2, 0),
        (beside_pair[0], 3, 0),
        (beside[1], 4, 0),
        (beside_pair[1], 5, 0),
        (across[0], 6, 0),
        (across[1], 6, part),
        (across_pair[0], 7, 0),
        (across_pair[1], 7, part),
    ]


def beside_of(shard):
    return swap(shard, "dp", 2), swap(shard, "dp", 4)


def across_of(beside, part):
    return swap(beside[1][:part], "dp", 2), swap(beside[0][part:], "dp", 4)


def pair_of(values):
    return tuple(swap(v, "dp", 1) for v in values)


def placed(pieces, position, rows):
    starts = jnp.stack([position(k) * rows + first for _, k, first in pieces]).astype(jnp.int32)
    return [v for v, _, _ in pieces], starts


def whole_weight(shard):
    return lax.all_gather(shard, "dp", axis=0, tiled=True)


def call(kernel, outs, ins, specs, scratch, name, out_specs=None):
    return pl.pallas_call(
        kernel,
        out_shape=outs,
        in_specs=specs,
        out_specs=out_specs or jax.tree.map(lambda _: VMEM, outs),
        scratch_shapes=scratch,
        name=name,
        compiler_params=pltpu.CompilerParams(vmem_limit_bytes=60 * 1024 * 1024),
    )(*ins)


def start_pieces(offsets, refs, target, sem, lo, hi):
    copies = []
    shift = lo if target.shape[1] == hi - lo else 0
    for k, ref in enumerate(refs):
        rows = ref.shape[0]
        copies.append(
            pltpu.make_async_copy(
                ref.at[:, pl.ds(lo, hi - lo)],
                target.at[pl.ds(pl.multiple_of(offsets[k], 16), rows), pl.ds(lo - shift, hi - lo)],
                sem.at[k],
            )
        )
    for one in copies:
        one.start()
    return copies


def wait_all(copies):
    for one in copies:
        one.wait()


def normal(rows_in):
    center = rows_in - jnp.mean(rows_in, axis=-1, keepdims=True)
    inverse = lax.rsqrt(jnp.mean(center * center, axis=-1, keepdims=True) + layer_eps)
    return center * inverse, inverse


def normal_back(grad_rows, normed, inverse):
    mean_grad = jnp.mean(grad_rows, axis=-1, keepdims=True)
    mean_proj = jnp.mean(grad_rows * normed, axis=-1, keepdims=True)
    return inverse * (grad_rows - mean_grad - normed * mean_proj)


def dot(left, right, dims=None):
    if dims is None:
        return jnp.dot(left, right, preferred_element_type=F32)
    return lax.dot_general(left, right, dims, preferred_element_type=F32)


def spans(total, width):
    return [(lo, min(lo + width, total)) for lo in range(0, total, width)]


def pack_rows(place_ref, piece_refs, latent, rows_out):
    gathered = jnp.concatenate([ref[latent] for ref in piece_refs], axis=0)
    slots = lax.broadcasted_iota(jnp.int32, (rows_out, gathered.shape[0]), 0)
    chosen = jnp.where(place_ref[latent] == slots, 1.0, 0.0).astype(BF)
    return dot(chosen, gathered)


def unpack_rows(slots_ref, latent, packed, out_refs):
    slots = slots_ref[latent]
    rows = lax.broadcasted_iota(jnp.int32, (slots.shape[0], packed.shape[0]), 1)
    spread = dot(jnp.where(slots == rows, 1.0, 0.0).astype(BF), packed).astype(BF)
    block = out_refs[0].shape[1]
    for k, out in enumerate(out_refs):
        out[latent] = spread[k * block : (k + 1) * block]


def home_kernel(at, rank, base, *refs):
    pieces, out = refs[:-1], refs[-1]
    group, slots, _ = pieces[0].shape
    for k, piece in enumerate(pieces):
        for j in range(group):
            latent = (at[0] ^ k) * group + j
            place = rank[latent]
            rows = lax.broadcasted_iota(jnp.int32, (place.shape[0], slots), 1)
            spread = dot(jnp.where(place == rows, 1.0, 0.0).astype(BF), piece[j])
            out[latent] = jnp.where(place >= 0, spread, base[latent].astype(F32)).astype(out.dtype)


def cut_kernel(first, top, bottom, top_out, bottom_out, top_held, bottom_held, load_sem, store_sem):
    rows = bottom.shape[0]
    loads = [
        pltpu.make_async_copy(top.at[pl.ds(0, first), :], top_held, load_sem.at[0]),
        pltpu.make_async_copy(bottom.at[pl.ds(first, rows - first), :], bottom_held, load_sem.at[1]),
    ]
    stores = [
        pltpu.make_async_copy(top_held, top_out, store_sem.at[0]),
        pltpu.make_async_copy(bottom_held, bottom_out, store_sem.at[1]),
    ]
    for one in loads:
        one.start()
    for load, store in zip(loads, stores):
        load.wait()
        store.start()
    wait_all(stores)


def split_parity(rows_low, order_ref, own_ref, other_ref):
    moved = dot(rows_low, order_ref[...]).astype(BF)
    width = own_ref.shape[1]
    own_ref[...] = moved[:, :width]
    other_ref[...] = moved[:, width:]


def enter_kernel(pieces, blocks, cap, *refs):
    (offsets, place, mod, order), refs = refs[:4], refs[4:]
    latents, refs = refs[:blocks], refs[blocks:]
    weights, refs = refs[:pieces], refs[pieces:]
    packed_out, qkv_out, own_out, other_out, weight, mixed, sem = refs
    width = qkv_out.shape[1]
    chunks = spans(width, width // 3)
    loads = [
        start_pieces(offsets, weights, weight, sem.at[i], lo, hi) for i, (lo, hi) in enumerate(chunks)
    ]
    for latent in range(mod.shape[0]):
        here = pl.ds(latent * cap, cap)
        rows = pack_rows(place, latents, latent, cap)
        packed_out[here, :] = rows.astype(BF)
        normed, _ = normal(rows)
        mixed[here, :] = (normed * (1.0 + mod[latent, 1:2, :]) + mod[latent, 0:1, :]).astype(BF)
    split_parity(mixed[...], order, own_out, other_out)
    for i, (lo, hi) in enumerate(chunks):
        wait_all(loads[i])
        qkv_out[:, lo:hi] = dot(mixed[...], weight[:, lo:hi]).astype(BF)


def cot_kernel(cap, place, mod, *refs):
    cots, (packed_out, mlp_out) = refs[:-2], refs[-2:]
    for latent in range(mod.shape[0]):
        here = pl.ds(latent * cap, cap)
        rows = pack_rows(place, cots, latent, cap)
        packed_out[here, :] = rows.astype(BF)
        mlp_out[here, :] = (mod[latent, 5:6, :] * rows).astype(BF)


def windows():
    found = []
    for head in range(HEADS):
        first = head * HEAD
        base = first // LANES * LANES
        width = LANES if first + HEAD <= base + LANES else 2 * LANES
        found.append((base, width, first - base))
    return found[::2] + found[1::2]


def head_mask(width, first, dtype):
    lane = lax.broadcasted_iota(jnp.int32, (1, width), 1)
    return jnp.where((lane >= first) & (lane < first + HEAD), 1.0, 0.0).astype(dtype)


def attend_kernel(pieces, cap, model, *refs):
    (offsets, live, qkv, packed, mod, order), refs = refs[:6], refs[6:]
    weights, refs = refs[:pieces], refs[pieces:]
    (own_att, other_att, proj_out, hidden_out, mixed_out, own_mix, other_mix), refs = (
        refs[:7],
        refs[7:],
    )
    weight, attended, sem = refs
    copies = start_pieces(offsets, weights, weight, sem, 3 * model, 4 * model)
    attended[...] = jnp.zeros_like(attended)

    def one_latent(latent, carry):
        here = pl.ds(pl.multiple_of(latent * cap, 16), cap)
        count = live[latent]
        seen = lax.broadcasted_iota(jnp.int32, (cap, cap), 1) < count
        for base, width, first in windows():
            low_mask = head_mask(width, first, BF)
            query = qkv[here, base : base + width] * low_mask
            key = qkv[here, model + base : model + base + width]
            value = qkv[here, 2 * model + base : 2 * model + base + width] * low_mask
            scores = jnp.where(seen, dot(query, key, NT), far_below)
            raised = jnp.exp2((scores - jnp.max(scores, axis=-1, keepdims=True)) * exp2_scale)
            share = 1.0 / jnp.sum(raised, axis=-1, keepdims=True)
            attended[here, base : base + width] += dot(raised.astype(BF), value) * share
        return carry

    lax.fori_loop(0, mod.shape[0], one_latent, 0)
    att_low = attended[...].astype(BF)
    split_parity(att_low, order, own_att, other_att)
    wait_all(copies)
    projected = dot(att_low, weight[...])
    proj_out[...] = projected
    for latent in range(mod.shape[0]):
        rows = slice(latent * cap, (latent + 1) * cap)
        hidden = packed[rows, :].astype(F32) + mod[latent, 2:3, :] * projected[rows]
        hidden_out[rows, :] = hidden
        normed, _ = normal(hidden)
        mixed_out[rows, :] = (
            normed * (1.0 + mod[latent, 4:5, :]) + mod[latent, 3:4, :]
        ).astype(BF)
    split_parity(mixed_out[...], order, own_mix, other_mix)


def unit_chunks(parity, half):
    found = []
    for side in (0, 1):
        base = (parity[0] ^ side) * half
        for lo, hi in spans(half, 768):
            found.append((side, lo, hi, pl.ds(pl.multiple_of(base + lo, LANES), hi - lo)))
    return found


def start_chunks(offsets, refs, target, sem, chunks):
    found = []
    for i, (_, _, _, cols) in enumerate(chunks):
        found.append(
            [
                pltpu.make_async_copy(
                    ref.at[:, cols],
                    target.at[pl.ds(pl.multiple_of(offsets[k], 16), ref.shape[0]), cols],
                    sem.at[i, k],
                )
                for k, ref in enumerate(refs)
            ]
        )
        for one in found[-1]:
            one.start()
    return found


def first_kernel(pieces, offsets, parity, mixed, bias, *refs):
    weights, refs = refs[:pieces], refs[pieces:]
    acts, slopes = refs[0:2], refs[2:4]
    weight, act, slope, load_sem, act_sem, slope_sem = refs[4:]
    half = acts[0].shape[1]
    chunks = unit_chunks(parity, half)
    loads = start_chunks(offsets, weights, weight, load_sem, chunks)
    stores = []
    for i, (side, lo, hi, cols) in enumerate(chunks):
        wait_all(loads[i])
        pre = dot(mixed[...], weight[:, cols]) + bias[:, cols]
        square = pre * pre
        curve = jnp.tanh(pre * (gelu_c + (gelu_c * gelu_k) * square))
        cdf = 0.5 + 0.5 * curve
        act[side, :, lo:hi] = (pre * cdf).astype(BF)
        bend = (0.5 * gelu_c) + (1.5 * gelu_c * gelu_k) * square
        slope[side, :, lo:hi] = (cdf + pre * bend * (1.0 - curve * curve)).astype(BF)
        here = pl.ds(lo, hi - lo)
        for held, out, sem in ((act, acts, act_sem), (slope, slopes, slope_sem)):
            stores.append(
                pltpu.make_async_copy(held.at[side, :, here], out[side].at[:, here], sem.at[i])
            )
            stores[-1].start()
    wait_all(stores)


def start_halves(offsets, refs, sides, target, sem):
    found = ([], [])
    for side in (0, 1):
        for k, ref in enumerate(refs):
            if sides[k] != side:
                continue
            rows = ref.shape[0]
            found[side].append(
                pltpu.make_async_copy(
                    ref, target.at[pl.ds(pl.multiple_of(offsets[k], 16), rows), :], sem.at[k]
                )
            )
            found[side][-1].start()
    return found


def slope_kernel(sides, *refs):
    (offsets, own_slope, other_slope, grad_mlp), refs = refs[:4], refs[4:]
    weights, refs = refs[: len(sides)], refs[len(sides) :]
    own_pre, other_pre, own_bias, other_bias, weight, pre, sem, out_sem = refs
    halves = start_halves(offsets, weights, sides, weight, sem)
    half = own_pre.shape[1]
    stores = []
    for side, (slope, pre_out, bias_out) in enumerate(
        ((own_slope, own_pre, own_bias), (other_slope, other_pre, other_bias))
    ):
        wait_all(halves[side])
        for lo, hi in spans(half, 768):
            grad_act = dot(grad_mlp[...], weight[side * half + lo : side * half + hi, :], NT)
            grad_pre = (grad_act * slope[:, lo:hi].astype(F32)).astype(BF)
            pre[side, :, lo:hi] = grad_pre
            here = pl.ds(lo, hi - lo)
            stores.append(
                pltpu.make_async_copy(
                    pre.at[side, :, here], pre_out.at[:, here], out_sem.at[len(stores)]
                )
            )
            stores[-1].start()
            bias_out[:, lo:hi] = jnp.sum(grad_pre.astype(F32), axis=0, keepdims=True)
    wait_all(stores)


def second_kernel(sides, blocks, cap, *refs):
    (offsets, own_act, other_act, grad_out, hidden, mod, slots), refs = refs[:7], refs[7:]
    weights, refs = refs[: len(sides)], refs[len(sides) :]
    onward, refs = refs[:4], refs[4:]
    outs, refs = refs[:blocks], refs[blocks:]
    (gate_grad, *onward_outs), refs = refs[:3], refs[3:]
    weight, sem = refs[:2]
    held, onward_sem = refs[2:6], refs[6]
    halves = start_halves(offsets, weights, sides, weight, sem)
    loads = start_onward(onward, held, onward_sem)
    half = own_act.shape[1]
    wait_all(halves[0])
    mlp = dot(own_act[...], weight[:half, :])
    wait_all(halves[1])
    mlp = mlp + dot(other_act[...], weight[half:, :])
    for latent in range(mod.shape[0]):
        rows = slice(latent * cap, (latent + 1) * cap)
        gate_grad[latent, :, :] = jnp.sum(
            grad_out[rows, :].astype(F32) * mlp[rows], axis=0, keepdims=True
        )
        block = (hidden[rows, :] + mod[latent, 5:6, :] * mlp[rows]).astype(BF)
        unpack_rows(slots, latent, block, outs)
    wait_all(end_onward(loads, held, onward_outs, onward_sem))


def hidden_kernel(pieces, first_pieces, cap, model, *refs):
    (first_at, offsets, parity, own_pre, other_pre, hidden_in, projected_in, grad_in, mod), refs = (
        refs[:9],
        refs[9:],
    )
    first_weights, refs = refs[:first_pieces], refs[first_pieces:]
    out_weights, refs = refs[:pieces], refs[pieces:]
    (grad_hidden_out, grad_proj_out, grad_att, mod_grads), refs = refs[:4], refs[4:]
    first, out_weight, hidden, projected, grad_out, grad_hidden, grad_proj = refs[:7]
    first_sem, out_sem, in_sem, store_sem = refs[7:]
    half = own_pre.shape[1]
    chunks = unit_chunks(parity, half)
    loads = start_chunks(first_at, first_weights, first, first_sem, chunks)
    later = [
        pltpu.make_async_copy(there, here, in_sem.at[i])
        for i, (there, here) in enumerate(
            ((hidden_in, hidden), (projected_in, projected), (grad_in, grad_out))
        )
    ]
    for one in later:
        one.start()
    last = start_pieces(offsets, out_weights, out_weight, out_sem, 3 * model, 4 * model)
    total = None
    for i, (side, lo, hi, cols) in enumerate(chunks):
        wait_all(loads[i])
        part = dot((own_pre, other_pre)[side][:, lo:hi], first[:, cols], NT)
        total = part if total is None else total + part
    wait_all(later)
    stores = []
    for latent in range(mod.shape[0]):
        rows = slice(latent * cap, (latent + 1) * cap)
        normed, inverse = normal(hidden[rows, :])
        grad_mixed = total[rows]
        mod_grads[latent, 0:1, :] = jnp.sum(grad_mixed, axis=0, keepdims=True)
        mod_grads[latent, 1:2, :] = jnp.sum(grad_mixed * normed, axis=0, keepdims=True)
        grad = grad_out[rows, :].astype(F32) + normal_back(
            grad_mixed * (1.0 + mod[latent, 4:5, :]), normed, inverse
        )
        grad_hidden[rows, :] = grad
        mod_grads[latent, 2:3, :] = jnp.sum(grad * projected[rows, :], axis=0, keepdims=True)
        grad_proj[rows, :] = (mod[latent, 2:3, :] * grad).astype(BF)
        here = pl.ds(latent * cap, cap)
        for held, out in ((grad_hidden, grad_hidden_out), (grad_proj, grad_proj_out)):
            stores.append(
                pltpu.make_async_copy(
                    held.at[here, :], out.at[here, :], store_sem.at[len(stores)]
                )
            )
            stores[-1].start()
    wait_all(last)
    grad_att[...] = dot(grad_proj[...], out_weight[...], NT).astype(BF)
    wait_all(stores)


def start_onward(ins, held, sem):
    loads = [pltpu.make_async_copy(a, b, sem.at[i]) for i, (a, b) in enumerate(zip(ins, held))]
    for one in loads:
        one.start()
    return loads


def end_onward(loads, held, outs, sem):
    keep_x, keep_y, far_x, far_y = held
    wait_all(loads)
    keep_x[...] = (keep_x[...].astype(F32) + far_y[...].astype(F32)).astype(BF)
    keep_y[...] = (keep_y[...].astype(F32) + far_x[...].astype(F32)).astype(BF)
    stores = [
        pltpu.make_async_copy(a, b, sem.at[4 + i]) for i, (a, b) in enumerate(zip(held[:2], outs))
    ]
    for one in stores:
        one.start()
    return stores


def attend_back_kernel(cap, model, *refs):
    (live, qkv, grad_att), onward, (grad_qkv, *onward_outs) = refs[:3], refs[3:7], refs[7:10]
    sums, held, onward_sem = refs[10], refs[11:15], refs[15]
    loads = start_onward(onward, held, onward_sem)
    sums[...] = jnp.zeros_like(sums)

    def one_latent(latent, carry):
        here = pl.ds(pl.multiple_of(latent * cap, 16), cap)
        count = live[latent]
        seen = lax.broadcasted_iota(jnp.int32, (cap, cap), 0) < count
        found = windows()
        for some in range(0, len(found), 4):
            heads = []
            for base, width, first in found[some : some + 4]:
                mask = head_mask(width, first, BF)
                cols = [slice(part + base, part + base + width) for part in (0, model, 2 * model)]
                query, key = qkv[here, cols[0]] * mask, qkv[here, cols[1]] * mask
                grad = grad_att[here, cols[0]] * mask
                heads.append(
                    (cols, query, key, grad, dot(key, query, NT), dot(qkv[here, cols[2]], grad, NT))
                )
            weights = []
            for _, _, _, _, scores, grad_probs in heads:
                scores = jnp.where(seen, scores, far_below)
                raised = jnp.exp2((scores - jnp.max(scores, axis=0, keepdims=True)) * exp2_scale)
                probs = raised * (1.0 / jnp.sum(raised, axis=0, keepdims=True))
                delta = jnp.sum(probs * grad_probs, axis=0, keepdims=True)
                weights.append(((probs * (grad_probs - delta)).astype(BF), probs.astype(BF)))
            for (cols, query, key, grad, _, _), (grad_scores, probs) in zip(heads, weights):
                sums[here, cols[0]] += dot(grad_scores, key, TN)
                sums[here, cols[1]] += dot(grad_scores, query)
                sums[here, cols[2]] += dot(probs, grad)
        return carry

    lax.fori_loop(0, live.shape[0], one_latent, 0)
    stores = end_onward(loads, held, onward_outs, onward_sem)
    grad_qkv[:, : 2 * model] = (sums[:, : 2 * model] * att_scale).astype(BF)
    grad_qkv[:, 2 * model :] = sums[:, 2 * model :].astype(BF)
    wait_all(stores)


def leave_kernel(pieces, blocks, cap, *refs):
    (
        offsets,
        parity,
        live,
        grad_qkv,
        packed,
        grad_hidden,
        mod,
        slots,
        mod_grads,
        gate_m,
        own_bias,
        other_bias,
    ), refs = refs[:12], refs[12:]
    weights, refs = refs[:pieces], refs[pieces:]
    outs, refs = refs[:blocks], refs[blocks:]
    payload, weight, rows_wide, sem = refs
    model = packed.shape[1]
    group, half = mod.shape[0], own_bias.shape[1]
    rows_wide[...] = jnp.zeros_like(rows_wide)
    lane = lax.broadcasted_iota(jnp.int32, (1, LANES), 1)
    kept = jnp.zeros((1, LANES), F32)
    for latent in range(group):
        at = slice(latent, latent + 1)
        rows_wide[at, 2 * model : 3 * model] = mod_grads[latent, 2:3, :]
        rows_wide[at, 3 * model : 4 * model] = mod_grads[latent, 0:1, :]
        rows_wide[at, 4 * model : 5 * model] = mod_grads[latent, 1:2, :]
        rows_wide[at, 5 * model :] = gate_m[latent]
        for digit in range(3):
            part = (live[latent] >> (3 * digit)) & 7
            kept = jnp.where(lane == 3 * latent + digit, part.astype(F32), kept)
    for side, bias in enumerate((own_bias, other_bias)):
        first = pl.multiple_of((parity[0] ^ side) * half, LANES)
        rows_wide[group : group + 1, pl.ds(first, half)] = bias[...]
    rows_wide[group : group + 1, 2 * half : 2 * half + LANES] = kept
    chunks = spans(weight.shape[1], model)
    loads = [
        start_pieces(offsets, weights, weight, sem.at[i], lo, hi) for i, (lo, hi) in enumerate(chunks)
    ]
    total = None
    for i, (lo, hi) in enumerate(chunks):
        wait_all(loads[i])
        part = dot(grad_qkv[:, lo:hi], weight[:, lo:hi], NT)
        total = part if total is None else total + part
    for latent in range(mod.shape[0]):
        rows = slice(latent * cap, (latent + 1) * cap)
        normed, inverse = normal(packed[rows, :].astype(F32))
        grad_mixed = total[rows]
        at = slice(latent, latent + 1)
        rows_wide[at, :model] = jnp.sum(grad_mixed, axis=0, keepdims=True)
        rows_wide[at, model : 2 * model] = jnp.sum(grad_mixed * normed, axis=0, keepdims=True)
        grad = grad_hidden[rows, :] + normal_back(
            grad_mixed * (1.0 + mod[latent, 1:2, :]), normed, inverse
        )
        unpack_rows(slots, latent, grad.astype(BF), outs)
    payload[...] = rows_wide[: group + 1, :].astype(BF)


def spread_kernel(corners, *refs):
    own, pair = refs[:corners], refs[corners : 2 * corners]
    (at, weight), refs = refs[2 * corners : 2 * corners + 2], refs[2 * corners + 2 :]
    cond_own, cond_pair, sent, kept, across, sums, rows, parts, wide_sums, sem = refs
    group = own[0].shape[0] - 1
    totals = []
    for q in range(corners):
        mine, theirs = own[q][...].astype(F32), pair[q][...].astype(F32)
        for side, wide in enumerate((mine, theirs)):
            first = (side * corners + q) * group
            rows[first : first + group, :] = wide[:group]
        totals.append(
            [
                sum(wide[latent : latent + 1] for latent in range(group))
                for wide in (mine, theirs)
            ]
            + [wide[group:] for wide in (mine, theirs)]
        )
    for i in range(2):
        by_corner = [one[2 * i] + one[2 * i + 1] for one in totals]
        while len(by_corner) > 1:
            by_corner = [a + b for a, b in zip(by_corner[::2], by_corner[1::2])]
        wide_sums[i : i + 1, :] = by_corner[0]
    low = rows[...].astype(BF)
    cond = dot(low, weight[...], NT)
    half = corners * group
    cond_own[...] = cond[:half]
    cond_pair[...] = cond[half:]
    count, _, width = parts.shape
    for j in range(count):
        cols = slice(j * width, (j + 1) * width)
        parts[j] = low[:, cols]
        for i in range(2):
            sums[count * i + j : count * i + j + 1, :] = wide_sums[i : i + 1, cols]
    copies = [
        pltpu.make_async_copy(parts.at[at[0] ^ k], out, sem.at[k])
        for k, out in ((1, sent.at[0]), (3, sent.at[1]), (0, kept), (2, across))
    ]
    for one in copies:
        one.start()
    wait_all(copies)


def by_columns(width):
    return width % (2 * LANES) == 0


def outer_kernel(rows, used, sides, *refs):
    block_at, refs = refs[0], refs[1:]
    total = sum(sides)
    lefts, refs = refs[: 2 * len(sides)], refs[2 * len(sides) :]
    rights, refs = refs[: 2 * total], refs[2 * total :]
    (far_x, far_y, near_x, near_y, keep, keep_x, keep_y), refs = refs[:7], refs[7:]
    result, sem = refs
    base, at = 0, 0
    for group, count in enumerate(sides):
        own_left, pair_left = lefts[2 * group : 2 * group + 2]
        left = jnp.concatenate([own_left[:, :used], pair_left[:, :used]], axis=0)
        for own, pair in zip(rights[2 * at : 2 * (at + count) : 2], rights[2 * at + 1 : 2 * (at + count) : 2]):
            width = own.shape[1]
            for lo, hi in spans(width, 768):
                right = jnp.concatenate([own[:, lo:hi], pair[:, lo:hi]], axis=0)
                result[:, base + lo : base + hi] = dot(left, right, TN).astype(BF)
            base += width
        at += count

    width = result.shape[1]

    def half_at(k, second):
        first = pl.multiple_of(block_at[k] * rows, 16)
        if by_columns(width):
            return result.at[pl.ds(first, rows), pl.ds(second * (width // 2), width // 2)]
        part, rest = halves_of(rows)
        return result.at[pl.ds(first + part, rest) if second else pl.ds(first, part), :]

    moves = [
        (half_at(3, 0), far_x),
        (half_at(3, 1), far_y),
        (half_at(1, 0), near_x),
        (half_at(2, 1), near_y),
        (result.at[pl.ds(pl.multiple_of(block_at[0] * rows, 16), rows), :], keep),
        (half_at(1, 1), keep_x),
        (half_at(2, 0), keep_y),
    ]
    copies = [pltpu.make_async_copy(a, b, sem.at[i]) for i, (a, b) in enumerate(moves)]
    for one in copies:
        one.start()
    wait_all(copies)


def reorder_kernel(unit, shard, whole):
    count = shard.shape[1] // unit
    for block in range(count):
        to = (block % 2) * (count // 2) + block // 2
        whole[:, to * unit : (to + 1) * unit] = shard[:, block * unit : (block + 1) * unit]


def fold_kernel(cuts, turned, *refs):
    (at, keep, near_top, near_bottom, far_top, far_bottom), refs = refs[:6], refs[6:]
    count = len(cuts[0])
    outs, refs = refs[: 3 * len(cuts)], refs[3 * len(cuts) :]
    scratch, sem = refs[:-1], refs[-1]
    wide = lambda ref: ref[...].astype(F32)
    near, far = (near_top, near_bottom), (far_top, far_bottom)
    columns = by_columns(keep.shape[1])
    axis = 1 if columns else 0
    cut = far_top.shape[axis]
    kept = (keep[:, :cut], keep[:, cut:]) if columns else (keep[:cut, :], keep[cut:, :])
    halves = [
        (one.astype(F32) + wide(a) + wide(b)).astype(BF) for one, a, b in zip(kept, near, far)
    ]
    whole = jnp.concatenate(halves, axis=axis)
    copies = []
    if turned:
        whole = whole.T
    for i, (group, parts) in enumerate(zip(cuts, scratch)):
        for j, pieces in enumerate(group):
            first = 0
            for lo, hi in pieces:
                if turned:
                    parts[j] = whole[lo:hi, :]
                else:
                    parts[j, :, first : first + hi - lo] = whole[:, lo:hi]
                first += hi - lo
        sent, own, across = outs[3 * i : 3 * i + 3]
        for k, out in ((1, sent.at[0]), (3, sent.at[1]), (0, own), (2, across)):
            copies.append(pltpu.make_async_copy(parts.at[at[0] ^ k], out, sem.at[len(copies)]))
    for one in copies:
        one.start()
    wait_all(copies)


def outer_pair(groups, rows, name):
    used = 4 * rows
    lefts = [v for left, _ in groups for v in left]
    rights = [v for _, pairs in groups for pair in pairs for v in pair]
    width = sum(v.shape[1] for v in rights) // 2
    sides = tuple(len(pairs) for _, pairs in groups)
    block_at = jnp.stack([(lax.axis_index("dp") ^ (2 * k)) // 2 for k in range(4)]).astype(jnp.int32)
    ins = [block_at, *lefts, *rights]
    part, rest = halves_of(rows)
    first, second = (part, width), (rest, width)
    if by_columns(width):
        first = second = (rows, width // 2)
    shapes = (first, second, first, second, (rows, width), second, first)
    outs = tuple(jax.ShapeDtypeStruct(shape, BF) for shape in shapes)
    return pl.pallas_call(
        functools.partial(outer_kernel, rows, used, sides),
        out_shape=outs,
        in_specs=[SMEM] + [VMEM] * (len(ins) - 1),
        out_specs=tuple(ANY for _ in outs),
        scratch_shapes=[pltpu.VMEM((used, width), BF), pltpu.SemaphoreType.DMA((7,))],
        name=name,
        compiler_params=pltpu.CompilerParams(vmem_limit_bytes=60 * 1024 * 1024),
    )(*ins)


def onward_kernel(keep_x, keep_y, far_x, far_y, on_x, on_y):
    on_x[...] = (keep_x[...].astype(F32) + far_y[...].astype(F32)).astype(BF)
    on_y[...] = (keep_y[...].astype(F32) + far_x[...].astype(F32)).astype(BF)


def onward(cut, far):
    keep_x, keep_y = cut[5:]
    outs = tuple(jax.ShapeDtypeStruct(v.shape, BF) for v in (keep_x, keep_y))
    ins = [keep_x, keep_y, *far]
    return call(onward_kernel, outs, ins, [VMEM] * 4, [], "onward")


def along_xy(pair):
    return swap(pair[0], "dp", 2), swap(pair[1], "dp", 4)


def fold(keep, near, last, cuts, name, turned=False):
    rows = keep.shape[0]
    count = lax.axis_size("seq")
    at = lax.axis_index("seq").reshape(1).astype(jnp.int32)
    widths = tuple(sum(hi - lo for lo, hi in group[0]) for group in cuts)
    blocks = [(w, rows) if turned else (rows, w) for w in widths]
    outs = tuple(
        jax.ShapeDtypeStruct(shape, BF) for block in blocks for shape in ((2,) + block, block, block)
    )
    return pl.pallas_call(
        functools.partial(fold_kernel, cuts, turned),
        out_shape=outs,
        in_specs=[SMEM] + [VMEM] * 5,
        out_specs=tuple(ANY for _ in outs),
        scratch_shapes=[pltpu.VMEM((count,) + block, BF) for block in blocks]
        + [pltpu.SemaphoreType.DMA((4 * len(cuts),))],
        name=name,
        compiler_params=pltpu.CompilerParams(vmem_limit_bytes=60 * 1024 * 1024),
    )(at, keep, near[0], near[1], last[1], last[0])


def plain_cuts(first, width, count):
    share = width // count
    return tuple(((first + j * share, first + (j + 1) * share),) for j in range(count))


def spread_plain(grad):
    grad = lax.psum_scatter(grad, "dp", scatter_dimension=0, tiled=True)
    return lax.psum_scatter(grad, "seq", scatter_dimension=1, tiled=True)


def body(
    latents,
    condition,
    keep_order,
    keep_count,
    ada_weight,
    ada_bias,
    qkv_weight,
    out_weight,
    fc1_weight,
    fc1_bias,
    fc2_weight,
    cotangent,
):
    latent_count, block_rows, model = latents.shape
    hidden_units = fc1_weight.shape[1]
    half_units = hidden_units // 2
    unit_rows = hidden_units // BLOCKS
    model_rows = model // BLOCKS
    dp_count, seq_count = lax.axis_size("dp"), lax.axis_size("seq")
    dp_at, seq_at = lax.axis_index("dp"), lax.axis_index("seq")
    group = latent_count // seq_count
    most = block_rows * 3 // 4
    cap = (seq_count - 1) * most + block_rows // 4
    rows_all = group * cap
    share = model // dp_count
    column_share = 6 * model // seq_count
    paired = dp_count == BLOCKS and seq_count == 4
    parity = (dp_at & 1) if paired else jnp.zeros_like(dp_at)
    parity_in = parity.reshape(1).astype(jnp.int32)
    part, _ = halves_of(model_rows)
    unit_part, _ = halves_of(unit_rows)
    whose = (lambda k: dp_at ^ k) if paired else (lambda k: jnp.int32(k))
    sds = jax.ShapeDtypeStruct
    dma = lambda n: pltpu.SemaphoreType.DMA((n,))
    fence = lambda *values: lax.optimization_barrier(values)

    def rank_of():
        slot = lax.broadcasted_iota(jnp.int32, (1, block_rows, 1), 1)
        token = lax.broadcasted_iota(jnp.int32, (1, 1, block_rows), 2)
        found = (keep_order[:, :, None] == token) & (slot < keep_count[:, :, None])
        return jnp.max(jnp.where(found, slot, -1), axis=1)

    def places_of(ranks):
        ranks = lax.dynamic_slice_in_dim(ranks, seq_at * group, group, 1)
        ranks = jnp.swapaxes(ranks, 0, 1)
        counts = jnp.sum((ranks >= 0).astype(jnp.int32), axis=2)
        starts = jnp.cumsum(counts, axis=1) - counts
        live = jnp.sum(counts, axis=1).astype(jnp.int32)
        place = jnp.where(ranks >= 0, ranks + starts[:, :, None], -1).reshape(
            group, seq_count * block_rows
        )
        slot = lax.broadcasted_iota(jnp.int32, (1, 1, most), 2)
        slots = jnp.where(slot < counts[:, :, None], starts[:, :, None] + slot, -1)
        return live, place[:, None, :], slots.reshape(group, seq_count * most, 1)

    def whole_slice(blocks_in, k):
        return lax.dynamic_slice_in_dim(blocks_in, (seq_at ^ k) * group, group, 0)

    rank = rank_of()

    def run_home(pieces, base, dtype, name):
        return call(
            home_kernel,
            sds((latent_count, block_rows, model), dtype),
            [seq_at.reshape(1).astype(jnp.int32), rank[:, :, None], base, *pieces],
            [SMEM] + [VMEM] * (2 + seq_count),
            [],
            name,
        )

    cond_wide = condition.astype(F32)
    silu_cond = jax.nn.silu(cond_wide).astype(BF)
    silu_parts = in_order(
        jnp.swapaxes(silu_cond.reshape(latent_count, dp_count, share), 0, 1), "dp"
    )

    def silu_of(rows):
        mine = lax.dynamic_slice_in_dim(rows, seq_at * group, group, 1)
        groups = rows.reshape(dp_count, seq_count, group, share)
        return mine, in_order(jnp.swapaxes(groups, 0, 1), "seq")


    def partial_mod(silu_rows):
        return jnp.dot(
            silu_rows.reshape(dp_count * group, share), ada_weight, preferred_element_type=F32
        ).reshape(dp_count, group, 6 * model)

    def whole_mod(total):
        return (total + ada_bias.astype(F32)).reshape(group, 6, model)

    unit_order = lambda v: jnp.swapaxes(
        v.reshape(v.shape[0], BLOCKS // 2, 2, unit_rows), 1, 2
    ).reshape(v.shape[0], hidden_units)
    bias_row = unit_order(fc1_bias.astype(F32)[None])

    pad = -(-(model // 2) // LANES) * LANES

    def order_of(parity):
        column = lax.broadcasted_iota(jnp.int32, (1, 2 * pad), 1)
        side, inner = column // pad, column % pad
        source = (2 * (inner // model_rows) + (parity ^ side)) * model_rows + inner % model_rows
        source = jnp.where(inner < model // 2, source, -1)
        return (lax.broadcasted_iota(jnp.int32, (model, 1), 0) == source).astype(BF)

    model_position = lambda k: whose(k)
    unit_position = lambda k: ((whose(k) & 1) ^ parity) * (BLOCKS // 2) + whose(k) // 2

    def run_enter(joint, place_row, mod, pieces, order):
        weights, offsets = joint
        return call(
            functools.partial(enter_kernel, len(weights), seq_count, cap),
            (
                sds((rows_all, model), BF),
                sds((rows_all, 3 * model), BF),
                sds((rows_all, pad), BF),
                sds((rows_all, pad), BF),
            ),
            [
                offsets,
                place_row,
                mod,
                order,
                *pieces,
                *weights,
            ],
            [SMEM, VMEM, VMEM, VMEM] + [VMEM] * seq_count + [ANY] * len(weights),
            [
                pltpu.VMEM((model, 3 * model), BF),
                pltpu.VMEM((rows_all, model), BF),
                pltpu.SemaphoreType.DMA((3, len(weights))),
            ],
            "enter",
        )

    def run_cot(place_row, mod, cot_pieces):
        low = sds((rows_all, model), BF)
        ins = [place_row, mod, *cot_pieces]
        return call(functools.partial(cot_kernel, cap), (low, low), ins, [VMEM] * len(ins), [], "cotangent")

    def run_attend(joint, live, qkv, packed, mod, order):
        weights, offsets = joint
        return call(
            functools.partial(attend_kernel, len(weights), cap, model),
            (
                sds((rows_all, pad), BF),
                sds((rows_all, pad), BF),
                sds((rows_all, model), F32),
                sds((rows_all, model), F32),
                sds((rows_all, model), BF),
                sds((rows_all, pad), BF),
                sds((rows_all, pad), BF),
            ),
            [
                offsets,
                live,
                qkv,
                packed,
                mod,
                order,
                *weights,
            ],
            [SMEM, SMEM, VMEM, VMEM, VMEM, VMEM] + [ANY] * len(weights),
            [
                pltpu.VMEM((model, model), BF),
                pltpu.VMEM((rows_all, model), F32),
                dma(len(weights)),
            ],
            "attend",
        )

    def run_first(first, mixed):
        weights, offsets = first
        half_rows = sds((rows_all, half_units), BF)
        chunks = 2 * len(spans(half_units, 768))
        return call(
            functools.partial(first_kernel, len(weights)),
            (half_rows,) * 4,
            [offsets, parity_in, mixed, bias_row, *weights],
            [SMEM, SMEM, VMEM, VMEM] + [ANY] * len(weights),
            [
                pltpu.VMEM((model, hidden_units), BF),
                pltpu.VMEM((2, rows_all, half_units), BF),
                pltpu.VMEM((2, rows_all, half_units), BF),
                pltpu.SemaphoreType.DMA((chunks, len(weights))),
                dma(chunks),
                dma(chunks),
            ],
            "first",
            (ANY,) * 4,
        )

    def run_slope(second, slopes, grad_mlp):
        weights, offsets, sides = second
        half_rows = sds((rows_all, half_units), BF)
        return call(
            functools.partial(slope_kernel, sides),
            (half_rows, half_rows, sds((1, half_units), F32), sds((1, half_units), F32)),
            [offsets, *slopes, grad_mlp, *weights],
            [SMEM] + [VMEM] * 3 + [ANY] * len(weights),
            [
                pltpu.VMEM((hidden_units, model), BF),
                pltpu.VMEM((2, rows_all, half_units), BF),
                dma(len(weights)),
                dma(2 * len(spans(half_units, 768))),
            ],
            "slope",
            (ANY, ANY, VMEM, VMEM),
        )

    def onward_parts(cut, far):
        ins = [cut[5], cut[6], *far]
        return (
            ins,
            tuple(sds(v.shape, BF) for v in ins[:2]),
            [pltpu.VMEM(v.shape, BF) for v in ins] + [dma(6)],
        )

    def run_second(second, acts, grad_out, hidden, mod, slots, cut, far):
        weights, offsets, sides = second
        ins, outs, scratch = onward_parts(cut, far)
        result = call(
            functools.partial(second_kernel, sides, seq_count, cap),
            tuple(sds((group, most, model), BF) for _ in range(seq_count))
            + (sds((group, 1, model), F32),)
            + outs,
            [offsets, *acts, grad_out, hidden, mod, slots, *weights, *ins],
            [SMEM] + [VMEM] * 6 + [ANY] * (len(weights) + 4),
            [pltpu.VMEM((hidden_units, model), BF), dma(len(weights))] + scratch,
            "second",
            (VMEM,) * (seq_count + 1) + (ANY, ANY),
        )
        return result[:seq_count], result[seq_count], result[seq_count + 1 :]

    def run_hidden(first, joint, pres, hidden, projected, grad_out, mod):
        (weights, offsets), (first_w, first_at) = joint, first
        wide, low = sds((rows_all, model), F32), sds((rows_all, model), BF)
        return call(
            functools.partial(hidden_kernel, len(weights), len(first_w), cap, model),
            (wide, low, low, sds((group, 3, model), F32)),
            [
                first_at,
                offsets,
                parity_in,
                *pres,
                hidden,
                projected,
                grad_out,
                mod,
                *first_w,
                *weights,
            ],
            [SMEM, SMEM, SMEM, VMEM, VMEM, ANY, ANY, ANY, VMEM]
            + [ANY] * (len(first_w) + len(weights)),
            [
                pltpu.VMEM((model, hidden_units), BF),
                pltpu.VMEM((model, model), BF),
                pltpu.VMEM((rows_all, model), F32),
                pltpu.VMEM((rows_all, model), F32),
                pltpu.VMEM((rows_all, model), BF),
                pltpu.VMEM((rows_all, model), F32),
                pltpu.VMEM((rows_all, model), BF),
                pltpu.SemaphoreType.DMA((2 * len(spans(half_units, 768)), len(first_w))),
                dma(len(weights)),
                dma(3),
                dma(2 * group),
            ],
            "hidden_back",
            (ANY, ANY, VMEM, VMEM),
        )

    def run_attend_back(live, qkv, grad_att, cut, far):
        ins, outs, scratch = onward_parts(cut, far)
        grad_qkv, *on = call(
            functools.partial(attend_back_kernel, cap, model),
            (sds((rows_all, 3 * model), BF),) + outs,
            [live, qkv, grad_att, *ins],
            [SMEM, VMEM, VMEM] + [ANY] * 4,
            [pltpu.VMEM((rows_all, 3 * model), F32)] + scratch,
            "attend_back",
            (VMEM, ANY, ANY),
        )
        return grad_qkv, on

    def run_leave(
        joint, grad_qkv, packed, grad_hidden, mod, slots, live, mod_grads, gate_m, biases
    ):
        weights, offsets = joint
        result = call(
            functools.partial(leave_kernel, len(weights), seq_count, cap),
            tuple(sds((group, most, model), BF) for _ in range(seq_count))
            + (sds((group + 1, 6 * model), BF),),
            [
                offsets,
                parity_in,
                live,
                grad_qkv,
                packed,
                grad_hidden,
                mod,
                slots,
                mod_grads,
                gate_m,
                *biases,
                *weights,
            ],
            [SMEM, SMEM, SMEM] + [VMEM] * 9 + [ANY] * len(weights),
            [
                pltpu.VMEM((model, 3 * model), BF),
                pltpu.VMEM((8, 6 * model), F32),
                pltpu.SemaphoreType.DMA((3, len(weights))),
            ],
            "leave",
        )
        return result[:seq_count], result[seq_count]

    def split_sums(sums):
        units = jnp.swapaxes(
            sums[1, :hidden_units].reshape(2, BLOCKS // 2, unit_rows), 0, 1
        ).reshape(hidden_units)
        digits = sums[1, hidden_units : hidden_units + 3 * group].reshape(group, 3)
        kept = jnp.sum(digits * jnp.array([1.0, 8.0, 64.0], F32))
        return sums[0], units, kept.reshape(1).astype(jnp.int32)

    def sums_of(gathered):
        wide = gathered.astype(F32)
        total = jnp.stack([jnp.sum(wide[:, :group], axis=1), wide[:, group]], axis=1)
        while total.shape[0] > 1:
            total = total.reshape((total.shape[0] // 2, 2) + total.shape[1:])
            total = total[:, 0] + total[:, 1]
        return total[0]

    def seq_columns(grad_mod_all):
        return in_order(
            jnp.stack(
                [
                    grad_mod_all[:, :, j * column_share : (j + 1) * column_share]
                    for j in range(seq_count)
                ]
            ),
            "seq",
        )

    def cond_product(grad_mod_all):
        return dot(grad_mod_all.reshape(dp_count * group, 6 * model), ada_weight, NT).reshape(
            dp_count, group, share
        )

    def ada_product(silu_all, columns):
        return dot(
            silu_all.reshape(seq_count * dp_count * group, share),
            columns.reshape(seq_count * dp_count * group, column_share),
            TN,
        )

    def cond_end(rows):
        rows = in_order(rows, "seq").reshape(latent_count, model)
        _, silu_back = jax.vjp(jax.nn.silu, cond_wide)
        return silu_back(rows)[0]

    def cond_mine_of(cols):
        return jnp.swapaxes(in_order(cols, "dp"), 0, 1).reshape(group, model)

    if not paired:
        order = order_of(parity)
        live, place_row, slots = places_of(gather_all(rank, "seq"))
        silu_rows, silu_all = silu_of(trade_all(silu_parts, "dp"))
        mod = whole_mod(sum_own(partial_mod(silu_rows), "dp"))
        to_whole = lambda v: [
            swap(whole_slice(v, k), "seq", k) if k else whole_slice(v, k)
            for k in range(seq_count)
        ]
        latent_pieces, cot_pieces = to_whole(latents), to_whole(cotangent)
        joint = whole_weight(jnp.concatenate([qkv_weight, out_weight], axis=1))
        joint = [joint], jnp.zeros((1,), jnp.int32)
        first = [whole_weight(unit_order(fc1_weight))], jnp.zeros((1,), jnp.int32)
        full = whole_weight(fc2_weight)
        second = placed(
            [(full[k * unit_rows : (k + 1) * unit_rows], k, 0) for k in range(BLOCKS)],
            unit_position,
            unit_rows,
        ) + (tuple(k & 1 for k in range(BLOCKS)),)
        packed, qkv, *mixa = run_enter(joint, place_row, mod, latent_pieces, order)
        grad_out, grad_mlp = run_cot(place_row, mod, cot_pieces)
        att_own, att_other, projected, hidden, mixed, *mixm = run_attend(
            joint, live, qkv, packed, mod, order
        )
        acts = run_first(first, mixed)
        *pres, bias_own, bias_other = run_slope(second, acts[2:], grad_mlp)
        none = [jnp.zeros((16, LANES), BF)] * 7
        block_pieces, gate_m_grad, _ = run_second(
            second, acts[:2], grad_out, hidden, mod, slots, none, none[:2]
        )
        grad_hidden, grad_proj, grad_att, mod_grads = run_hidden(
            first, joint, pres, hidden, projected, grad_out, mod
        )
        grad_qkv, _ = run_attend_back(live, qkv, grad_att, none, none[:2])
        latent_grads, payload = run_leave(
            joint,
            grad_qkv,
            packed,
            grad_hidden,
            mod,
            slots,
            live,
            mod_grads,
            gate_m_grad,
            (bias_own, bias_other),
        )
        gathered = gather_all(payload, "dp")
        grad_mod_all = gathered[:, :group]
        sums = sums_of(gathered)
        for step in steps_of("seq"):
            sums = sums + swap(sums, "seq", step)
        ada_bias_grad, fc1_bias_grad, kept_total = split_sums(sums)
        ada_grad = ada_product(silu_all, trade_all(seq_columns(grad_mod_all), "seq"))
        cond_cols = trade_all(cond_product(grad_mod_all), "dp")
        condition_grad = cond_end(gather_all(cond_mine_of(cond_cols), "seq"))

        def mixed_sides(own, other, width):
            both = jnp.stack([own[:, : 4 * width], other[:, : 4 * width]], axis=1)
            return jnp.swapaxes(both.reshape(rows_all, 2, 4, width), 1, 2).reshape(
                rows_all, BLOCKS * width
            )

        product = lambda a, b: spread_plain(dot(a, b, TN))
        fc2_grad = product(mixed_sides(acts[0], acts[1], unit_rows), grad_mlp)
        fc1_grad = product(
            mixed_sides(*mixm, model_rows), mixed_sides(pres[0], pres[1], unit_rows)
        )
        out_grad = product(mixed_sides(att_own, att_other, model_rows), grad_proj)
        qkv_grad = product(mixed_sides(*mixa, model_rows), grad_qkv)
        home = lambda pieces: [swap(v, "seq", k) if k else v for k, v in enumerate(pieces)]
        block_out = run_home(home(block_pieces), latents, BF, "home_out")
        latents_grad = run_home(home(latent_grads), cotangent, F32, "home_grad")
        return (
            block_out,
            latents_grad,
            condition_grad,
            ada_grad,
            ada_bias_grad,
            qkv_grad,
            out_grad,
            fc1_grad,
            fc1_bias_grad,
            fc2_grad,
            kept_total,
        )

    def trade(value, axis, step):
        split = value.reshape((-1, 2, step) + value.shape[1:])
        return jnp.stack([split[:, 0], swap(split[:, 1], axis, step)], axis=1).reshape(value.shape)

    def grow(value, axis, step):
        return jnp.concatenate([value, swap(value, axis, step)], axis=0)

    def columns_first(parts):
        sent, own, across = parts
        return swap(sent, "seq", 1), own, across

    def columns_second(state):
        near, own, across = state
        on = (across.astype(F32) + near[1].astype(F32)).astype(BF)
        return swap(on, "seq", 2), own, near

    def columns_sum(state):
        far, own, near = state
        return own.astype(F32) + near[0].astype(F32) + far.astype(F32)

    def tails(beside, first):
        rows, width = beside[0].shape
        return call(
            functools.partial(cut_kernel, first),
            (sds((first, width), BF), sds((rows - first, width), BF)),
            [beside[1], beside[0]],
            [ANY, ANY],
            [pltpu.VMEM((first, width), BF), pltpu.VMEM((rows - first, width), BF), dma(2), dma(2)],
            "cut",
            (ANY, ANY),
        )

    joint_own = jnp.concatenate([qkv_weight, out_weight], axis=1)

    corners_of = lambda value: [swap(value[q], "dp", 2 * q) for q in (1, 2, 3)]

    corners = silu_parts.reshape(4, 2, latent_count, share)
    corners = jnp.stack([corners[0], *corners_of(corners)])
    ranks = grow(rank[None], "seq", 1)
    corners, joint_own, fc1_in, latents_in, cot_in, ranks, parity_late = fence(
        corners, joint_own, fc1_weight, latents, cotangent, ranks, parity
    )

    joint_beside = beside_of(joint_own)
    ranks = grow(ranks, "seq", 2)
    latent_pieces = [whole_slice(latents_in, k) for k in range(seq_count)]
    latent_1 = swap(latent_pieces[1], "seq", 1)
    latent_2 = swap(latent_pieces[2], "seq", 2)
    silu_corners = trade(corners.reshape(8, latent_count, share), "dp", 1)
    silu_rows, silu_all = silu_of(silu_corners)
    silu_all = jnp.swapaxes(silu_all.reshape(seq_count, 4, 2, group, share), 1, 2)
    pairs = partial_mod(silu_rows).reshape(4, 2, group, 6 * model)
    corners = pairs[:, 0] + swap(pairs[:, 1], "dp", 1)
    parity_late, fc1_in, cot_in = after((parity_late, fc1_in, cot_in), corners)
    order = order_of(parity_late)
    first_own = call(
        functools.partial(reorder_kernel, unit_rows),
        sds(fc1_in.shape, BF),
        [fc1_in],
        [VMEM],
        [],
        "reorder",
    )
    cot_pieces = [whole_slice(cot_in, k) for k in range(seq_count)]
    (
        joint_beside,
        latent_1,
        latent_2,
        latent_last,
        silu_all,
        corners,
        joint_own,
        order,
        first_own,
        cot_pieces,
        ranks,
    ) = fence(
        joint_beside,
        latent_1,
        latent_2,
        latent_pieces[3],
        silu_all,
        corners,
        joint_own,
        order,
        first_own,
        cot_pieces,
        ranks,
    )

    sums = corners_of(corners)
    joint_tails = tails(joint_beside, part)
    sums, joint_tails, joint_beside, joint_own, ranks, latent_last = fence(
        sums, joint_tails, joint_beside, joint_own, ranks, latent_last
    )
    latent_3 = swap(latent_last, "seq", 3)
    joint_across = (swap(joint_tails[0], "dp", 2), swap(joint_tails[1], "dp", 4))
    mod = whole_mod(sum(sums, corners[0]))
    joint_pair, joint_x_pair, joint_y_pair = pair_of((joint_own, *joint_beside))
    live, place_row, slots = places_of(ranks)
    (
        joint_across,
        latent_3,
        mod,
        joint_pair,
        joint_x_pair,
        joint_y_pair,
        live,
        place_row,
        slots,
        first_own,
        cot_pieces,
    ) = fence(
        joint_across,
        latent_3,
        mod,
        joint_pair,
        joint_x_pair,
        joint_y_pair,
        live,
        place_row,
        slots,
        first_own,
        cot_pieces,
    )

    first_beside = beside_of(first_own)
    cot_1 = swap(cot_pieces[1], "seq", 1)
    cot_2 = swap(cot_pieces[2], "seq", 2)
    cot_3 = swap(cot_pieces[3], "seq", 3)
    joint = placed(
        pieces_of(
            joint_own,
            joint_pair,
            joint_beside,
            (joint_x_pair, joint_y_pair),
            joint_across,
            pair_of(joint_across),
            part,
        ),
        model_position,
        model_rows,
    )
    packed, qkv, mixa_own, mixa_other = run_enter(
        joint, place_row, mod, (latent_pieces[0], latent_1, latent_2, latent_3), order
    )
    att_own, att_other, projected, hidden, mixed, mixm_own, mixm_other = run_attend(
        joint, live, qkv, packed, mod, order
    )
    first_beside, cot_1, cot_2, cot_3, mixed, first_own = fence(
        first_beside, cot_1, cot_2, cot_3, mixed, first_own
    )

    first_tails = tails(first_beside, part)
    first_across = (swap(first_tails[0], "dp", 2), swap(first_tails[1], "dp", 4))
    first_pair, first_x_pair, first_y_pair = pair_of((first_own, *first_beside))
    grad_out, grad_mlp = run_cot(place_row, mod, (cot_pieces[0], cot_1, cot_2, cot_3))
    second_own = (fc2_weight[:unit_part], fc2_weight[unit_part:])
    (
        first_across,
        first_pair,
        first_x_pair,
        first_y_pair,
        grad_out,
        grad_mlp,
        second_own,
        second_in,
    ) = fence(
        first_across,
        first_pair,
        first_x_pair,
        first_y_pair,
        grad_out,
        grad_mlp,
        second_own,
        fc2_weight,
    )

    second_ahead = swap(second_own[1], "dp", 2), swap(second_own[0], "dp", 4)
    first = placed(
        pieces_of(
            first_own,
            first_pair,
            first_beside,
            (first_x_pair, first_y_pair),
            first_across,
            pair_of(first_across),
            part,
        ),
        model_position,
        model_rows,
    )
    (grad_mlp_pair,) = pair_of((grad_mlp,))
    acts = run_first(first, mixed)
    second_ahead, second_own, grad_mlp_pair, acts = fence(
        second_ahead, second_own, grad_mlp_pair, acts
    )

    second_behind = swap(second_own[0], "dp", 2), swap(second_own[1], "dp", 4)
    (second_pair,) = pair_of((second_in,))
    (act_pair,) = pair_of((acts[1],))
    fc2_cut = outer_pair(
        [((acts[0], act_pair), [(grad_mlp, grad_mlp_pair)])], unit_rows, "fc2_grad"
    )
    second_behind, second_pair, second_ahead, fc2_cut, mixm_other, att_other, mixa_other = fence(
        second_behind, second_pair, second_ahead, fc2_cut, mixm_other, att_other, mixa_other
    )

    second_across = swap(second_ahead[1], "dp", 2), swap(second_ahead[0], "dp", 4)
    second_ahead_pair, second_behind_pair = pair_of(second_ahead), pair_of(second_behind)
    mixm_pair, att_pair, mixa_pair = pair_of((mixm_other, att_other, mixa_other))
    (
        second_across,
        second_ahead_pair,
        second_behind_pair,
        mixm_pair,
        att_pair,
        mixa_pair,
        fc2_cut,
        acts,
    ) = fence(
        second_across,
        second_ahead_pair,
        second_behind_pair,
        mixm_pair,
        att_pair,
        mixa_pair,
        fc2_cut,
        acts,
    )

    fc2_far = along_xy(fc2_cut[:2])
    pieces = [(second_in, 0, 0), (second_pair, 1, 0)]
    for side, ahead, behind, beyond in (
        (0, second_ahead, second_behind, second_across),
        (1, second_ahead_pair, second_behind_pair, pair_of(second_across)),
    ):
        pieces += [
            (behind[0], 2 + side, 0),
            (ahead[0], 2 + side, unit_part),
            (ahead[1], 4 + side, 0),
            (behind[1], 4 + side, unit_part),
            (beyond[0], 6 + side, 0),
            (beyond[1], 6 + side, unit_part),
        ]
    second = placed(pieces, unit_position, unit_rows) + (tuple(k & 1 for _, k, _ in pieces),)
    pre_own, pre_other, bias_own, bias_other = run_slope(second, acts[2:], grad_mlp)
    fc2_far, fc2_cut, pre_own, pre_other, acts = fence(
        fc2_far, fc2_cut, pre_own, pre_other, acts
    )

    fc2_near = along_xy(fc2_cut[2:4])
    pre_other_pair, pre_own_pair = pair_of((pre_own, pre_other))
    block_pieces, gate_m_grad, on = run_second(
        second, acts[:2], grad_out, hidden, mod, slots, fc2_cut, fc2_far
    )
    fc2_near, on, pre_other_pair, pre_own_pair, block_pieces, gate_m_grad = fence(
        fc2_near, on, pre_other_pair, pre_own_pair, block_pieces, gate_m_grad
    )

    fc2_last = along_xy(on)
    block_1 = swap(block_pieces[1], "seq", 1)
    block_2 = swap(block_pieces[2], "seq", 2)
    fc1_cut = outer_pair(
        [((mixm_own, mixm_pair), [(pre_own, pre_own_pair), (pre_other, pre_other_pair)])],
        model_rows,
        "fc1_grad",
    )
    fc2_last, block_1, block_2, block_3, fc1_cut, pre_own, pre_other, fc2_near = fence(
        fc2_last, block_1, block_2, block_pieces[3], fc1_cut, pre_own, pre_other, fc2_near
    )

    fc1_far = along_xy(fc1_cut[:2])
    block_3 = swap(block_3, "seq", 3)
    grad_hidden, grad_proj, grad_att, mod_grads = run_hidden(
        first, joint, (pre_own, pre_other), hidden, projected, grad_out, mod
    )
    fc1_far, fc1_cut, grad_proj, grad_att, block_3, fc2_near, fc2_last = fence(
        fc1_far, fc1_cut, grad_proj, grad_att, block_3, fc2_near, fc2_last
    )

    fc1_near = along_xy(fc1_cut[2:4])
    (proj_pair,) = pair_of((grad_proj,))
    fc2_parts = fold(
        fc2_cut[4],
        fc2_near,
        fc2_last,
        (plain_cuts(0, model, seq_count),),
        "fc2_fold",
        True,
    )
    grad_qkv, on = run_attend_back(after(live, fc2_parts), qkv, grad_att, fc1_cut, fc1_far)
    fc1_near, on, fc2_parts, proj_pair, grad_qkv = fence(
        fc1_near, on, fc2_parts, proj_pair, grad_qkv
    )

    fc1_last = along_xy(on)
    (qkv_pair,) = pair_of((grad_qkv,))
    fc2_state = columns_first(fc2_parts)
    latent_grads, payload = run_leave(
        joint,
        grad_qkv,
        packed,
        grad_hidden,
        mod,
        slots,
        live,
        mod_grads,
        gate_m_grad,
        (bias_own, bias_other),
    )
    fc1_last, qkv_pair, latent_grads, payload, fc1_near, grad_qkv, fc2_state = fence(
        fc1_last, qkv_pair, latent_grads, payload, fc1_near, grad_qkv, fc2_state
    )

    corners = [payload] + [swap(payload, "dp", 2 * q) for q in (1, 2, 3)]
    latent_1 = swap(latent_grads[1], "seq", 1)
    latent_2 = swap(latent_grads[2], "seq", 2)
    last_cut = outer_pair(
        [
            ((mixa_own, mixa_pair), [(grad_qkv, qkv_pair)]),
            ((att_own, att_pair), [(grad_proj, proj_pair)]),
        ],
        model_rows,
        "last_grad",
    )
    corners, latent_1, latent_2, last_cut, fc1_last, block_pieces, fc2_state = fence(
        corners, latent_1, latent_2, last_cut, fc1_last, block_pieces, fc2_state
    )

    last_far = along_xy(last_cut[:2])
    corner_pairs = pair_of(corners)
    fc1_cuts = tuple(
        tuple((lo, lo + unit_rows) for lo in (j * unit_rows, half_units + j * unit_rows))
        for j in range(seq_count)
    )
    fc1_parts = fold(fc1_cut[4], fc1_near, fc1_last, (fc1_cuts,), "fc1_fold")
    fc2_state = columns_second(fc2_state)
    rows_here = 8 * group
    cond_own, cond_pair, column_sent, column_own, column_across, sums = call(
        functools.partial(spread_kernel, 4),
        (
            sds((rows_here // 2, share), F32),
            sds((rows_here // 2, share), F32),
            sds((2, rows_here, column_share), BF),
            sds((rows_here, column_share), BF),
            sds((rows_here, column_share), BF),
            sds((2 * seq_count, column_share), F32),
        ),
        [*corners, *corner_pairs, seq_at.reshape(1).astype(jnp.int32), ada_weight],
        [VMEM] * 8 + [SMEM, VMEM],
        [
            pltpu.VMEM((rows_here, 6 * model), F32),
            pltpu.VMEM((seq_count, rows_here, column_share), BF),
            pltpu.VMEM((8, 6 * model), F32),
            dma(seq_count),
        ],
        "spread",
        (VMEM, VMEM, ANY, ANY, ANY, VMEM),
    )
    (
        last_far,
        last_cut,
        cond_own,
        cond_pair,
        column_sent,
        sums,
        fc1_parts,
        block_pieces,
        latent_3,
        fc2_state,
    ) = fence(
        last_far,
        last_cut,
        cond_own,
        cond_pair,
        column_sent,
        sums,
        fc1_parts,
        block_pieces,
        latent_grads[3],
        fc2_state,
    )

    last_near = along_xy(last_cut[2:4])
    on = onward(last_cut, last_far)
    (cond_pair,) = pair_of((cond_pair,))
    sums = sums.astype(BF)
    column_sent = jnp.concatenate([column_sent, jnp.stack([sums, sums])], axis=1)
    fc1_state = columns_first(fc1_parts)
    latent_3 = swap(latent_3, "seq", 3)
    block_out = run_home(
        after((block_pieces[0], block_1, block_2, block_3), on), latents, BF, "home_out"
    )
    last_near, on, sums, column_sent, cond_pair, fc1_state, latent_3, block_out = fence(
        last_near, on, sums, column_sent, cond_pair, fc1_state, latent_3, block_out
    )

    last_last = along_xy(on)
    fc1_state = columns_second(fc1_state)
    column_near = swap(column_sent, "seq", 1)
    (
        last_last,
        sums,
        column_near,
        fc1_state,
        fc2_state,
        last_near,
        cond_own,
        cond_pair,
        latent_3,
    ) = fence(
        last_last,
        sums,
        column_near,
        fc1_state,
        fc2_state,
        last_near,
        cond_own,
        cond_pair,
        latent_3,
    )

    qkv_share, out_share = 3 * model // seq_count, model // seq_count
    last_cuts = tuple(
        (
            (j * qkv_share, (j + 1) * qkv_share),
            (3 * model + j * out_share, 3 * model + (j + 1) * out_share),
        )
        for j in range(seq_count)
    )
    last_parts = fold(last_cut[4], last_near, last_last, (last_cuts,), "last_fold")
    last_state = columns_first(last_parts)
    cond_own, cond_pair = after((cond_own, cond_pair), last_parts)
    cond_cols = jnp.stack([cond_own, cond_pair], axis=1).reshape(4, group, 2, share)
    cond_cols = jnp.swapaxes(cond_cols, 1, 2)
    cond_cols = jnp.stack([cond_cols[0], *corners_of(cond_cols)])
    cond_mine = cond_mine_of(cond_cols.reshape(8, group, share))
    cond_rows = [swap(cond_mine, "seq", k) if k else cond_mine for k in range(seq_count)]
    condition_grad = cond_end(jnp.stack(cond_rows))
    sums, column_near, fc1_state, fc2_state = after(
        (sums, column_near, fc1_state, fc2_state), cond_mine
    )
    sums = (sums.astype(F32) + column_near[0, rows_here:].astype(F32)).astype(BF)
    column_far = swap(
        jnp.stack([jnp.concatenate([column_across, sums], axis=0), column_near[1]]), "seq", 2
    )
    sums = sums.astype(F32) + column_far[0, rows_here:].astype(F32)
    column_far, column_near = column_far[:, :rows_here], column_near[:, :rows_here]
    columns = jnp.stack([column_own, column_near[0], column_far[0], column_far[1]])
    ada_grad = ada_product(silu_all, columns)
    fc2_grad = columns_sum(fc2_state).T
    fc1_grad = columns_sum(fc1_state)
    fc1_grad = jnp.where(
        parity == 1,
        jnp.concatenate([fc1_grad[:, unit_rows:], fc1_grad[:, :unit_rows]], axis=1),
        fc1_grad,
    )
    last_state, condition_grad, sums, ada_grad, fc1_grad, fc2_grad, latent_3 = fence(
        last_state, condition_grad, sums, ada_grad, fc1_grad, fc2_grad, latent_3
    )

    latents_grad = run_home(
        (latent_grads[0], latent_1, latent_2, latent_3), cotangent, F32, "home_grad"
    )
    far, own, near = columns_second(last_state)
    qkv_grad = columns_sum((far[:, :qkv_share], own[:, :qkv_share], near[:, :, :qkv_share]))
    out_grad = columns_sum((far[:, qkv_share:], own[:, qkv_share:], near[:, :, qkv_share:]))
    ada_bias_grad, fc1_bias_grad, kept_total = split_sums(sums.reshape(2, 6 * model))
    return (
        block_out,
        latents_grad,
        condition_grad,
        ada_grad,
        ada_bias_grad,
        qkv_grad,
        out_grad,
        fc1_grad,
        fc1_bias_grad,
        fc2_grad,
        kept_total,
    )


def solution(mesh):
    placed = (
        P("dp", "seq", None),
        P("dp", None),
        P("dp", "seq"),
        P("dp", "seq"),
        P("dp", None),
        P(),
        P("dp", None),
        P("dp", None),
        P("dp", None),
        P(),
        P("dp", None),
        P("dp", "seq", None),
    )
    return jax.shard_map(
        body,
        mesh=mesh,
        in_specs=placed,
        out_specs=(
            P("dp", "seq", None),
            P("dp", "seq", None),
            P("dp", None),
            P("dp", "seq"),
            P(),
            P("dp", "seq"),
            P("dp", "seq"),
            P("dp", "seq"),
            P(),
            P("dp", "seq"),
            P(),
        ),
        check_vma=False,
    )
```

```python
import functools
import math

import jax
import jax.numpy as jnp
from jax import lax
from jax.experimental import pallas as pl
from jax.experimental.pallas import tpu as pltpu
from jax.sharding import PartitionSpec as P

HEADS = 16
HEAD = 72
LANES = 128
BLOCKS = 8

layer_eps = 1e-06
far_below = -1e30
att_scale = 1.0 / math.sqrt(HEAD)
exp2_scale = att_scale / math.log(2.0)
gelu_c = math.sqrt(2.0 / math.pi)
gelu_k = 0.044715

BF = jnp.bfloat16
F32 = jnp.float32
VMEM = pl.BlockSpec(memory_space=pltpu.VMEM)
SMEM = pl.BlockSpec(memory_space=pltpu.SMEM)
ANY = pl.BlockSpec(memory_space=pl.ANY)
NT = (((1,), (1,)), ((), ()))
TN = (((0,), (0,)), ((), ()))


def swap(value, axis, step):
    return lax.ppermute(value, axis, [(i, i ^ step) for i in range(lax.axis_size(axis))])


def steps_of(axis):
    count = lax.axis_size(axis)
    return [1 << i for i in range(count.bit_length() - 1)]


def bit_set(axis, step):
    return (lax.axis_index(axis) & step) != 0


def gather_all(value, axis):
    value = value[None]
    for step in steps_of(axis):
        value = jnp.concatenate([value, swap(value, axis, step)], axis=0)
    return value


def sum_own(value, axis):
    for step in reversed(steps_of(axis)):
        value = value[:step] + swap(value[step:], axis, step)
    return value[0]


def trade_all(value, axis):
    count = value.shape[0]
    rest = value.shape[1:]
    for step in steps_of(axis):
        split = value.reshape((count // (2 * step), 2, step) + rest)
        value = jnp.stack([split[:, 0], swap(split[:, 1], axis, step)], axis=1).reshape(
            (count,) + rest
        )
    return value


def in_order(value, axis):
    count = value.shape[0]
    rest = value.shape[1:]
    for step in steps_of(axis):
        split = value.reshape((count // (2 * step), 2, step) + rest)
        value = jnp.where(bit_set(axis, step), split[:, ::-1], split).reshape((count,) + rest)
    return value


def sum_everywhere(value):
    for axis in ("dp", "seq"):
        for step in steps_of(axis):
            value = value + swap(value, axis, step)
    return value


def after(value, *earlier):
    return lax.optimization_barrier((value,) + earlier)[0]


def halves_of(rows):
    first = (rows // 2 + 15) // 16 * 16
    return first, rows - first


def pieces_of(own, own_pair, beside, beside_pair, across, across_pair, part):
    return [
        (own, 0, 0),
        (own_pair, 1, 0),
        (beside[0], 2, 0),
        (beside_pair[0], 3, 0),
        (beside[1], 4, 0),
        (beside_pair[1], 5, 0),
        (across[0], 6, 0),
        (across[1], 6, part),
        (across_pair[0], 7, 0),
        (across_pair[1], 7, part),
    ]


def beside_of(shard):
    return swap(shard, "dp", 2), swap(shard, "dp", 4)


def across_of(beside, part):
    return swap(beside[1][:part], "dp", 2), swap(beside[0][part:], "dp", 4)


def pair_of(values):
    return tuple(swap(v, "dp", 1) for v in values)


def placed(pieces, position, rows):
    starts = jnp.stack([position(k) * rows + first for _, k, first in pieces]).astype(jnp.int32)
    return [v for v, _, _ in pieces], starts


def whole_weight(shard):
    return lax.all_gather(shard, "dp", axis=0, tiled=True)


def call(kernel, outs, ins, specs, scratch, name, out_specs=None):
    return pl.pallas_call(
        kernel,
        out_shape=outs,
        in_specs=specs,
        out_specs=out_specs or jax.tree.map(lambda _: VMEM, outs),
        scratch_shapes=scratch,
        name=name,
        compiler_params=pltpu.CompilerParams(vmem_limit_bytes=60 * 1024 * 1024),
    )(*ins)


def start_pieces(offsets, refs, target, sem, lo, hi):
    copies = []
    shift = lo if target.shape[1] == hi - lo else 0
    for k, ref in enumerate(refs):
        rows = ref.shape[0]
        copies.append(
            pltpu.make_async_copy(
                ref.at[:, pl.ds(lo, hi - lo)],
                target.at[pl.ds(pl.multiple_of(offsets[k], 16), rows), pl.ds(lo - shift, hi - lo)],
                sem.at[k],
            )
        )
    for one in copies:
        one.start()
    return copies


def wait_all(copies):
    for one in copies:
        one.wait()


def normal(rows_in):
    center = rows_in - jnp.mean(rows_in, axis=-1, keepdims=True)
    inverse = lax.rsqrt(jnp.mean(center * center, axis=-1, keepdims=True) + layer_eps)
    return center * inverse, inverse


def normal_back(grad_rows, normed, inverse):
    mean_grad = jnp.mean(grad_rows, axis=-1, keepdims=True)
    mean_proj = jnp.mean(grad_rows * normed, axis=-1, keepdims=True)
    return inverse * (grad_rows - mean_grad - normed * mean_proj)


def dot(left, right, dims=None):
    if dims is None:
        return jnp.dot(left, right, preferred_element_type=F32)
    return lax.dot_general(left, right, dims, preferred_element_type=F32)


def spans(total, width):
    return [(lo, min(lo + width, total)) for lo in range(0, total, width)]


def pack_rows(place_ref, piece_refs, latent, rows_out):
    gathered = jnp.concatenate([ref[latent] for ref in piece_refs], axis=0)
    slots = lax.broadcasted_iota(jnp.int32, (rows_out, gathered.shape[0]), 0)
    chosen = jnp.where(place_ref[latent] == slots, 1.0, 0.0).astype(BF)
    return dot(chosen, gathered)


def unpack_rows(slots_ref, latent, packed, out_refs):
    slots = slots_ref[latent]
    rows = lax.broadcasted_iota(jnp.int32, (slots.shape[0], packed.shape[0]), 1)
    spread = dot(jnp.where(slots == rows, 1.0, 0.0).astype(BF), packed).astype(BF)
    block = out_refs[0].shape[1]
    for k, out in enumerate(out_refs):
        out[latent] = spread[k * block : (k + 1) * block]


def home_kernel(at, rank, base, *refs):
    pieces, out = refs[:-1], refs[-1]
    group, slots, _ = pieces[0].shape
    for k, piece in enumerate(pieces):
        for j in range(group):
            latent = (at[0] ^ k) * group + j
            place = rank[latent]
            rows = lax.broadcasted_iota(jnp.int32, (place.shape[0], slots), 1)
            spread = dot(jnp.where(place == rows, 1.0, 0.0).astype(BF), piece[j])
            out[latent] = jnp.where(place >= 0, spread, base[latent].astype(F32)).astype(out.dtype)


def cut_kernel(first, top, bottom, top_out, bottom_out, top_held, bottom_held, load_sem, store_sem):
    rows = bottom.shape[0]
    loads = [
        pltpu.make_async_copy(top.at[pl.ds(0, first), :], top_held, load_sem.at[0]),
        pltpu.make_async_copy(bottom.at[pl.ds(first, rows - first), :], bottom_held, load_sem.at[1]),
    ]
    stores = [
        pltpu.make_async_copy(top_held, top_out, store_sem.at[0]),
        pltpu.make_async_copy(bottom_held, bottom_out, store_sem.at[1]),
    ]
    for one in loads:
        one.start()
    for load, store in zip(loads, stores):
        load.wait()
        store.start()
    wait_all(stores)


def split_parity(rows_low, order_ref, own_ref, other_ref):
    moved = dot(rows_low, order_ref[...]).astype(BF)
    width = own_ref.shape[1]
    own_ref[...] = moved[:, :width]
    other_ref[...] = moved[:, width:]


def enter_kernel(pieces, blocks, cap, *refs):
    (offsets, place, mod, order), refs = refs[:4], refs[4:]
    latents, refs = refs[:blocks], refs[blocks:]
    weights, refs = refs[:pieces], refs[pieces:]
    packed_out, qkv_out, own_out, other_out, weight, mixed, sem = refs
    width = qkv_out.shape[1]
    chunks = spans(width, width // 3)
    loads = [
        start_pieces(offsets, weights, weight, sem.at[i], lo, hi) for i, (lo, hi) in enumerate(chunks)
    ]
    for latent in range(mod.shape[0]):
        here = pl.ds(latent * cap, cap)
        rows = pack_rows(place, latents, latent, cap)
        packed_out[here, :] = rows.astype(BF)
        normed, _ = normal(rows)
        mixed[here, :] = (normed * (1.0 + mod[latent, 1:2, :]) + mod[latent, 0:1, :]).astype(BF)
    split_parity(mixed[...], order, own_out, other_out)
    for i, (lo, hi) in enumerate(chunks):
        wait_all(loads[i])
        qkv_out[:, lo:hi] = dot(mixed[...], weight[:, lo:hi]).astype(BF)


def cot_kernel(cap, place, mod, *refs):
    cots, (packed_out, mlp_out) = refs[:-2], refs[-2:]
    for latent in range(mod.shape[0]):
        here = pl.ds(latent * cap, cap)
        rows = pack_rows(place, cots, latent, cap)
        packed_out[here, :] = rows.astype(BF)
        mlp_out[here, :] = (mod[latent, 5:6, :] * rows).astype(BF)


def windows():
    found = []
    for head in range(HEADS):
        first = head * HEAD
        base = first // LANES * LANES
        width = LANES if first + HEAD <= base + LANES else 2 * LANES
        found.append((base, width, first - base))
    return found[::2] + found[1::2]


def head_mask(width, first, dtype):
    lane = lax.broadcasted_iota(jnp.int32, (1, width), 1)
    return jnp.where((lane >= first) & (lane < first + HEAD), 1.0, 0.0).astype(dtype)


def attend_kernel(pieces, cap, model, *refs):
    (offsets, live, qkv, packed, mod, order), refs = refs[:6], refs[6:]
    weights, refs = refs[:pieces], refs[pieces:]
    (own_att, other_att, proj_out, hidden_out, mixed_out, own_mix, other_mix), refs = (
        refs[:7],
        refs[7:],
    )
    weight, attended, sem = refs
    copies = start_pieces(offsets, weights, weight, sem, 3 * model, 4 * model)
    attended[...] = jnp.zeros_like(attended)

    def one_latent(latent, carry):
        here = pl.ds(pl.multiple_of(latent * cap, 16), cap)
        count = live[latent]
        seen = lax.broadcasted_iota(jnp.int32, (cap, cap), 1) < count
        for base, width, first in windows():
            low_mask = head_mask(width, first, BF)
            query = qkv[here, base : base + width] * low_mask
            key = qkv[here, model + base : model + base + width]
            value = qkv[here, 2 * model + base : 2 * model + base + width] * low_mask
            scores = jnp.where(seen, dot(query, key, NT), far_below)
            raised = jnp.exp2((scores - jnp.max(scores, axis=-1, keepdims=True)) * exp2_scale)
            share = 1.0 / jnp.sum(raised, axis=-1, keepdims=True)
            attended[here, base : base + width] += dot(raised.astype(BF), value) * share
        return carry

    lax.fori_loop(0, mod.shape[0], one_latent, 0)
    att_low = attended[...].astype(BF)
    split_parity(att_low, order, own_att, other_att)
    wait_all(copies)
    projected = dot(att_low, weight[...])
    proj_out[...] = projected
    for latent in range(mod.shape[0]):
        rows = slice(latent * cap, (latent + 1) * cap)
        hidden = packed[rows, :].astype(F32) + mod[latent, 2:3, :] * projected[rows]
        hidden_out[rows, :] = hidden
        normed, _ = normal(hidden)
        mixed_out[rows, :] = (
            normed * (1.0 + mod[latent, 4:5, :]) + mod[latent, 3:4, :]
        ).astype(BF)
    split_parity(mixed_out[...], order, own_mix, other_mix)


def unit_chunks(parity, half):
    found = []
    for side in (0, 1):
        base = (parity[0] ^ side) * half
        for lo, hi in spans(half, 768):
            found.append((side, lo, hi, pl.ds(pl.multiple_of(base + lo, LANES), hi - lo)))
    return found


def start_chunks(offsets, refs, target, sem, chunks):
    found = []
    for i, (_, _, _, cols) in enumerate(chunks):
        found.append(
            [
                pltpu.make_async_copy(
                    ref.at[:, cols],
                    target.at[pl.ds(pl.multiple_of(offsets[k], 16), ref.shape[0]), cols],
                    sem.at[i, k],
                )
                for k, ref in enumerate(refs)
            ]
        )
        for one in found[-1]:
            one.start()
    return found


def first_kernel(pieces, offsets, parity, mixed, bias, *refs):
    weights, refs = refs[:pieces], refs[pieces:]
    acts, slopes = refs[0:2], refs[2:4]
    weight, act, slope, load_sem, act_sem, slope_sem = refs[4:]
    half = acts[0].shape[1]
    chunks = unit_chunks(parity, half)
    loads = start_chunks(offsets, weights, weight, load_sem, chunks)
    stores = []
    for i, (side, lo, hi, cols) in enumerate(chunks):
        wait_all(loads[i])
        pre = dot(mixed[...], weight[:, cols]) + bias[:, cols]
        square = pre * pre
        curve = jnp.tanh(pre * (gelu_c + (gelu_c * gelu_k) * square))
        cdf = 0.5 + 0.5 * curve
        act[side, :, lo:hi] = (pre * cdf).astype(BF)
        bend = (0.5 * gelu_c) + (1.5 * gelu_c * gelu_k) * square
        slope[side, :, lo:hi] = (cdf + pre * bend * (1.0 - curve * curve)).astype(BF)
        here = pl.ds(lo, hi - lo)
        for held, out, sem in ((act, acts, act_sem), (slope, slopes, slope_sem)):
            stores.append(
                pltpu.make_async_copy(held.at[side, :, here], out[side].at[:, here], sem.at[i])
            )
            stores[-1].start()
    wait_all(stores)


def start_halves(offsets, refs, sides, target, sem):
    found = ([], [])
    for side in (0, 1):
        for k, ref in enumerate(refs):
            if sides[k] != side:
                continue
            rows = ref.shape[0]
            found[side].append(
                pltpu.make_async_copy(
                    ref, target.at[pl.ds(pl.multiple_of(offsets[k], 16), rows), :], sem.at[k]
                )
            )
            found[side][-1].start()
    return found


def slope_kernel(sides, *refs):
    (offsets, own_slope, other_slope, grad_mlp), refs = refs[:4], refs[4:]
    weights, refs = refs[: len(sides)], refs[len(sides) :]
    own_pre, other_pre, own_bias, other_bias, weight, pre, sem, out_sem = refs
    halves = start_halves(offsets, weights, sides, weight, sem)
    half = own_pre.shape[1]
    stores = []
    for side, (slope, pre_out, bias_out) in enumerate(
        ((own_slope, own_pre, own_bias), (other_slope, other_pre, other_bias))
    ):
        wait_all(halves[side])
        for lo, hi in spans(half, 768):
            grad_act = dot(grad_mlp[...], weight[side * half + lo : side * half + hi, :], NT)
            grad_pre = (grad_act * slope[:, lo:hi].astype(F32)).astype(BF)
            pre[side, :, lo:hi] = grad_pre
            here = pl.ds(lo, hi - lo)
            stores.append(
                pltpu.make_async_copy(
                    pre.at[side, :, here], pre_out.at[:, here], out_sem.at[len(stores)]
                )
            )
            stores[-1].start()
            bias_out[:, lo:hi] = jnp.sum(grad_pre.astype(F32), axis=0, keepdims=True)
    wait_all(stores)


def second_kernel(sides, blocks, cap, *refs):
    (offsets, own_act, other_act, grad_out, hidden, mod, slots), refs = refs[:7], refs[7:]
    weights, refs = refs[: len(sides)], refs[len(sides) :]
    onward, refs = refs[:4], refs[4:]
    outs, refs = refs[:blocks], refs[blocks:]
    (gate_grad, *onward_outs), refs = refs[:3], refs[3:]
    weight, sem = refs[:2]
    held, onward_sem = refs[2:6], refs[6]
    halves = start_halves(offsets, weights, sides, weight, sem)
    loads = start_onward(onward, held, onward_sem)
    half = own_act.shape[1]
    wait_all(halves[0])
    mlp = dot(own_act[...], weight[:half, :])
    wait_all(halves[1])
    mlp = mlp + dot(other_act[...], weight[half:, :])
    for latent in range(mod.shape[0]):
        rows = slice(latent * cap, (latent + 1) * cap)
        gate_grad[latent, :, :] = jnp.sum(
            grad_out[rows, :].astype(F32) * mlp[rows], axis=0, keepdims=True
        )
        block = (hidden[rows, :] + mod[latent, 5:6, :] * mlp[rows]).astype(BF)
        unpack_rows(slots, latent, block, outs)
    wait_all(end_onward(loads, held, onward_outs, onward_sem))


def hidden_kernel(pieces, first_pieces, cap, model, *refs):
    (first_at, offsets, parity, own_pre, other_pre, hidden_in, projected_in, grad_in, mod), refs = (
        refs[:9],
        refs[9:],
    )
    first_weights, refs = refs[:first_pieces], refs[first_pieces:]
    out_weights, refs = refs[:pieces], refs[pieces:]
    (grad_hidden_out, grad_proj_out, grad_att, mod_grads), refs = refs[:4], refs[4:]
    first, out_weight, hidden, projected, grad_out, grad_hidden, grad_proj = refs[:7]
    first_sem, out_sem, in_sem, store_sem = refs[7:]
    half = own_pre.shape[1]
    chunks = unit_chunks(parity, half)
    loads = start_chunks(first_at, first_weights, first, first_sem, chunks)
    later = [
        pltpu.make_async_copy(there, here, in_sem.at[i])
        for i, (there, here) in enumerate(
            ((hidden_in, hidden), (projected_in, projected), (grad_in, grad_out))
        )
    ]
    for one in later:
        one.start()
    last = start_pieces(offsets, out_weights, out_weight, out_sem, 3 * model, 4 * model)
    total = None
    for i, (side, lo, hi, cols) in enumerate(chunks):
        wait_all(loads[i])
        part = dot((own_pre, other_pre)[side][:, lo:hi], first[:, cols], NT)
        total = part if total is None else total + part
    wait_all(later)
    stores = []
    for latent in range(mod.shape[0]):
        rows = slice(latent * cap, (latent + 1) * cap)
        normed, inverse = normal(hidden[rows, :])
        grad_mixed = total[rows]
        mod_grads[latent, 0:1, :] = jnp.sum(grad_mixed, axis=0, keepdims=True)
        mod_grads[latent, 1:2, :] = jnp.sum(grad_mixed * normed, axis=0, keepdims=True)
        grad = grad_out[rows, :].astype(F32) + normal_back(
            grad_mixed * (1.0 + mod[latent, 4:5, :]), normed, inverse
        )
        grad_hidden[rows, :] = grad
        mod_grads[latent, 2:3, :] = jnp.sum(grad * projected[rows, :], axis=0, keepdims=True)
        grad_proj[rows, :] = (mod[latent, 2:3, :] * grad).astype(BF)
        here = pl.ds(latent * cap, cap)
        for held, out in ((grad_hidden, grad_hidden_out), (grad_proj, grad_proj_out)):
            stores.append(
                pltpu.make_async_copy(
                    held.at[here, :], out.at[here, :], store_sem.at[len(stores)]
                )
            )
            stores[-1].start()
    wait_all(last)
    grad_att[...] = dot(grad_proj[...], out_weight[...], NT).astype(BF)
    wait_all(stores)


def start_onward(ins, held, sem):
    loads = [pltpu.make_async_copy(a, b, sem.at[i]) for i, (a, b) in enumerate(zip(ins, held))]
    for one in loads:
        one.start()
    return loads


def end_onward(loads, held, outs, sem):
    keep_x, keep_y, far_x, far_y = held
    wait_all(loads)
    keep_x[...] = (keep_x[...].astype(F32) + far_y[...].astype(F32)).astype(BF)
    keep_y[...] = (keep_y[...].astype(F32) + far_x[...].astype(F32)).astype(BF)
    stores = [
        pltpu.make_async_copy(a, b, sem.at[4 + i]) for i, (a, b) in enumerate(zip(held[:2], outs))
    ]
    for one in stores:
        one.start()
    return stores


def attend_back_kernel(cap, model, *refs):
    (live, qkv, grad_att), onward, (grad_qkv, *onward_outs) = refs[:3], refs[3:7], refs[7:10]
    sums, held, onward_sem = refs[10], refs[11:15], refs[15]
    loads = start_onward(onward, held, onward_sem)
    sums[...] = jnp.zeros_like(sums)

    def one_latent(latent, carry):
        here = pl.ds(pl.multiple_of(latent * cap, 16), cap)
        count = live[latent]
        seen = lax.broadcasted_iota(jnp.int32, (cap, cap), 0) < count
        found = windows()
        for some in range(0, len(found), 4):
            heads = []
            for base, width, first in found[some : some + 4]:
                mask = head_mask(width, first, BF)
                cols = [slice(part + base, part + base + width) for part in (0, model, 2 * model)]
                query, key = qkv[here, cols[0]] * mask, qkv[here, cols[1]] * mask
                grad = grad_att[here, cols[0]] * mask
                heads.append(
                    (cols, query, key, grad, dot(key, query, NT), dot(qkv[here, cols[2]], grad, NT))
                )
            weights = []
            for _, _, _, _, scores, grad_probs in heads:
                scores = jnp.where(seen, scores, far_below)
                raised = jnp.exp2((scores - jnp.max(scores, axis=0, keepdims=True)) * exp2_scale)
                probs = raised * (1.0 / jnp.sum(raised, axis=0, keepdims=True))
                delta = jnp.sum(probs * grad_probs, axis=0, keepdims=True)
                weights.append(((probs * (grad_probs - delta)).astype(BF), probs.astype(BF)))
            for (cols, query, key, grad, _, _), (grad_scores, probs) in zip(heads, weights):
                sums[here, cols[0]] += dot(grad_scores, key, TN)
                sums[here, cols[1]] += dot(grad_scores, query)
                sums[here, cols[2]] += dot(probs, grad)
        return carry

    lax.fori_loop(0, live.shape[0], one_latent, 0)
    stores = end_onward(loads, held, onward_outs, onward_sem)
    grad_qkv[:, : 2 * model] = (sums[:, : 2 * model] * att_scale).astype(BF)
    grad_qkv[:, 2 * model :] = sums[:, 2 * model :].astype(BF)
    wait_all(stores)


def leave_kernel(pieces, blocks, cap, *refs):
    (
        offsets,
        parity,
        live,
        grad_qkv,
        packed,
        grad_hidden,
        mod,
        slots,
        mod_grads,
        gate_m,
        own_bias,
        other_bias,
    ), refs = refs[:12], refs[12:]
    weights, refs = refs[:pieces], refs[pieces:]
    outs, refs = refs[:blocks], refs[blocks:]
    payload, weight, rows_wide, sem = refs
    model = packed.shape[1]
    group, half = mod.shape[0], own_bias.shape[1]
    rows_wide[...] = jnp.zeros_like(rows_wide)
    lane = lax.broadcasted_iota(jnp.int32, (1, LANES), 1)
    kept = jnp.zeros((1, LANES), F32)
    for latent in range(group):
        at = slice(latent, latent + 1)
        rows_wide[at, 2 * model : 3 * model] = mod_grads[latent, 2:3, :]
        rows_wide[at, 3 * model : 4 * model] = mod_grads[latent, 0:1, :]
        rows_wide[at, 4 * model : 5 * model] = mod_grads[latent, 1:2, :]
        rows_wide[at, 5 * model :] = gate_m[latent]
        for digit in range(3):
            part = (live[latent] >> (3 * digit)) & 7
            kept = jnp.where(lane == 3 * latent + digit, part.astype(F32), kept)
    for side, bias in enumerate((own_bias, other_bias)):
        first = pl.multiple_of((parity[0] ^ side) * half, LANES)
        rows_wide[group : group + 1, pl.ds(first, half)] = bias[...]
    rows_wide[group : group + 1, 2 * half : 2 * half + LANES] = kept
    chunks = spans(weight.shape[1], model)
    loads = [
        start_pieces(offsets, weights, weight, sem.at[i], lo, hi) for i, (lo, hi) in enumerate(chunks)
    ]
    total = None
    for i, (lo, hi) in enumerate(chunks):
        wait_all(loads[i])
        part = dot(grad_qkv[:, lo:hi], weight[:, lo:hi], NT)
        total = part if total is None else total + part
    for latent in range(mod.shape[0]):
        rows = slice(latent * cap, (latent + 1) * cap)
        normed, inverse = normal(packed[rows, :].astype(F32))
        grad_mixed = total[rows]
        at = slice(latent, latent + 1)
        rows_wide[at, :model] = jnp.sum(grad_mixed, axis=0, keepdims=True)
        rows_wide[at, model : 2 * model] = jnp.sum(grad_mixed * normed, axis=0, keepdims=True)
        grad = grad_hidden[rows, :] + normal_back(
            grad_mixed * (1.0 + mod[latent, 1:2, :]), normed, inverse
        )
        unpack_rows(slots, latent, grad.astype(BF), outs)
    payload[...] = rows_wide[: group + 1, :].astype(BF)


def spread_kernel(corners, *refs):
    own, pair = refs[:corners], refs[corners : 2 * corners]
    (at, weight), refs = refs[2 * corners : 2 * corners + 2], refs[2 * corners + 2 :]
    cond_own, cond_pair, sent, kept, across, sums, rows, parts, wide_sums, sem = refs
    group = own[0].shape[0] - 1
    totals = []
    for q in range(corners):
        mine, theirs = own[q][...].astype(F32), pair[q][...].astype(F32)
        for side, wide in enumerate((mine, theirs)):
            first = (side * corners + q) * group
            rows[first : first + group, :] = wide[:group]
        totals.append(
            [
                sum(wide[latent : latent + 1] for latent in range(group))
                for wide in (mine, theirs)
            ]
            + [wide[group:] for wide in (mine, theirs)]
        )
    for i in range(2):
        by_corner = [one[2 * i] + one[2 * i + 1] for one in totals]
        while len(by_corner) > 1:
            by_corner = [a + b for a, b in zip(by_corner[::2], by_corner[1::2])]
        wide_sums[i : i + 1, :] = by_corner[0]
    low = rows[...].astype(BF)
    cond = dot(low, weight[...], NT)
    half = corners * group
    cond_own[...] = cond[:half]
    cond_pair[...] = cond[half:]
    count, _, width = parts.shape
    for j in range(count):
        cols = slice(j * width, (j + 1) * width)
        parts[j] = low[:, cols]
        for i in range(2):
            sums[count * i + j : count * i + j + 1, :] = wide_sums[i : i + 1, cols]
    copies = [
        pltpu.make_async_copy(parts.at[at[0] ^ k], out, sem.at[k])
        for k, out in ((1, sent.at[0]), (3, sent.at[1]), (0, kept), (2, across))
    ]
    for one in copies:
        one.start()
    wait_all(copies)


def by_columns(width):
    return width % (2 * LANES) == 0


def outer_kernel(rows, used, sides, *refs):
    block_at, refs = refs[0], refs[1:]
    total = sum(sides)
    lefts, refs = refs[: 2 * len(sides)], refs[2 * len(sides) :]
    rights, refs = refs[: 2 * total], refs[2 * total :]
    (far_x, far_y, near_x, near_y, keep, keep_x, keep_y), refs = refs[:7], refs[7:]
    result, sem = refs
    base, at = 0, 0
    for group, count in enumerate(sides):
        own_left, pair_left = lefts[2 * group : 2 * group + 2]
        left = jnp.concatenate([own_left[:, :used], pair_left[:, :used]], axis=0)
        for own, pair in zip(rights[2 * at : 2 * (at + count) : 2], rights[2 * at + 1 : 2 * (at + count) : 2]):
            width = own.shape[1]
            for lo, hi in spans(width, 768):
                right = jnp.concatenate([own[:, lo:hi], pair[:, lo:hi]], axis=0)
                result[:, base + lo : base + hi] = dot(left, right, TN).astype(BF)
            base += width
        at += count

    width = result.shape[1]

    def half_at(k, second):
        first = pl.multiple_of(block_at[k] * rows, 16)
        if by_columns(width):
            return result.at[pl.ds(first, rows), pl.ds(second * (width // 2), width // 2)]
        part, rest = halves_of(rows)
        return result.at[pl.ds(first + part, rest) if second else pl.ds(first, part), :]

    moves = [
        (half_at(3, 0), far_x),
        (half_at(3, 1), far_y),
        (half_at(1, 0), near_x),
        (half_at(2, 1), near_y),
        (result.at[pl.ds(pl.multiple_of(block_at[0] * rows, 16), rows), :], keep),
        (half_at(1, 1), keep_x),
        (half_at(2, 0), keep_y),
    ]
    copies = [pltpu.make_async_copy(a, b, sem.at[i]) for i, (a, b) in enumerate(moves)]
    for one in copies:
        one.start()
    wait_all(copies)


def reorder_kernel(unit, shard, whole):
    count = shard.shape[1] // unit
    for block in range(count):
        to = (block % 2) * (count // 2) + block // 2
        whole[:, to * unit : (to + 1) * unit] = shard[:, block * unit : (block + 1) * unit]


def fold_kernel(cuts, turned, *refs):
    (at, keep, near_top, near_bottom, far_top, far_bottom), refs = refs[:6], refs[6:]
    count = len(cuts[0])
    outs, refs = refs[: 3 * len(cuts)], refs[3 * len(cuts) :]
    scratch, sem = refs[:-1], refs[-1]
    wide = lambda ref: ref[...].astype(F32)
    near, far = (near_top, near_bottom), (far_top, far_bottom)
    columns = by_columns(keep.shape[1])
    axis = 1 if columns else 0
    cut = far_top.shape[axis]
    kept = (keep[:, :cut], keep[:, cut:]) if columns else (keep[:cut, :], keep[cut:, :])
    halves = [
        (one.astype(F32) + wide(a) + wide(b)).astype(BF) for one, a, b in zip(kept, near, far)
    ]
    whole = jnp.concatenate(halves, axis=axis)
    copies = []
    if turned:
        whole = whole.T
    for i, (group, parts) in enumerate(zip(cuts, scratch)):
        for j, pieces in enumerate(group):
            first = 0
            for lo, hi in pieces:
                if turned:
                    parts[j] = whole[lo:hi, :]
                else:
                    parts[j, :, first : first + hi - lo] = whole[:, lo:hi]
                first += hi - lo
        sent, own, across = outs[3 * i : 3 * i + 3]
        for k, out in ((1, sent.at[0]), (3, sent.at[1]), (0, own), (2, across)):
            copies.append(pltpu.make_async_copy(parts.at[at[0] ^ k], out, sem.at[len(copies)]))
    for one in copies:
        one.start()
    wait_all(copies)


def outer_pair(groups, rows, name):
    used = 4 * rows
    lefts = [v for left, _ in groups for v in left]
    rights = [v for _, pairs in groups for pair in pairs for v in pair]
    width = sum(v.shape[1] for v in rights) // 2
    sides = tuple(len(pairs) for _, pairs in groups)
    block_at = jnp.stack([(lax.axis_index("dp") ^ (2 * k)) // 2 for k in range(4)]).astype(jnp.int32)
    ins = [block_at, *lefts, *rights]
    part, rest = halves_of(rows)
    first, second = (part, width), (rest, width)
    if by_columns(width):
        first = second = (rows, width // 2)
    shapes = (first, second, first, second, (rows, width), second, first)
    outs = tuple(jax.ShapeDtypeStruct(shape, BF) for shape in shapes)
    return pl.pallas_call(
        functools.partial(outer_kernel, rows, used, sides),
        out_shape=outs,
        in_specs=[SMEM] + [VMEM] * (len(ins) - 1),
        out_specs=tuple(ANY for _ in outs),
        scratch_shapes=[pltpu.VMEM((used, width), BF), pltpu.SemaphoreType.DMA((7,))],
        name=name,
        compiler_params=pltpu.CompilerParams(vmem_limit_bytes=60 * 1024 * 1024),
    )(*ins)


def onward_kernel(keep_x, keep_y, far_x, far_y, on_x, on_y):
    on_x[...] = (keep_x[...].astype(F32) + far_y[...].astype(F32)).astype(BF)
    on_y[...] = (keep_y[...].astype(F32) + far_x[...].astype(F32)).astype(BF)


def onward(cut, far):
    keep_x, keep_y = cut[5:]
    outs = tuple(jax.ShapeDtypeStruct(v.shape, BF) for v in (keep_x, keep_y))
    ins = [keep_x, keep_y, *far]
    return call(onward_kernel, outs, ins, [VMEM] * 4, [], "onward")


def along_xy(pair):
    return swap(pair[0], "dp", 2), swap(pair[1], "dp", 4)


def fold(keep, near, last, cuts, name, turned=False):
    rows = keep.shape[0]
    count = lax.axis_size("seq")
    at = lax.axis_index("seq").reshape(1).astype(jnp.int32)
    widths = tuple(sum(hi - lo for lo, hi in group[0]) for group in cuts)
    blocks = [(w, rows) if turned else (rows, w) for w in widths]
    outs = tuple(
        jax.ShapeDtypeStruct(shape, BF) for block in blocks for shape in ((2,) + block, block, block)
    )
    return pl.pallas_call(
        functools.partial(fold_kernel, cuts, turned),
        out_shape=outs,
        in_specs=[SMEM] + [VMEM] * 5,
        out_specs=tuple(ANY for _ in outs),
        scratch_shapes=[pltpu.VMEM((count,) + block, BF) for block in blocks]
        + [pltpu.SemaphoreType.DMA((4 * len(cuts),))],
        name=name,
        compiler_params=pltpu.CompilerParams(vmem_limit_bytes=60 * 1024 * 1024),
    )(at, keep, near[0], near[1], last[1], last[0])


def plain_cuts(first, width, count):
    share = width // count
    return tuple(((first + j * share, first + (j + 1) * share),) for j in range(count))


def spread_plain(grad):
    grad = lax.psum_scatter(grad, "dp", scatter_dimension=0, tiled=True)
    return lax.psum_scatter(grad, "seq", scatter_dimension=1, tiled=True)


def body(
    latents,
    condition,
    keep_order,
    keep_count,
    ada_weight,
    ada_bias,
    qkv_weight,
    out_weight,
    fc1_weight,
    fc1_bias,
    fc2_weight,
    cotangent,
):
    latent_count, block_rows, model = latents.shape
    hidden_units = fc1_weight.shape[1]
    half_units = hidden_units // 2
    unit_rows = hidden_units // BLOCKS
    model_rows = model // BLOCKS
    dp_count, seq_count = lax.axis_size("dp"), lax.axis_size("seq")
    dp_at, seq_at = lax.axis_index("dp"), lax.axis_index("seq")
    group = latent_count // seq_count
    most = block_rows * 3 // 4
    cap = (seq_count - 1) * most + block_rows // 4
    rows_all = group * cap
    share = model // dp_count
    column_share = 6 * model // seq_count
    paired = dp_count == BLOCKS and seq_count == 4
    parity = (dp_at & 1) if paired else jnp.zeros_like(dp_at)
    parity_in = parity.reshape(1).astype(jnp.int32)
    part, _ = halves_of(model_rows)
    unit_part, _ = halves_of(unit_rows)
    whose = (lambda k: dp_at ^ k) if paired else (lambda k: jnp.int32(k))
    sds = jax.ShapeDtypeStruct
    dma = lambda n: pltpu.SemaphoreType.DMA((n,))
    fence = lambda *values: lax.optimization_barrier(values)

    def rank_of():
        slot = lax.broadcasted_iota(jnp.int32, (1, block_rows, 1), 1)
        token = lax.broadcasted_iota(jnp.int32, (1, 1, block_rows), 2)
        found = (keep_order[:, :, None] == token) & (slot < keep_count[:, :, None])
        return jnp.max(jnp.where(found, slot, -1), axis=1)

    def places_of(ranks):
        ranks = lax.dynamic_slice_in_dim(ranks, seq_at * group, group, 1)
        ranks = jnp.swapaxes(ranks, 0, 1)
        counts = jnp.sum((ranks >= 0).astype(jnp.int32), axis=2)
        starts = jnp.cumsum(counts, axis=1) - counts
        live = jnp.sum(counts, axis=1).astype(jnp.int32)
        place = jnp.where(ranks >= 0, ranks + starts[:, :, None], -1).reshape(
            group, seq_count * block_rows
        )
        slot = lax.broadcasted_iota(jnp.int32, (1, 1, most), 2)
        slots = jnp.where(slot < counts[:, :, None], starts[:, :, None] + slot, -1)
        return live, place[:, None, :], slots.reshape(group, seq_count * most, 1)

    def whole_slice(blocks_in, k):
        return lax.dynamic_slice_in_dim(blocks_in, (seq_at ^ k) * group, group, 0)

    rank = rank_of()

    def run_home(pieces, base, dtype, name):
        return call(
            home_kernel,
            sds((latent_count, block_rows, model), dtype),
            [seq_at.reshape(1).astype(jnp.int32), rank[:, :, None], base, *pieces],
            [SMEM] + [VMEM] * (2 + seq_count),
            [],
            name,
        )

    cond_wide = condition.astype(F32)
    silu_cond = jax.nn.silu(cond_wide).astype(BF)
    silu_parts = in_order(
        jnp.swapaxes(silu_cond.reshape(latent_count, dp_count, share), 0, 1), "dp"
    )

    def silu_of(rows):
        mine = lax.dynamic_slice_in_dim(rows, seq_at * group, group, 1)
        groups = rows.reshape(dp_count, seq_count, group, share)
        return mine, in_order(jnp.swapaxes(groups, 0, 1), "seq")


    def partial_mod(silu_rows):
        return jnp.dot(
            silu_rows.reshape(dp_count * group, share), ada_weight, preferred_element_type=F32
        ).reshape(dp_count, group, 6 * model)

    def whole_mod(total):
        return (total + ada_bias.astype(F32)).reshape(group, 6, model)

    unit_order = lambda v: jnp.swapaxes(
        v.reshape(v.shape[0], BLOCKS // 2, 2, unit_rows), 1, 2
    ).reshape(v.shape[0], hidden_units)
    bias_row = unit_order(fc1_bias.astype(F32)[None])

    pad = -(-(model // 2) // LANES) * LANES

    def order_of(parity):
        column = lax.broadcasted_iota(jnp.int32, (1, 2 * pad), 1)
        side, inner = column // pad, column % pad
        source = (2 * (inner // model_rows) + (parity ^ side)) * model_rows + inner % model_rows
        source = jnp.where(inner < model // 2, source, -1)
        return (lax.broadcasted_iota(jnp.int32, (model, 1), 0) == source).astype(BF)

    model_position = lambda k: whose(k)
    unit_position = lambda k: ((whose(k) & 1) ^ parity) * (BLOCKS // 2) + whose(k) // 2

    def run_enter(joint, place_row, mod, pieces, order):
        weights, offsets = joint
        return call(
            functools.partial(enter_kernel, len(weights), seq_count, cap),
            (
                sds((rows_all, model), BF),
                sds((rows_all, 3 * model), BF),
                sds((rows_all, pad), BF),
                sds((rows_all, pad), BF),
            ),
            [
                offsets,
                place_row,
                mod,
                order,
                *pieces,
                *weights,
            ],
            [SMEM, VMEM, VMEM, VMEM] + [VMEM] * seq_count + [ANY] * len(weights),
            [
                pltpu.VMEM((model, 3 * model), BF),
                pltpu.VMEM((rows_all, model), BF),
                pltpu.SemaphoreType.DMA((3, len(weights))),
            ],
            "enter",
        )

    def run_cot(place_row, mod, cot_pieces):
        low = sds((rows_all, model), BF)
        ins = [place_row, mod, *cot_pieces]
        return call(functools.partial(cot_kernel, cap), (low, low), ins, [VMEM] * len(ins), [], "cotangent")

    def run_attend(joint, live, qkv, packed, mod, order):
        weights, offsets = joint
        return call(
            functools.partial(attend_kernel, len(weights), cap, model),
            (
                sds((rows_all, pad), BF),
                sds((rows_all, pad), BF),
                sds((rows_all, model), F32),
                sds((rows_all, model), F32),
                sds((rows_all, model), BF),
                sds((rows_all, pad), BF),
                sds((rows_all, pad), BF),
            ),
            [
                offsets,
                live,
                qkv,
                packed,
                mod,
                order,
                *weights,
            ],
            [SMEM, SMEM, VMEM, VMEM, VMEM, VMEM] + [ANY] * len(weights),
            [
                pltpu.VMEM((model, model), BF),
                pltpu.VMEM((rows_all, model), F32),
                dma(len(weights)),
            ],
            "attend",
        )

    def run_first(first, mixed):
        weights, offsets = first
        half_rows = sds((rows_all, half_units), BF)
        chunks = 2 * len(spans(half_units, 768))
        return call(
            functools.partial(first_kernel, len(weights)),
            (half_rows,) * 4,
            [offsets, parity_in, mixed, bias_row, *weights],
            [SMEM, SMEM, VMEM, VMEM] + [ANY] * len(weights),
            [
                pltpu.VMEM((model, hidden_units), BF),
                pltpu.VMEM((2, rows_all, half_units), BF),
                pltpu.VMEM((2, rows_all, half_units), BF),
                pltpu.SemaphoreType.DMA((chunks, len(weights))),
                dma(chunks),
                dma(chunks),
            ],
            "first",
            (ANY,) * 4,
        )

    def run_slope(second, slopes, grad_mlp):
        weights, offsets, sides = second
        half_rows = sds((rows_all, half_units), BF)
        return call(
            functools.partial(slope_kernel, sides),
            (half_rows, half_rows, sds((1, half_units), F32), sds((1, half_units), F32)),
            [offsets, *slopes, grad_mlp, *weights],
            [SMEM] + [VMEM] * 3 + [ANY] * len(weights),
            [
                pltpu.VMEM((hidden_units, model), BF),
                pltpu.VMEM((2, rows_all, half_units), BF),
                dma(len(weights)),
                dma(2 * len(spans(half_units, 768))),
            ],
            "slope",
            (ANY, ANY, VMEM, VMEM),
        )

    def onward_parts(cut, far):
        ins = [cut[5], cut[6], *far]
        return (
            ins,
            tuple(sds(v.shape, BF) for v in ins[:2]),
            [pltpu.VMEM(v.shape, BF) for v in ins] + [dma(6)],
        )

    def run_second(second, acts, grad_out, hidden, mod, slots, cut, far):
        weights, offsets, sides = second
        ins, outs, scratch = onward_parts(cut, far)
        result = call(
            functools.partial(second_kernel, sides, seq_count, cap),
            tuple(sds((group, most, model), BF) for _ in range(seq_count))
            + (sds((group, 1, model), F32),)
            + outs,
            [offsets, *acts, grad_out, hidden, mod, slots, *weights, *ins],
            [SMEM] + [VMEM] * 6 + [ANY] * (len(weights) + 4),
            [pltpu.VMEM((hidden_units, model), BF), dma(len(weights))] + scratch,
            "second",
            (VMEM,) * (seq_count + 1) + (ANY, ANY),
        )
        return result[:seq_count], result[seq_count], result[seq_count + 1 :]

    def run_hidden(first, joint, pres, hidden, projected, grad_out, mod):
        (weights, offsets), (first_w, first_at) = joint, first
        wide, low = sds((rows_all, model), F32), sds((rows_all, model), BF)
        return call(
            functools.partial(hidden_kernel, len(weights), len(first_w), cap, model),
            (wide, low, low, sds((group, 3, model), F32)),
            [
                first_at,
                offsets,
                parity_in,
                *pres,
                hidden,
                projected,
                grad_out,
                mod,
                *first_w,
                *weights,
            ],
            [SMEM, SMEM, SMEM, VMEM, VMEM, ANY, ANY, ANY, VMEM]
            + [ANY] * (len(first_w) + len(weights)),
            [
                pltpu.VMEM((model, hidden_units), BF),
                pltpu.VMEM((model, model), BF),
                pltpu.VMEM((rows_all, model), F32),
                pltpu.VMEM((rows_all, model), F32),
                pltpu.VMEM((rows_all, model), BF),
                pltpu.VMEM((rows_all, model), F32),
                pltpu.VMEM((rows_all, model), BF),
                pltpu.SemaphoreType.DMA((2 * len(spans(half_units, 768)), len(first_w))),
                dma(len(weights)),
                dma(3),
                dma(2 * group),
            ],
            "hidden_back",
            (ANY, ANY, VMEM, VMEM),
        )

    def run_attend_back(live, qkv, grad_att, cut, far):
        ins, outs, scratch = onward_parts(cut, far)
        grad_qkv, *on = call(
            functools.partial(attend_back_kernel, cap, model),
            (sds((rows_all, 3 * model), BF),) + outs,
            [live, qkv, grad_att, *ins],
            [SMEM, VMEM, VMEM] + [ANY] * 4,
            [pltpu.VMEM((rows_all, 3 * model), F32)] + scratch,
            "attend_back",
            (VMEM, ANY, ANY),
        )
        return grad_qkv, on

    def run_leave(
        joint, grad_qkv, packed, grad_hidden, mod, slots, live, mod_grads, gate_m, biases
    ):
        weights, offsets = joint
        result = call(
            functools.partial(leave_kernel, len(weights), seq_count, cap),
            tuple(sds((group, most, model), BF) for _ in range(seq_count))
            + (sds((group + 1, 6 * model), BF),),
            [
                offsets,
                parity_in,
                live,
                grad_qkv,
                packed,
                grad_hidden,
                mod,
                slots,
                mod_grads,
                gate_m,
                *biases,
                *weights,
            ],
            [SMEM, SMEM, SMEM] + [VMEM] * 9 + [ANY] * len(weights),
            [
                pltpu.VMEM((model, 3 * model), BF),
                pltpu.VMEM((8, 6 * model), F32),
                pltpu.SemaphoreType.DMA((3, len(weights))),
            ],
            "leave",
        )
        return result[:seq_count], result[seq_count]

    def split_sums(sums):
        units = jnp.swapaxes(
            sums[1, :hidden_units].reshape(2, BLOCKS // 2, unit_rows), 0, 1
        ).reshape(hidden_units)
        digits = sums[1, hidden_units : hidden_units + 3 * group].reshape(group, 3)
        kept = jnp.sum(digits * jnp.array([1.0, 8.0, 64.0], F32))
        return sums[0], units, kept.reshape(1).astype(jnp.int32)

    def sums_of(gathered):
        wide = gathered.astype(F32)
        total = jnp.stack([jnp.sum(wide[:, :group], axis=1), wide[:, group]], axis=1)
        while total.shape[0] > 1:
            total = total.reshape((total.shape[0] // 2, 2) + total.shape[1:])
            total = total[:, 0] + total[:, 1]
        return total[0]

    def seq_columns(grad_mod_all):
        return in_order(
            jnp.stack(
                [
                    grad_mod_all[:, :, j * column_share : (j + 1) * column_share]
                    for j in range(seq_count)
                ]
            ),
            "seq",
        )

    def cond_product(grad_mod_all):
        return dot(grad_mod_all.reshape(dp_count * group, 6 * model), ada_weight, NT).reshape(
            dp_count, group, share
        )

    def ada_product(silu_all, columns):
        return dot(
            silu_all.reshape(seq_count * dp_count * group, share),
            columns.reshape(seq_count * dp_count * group, column_share),
            TN,
        )

    def cond_end(rows):
        rows = in_order(rows, "seq").reshape(latent_count, model)
        _, silu_back = jax.vjp(jax.nn.silu, cond_wide)
        return silu_back(rows)[0]

    def cond_mine_of(cols):
        return jnp.swapaxes(in_order(cols, "dp"), 0, 1).reshape(group, model)

    if not paired:
        order = order_of(parity)
        live, place_row, slots = places_of(gather_all(rank, "seq"))
        silu_rows, silu_all = silu_of(trade_all(silu_parts, "dp"))
        mod = whole_mod(sum_own(partial_mod(silu_rows), "dp"))
        to_whole = lambda v: [
            swap(whole_slice(v, k), "seq", k) if k else whole_slice(v, k)
            for k in range(seq_count)
        ]
        latent_pieces, cot_pieces = to_whole(latents), to_whole(cotangent)
        joint = whole_weight(jnp.concatenate([qkv_weight, out_weight], axis=1))
        joint = [joint], jnp.zeros((1,), jnp.int32)
        first = [whole_weight(unit_order(fc1_weight))], jnp.zeros((1,), jnp.int32)
        full = whole_weight(fc2_weight)
        second = placed(
            [(full[k * unit_rows : (k + 1) * unit_rows], k, 0) for k in range(BLOCKS)],
            unit_position,
            unit_rows,
        ) + (tuple(k & 1 for k in range(BLOCKS)),)
        packed, qkv, *mixa = run_enter(joint, place_row, mod, latent_pieces, order)
        grad_out, grad_mlp = run_cot(place_row, mod, cot_pieces)
        att_own, att_other, projected, hidden, mixed, *mixm = run_attend(
            joint, live, qkv, packed, mod, order
        )
        acts = run_first(first, mixed)
        *pres, bias_own, bias_other = run_slope(second, acts[2:], grad_mlp)
        none = [jnp.zeros((16, LANES), BF)] * 7
        block_pieces, gate_m_grad, _ = run_second(
            second, acts[:2], grad_out, hidden, mod, slots, none, none[:2]
        )
        grad_hidden, grad_proj, grad_att, mod_grads = run_hidden(
            first, joint, pres, hidden, projected, grad_out, mod
        )
        grad_qkv, _ = run_attend_back(live, qkv, grad_att, none, none[:2])
        latent_grads, payload = run_leave(
            joint,
            grad_qkv,
            packed,
            grad_hidden,
            mod,
            slots,
            live,
            mod_grads,
            gate_m_grad,
            (bias_own, bias_other),
        )
        gathered = gather_all(payload, "dp")
        grad_mod_all = gathered[:, :group]
        sums = sums_of(gathered)
        for step in steps_of("seq"):
            sums = sums + swap(sums, "seq", step)
        ada_bias_grad, fc1_bias_grad, kept_total = split_sums(sums)
        ada_grad = ada_product(silu_all, trade_all(seq_columns(grad_mod_all), "seq"))
        cond_cols = trade_all(cond_product(grad_mod_all), "dp")
        condition_grad = cond_end(gather_all(cond_mine_of(cond_cols), "seq"))

        def mixed_sides(own, other, width):
            both = jnp.stack([own[:, : 4 * width], other[:, : 4 * width]], axis=1)
            return jnp.swapaxes(both.reshape(rows_all, 2, 4, width), 1, 2).reshape(
                rows_all, BLOCKS * width
            )

        product = lambda a, b: spread_plain(dot(a, b, TN))
        fc2_grad = product(mixed_sides(acts[0], acts[1], unit_rows), grad_mlp)
        fc1_grad = product(
            mixed_sides(*mixm, model_rows), mixed_sides(pres[0], pres[1], unit_rows)
        )
        out_grad = product(mixed_sides(att_own, att_other, model_rows), grad_proj)
        qkv_grad = product(mixed_sides(*mixa, model_rows), grad_qkv)
        home = lambda pieces: [swap(v, "seq", k) if k else v for k, v in enumerate(pieces)]
        block_out = run_home(home(block_pieces), latents, BF, "home_out")
        latents_grad = run_home(home(latent_grads), cotangent, F32, "home_grad")
        return (
            block_out,
            latents_grad,
            condition_grad,
            ada_grad,
            ada_bias_grad,
            qkv_grad,
            out_grad,
            fc1_grad,
            fc1_bias_grad,
            fc2_grad,
            kept_total,
        )

    def trade(value, axis, step):
        split = value.reshape((-1, 2, step) + value.shape[1:])
        return jnp.stack([split[:, 0], swap(split[:, 1], axis, step)], axis=1).reshape(value.shape)

    def grow(value, axis, step):
        return jnp.concatenate([value, swap(value, axis, step)], axis=0)

    def columns_first(parts):
        sent, own, across = parts
        return swap(sent, "seq", 1), own, across

    def columns_second(state):
        near, own, across = state
        on = (across.astype(F32) + near[1].astype(F32)).astype(BF)
        return swap(on, "seq", 2), own, near

    def columns_sum(state):
        far, own, near = state
        return own.astype(F32) + near[0].astype(F32) + far.astype(F32)

    def tails(beside, first):
        rows, width = beside[0].shape
        return call(
            functools.partial(cut_kernel, first),
            (sds((first, width), BF), sds((rows - first, width), BF)),
            [beside[1], beside[0]],
            [ANY, ANY],
            [pltpu.VMEM((first, width), BF), pltpu.VMEM((rows - first, width), BF), dma(2), dma(2)],
            "cut",
            (ANY, ANY),
        )

    joint_own = jnp.concatenate([qkv_weight, out_weight], axis=1)

    corners_of = lambda value: [swap(value[q], "dp", 2 * q) for q in (1, 2, 3)]

    corners = silu_parts.reshape(4, 2, latent_count, share)
    corners = jnp.stack([corners[0], *corners_of(corners)])
    ranks = grow(rank[None], "seq", 1)
    corners, joint_own, fc1_in, latents_in, cot_in, ranks, parity_late = fence(
        corners, joint_own, fc1_weight, latents, cotangent, ranks, parity
    )

    joint_beside = beside_of(joint_own)
    ranks = grow(ranks, "seq", 2)
    latent_pieces = [whole_slice(latents_in, k) for k in range(seq_count)]
    latent_1 = swap(latent_pieces[1], "seq", 1)
    latent_2 = swap(latent_pieces[2], "seq", 2)
    silu_corners = trade(corners.reshape(8, latent_count, share), "dp", 1)
    silu_rows, silu_all = silu_of(silu_corners)
    silu_all = jnp.swapaxes(silu_all.reshape(seq_count, 4, 2, group, share), 1, 2)
    pairs = partial_mod(silu_rows).reshape(4, 2, group, 6 * model)
    corners = pairs[:, 0] + swap(pairs[:, 1], "dp", 1)
    parity_late, fc1_in, cot_in = after((parity_late, fc1_in, cot_in), corners)
    order = order_of(parity_late)
    first_own = call(
        functools.partial(reorder_kernel, unit_rows),
        sds(fc1_in.shape, BF),
        [fc1_in],
        [VMEM],
        [],
        "reorder",
    )
    cot_pieces = [whole_slice(cot_in, k) for k in range(seq_count)]
    (
        joint_beside,
        latent_1,
        latent_2,
        latent_last,
        silu_all,
        corners,
        joint_own,
        order,
        first_own,
        cot_pieces,
        ranks,
    ) = fence(
        joint_beside,
        latent_1,
        latent_2,
        latent_pieces[3],
        silu_all,
        corners,
        joint_own,
        order,
        first_own,
        cot_pieces,
        ranks,
    )

    sums = corners_of(corners)
    joint_tails = tails(joint_beside, part)
    sums, joint_tails, joint_beside, joint_own, ranks, latent_last = fence(
        sums, joint_tails, joint_beside, joint_own, ranks, latent_last
    )
    joint_across = (swap(joint_tails[0], "dp", 2), swap(joint_tails[1], "dp", 4))
    mod = whole_mod(sum(sums, corners[0]))
    joint_pair, joint_x_pair, joint_y_pair = pair_of((joint_own, *joint_beside))
    latent_3 = swap(after(latent_last, joint_pair), "seq", 3)
    live, place_row, slots = places_of(ranks)
    (
        joint_across,
        latent_3,
        mod,
        joint_pair,
        joint_x_pair,
        joint_y_pair,
        live,
        place_row,
        slots,
        first_own,
        cot_pieces,
    ) = fence(
        joint_across,
        latent_3,
        mod,
        joint_pair,
        joint_x_pair,
        joint_y_pair,
        live,
        place_row,
        slots,
        first_own,
        cot_pieces,
    )

    first_beside = beside_of(first_own)
    cot_1 = swap(cot_pieces[1], "seq", 1)
    cot_2 = swap(cot_pieces[2], "seq", 2)
    cot_3 = swap(cot_pieces[3], "seq", 3)
    joint = placed(
        pieces_of(
            joint_own,
            joint_pair,
            joint_beside,
            (joint_x_pair, joint_y_pair),
            joint_across,
            pair_of(joint_across),
            part,
        ),
        model_position,
        model_rows,
    )
    packed, qkv, mixa_own, mixa_other = run_enter(
        joint, place_row, mod, (latent_pieces[0], latent_1, latent_2, latent_3), order
    )
    att_own, att_other, projected, hidden, mixed, mixm_own, mixm_other = run_attend(
        joint, live, qkv, packed, mod, order
    )
    first_beside, cot_1, cot_2, cot_3, mixed, first_own = fence(
        first_beside, cot_1, cot_2, cot_3, mixed, first_own
    )

    first_tails = tails(first_beside, part)
    first_across = (swap(first_tails[0], "dp", 2), swap(first_tails[1], "dp", 4))
    first_pair, first_x_pair, first_y_pair = pair_of((first_own, *first_beside))
    grad_out, grad_mlp = run_cot(place_row, mod, (cot_pieces[0], cot_1, cot_2, cot_3))
    second_own = (fc2_weight[:unit_part], fc2_weight[unit_part:])
    (
        first_across,
        first_pair,
        first_x_pair,
        first_y_pair,
        grad_out,
        grad_mlp,
        second_own,
        second_in,
    ) = fence(
        first_across,
        first_pair,
        first_x_pair,
        first_y_pair,
        grad_out,
        grad_mlp,
        second_own,
        fc2_weight,
    )

    second_ahead = swap(second_own[1], "dp", 2), swap(second_own[0], "dp", 4)
    first = placed(
        pieces_of(
            first_own,
            first_pair,
            first_beside,
            (first_x_pair, first_y_pair),
            first_across,
            pair_of(first_across),
            part,
        ),
        model_position,
        model_rows,
    )
    (grad_mlp_pair,) = pair_of((grad_mlp,))
    acts = run_first(first, mixed)
    second_ahead, second_own, grad_mlp_pair, acts = fence(
        second_ahead, second_own, grad_mlp_pair, acts
    )

    second_behind = swap(second_own[0], "dp", 2), swap(second_own[1], "dp", 4)
    (second_pair,) = pair_of((second_in,))
    (act_pair,) = pair_of((acts[1],))
    fc2_cut = outer_pair(
        [((acts[0], act_pair), [(grad_mlp, grad_mlp_pair)])], unit_rows, "fc2_grad"
    )
    second_behind, second_pair, second_ahead, fc2_cut, mixm_other, att_other, mixa_other = fence(
        second_behind, second_pair, second_ahead, fc2_cut, mixm_other, att_other, mixa_other
    )

    second_across = swap(second_ahead[1], "dp", 2), swap(second_ahead[0], "dp", 4)
    second_ahead_pair, second_behind_pair = pair_of(second_ahead), pair_of(second_behind)
    mixm_pair, att_pair, mixa_pair = pair_of((mixm_other, att_other, mixa_other))
    (
        second_across,
        second_ahead_pair,
        second_behind_pair,
        mixm_pair,
        att_pair,
        mixa_pair,
        fc2_cut,
        acts,
    ) = fence(
        second_across,
        second_ahead_pair,
        second_behind_pair,
        mixm_pair,
        att_pair,
        mixa_pair,
        fc2_cut,
        acts,
    )

    fc2_far = along_xy(fc2_cut[:2])
    pieces = [(second_in, 0, 0), (second_pair, 1, 0)]
    for side, ahead, behind, beyond in (
        (0, second_ahead, second_behind, second_across),
        (1, second_ahead_pair, second_behind_pair, pair_of(second_across)),
    ):
        pieces += [
            (behind[0], 2 + side, 0),
            (ahead[0], 2 + side, unit_part),
            (ahead[1], 4 + side, 0),
            (behind[1], 4 + side, unit_part),
            (beyond[0], 6 + side, 0),
            (beyond[1], 6 + side, unit_part),
        ]
    second = placed(pieces, unit_position, unit_rows) + (tuple(k & 1 for _, k, _ in pieces),)
    pre_own, pre_other, bias_own, bias_other = run_slope(second, acts[2:], grad_mlp)
    fc2_far, fc2_cut, pre_own, pre_other, acts = fence(
        fc2_far, fc2_cut, pre_own, pre_other, acts
    )

    fc2_near = along_xy(fc2_cut[2:4])
    pre_other_pair, pre_own_pair = pair_of((pre_own, pre_other))
    block_pieces, gate_m_grad, on = run_second(
        second, acts[:2], grad_out, hidden, mod, slots, fc2_cut, fc2_far
    )
    fc2_near, on, pre_other_pair, pre_own_pair, block_pieces, gate_m_grad = fence(
        fc2_near, on, pre_other_pair, pre_own_pair, block_pieces, gate_m_grad
    )

    fc2_last = along_xy(on)
    block_1 = swap(block_pieces[1], "seq", 1)
    block_2 = swap(block_pieces[2], "seq", 2)
    fc1_cut = outer_pair(
        [((mixm_own, mixm_pair), [(pre_own, pre_own_pair), (pre_other, pre_other_pair)])],
        model_rows,
        "fc1_grad",
    )
    fc2_last, block_1, block_2, block_3, fc1_cut, pre_own, pre_other, fc2_near = fence(
        fc2_last, block_1, block_2, block_pieces[3], fc1_cut, pre_own, pre_other, fc2_near
    )

    fc1_far = along_xy(fc1_cut[:2])
    block_3 = swap(block_3, "seq", 3)
    grad_hidden, grad_proj, grad_att, mod_grads = run_hidden(
        first, joint, (pre_own, pre_other), hidden, projected, grad_out, mod
    )
    fc1_far, fc1_cut, grad_proj, grad_att, block_3, fc2_near, fc2_last = fence(
        fc1_far, fc1_cut, grad_proj, grad_att, block_3, fc2_near, fc2_last
    )

    fc1_near = along_xy(fc1_cut[2:4])
    (proj_pair,) = pair_of((grad_proj,))
    fc2_parts = fold(
        fc2_cut[4],
        fc2_near,
        fc2_last,
        (plain_cuts(0, model, seq_count),),
        "fc2_fold",
        True,
    )
    grad_qkv, on = run_attend_back(after(live, fc2_parts), qkv, grad_att, fc1_cut, fc1_far)
    fc1_near, on, fc2_parts, proj_pair, grad_qkv = fence(
        fc1_near, on, fc2_parts, proj_pair, grad_qkv
    )

    fc1_last = along_xy(on)
    (qkv_pair,) = pair_of((grad_qkv,))
    fc2_state = columns_first(fc2_parts)
    latent_grads, payload = run_leave(
        joint,
        grad_qkv,
        packed,
        grad_hidden,
        mod,
        slots,
        live,
        mod_grads,
        gate_m_grad,
        (bias_own, bias_other),
    )
    fc1_last, qkv_pair, latent_grads, payload, fc1_near, grad_qkv, fc2_state = fence(
        fc1_last, qkv_pair, latent_grads, payload, fc1_near, grad_qkv, fc2_state
    )

    corners = [payload] + [swap(payload, "dp", 2 * q) for q in (1, 2, 3)]
    latent_1 = swap(latent_grads[1], "seq", 1)
    latent_2 = swap(latent_grads[2], "seq", 2)
    last_cut = outer_pair(
        [
            ((mixa_own, mixa_pair), [(grad_qkv, qkv_pair)]),
            ((att_own, att_pair), [(grad_proj, proj_pair)]),
        ],
        model_rows,
        "last_grad",
    )
    corners, latent_1, latent_2, last_cut, fc1_last, block_pieces, fc2_state = fence(
        corners, latent_1, latent_2, last_cut, fc1_last, block_pieces, fc2_state
    )

    last_far = along_xy(last_cut[:2])
    corner_pairs = pair_of(corners)
    fc1_cuts = tuple(
        tuple((lo, lo + unit_rows) for lo in (j * unit_rows, half_units + j * unit_rows))
        for j in range(seq_count)
    )
    fc1_parts = fold(fc1_cut[4], fc1_near, fc1_last, (fc1_cuts,), "fc1_fold")
    fc2_state = columns_second(fc2_state)
    rows_here = 8 * group
    cond_own, cond_pair, column_sent, column_own, column_across, sums = call(
        functools.partial(spread_kernel, 4),
        (
            sds((rows_here // 2, share), F32),
            sds((rows_here // 2, share), F32),
            sds((2, rows_here, column_share), BF),
            sds((rows_here, column_share), BF),
            sds((rows_here, column_share), BF),
            sds((2 * seq_count, column_share), F32),
        ),
        [*corners, *corner_pairs, seq_at.reshape(1).astype(jnp.int32), ada_weight],
        [VMEM] * 8 + [SMEM, VMEM],
        [
            pltpu.VMEM((rows_here, 6 * model), F32),
            pltpu.VMEM((seq_count, rows_here, column_share), BF),
            pltpu.VMEM((8, 6 * model), F32),
            dma(seq_count),
        ],
        "spread",
        (VMEM, VMEM, ANY, ANY, ANY, VMEM),
    )
    (
        last_far,
        last_cut,
        cond_own,
        cond_pair,
        column_sent,
        sums,
        fc1_parts,
        block_pieces,
        latent_3,
        fc2_state,
    ) = fence(
        last_far,
        last_cut,
        cond_own,
        cond_pair,
        column_sent,
        sums,
        fc1_parts,
        block_pieces,
        latent_grads[3],
        fc2_state,
    )

    last_near = along_xy(last_cut[2:4])
    on = onward(last_cut, last_far)
    (cond_pair,) = pair_of((cond_pair,))
    sums = sums.astype(BF)
    column_sent = jnp.concatenate([column_sent, jnp.stack([sums, sums])], axis=1)
    fc1_state = columns_first(fc1_parts)
    latent_3 = swap(latent_3, "seq", 3)
    block_out = run_home(
        after((block_pieces[0], block_1, block_2, block_3), on), latents, BF, "home_out"
    )
    last_near, on, sums, column_sent, cond_pair, fc1_state, latent_3, block_out = fence(
        last_near, on, sums, column_sent, cond_pair, fc1_state, latent_3, block_out
    )

    last_last = along_xy(on)
    fc1_state = columns_second(fc1_state)
    column_near = swap(column_sent, "seq", 1)
    (
        last_last,
        sums,
        column_near,
        fc1_state,
        fc2_state,
        last_near,
        cond_own,
        cond_pair,
        latent_3,
    ) = fence(
        last_last,
        sums,
        column_near,
        fc1_state,
        fc2_state,
        last_near,
        cond_own,
        cond_pair,
        latent_3,
    )

    qkv_share, out_share = 3 * model // seq_count, model // seq_count
    last_cuts = tuple(
        (
            (j * qkv_share, (j + 1) * qkv_share),
            (3 * model + j * out_share, 3 * model + (j + 1) * out_share),
        )
        for j in range(seq_count)
    )
    last_parts = fold(last_cut[4], last_near, last_last, (last_cuts,), "last_fold")
    last_state = columns_first(last_parts)
    cond_own, cond_pair = after((cond_own, cond_pair), last_parts)
    cond_cols = jnp.stack([cond_own, cond_pair], axis=1).reshape(4, group, 2, share)
    cond_cols = jnp.swapaxes(cond_cols, 1, 2)
    cond_cols = jnp.stack([cond_cols[0], *corners_of(cond_cols)])
    cond_mine = cond_mine_of(cond_cols.reshape(8, group, share))
    cond_rows = [swap(cond_mine, "seq", k) if k else cond_mine for k in range(seq_count)]
    condition_grad = cond_end(jnp.stack(cond_rows))
    sums, column_near, fc1_state, fc2_state = after(
        (sums, column_near, fc1_state, fc2_state), cond_mine
    )
    sums = (sums.astype(F32) + column_near[0, rows_here:].astype(F32)).astype(BF)
    column_far = swap(
        jnp.stack([jnp.concatenate([column_across, sums], axis=0), column_near[1]]), "seq", 2
    )
    sums = sums.astype(F32) + column_far[0, rows_here:].astype(F32)
    column_far, column_near = column_far[:, :rows_here], column_near[:, :rows_here]
    columns = jnp.stack([column_own, column_near[0], column_far[0], column_far[1]])
    ada_grad = ada_product(silu_all, columns)
    fc2_grad = columns_sum(fc2_state).T
    fc1_grad = columns_sum(fc1_state)
    fc1_grad = jnp.where(
        parity == 1,
        jnp.concatenate([fc1_grad[:, unit_rows:], fc1_grad[:, :unit_rows]], axis=1),
        fc1_grad,
    )
    last_state, condition_grad, sums, ada_grad, fc1_grad, fc2_grad, latent_3 = fence(
        last_state, condition_grad, sums, ada_grad, fc1_grad, fc2_grad, latent_3
    )

    latents_grad = run_home(
        (latent_grads[0], latent_1, latent_2, latent_3), cotangent, F32, "home_grad"
    )
    far, own, near = columns_second(last_state)
    qkv_grad = columns_sum((far[:, :qkv_share], own[:, :qkv_share], near[:, :, :qkv_share]))
    out_grad = columns_sum((far[:, qkv_share:], own[:, qkv_share:], near[:, :, qkv_share:]))
    ada_bias_grad, fc1_bias_grad, kept_total = split_sums(sums.reshape(2, 6 * model))
    return (
        block_out,
        latents_grad,
        condition_grad,
        ada_grad,
        ada_bias_grad,
        qkv_grad,
        out_grad,
        fc1_grad,
        fc1_bias_grad,
        fc2_grad,
        kept_total,
    )


def solution(mesh):
    placed = (
        P("dp", "seq", None),
        P("dp", None),
        P("dp", "seq"),
        P("dp", "seq"),
        P("dp", None),
        P(),
        P("dp", None),
        P("dp", None),
        P("dp", None),
        P(),
        P("dp", None),
        P("dp", "seq", None),
    )
    return jax.shard_map(
        body,
        mesh=mesh,
        in_specs=placed,
        out_specs=(
            P("dp", "seq", None),
            P("dp", "seq", None),
            P("dp", None),
            P("dp", "seq"),
            P(),
            P("dp", "seq"),
            P("dp", "seq"),
            P("dp", "seq"),
            P(),
            P("dp", "seq"),
            P(),
        ),
        check_vma=False,
    )
```
